32 devices in a mesh: width: 4 (over y, x), shard: 8 (over z, core).
Axes of the slice: x: 2, y: 2, z: 4, core: 2. Of those that a mesh axis runs over, the one named last changes fastest.
Arguments:
- layer_input: bfloat16 [32768, 768], P(('width', 'shard')), may hold values from -6 to 6
- segment_ids: int32 [64, 512], P(('width', 'shard')), may hold values from 0 to 3, never falling along the last dimension, each value on 1 to 256 neighbouring positions
- group_heads: int32 [4], P('width'), may hold values from 3 to 12, as said below
- w_query: float32 [768, 768], P('shard'), may hold values from -0.21875 to 0.21875
- b_query: float32 [768], P('shard'), may hold values from -3 to 3
- w_key: float32 [768, 768], P('shard'), may hold values from -0.21875 to 0.21875
- w_value: float32 [768, 768], P('shard'), may hold values from -0.21875 to 0.21875
- b_value: float32 [768], P('shard'), may hold values from -3 to 3
- w_out: float32 [768, 768], P('shard'), may hold values from -1.75 to 1.75
- b_out: float32 [768], P('shard'), may hold values from -2 to 2
- gain_one: float32 [768], P('shard'), may hold values from 0.25 to 1.75
- shift_one: float32 [768], P('shard'), may hold values from -2 to 2
- w_inner: float32 [768, 3072], P('shard'), may hold values from -0.21875 to 0.21875
- b_inner: float32 [3072], P('shard'), may hold values from -3 to 3
- w_outer: float32 [3072, 768], P('shard'), may hold values from -0.21875 to 0.21875
- b_outer: float32 [768], P('shard'), may hold values from -2 to 2
- gain_two: float32 [768], P('shard'), may hold values from 0.25 to 1.75
- shift_two: float32 [768], P('shard'), may hold values from -2 to 2
- out_grad: bfloat16 [32768, 768], P(('width', 'shard')), may hold values from -6 to 6
Outputs:
- layer_output: bfloat16 [32768, 768], P(('width', 'shard'))
- input_grad: bfloat16 [32768, 768], P(('width', 'shard'))
- w_query_grad: float32 [768, 768], P('shard')
- b_query_grad: float32 [768], P('shard')
- w_key_grad: float32 [768, 768], P('shard')
- w_value_grad: float32 [768, 768], P('shard')
- b_value_grad: float32 [768], P('shard')
- w_out_grad: float32 [768, 768], P('shard')
- b_out_grad: float32 [768], P('shard')
- gain_one_grad: float32 [768], P('shard')
- shift_one_grad: float32 [768], P('shard')
- w_inner_grad: float32 [768, 3072], P('shard')
- b_inner_grad: float32 [3072], P('shard')
- w_outer_grad: float32 [3072, 768], P('shard')
- b_outer_grad: float32 [768], P('shard')
- gain_two_grad: float32 [768], P('shard')
- shift_two_grad: float32 [768], P('shard')
The draws below stay inside these ranges and needn't reach their ends.
Inputs may be any that keep to these rules, and one draw needn't show every extreme that they name: `group_heads`: the 4 groups keep 1, 2, 3 and 4 times 12 // 4 leading heads, each multiple on exactly one group, and 256 leading neurons for each kept head. `segment_ids`: within each row of 512 tokens the ids never fall; a token attends only to tokens of its own row with its own id.
All inputs are finite; a program needn't handle non-finite values.
Results may differ from the reference program's by a relative error of at most 0.017.
The reference program's roundings to bfloat16 on the way count: a program that leaves them out, or rounds other values in their place, can miss the bound.
Values may be sent and summed in bfloat16 or wider, within the bound.
A program may use at most 192 MiB of HBM per device.

```python
import math
import jax
import jax.numpy as jnp
import numpy as np
from jax import lax

HEADS = 12
HEAD_DIM = 64
FF = 3072
D = 768
SEQ = 512
ROWS = 64
TOKENS = 32768
N_WIDTH = 4


def draw_group_heads(key, part):
    key = jax.random.fold_in(key, 7)
    order = jax.random.permutation(key, N_WIDTH)
    return (HEADS // N_WIDTH * (order + 1)).astype(jnp.int32)


def steps_of(stream_key, shape, shards, low, top_value):
    level = 1.0
    for position, blocks in shards:
        heights = jax.random.uniform(jax.random.fold_in(jax.random.fold_in(stream_key, 6), position), (blocks,), jnp.float32, low / len(shards), top_value / len(shards))
        level = level * jnp.repeat(jnp.exp(heights), shape[position] // blocks).reshape((-1,) + (1,) * (len(shape) - 1 - position))
    return level


def length_profile(count, total, reach, skew):
    weights = [(1 << 20) // math.isqrt(standing ** skew) + 1 for standing in range(2, count + 1)]
    rest, given = total - reach - (count - 1), [1] * (count - 1)
    while rest > 0:
        free = [i for i in range(count - 1) if given[i] < reach]
        pool, remaining = sum([weights[i] for i in free]), rest
        for i in free:
            more = min(reach - given[i], max(1, remaining * weights[i] // pool), rest)
            given[i] = given[i] + more
            rest = rest - more
    return np.array([reach] + given)


def ragged_sizes(rng, number_of, total, bound, skew):
    if number_of == 2:
        one = jax.random.randint(rng, (), max(1, total - bound), min(bound, total - 1) + 1)
        return jnp.stack([one, total - one])
    tallies = jnp.asarray(length_profile(number_of, total, bound, skew), jnp.int32)
    pairs = (number_of - 1) // 2
    source_of, receiver = tallies[1:1 + 2 * pairs:2], tallies[2:2 + 2 * pairs:2]
    room = jnp.minimum(source_of - 1, bound - receiver)
    moved = jax.random.randint(jax.random.fold_in(rng, 1), (pairs,), 0, 1 << 20) % (room + 1)
    tallies = tallies.at[1:1 + 2 * pairs:2].set(source_of - moved).at[2:2 + 2 * pairs:2].set(receiver + moved)
    return tallies[jax.random.permutation(jax.random.fold_in(rng, 2), number_of)]


def centred(stream_key, extent, scale, most, cuts=(), dtype=jnp.bfloat16):
    entries = scale * jax.random.normal(stream_key, extent, jnp.float32)
    if cuts:
        entries = entries * steps_of(stream_key, extent, cuts, -0.22, 0.18)
    return jnp.clip(entries, -most, most).astype(dtype)


def setup_inputs(seed: int = 0) -> dict:
    arg_keys = jax.random.split(jax.random.key(seed), 20)
    return {
        "layer_input": centred(arg_keys[0], (TOKENS, D), 1.0, 6.0, ((0, 32),)),
        "segment_ids": jax.vmap(lambda own: jnp.searchsorted(jnp.cumsum(ragged_sizes(own, 4, SEQ, SEQ // 2, 0)), jnp.arange(SEQ), side="right"))(jax.random.split(arg_keys[1], ROWS)).reshape((ROWS, SEQ)).astype(jnp.int32),
        "group_heads": draw_group_heads(jax.random.fold_in(arg_keys[19], 71), 0),
        "w_query": centred(arg_keys[3], (D, D), D ** -0.5, 0.21875, ((0, 8),), jnp.float32),
        "b_query": centred(arg_keys[4], (D,), 0.5, 3.0, ((0, 8),), jnp.float32),
        "w_key": centred(arg_keys[5], (D, D), D ** -0.5, 0.21875, ((0, 8),), jnp.float32),
        "w_value": centred(arg_keys[6], (D, D), D ** -0.5, 0.21875, ((0, 8),), jnp.float32),
        "b_value": centred(arg_keys[7], (D,), 0.5, 3.0, ((0, 8),), jnp.float32),
        "w_out": centred(arg_keys[8], (D, D), (D // 64) ** -0.5, 1.75, ((0, 8),), jnp.float32),
        "b_out": centred(arg_keys[9], (D,), 0.3, 2.0, ((0, 8),), jnp.float32),
        "gain_one": jnp.clip(1.0 + 0.15 * jax.random.normal(arg_keys[10], (D,), jnp.float32), 0.25, 1.75),
        "shift_one": centred(arg_keys[11], (D,), 0.3, 2.0, ((0, 8),), jnp.float32),
        "w_inner": centred(arg_keys[12], (D, FF), D ** -0.5, 0.21875, ((0, 8),), jnp.float32),
        "b_inner": centred(arg_keys[13], (FF,), 0.5, 3.0, ((0, 8),), jnp.float32),
        "w_outer": centred(arg_keys[14], (FF, D), (FF // 4) ** -0.5, 0.21875, ((0, 8),), jnp.float32),
        "b_outer": centred(arg_keys[15], (D,), 0.3, 2.0, ((0, 8),), jnp.float32),
        "gain_two": jnp.clip(1.0 + 0.15 * jax.random.normal(arg_keys[16], (D,), jnp.float32), 0.25, 1.75),
        "shift_two": centred(arg_keys[17], (D,), 0.3, 2.0, ((0, 8),), jnp.float32),
        "out_grad": centred(arg_keys[18], (TOKENS, D), 1.0, 6.0, ((0, 32),)),
    }


@jax.custom_vjp
def low(v):
    return lax.optimization_barrier(v.astype(jnp.bfloat16)).astype(jnp.float32)

@jax.custom_vjp
def low_back(v):
    return v

def low_keep(v):
    return (low(v), None)

def low_pass(kept, grad):
    return (grad,)

def back_keep(v):
    return (v, None)

def back_low(kept, grad):
    return (low(grad),)
low.defvjp(low_keep, low_pass)
low_back.defvjp(back_keep, back_low)
HIGH = lax.Precision.HIGHEST

def norm_rows(total, gain, shift):
    row_mean = lax.optimization_barrier(jnp.mean(total, axis=-1, keepdims=True))
    centered = total - row_mean
    variance = lax.optimization_barrier(jnp.mean(centered * centered, axis=-1, keepdims=True))
    return centered * lax.rsqrt(variance + 1e-06) * gain + shift

def layer_row(params, inputs, segment_row, kept_heads):
    w_query, b_query, w_key, w_value, b_value, w_out, b_out, gain_one, shift_one, w_inner, b_inner, w_outer, b_outer, gain_two, shift_two = params
    head_mask = (jnp.arange(D) // HEAD_DIM < kept_heads).astype(jnp.float32)
    unit_mask = (jnp.arange(FF) // (FF // HEADS) < kept_heads).astype(jnp.float32)
    queries = low(low_back(jnp.dot(inputs, w_query, precision=HIGH) + b_query)).reshape(SEQ, HEADS, HEAD_DIM)
    keys = low(low_back(jnp.dot(inputs, w_key, precision=HIGH))).reshape(SEQ, HEADS, HEAD_DIM)
    values = low(low_back(jnp.dot(inputs, w_value, precision=HIGH) + b_value)).reshape(SEQ, HEADS, HEAD_DIM)
    scores = low_back(jnp.einsum('qhd,khd->hqk', queries, keys, precision=HIGH) * HEAD_DIM ** (-0.5))
    same_doc = segment_row[:, None] == segment_row[None, :]
    scores = jnp.where(same_doc[None], scores, -1e+30)
    probs = low(jax.nn.softmax(scores, axis=-1))
    attended = jnp.einsum('hqk,khd->qhd', probs, values, precision=HIGH).reshape(SEQ, D)
    attended = low_back(low(attended * head_mask))
    branch = low_back(jnp.dot(attended, w_out, precision=HIGH) + b_out)
    hidden = norm_rows(inputs + branch, gain_one, shift_one)
    inner = low_back(jnp.dot(low(hidden), w_inner, precision=HIGH) + b_inner)
    active = low(jax.nn.gelu(inner, approximate=False) * unit_mask)
    outer = low_back(jnp.dot(active, w_outer, precision=HIGH) + b_outer)
    return norm_rows(hidden + outer, gain_two, shift_two)

def reference(layer_input, segment_ids, group_heads, w_query, b_query, w_key, w_value, b_value, w_out, b_out, gain_one, shift_one, w_inner, b_inner, w_outer, b_outer, gain_two, shift_two, out_grad):
    heads_per_row = jnp.repeat(group_heads, ROWS // N_WIDTH)

    def forward(params, inputs):
        rounded = tuple((low(item) for item in params))
        rows_in = inputs.reshape(ROWS, SEQ, D)
        checked = jax.checkpoint(layer_row)

        def one_row(parts):
            return checked(rounded, parts[0], parts[1], parts[2])
        result = lax.map(one_row, (rows_in, segment_ids, heads_per_row))
        return result.reshape(TOKENS, D)
    params = (w_query, b_query, w_key, w_value, b_value, w_out, b_out, gain_one, shift_one, w_inner, b_inner, w_outer, b_outer, gain_two, shift_two)
    output, pullback = jax.vjp(forward, params, layer_input.astype(jnp.float32))
    param_grads, input_grad = pullback(out_grad.astype(jnp.float32))
    return (output.astype(jnp.bfloat16), input_grad.astype(jnp.bfloat16), param_grads[0], param_grads[1], param_grads[2], param_grads[3], param_grads[4], param_grads[5], param_grads[6], param_grads[7], param_grads[8], param_grads[9], param_grads[10], param_grads[11], param_grads[12], param_grads[13], param_grads[14])
```

```python
import functools
import jax
import jax.numpy as jnp
from jax import lax
from jax.experimental import pallas as pl
from jax.experimental.pallas import tpu as pltpu
from jax.sharding import PartitionSpec as P

HEADS = 12
HEAD_DIM = 64
FF = 3072
D = 768
SEQ = 512
MESH = pl.DeviceIdType.MESH
BF = jnp.bfloat16
F32 = jnp.float32
TR = 96
HR = 48


def places():
    w = lax.axis_index("width")
    s = lax.axis_index("shard")
    return dict(
        w=w,
        s=s,
        c=lax.rem(s, 2),
        z=lax.div(s, 2),
        sib=s + 1 - 2 * lax.rem(s, 2),
        xw=w + 1 - 2 * lax.rem(w, 2),
        yw=lax.rem(w + 2, 4),
        dw=3 - w,
        zp=lax.rem(s + 2, 8),
        zm=lax.rem(s + 6, 8),
        zo=lax.rem(s + 4, 8),
    )


class Copies:
    def __init__(self, send, recv):
        self.send, self.recv, self.count, self.all = send, recv, 0, []

    def start(self, src, dst, device):
        k = self.count
        self.count += 1
        copy = pltpu.make_async_remote_copy(
            src_ref=src,
            dst_ref=dst,
            send_sem=self.send.at[k],
            recv_sem=self.recv.at[k],
            device_id=device,
            device_id_type=MESH,
        )
        copy.start()
        self.all.append(copy)
        return copy

    def finish(self):
        for copy in self.all:
            copy.wait_send()


def greet(devices):
    barrier = pltpu.get_barrier_semaphore()
    for device in devices:
        pl.semaphore_signal(barrier, inc=1, device_id=device, device_id_type=MESH)
    pl.semaphore_wait(barrier, len(devices))


def partners(p):
    out = [(p["xw"], p["s"]), (p["yw"], p["s"]), (p["dw"], p["s"])]
    for k in range(1, 8):
        out.append((p["w"], lax.rem(p["s"] + k, 8)))
    return out


GATHER_COPIES = 67


def slot(m, full, q, s):
    return full.at[s, q] if m == 2 else full.at[q, s]


def slots(m, full, s):
    return full.at[s] if m == 2 else full.at[:, s]


def gather_kernel(wq, wk, wv, wo, wi, wr, vec, fa, fi, fo, fv, own, ssem, rsem, lsem):
    p = places()
    w, s = p["w"], p["s"]
    full = (fa, fi, fo)
    for q, ref in enumerate((wq, wk, wv, wo)):
        own[0, q] = ref[...].astype(BF)
    for q in range(4):
        own[1, q] = wi[:, q * D : (q + 1) * D].astype(BF)
        own[2, q] = wr[q * TR : (q + 1) * TR, :].astype(BF)
    greet(partners(p))
    cp = Copies(ssem, rsem)
    xdev, ydev = (p["xw"], s), (p["yw"], s)
    zpdev, zmdev, sib = (w, p["zp"]), (w, p["zm"]), (w, p["sib"])
    got = {}
    for m in range(3):
        got[m, "zm"] = cp.start(own.at[m, w], slot(m, full[m], w, s), zpdev)
        got[m, "zp"] = cp.start(own.at[m, w], slot(m, full[m], w, s), zmdev)
        got[m, "c"] = cp.start(own.at[m], slots(m, full[m], s), sib)
    vcopies = [
        cp.start(vec, fv.at[s], (w, lax.rem(s + k, 8))) for k in range(1, 8)
    ]
    local = [pltpu.make_async_copy(own.at[m], slots(m, full[m], s), lsem.at[m]) for m in range(3)]
    local.append(pltpu.make_async_copy(vec, fv.at[s], lsem.at[3]))
    for copy in local:
        copy.start()

    def half(ref, top):
        return ref.at[0:HR] if top else ref.at[HR:TR]

    def to_plane(m, name):
        tile = slot(m, full[m], w, p[name])
        got[m, name, "x"] = cp.start(tile, tile, xdev)
        got[m, name, "y"] = cp.start(tile, tile, ydev)

    def stage1(m):
        got[m, "zm"].wait_recv()
        tile = half(slot(m, full[m], w, p["zm"]), True)
        got[m, "top"] = cp.start(tile, tile, zpdev)
        to_plane(m, "zm")
        got[m, "zp"].wait_recv()
        tile = half(slot(m, full[m], w, p["zp"]), False)
        got[m, "bot"] = cp.start(tile, tile, zmdev)
        to_plane(m, "zp")

    def stage2(m):
        got[m, "top"].wait_recv()
        got[m, "bot"].wait_recv()
        to_plane(m, "zo")

    def stage3(m):
        for name in ("zm", "zp", "zo"):
            got[m, name, "x"].wait_recv()
            tile = half(slot(m, full[m], p["xw"], p[name]), True)
            got[m, name, "dy"] = cp.start(tile, tile, ydev)
            got[m, name, "y"].wait_recv()
            tile = half(slot(m, full[m], p["yw"], p[name]), False)
            got[m, name, "dx"] = cp.start(tile, tile, xdev)

    def stage4(m):
        for name in ("zm", "zp", "zo"):
            got[m, name, "dy"].wait_recv()
            got[m, name, "dx"].wait_recv()
            block = slots(m, full[m], p[name])
            got[m, name, "c"] = cp.start(block, block, sib)

    stage1(0)
    stage1(1)
    stage2(0)
    stage1(2)
    stage2(1)
    stage3(0)
    stage2(2)
    stage3(1)
    stage4(0)
    stage3(2)
    stage4(1)
    stage4(2)
    for m in range(3):
        got[m, "c"].wait_recv()
        for name in ("zm", "zp", "zo"):
            got[m, name, "c"].wait_recv()
    for copy in vcopies:
        copy.wait_recv()
    for copy in local:
        copy.wait()
    cp.finish()
    assert cp.count == GATHER_COPIES, cp.count


def gather_fast(wq, wk, wv, wo, wi, wr, vec):
    vm = pl.BlockSpec(memory_space=pltpu.VMEM)
    anyspace = pl.BlockSpec(memory_space=pl.ANY)
    return pl.pallas_call(
        gather_kernel,
        out_shape=(
            jax.ShapeDtypeStruct((4, 8, TR, D), BF),
            jax.ShapeDtypeStruct((4, 8, TR, D), BF),
            jax.ShapeDtypeStruct((8, 4, TR, D), BF),
            jax.ShapeDtypeStruct((8, 16, D), BF),
        ),
        in_specs=[vm] * 7,
        out_specs=(anyspace,) * 4,
        scratch_shapes=[
            pltpu.VMEM((3, 4, TR, D), BF),
            pltpu.SemaphoreType.DMA((GATHER_COPIES,)),
            pltpu.SemaphoreType.DMA((GATHER_COPIES,)),
            pltpu.SemaphoreType.DMA((4,)),
        ],
        compiler_params=pltpu.CompilerParams(
            collective_id=0, has_side_effects=True, vmem_limit_bytes=60 << 20
        ),
        name="gather",
    )(wq, wk, wv, wo, wi, wr, vec)


REDUCE_COPIES = 6 + 3 * 15 + 7


def reduce_kernel(
    gq, gk, gv, go, gi, gr, gvec,
    oq, ok, ov, oo, oi, our, ovec,
    held, landed, dx, dy, rx, ry, qz, dzp, dzm, rzp, rzm, outb,
    vheld, vrecv, vplane, vz,
    ssem, rsem, lsem,
):
    p = places()
    w, s, c, z = p["w"], p["s"], p["c"], p["z"]
    greet(partners(p))
    cp = Copies(ssem, rsem)
    xdev, ydev, ddev = (p["xw"], s), (p["yw"], s), (p["dw"], s)
    zpdev, zmdev, sib = (w, p["zp"]), (w, p["zm"]), (w, p["sib"])
    zp, zm, zo = lax.rem(z + 1, 4), lax.rem(z + 3, 4), lax.rem(z + 2, 4)
    got = {}
    local = {}

    def half_of(m, core):
        if m == 0:
            return [(g.at[:, core], (0, q)) for q, g in enumerate((gq, gk, gv, go))]
        if m == 1:
            return [(gi.at[:, :, core], (1,))]
        return [(gr.at[:, core], (2,))]

    count = 0
    order = (2, 1, 0)
    got["v", "c"] = cp.start(gvec.at[:, 1 - c], vrecv, sib)
    for m in order:
        got[m, "c"] = []
        local[m] = []
        for src, at in half_of(m, 1 - c):
            got[m, "c"].append(cp.start(src, landed.at[at], sib))
        for src, at in half_of(m, c):
            copy = pltpu.make_async_copy(src, held.at[at], lsem.at[count])
            copy.start()
            local[m].append(copy)
            count += 1

    def quarter(m, q, rows=slice(None)):
        return (m, slice(None), q, rows) if m == 2 else (m, q, slice(None), rows)

    TOP, BOT = slice(0, HR), slice(HR, TR)

    def add_pair(m):
        for copy in local[m]:
            copy.wait()
        for copy in got[m, "c"]:
            copy.wait_recv()

        def one(i, _):
            for j in range(4):
                held[m, i, j] = (held[m, i, j].astype(F32) + landed[m, i, j].astype(F32)).astype(BF)
            return 0

        lax.fori_loop(0, 4, one, 0)

    def plane1(m):
        got[m, "dx"] = cp.start(held.at[quarter(m, p["dw"], TOP)], dx.at[m], xdev)
        got[m, "dy"] = cp.start(held.at[quarter(m, p["dw"], BOT)], dy.at[m], ydev)
        got[m, "x1"] = cp.start(held.at[quarter(m, p["xw"], TOP)], rx.at[m, :, TOP], xdev)
        got[m, "y1"] = cp.start(held.at[quarter(m, p["yw"], BOT)], ry.at[m, :, BOT], ydev)

    def plane2(m):
        got[m, "dx"].wait_recv()
        at = quarter(m, p["yw"], TOP)
        held[at] = (held[at].astype(F32) + dx[m].astype(F32)).astype(BF)
        got[m, "y2"] = cp.start(held.at[at], ry.at[m, :, TOP], ydev)
        got[m, "dy"].wait_recv()
        at = quarter(m, p["xw"], BOT)
        held[at] = (held[at].astype(F32) + dy[m].astype(F32)).astype(BF)
        got[m, "x2"] = cp.start(held.at[at], rx.at[m, :, BOT], xdev)

    def plane3(m):
        for name in ("x1", "y1", "x2", "y2"):
            got[m, name].wait_recv()
        qz[m] = (held[quarter(m, w)].astype(F32) + rx[m].astype(F32) + ry[m].astype(F32)).astype(BF)

    def ring1(m):
        got[m, "dzp"] = cp.start(qz.at[m, zo, TOP], dzp.at[m], zpdev)
        got[m, "dzm"] = cp.start(qz.at[m, zo, BOT], dzm.at[m], zmdev)
        got[m, "p1"] = cp.start(qz.at[m, zp, BOT], rzp.at[m, BOT], zpdev)
        got[m, "m1"] = cp.start(qz.at[m, zm, TOP], rzm.at[m, TOP], zmdev)

    def ring2(m):
        got[m, "dzp"].wait_recv()
        qz[m, zp, TOP] = (qz[m, zp, TOP].astype(F32) + dzp[m].astype(F32)).astype(BF)
        got[m, "p2"] = cp.start(qz.at[m, zp, TOP], rzp.at[m, TOP], zpdev)
        got[m, "dzm"].wait_recv()
        qz[m, zm, BOT] = (qz[m, zm, BOT].astype(F32) + dzm[m].astype(F32)).astype(BF)
        got[m, "m2"] = cp.start(qz.at[m, zm, BOT], rzm.at[m, BOT], zmdev)

    def ring3(m):
        for name in ("p1", "m1", "p2", "m2"):
            got[m, name].wait_recv()
        outb[m, w] = (qz[m, z].astype(F32) + rzp[m].astype(F32) + rzm[m].astype(F32)).astype(BF)
        tile = outb.at[m, w]
        got[m, "gx"] = cp.start(tile, tile, xdev)
        got[m, "gy"] = cp.start(tile, tile, ydev)
        got[m, "gd"] = cp.start(tile, tile, ddev)

    def last(m):
        for name in ("gx", "gy", "gd"):
            got[m, name].wait_recv()
        if m == 0:
            for q, ref in enumerate((oq, ok, ov, oo)):
                ref[...] = outb[0, q].astype(F32)
        for q in range(4):
            if m == 1:
                oi[:, q * D : (q + 1) * D] = outb[1, q].astype(F32)
            if m == 2:
                our[q * TR : (q + 1) * TR, :] = outb[2, q].astype(F32)

    def vec_plane():
        got["v", "c"].wait_recv()
        vheld[...] = gvec[:, c] + vrecv[...]
        vplane[w] = vheld[...]
        got["v", "plane"] = [cp.start(vheld, vplane.at[w], d) for d in (xdev, ydev, ddev)]

    def vec_ring():
        for copy in got["v", "plane"]:
            copy.wait_recv()
        vheld2 = (vplane[0] + vplane[1]) + (vplane[2] + vplane[3])
        vheld[...] = vheld2
        vz[z] = vheld[z]
        got["v", "z"] = [
            cp.start(vheld.at[t], vz.at[z], (w, 2 * t + c)) for t in (zp, zm, zo)
        ]

    def vec_last():
        for copy in got["v", "z"]:
            copy.wait_recv()
        ovec[...] = (vz[0] + vz[1]) + (vz[2] + vz[3])

    a, b, d = order
    add_pair(a)
    plane1(a)
    add_pair(b)
    plane1(b)
    add_pair(d)
    plane1(d)
    vec_plane()
    plane2(a)
    plane2(b)
    plane3(a)
    ring1(a)
    plane2(d)
    plane3(b)
    ring1(b)
    ring2(a)
    for copy in got["v", "plane"]:
        copy.wait_send()
    cp.all = [copy for copy in cp.all if all(copy is not other for other in got["v", "plane"])]
    vec_ring()
    plane3(d)
    ring1(d)
    ring3(a)
    ring2(b)
    ring3(b)
    ring2(d)
    last(a)
    ring3(d)
    last(b)
    vec_last()
    last(d)
    cp.finish()
    assert cp.count == REDUCE_COPIES, cp.count


def reduce_fast(gq, gk, gv, go, gi, gr, gvec):
    vm = pl.BlockSpec(memory_space=pltpu.VMEM)
    anyspace = pl.BlockSpec(memory_space=pl.ANY)
    square = (4, 2, TR, D)
    return pl.pallas_call(
        reduce_kernel,
        out_shape=tuple(jax.ShapeDtypeStruct((TR, D), F32) for _ in range(4))
        + (
            jax.ShapeDtypeStruct((TR, FF), F32),
            jax.ShapeDtypeStruct((FF // 8, D), F32),
            jax.ShapeDtypeStruct((8, D), F32),
        ),
        in_specs=[anyspace] * 6 + [vm],
        out_specs=(vm,) * 7,
        scratch_shapes=[
            pltpu.VMEM((3, 4, 4, TR, D), BF),
            pltpu.VMEM((3, 4, 4, TR, D), BF),
            pltpu.VMEM((3, 4, HR, D), BF),
            pltpu.VMEM((3, 4, HR, D), BF),
            pltpu.VMEM((3, 4, TR, D), BF),
            pltpu.VMEM((3, 4, TR, D), BF),
            pltpu.VMEM((3, 4, TR, D), BF),
            pltpu.VMEM((3, HR, D), BF),
            pltpu.VMEM((3, HR, D), BF),
            pltpu.VMEM((3, TR, D), BF),
            pltpu.VMEM((3, TR, D), BF),
            pltpu.VMEM((3, 4, TR, D), BF),
            pltpu.VMEM((4, 8, D), F32),
            pltpu.VMEM((4, 8, D), F32),
            pltpu.VMEM((4, 4, 8, D), F32),
            pltpu.VMEM((4, 8, D), F32),
            pltpu.SemaphoreType.DMA((REDUCE_COPIES,)),
            pltpu.SemaphoreType.DMA((REDUCE_COPIES,)),
            pltpu.SemaphoreType.DMA((6,)),
        ],
        compiler_params=pltpu.CompilerParams(
            collective_id=1, has_side_effects=True, vmem_limit_bytes=60 << 20
        ),
        name="reduce",
    )(
        gq.reshape(square), gk.reshape(square), gv.reshape(square), go.reshape(square),
        gi.reshape((4,) + square), gr.reshape((4, 2, 4, TR, D)), gvec.reshape((4, 2, 8, D)),
    )

def kernels_fit():
    return lax.axis_size("width") == 4 and lax.axis_size("shard") == 8


def gather(wq, wk, wv, wo, wi, wr, eight, b_inner):
    if kernels_fit():
        vec = jnp.pad(
            jnp.stack([jnp.concatenate(eight), jnp.pad(b_inner, (0, D - FF // 8))]), ((0, 14), (0, 0))
        ).astype(BF)
        fa, fi, fo, fv = gather_fast(wq, wk, wv, wo, wi, wr, vec)
        fa, fi, fo = fa.reshape(4, D, D), fi.reshape(4, D, D), fo.reshape(FF, D)
        rows = fv[:, 0].reshape(8, 8, TR).astype(F32)
        vectors = tuple(rows[:, k].reshape(D) for k in range(8))
        return (*(fa[q] for q in range(4)), fi, fo, vectors, fv[:, 1, : FF // 8].reshape(FF).astype(F32))

    def whole(a):
        return lax.all_gather(a.astype(BF), "shard", axis=0, tiled=True)

    fi = whole(wi)
    fi = jnp.stack([fi[:, q * D : (q + 1) * D] for q in range(4)])
    vectors = tuple(whole(a).astype(F32) for a in eight)
    return (whole(wq), whole(wk), whole(wv), whole(wo), fi, whole(wr), vectors, whole(b_inner).astype(F32))


def reduce(gq, gk, gv, go, gi, gr, eight, b_inner):
    if kernels_fit():
        first = jnp.stack([a.reshape(8, TR) for a in eight], axis=1).reshape(8, 1, D)
        second = jnp.pad(b_inner.reshape(8, 1, FF // 8), ((0, 0), (0, 0), (0, D - FF // 8)))
        vec = jnp.pad(jnp.concatenate([first, second], axis=1), ((0, 0), (0, 6), (0, 0)))
        *matrices, ovec = reduce_fast(gq, gk, gv, go, gi, gr, vec)
        vectors = tuple(ovec[0, k * TR : (k + 1) * TR] for k in range(8))
        return matrices, vectors, ovec[1, : FF // 8]

    def owned(a):
        a = lax.psum_scatter(a, "shard", scatter_dimension=0, tiled=True)
        return lax.psum(a.astype(BF), "width").astype(F32)

    gi = jnp.concatenate([gi[q] for q in range(4)], axis=1)
    matrices = tuple(owned(a.astype(F32)) for a in (gq, gk, gv, go, gi, gr))
    return matrices, tuple(owned(a) for a in eight), owned(b_inner)


def to_half(value):
    return value.astype(jnp.bfloat16)


def norm_parts(total):
    row_mean = jnp.mean(total, axis=-1, keepdims=True)
    centered = total - row_mean
    inverse = lax.rsqrt(jnp.mean(centered * centered, axis=-1, keepdims=True) + 1e-06)
    return (centered * inverse, inverse)


def norm_back(grad_normed, normed, inverse):
    first = jnp.mean(grad_normed, axis=-1, keepdims=True)
    second = jnp.mean(grad_normed * normed, axis=-1, keepdims=True)
    return inverse * (grad_normed - first - normed * second)


def row_scores(query_row, key_row, segment_row, score_scale):
    scores = (
        jnp.einsum("qhd,khd->hqk", query_row, key_row, preferred_element_type=jnp.float32)
        * score_scale
    )
    same_doc = segment_row[:, None] == segment_row[None, :]
    return jnp.where(same_doc[None], scores, -1e30)


def column_sum(value):
    return jnp.sum(value.astype(jnp.float32), axis=0)


def weight_grad(left, right):
    return jnp.einsum("ti,tj->ij", left, right, preferred_element_type=jnp.float32)


def back_product(grad_rows, weight):
    return jnp.einsum("tj,ij->ti", grad_rows, weight, preferred_element_type=jnp.float32)


def forward_product(rows_in, weight):
    return jnp.dot(rows_in, weight, preferred_element_type=jnp.float32)


def body(
    layer_input,
    segment_ids,
    group_heads,
    w_query,
    b_query,
    w_key,
    w_value,
    b_value,
    w_out,
    b_out,
    gain_one,
    shift_one,
    w_inner,
    b_inner,
    w_outer,
    b_outer,
    gain_two,
    shift_two,
    out_grad,
):
    score_scale = HEAD_DIM ** (-0.5)
    kept_heads = group_heads[0]
    head_mask = (jnp.arange(D) // HEAD_DIM < kept_heads).astype(jnp.float32)
    unit_mask = (jnp.arange(FF) // (FF // HEADS) < kept_heads).astype(jnp.float32)
    gathered = gather(w_query, w_key, w_value, w_out, w_inner, w_outer, (b_query, b_value, b_out, gain_one, shift_one, b_outer, gain_two, shift_two), b_inner)
    full_query, full_key, full_value, full_out, full_inner, full_outer, vectors, bias_inner = gathered
    bias_query, bias_value, bias_out, gain_first, shift_first, bias_outer, gain_second, shift_second = vectors
    queries = to_half(forward_product(layer_input, full_query) + bias_query)
    keys = to_half(forward_product(layer_input, full_key))
    values = to_half(forward_product(layer_input, full_value) + bias_value)
    row_count = layer_input.shape[0] // SEQ
    attended_rows = []
    log_rows = []
    for row_index in range(row_count):
        window = slice(row_index * SEQ, (row_index + 1) * SEQ)
        query_row = queries[window].reshape(SEQ, HEADS, HEAD_DIM)
        key_row = keys[window].reshape(SEQ, HEADS, HEAD_DIM)
        value_row = values[window].reshape(SEQ, HEADS, HEAD_DIM)
        scores = row_scores(query_row, key_row, segment_ids[row_index], score_scale)
        top_score = jnp.max(scores, axis=-1, keepdims=True)
        expanded = jnp.exp(scores - top_score)
        denominator = jnp.sum(expanded, axis=-1, keepdims=True)
        probs_low = to_half(expanded / denominator)
        attended_rows.append(
            jnp.einsum(
                "hqk,khd->qhd", probs_low, value_row, preferred_element_type=jnp.float32
            ).reshape(SEQ, D)
        )
        log_rows.append(top_score + jnp.log(denominator))
    attended = to_half(jnp.concatenate(attended_rows, axis=0) * head_mask)
    branch = forward_product(attended, full_out) + bias_out
    normed_one, inverse_one = norm_parts(layer_input.astype(jnp.float32) + branch)
    hidden = normed_one * gain_first + shift_first
    hidden_low = to_half(hidden)
    inner = jnp.concatenate([forward_product(hidden_low, full_inner[q]) for q in range(4)], axis=1) + bias_inner

    def gelu_exact(value):
        return jax.nn.gelu(value, approximate=False)

    gelu_value, gelu_pull = jax.vjp(gelu_exact, inner)
    active = to_half(gelu_value * unit_mask)
    outer = forward_product(active, full_outer) + bias_outer
    normed_two, inverse_two = norm_parts(hidden + outer)
    layer_output = to_half(normed_two * gain_second + shift_second)
    top_grad = out_grad.astype(jnp.float32)
    shift_two_grad = jnp.sum(top_grad, axis=0)
    gain_two_grad = jnp.sum(top_grad * normed_two, axis=0)
    res_two_grad = norm_back(top_grad * gain_second, normed_two, inverse_two)
    outer_grad = to_half(res_two_grad)
    b_outer_grad = column_sum(outer_grad)
    w_outer_grad = weight_grad(active, outer_grad)
    active_grad = back_product(outer_grad, full_outer)
    inner_grad = to_half(gelu_pull(active_grad * unit_mask)[0])
    b_inner_grad = column_sum(inner_grad)
    w_inner_grad = jnp.stack([to_half(weight_grad(hidden_low, inner_grad[:, q * D : (q + 1) * D])) for q in range(4)])
    hidden_grad = res_two_grad + sum(back_product(inner_grad[:, q * D : (q + 1) * D], full_inner[q]) for q in range(4))
    shift_one_grad = jnp.sum(hidden_grad, axis=0)
    gain_one_grad = jnp.sum(hidden_grad * normed_one, axis=0)
    res_one_grad = norm_back(hidden_grad * gain_first, normed_one, inverse_one)
    branch_grad = to_half(res_one_grad)
    b_out_grad = column_sum(branch_grad)
    w_out_grad = weight_grad(attended, branch_grad)
    attended_grad = to_half(back_product(branch_grad, full_out)) * to_half(head_mask)
    query_rows = []
    key_rows = []
    value_rows = []
    for row_index in range(row_count):
        window = slice(row_index * SEQ, (row_index + 1) * SEQ)
        query_row = queries[window].reshape(SEQ, HEADS, HEAD_DIM)
        key_row = keys[window].reshape(SEQ, HEADS, HEAD_DIM)
        value_row = values[window].reshape(SEQ, HEADS, HEAD_DIM)
        grad_row = attended_grad[window].reshape(SEQ, HEADS, HEAD_DIM)
        scores = row_scores(query_row, key_row, segment_ids[row_index], score_scale)
        probs = jnp.exp(scores - log_rows[row_index])
        prob_grad = jnp.einsum(
            "qhd,khd->hqk", grad_row, value_row, preferred_element_type=jnp.float32
        )
        value_rows.append(
            jnp.einsum(
                "hqk,qhd->khd", to_half(probs), grad_row, preferred_element_type=jnp.float32
            ).reshape(SEQ, D)
        )
        score_grad = to_half(
            probs * (prob_grad - jnp.sum(probs * prob_grad, axis=-1, keepdims=True))
        )
        query_rows.append(
            (
                jnp.einsum("hqk,khd->qhd", score_grad, key_row, preferred_element_type=jnp.float32)
                * score_scale
            ).reshape(SEQ, D)
        )
        key_rows.append(
            (
                jnp.einsum(
                    "hqk,qhd->khd", score_grad, query_row, preferred_element_type=jnp.float32
                )
                * score_scale
            ).reshape(SEQ, D)
        )
    query_grad = to_half(jnp.concatenate(query_rows, axis=0))
    key_grad = to_half(jnp.concatenate(key_rows, axis=0))
    value_grad = to_half(jnp.concatenate(value_rows, axis=0))
    b_query_grad = column_sum(query_grad)
    b_value_grad = column_sum(value_grad)
    w_query_grad = weight_grad(layer_input, query_grad)
    w_key_grad = weight_grad(layer_input, key_grad)
    w_value_grad = weight_grad(layer_input, value_grad)
    input_grad = to_half(
        res_one_grad
        + back_product(query_grad, full_query)
        + back_product(key_grad, full_key)
        + back_product(value_grad, full_value)
    )
    matrices, vectors, b_inner_grad = reduce(
        to_half(w_query_grad), to_half(w_key_grad), to_half(w_value_grad), to_half(w_out_grad), w_inner_grad, to_half(w_outer_grad),
        (b_query_grad, b_value_grad, b_out_grad, gain_one_grad, shift_one_grad, b_outer_grad, gain_two_grad, shift_two_grad), b_inner_grad)
    return (
        layer_output,
        input_grad,
        matrices[0],
        vectors[0],
        matrices[1],
        matrices[2],
        vectors[1],
        matrices[3],
        vectors[2],
        vectors[3],
        vectors[4],
        matrices[4],
        b_inner_grad,
        matrices[5],
        vectors[5],
        vectors[6],
        vectors[7],
    )


def solution(mesh):
    placed = (
        P(("width", "shard"), None),
        P(("width", "shard"), None),
        P("width"),
        P("shard", None),
        P("shard"),
        P("shard", None),
        P("shard", None),
        P("shard"),
        P("shard", None),
        P("shard"),
        P("shard"),
        P("shard"),
        P("shard", None),
        P("shard"),
        P("shard", None),
        P("shard"),
        P("shard"),
        P("shard"),
        P(("width", "shard"), None),
    )
    return jax.shard_map(
        body,
        mesh=mesh,
        in_specs=placed,
        out_specs=(
            P(("width", "shard"), None),
            P(("width", "shard"), None),
            P("shard", None),
            P("shard"),
            P("shard", None),
            P("shard", None),
            P("shard"),
            P("shard", None),
            P("shard"),
            P("shard"),
            P("shard"),
            P("shard", None),
            P("shard"),
            P("shard", None),
            P("shard"),
            P("shard"),
            P("shard"),
        ),
        check_vma=False,
    )
```

```python
import functools
import jax
import jax.numpy as jnp
from jax import lax
from jax.experimental import pallas as pl
from jax.experimental.pallas import tpu as pltpu
from jax.sharding import PartitionSpec as P

HEADS = 12
HEAD_DIM = 64
FF = 3072
D = 768
SEQ = 512
MESH = pl.DeviceIdType.MESH
BF = jnp.bfloat16
F32 = jnp.float32
TR = 96
HR = 48


def places():
    w = lax.axis_index("width")
    s = lax.axis_index("shard")
    return dict(
        w=w,
        s=s,
        c=lax.rem(s, 2),
        z=lax.div(s, 2),
        sib=s + 1 - 2 * lax.rem(s, 2),
        xw=w + 1 - 2 * lax.rem(w, 2),
        yw=lax.rem(w + 2, 4),
        dw=3 - w,
        zp=lax.rem(s + 2, 8),
        zm=lax.rem(s + 6, 8),
        zo=lax.rem(s + 4, 8),
    )


class Copies:
    def __init__(self, send, recv):
        self.send, self.recv, self.count, self.all = send, recv, 0, []

    def start(self, src, dst, device):
        k = self.count
        self.count += 1
        copy = pltpu.make_async_remote_copy(
            src_ref=src,
            dst_ref=dst,
            send_sem=self.send.at[k],
            recv_sem=self.recv.at[k],
            device_id=device,
            device_id_type=MESH,
        )
        copy.start()
        self.all.append(copy)
        return copy

    def finish(self):
        for copy in self.all:
            copy.wait_send()


def greet(devices):
    barrier = pltpu.get_barrier_semaphore()
    for device in devices:
        pl.semaphore_signal(barrier, inc=1, device_id=device, device_id_type=MESH)
    pl.semaphore_wait(barrier, len(devices))


def partners(p):
    out = [(p["xw"], p["s"]), (p["yw"], p["s"]), (p["dw"], p["s"])]
    for k in range(1, 8):
        out.append((p["w"], lax.rem(p["s"] + k, 8)))
    return out


GATHER_COPIES = 67


def slot(m, full, q, s):
    return full.at[s, q] if m == 2 else full.at[q, s]


def slots(m, full, s):
    return full.at[s] if m == 2 else full.at[:, s]


def gather_kernel(wq, wk, wv, wo, wi, wr, vec, fa, fi, fo, fv, own, ssem, rsem, lsem):
    p = places()
    w, s = p["w"], p["s"]
    full = (fa, fi, fo)
    for q, ref in enumerate((wq, wk, wv, wo)):
        own[0, q] = ref[...].astype(BF)
    for q in range(4):
        own[1, q] = wi[:, q * D : (q + 1) * D].astype(BF)
        own[2, q] = wr[q * TR : (q + 1) * TR, :].astype(BF)
    greet(partners(p))
    cp = Copies(ssem, rsem)
    xdev, ydev = (p["xw"], s), (p["yw"], s)
    zpdev, zmdev, sib = (w, p["zp"]), (w, p["zm"]), (w, p["sib"])
    got = {}
    for m in range(3):
        got[m, "zm"] = cp.start(own.at[m, w], slot(m, full[m], w, s), zpdev)
        got[m, "zp"] = cp.start(own.at[m, w], slot(m, full[m], w, s), zmdev)
        got[m, "c"] = cp.start(own.at[m], slots(m, full[m], s), sib)
    vcopies = [
        cp.start(vec, fv.at[s], (w, lax.rem(s + k, 8))) for k in range(1, 8)
    ]
    local = [pltpu.make_async_copy(own.at[m], slots(m, full[m], s), lsem.at[m]) for m in range(3)]
    local.append(pltpu.make_async_copy(vec, fv.at[s], lsem.at[3]))
    for copy in local:
        copy.start()

    def half(ref, top):
        return ref.at[0:HR] if top else ref.at[HR:TR]

    def to_plane(m, name):
        tile = slot(m, full[m], w, p[name])
        got[m, name, "x"] = cp.start(tile, tile, xdev)
        got[m, name, "y"] = cp.start(tile, tile, ydev)

    def stage1(m):
        got[m, "zm"].wait_recv()
        tile = half(slot(m, full[m], w, p["zm"]), True)
        got[m, "top"] = cp.start(tile, tile, zpdev)
        to_plane(m, "zm")
        got[m, "zp"].wait_recv()
        tile = half(slot(m, full[m], w, p["zp"]), False)
        got[m, "bot"] = cp.start(tile, tile, zmdev)
        to_plane(m, "zp")

    def stage2(m):
        got[m, "top"].wait_recv()
        got[m, "bot"].wait_recv()
        to_plane(m, "zo")

    def stage3(m):
        for name in ("zm", "zp", "zo"):
            got[m, name, "x"].wait_recv()
            tile = half(slot(m, full[m], p["xw"], p[name]), True)
            got[m, name, "dy"] = cp.start(tile, tile, ydev)
            got[m, name, "y"].wait_recv()
            tile = half(slot(m, full[m], p["yw"], p[name]), False)
            got[m, name, "dx"] = cp.start(tile, tile, xdev)

    def stage4(m):
        for name in ("zm", "zp", "zo"):
            got[m, name, "dy"].wait_recv()
            got[m, name, "dx"].wait_recv()
            block = slots(m, full[m], p[name])
            got[m, name, "c"] = cp.start(block, block, sib)

    stage1(0)
    stage1(1)
    stage2(0)
    stage1(2)
    stage2(1)
    stage3(0)
    stage2(2)
    stage3(1)
    stage4(0)
    stage3(2)
    stage4(1)
    stage4(2)
    for m in range(3):
        got[m, "c"].wait_recv()
        for name in ("zm", "zp", "zo"):
            got[m, name, "c"].wait_recv()
    for copy in vcopies:
        copy.wait_recv()
    for copy in local:
        copy.wait()
    cp.finish()
    assert cp.count == GATHER_COPIES, cp.count


def gather_fast(wq, wk, wv, wo, wi, wr, vec):
    vm = pl.BlockSpec(memory_space=pltpu.VMEM)
    anyspace = pl.BlockSpec(memory_space=pl.ANY)
    return pl.pallas_call(
        gather_kernel,
        out_shape=(
            jax.ShapeDtypeStruct((4, 8, TR, D), BF),
            jax.ShapeDtypeStruct((4, 8, TR, D), BF),
            jax.ShapeDtypeStruct((8, 4, TR, D), BF),
            jax.ShapeDtypeStruct((8, 16, D), BF),
        ),
        in_specs=[vm] * 7,
        out_specs=(anyspace,) * 4,
        scratch_shapes=[
            pltpu.VMEM((3, 4, TR, D), BF),
            pltpu.SemaphoreType.DMA((GATHER_COPIES,)),
            pltpu.SemaphoreType.DMA((GATHER_COPIES,)),
            pltpu.SemaphoreType.DMA((4,)),
        ],
        compiler_params=pltpu.CompilerParams(
            collective_id=0, has_side_effects=True, vmem_limit_bytes=60 << 20
        ),
        name="gather",
    )(wq, wk, wv, wo, wi, wr, vec)


REDUCE_COPIES = 6 + 3 * 15 + 7


def reduce_kernel(
    gq, gk, gv, go, gi, gr, gvec,
    oq, ok, ov, oo, oi, our, ovec,
    held, landed, dx, dy, rx, ry, qz, dzp, dzm, rzp, rzm, outb,
    vheld, vrecv, vplane, vz,
    ssem, rsem, lsem,
):
    p = places()
    w, s, c, z = p["w"], p["s"], p["c"], p["z"]
    greet(partners(p))
    cp = Copies(ssem, rsem)
    xdev, ydev, ddev = (p["xw"], s), (p["yw"], s), (p["dw"], s)
    zpdev, zmdev, sib = (w, p["zp"]), (w, p["zm"]), (w, p["sib"])
    zp, zm, zo = lax.rem(z + 1, 4), lax.rem(z + 3, 4), lax.rem(z + 2, 4)
    got = {}
    local = {}

    def half_of(m, core):
        if m == 0:
            return [(g.at[:, core], (0, q)) for q, g in enumerate((gq, gk, gv, go))]
        if m == 1:
            return [(gi.at[:, :, core], (1,))]
        return [(gr.at[:, core], (2,))]

    count = 0
    order = (2, 1, 0)
    got["v", "c"] = cp.start(gvec.at[:, 1 - c], vrecv, sib)
    for m in order:
        got[m, "c"] = []
        local[m] = []
        for src, at in half_of(m, 1 - c):
            got[m, "c"].append(cp.start(src, landed.at[at], sib))
        for src, at in half_of(m, c):
            copy = pltpu.make_async_copy(src, held.at[at], lsem.at[count])
            copy.start()
            local[m].append(copy)
            count += 1

    def quarter(m, q, rows=slice(None)):
        return (m, slice(None), q, rows) if m == 2 else (m, q, slice(None), rows)

    TOP, BOT = slice(0, HR), slice(HR, TR)

    def add_pair(m):
        for copy in local[m]:
            copy.wait()
        for copy in got[m, "c"]:
            copy.wait_recv()

        def one(i, _):
            for j in range(4):
                held[m, i, j] = (held[m, i, j].astype(F32) + landed[m, i, j].astype(F32)).astype(BF)
            return 0

        lax.fori_loop(0, 4, one, 0)

    def plane1(m):
        got[m, "dx"] = cp.start(held.at[quarter(m, p["dw"], TOP)], dx.at[m], xdev)
        got[m, "dy"] = cp.start(held.at[quarter(m, p["dw"], BOT)], dy.at[m], ydev)
        got[m, "x1"] = cp.start(held.at[quarter(m, p["xw"], TOP)], rx.at[m, :, TOP], xdev)
        got[m, "y1"] = cp.start(held.at[quarter(m, p["yw"], BOT)], ry.at[m, :, BOT], ydev)

    def plane2(m):
        got[m, "dx"].wait_recv()
        at = quarter(m, p["yw"], TOP)
        held[at] = (held[at].astype(F32) + dx[m].astype(F32)).astype(BF)
        got[m, "y2"] = cp.start(held.at[at], ry.at[m, :, TOP], ydev)
        got[m, "dy"].wait_recv()
        at = quarter(m, p["xw"], BOT)
        held[at] = (held[at].astype(F32) + dy[m].astype(F32)).astype(BF)
        got[m, "x2"] = cp.start(held.at[at], rx.at[m, :, BOT], xdev)

    def plane3(m):
        for name in ("x1", "y1", "x2", "y2"):
            got[m, name].wait_recv()
        qz[m] = (held[quarter(m, w)].astype(F32) + rx[m].astype(F32) + ry[m].astype(F32)).astype(BF)

    def ring1(m):
        got[m, "dzp"] = cp.start(qz.at[m, zo, TOP], dzp.at[m], zpdev)
        got[m, "dzm"] = cp.start(qz.at[m, zo, BOT], dzm.at[m], zmdev)
        got[m, "p1"] = cp.start(qz.at[m, zp, BOT], rzp.at[m, BOT], zpdev)
        got[m, "m1"] = cp.start(qz.at[m, zm, TOP], rzm.at[m, TOP], zmdev)

    def ring2(m):
        got[m, "dzp"].wait_recv()
        qz[m, zp, TOP] = (qz[m, zp, TOP].astype(F32) + dzp[m].astype(F32)).astype(BF)
        got[m, "p2"] = cp.start(qz.at[m, zp, TOP], rzp.at[m, TOP], zpdev)
        got[m, "dzm"].wait_recv()
        qz[m, zm, BOT] = (qz[m, zm, BOT].astype(F32) + dzm[m].astype(F32)).astype(BF)
        got[m, "m2"] = cp.start(qz.at[m, zm, BOT], rzm.at[m, BOT], zmdev)

    def ring3(m):
        for name in ("p1", "m1", "p2", "m2"):
            got[m, name].wait_recv()
        outb[m, w] = (qz[m, z].astype(F32) + rzp[m].astype(F32) + rzm[m].astype(F32)).astype(BF)
        tile = outb.at[m, w]
        got[m, "gx"] = cp.start(tile, tile, xdev)
        got[m, "gy"] = cp.start(tile, tile, ydev)
        got[m, "gd"] = cp.start(tile, tile, ddev)

    def last(m):
        for name in ("gx", "gy", "gd"):
            got[m, name].wait_recv()
        if m == 0:
            for q, ref in enumerate((oq, ok, ov, oo)):
                ref[...] = outb[0, q].astype(F32)
        for q in range(4):
            if m == 1:
                oi[:, q * D : (q + 1) * D] = outb[1, q].astype(F32)
            if m == 2:
                our[q * TR : (q + 1) * TR, :] = outb[2, q].astype(F32)

    def vec_plane():
        got["v", "c"].wait_recv()
        vheld[...] = gvec[:, c] + vrecv[...]
        vplane[w] = vheld[...]
        got["v", "plane"] = [cp.start(vheld, vplane.at[w], d) for d in (xdev, ydev, ddev)]

    def vec_ring():
        for copy in got["v", "plane"]:
            copy.wait_recv()
        vheld2 = (vplane[0] + vplane[1]) + (vplane[2] + vplane[3])
        vheld[...] = vheld2
        vz[z] = vheld[z]
        got["v", "z"] = [
            cp.start(vheld.at[t], vz.at[z], (w, 2 * t + c)) for t in (zp, zm, zo)
        ]

    def vec_last():
        for copy in got["v", "z"]:
            copy.wait_recv()
        ovec[...] = (vz[0] + vz[1]) + (vz[2] + vz[3])

    a, b, d = order
    add_pair(a)
    plane1(a)
    add_pair(b)
    plane1(b)
    add_pair(d)
    plane1(d)
    vec_plane()
    plane2(a)
    plane2(b)
    plane3(a)
    ring1(a)
    plane2(d)
    plane3(b)
    ring1(b)
    ring2(a)
    for copy in got["v", "plane"]:
        copy.wait_send()
    cp.all = [copy for copy in cp.all if all(copy is not other for other in got["v", "plane"])]
    vec_ring()
    plane3(d)
    ring1(d)
    ring3(a)
    ring2(b)
    ring3(b)
    ring2(d)
    last(a)
    ring3(d)
    last(b)
    vec_last()
    last(d)
    cp.finish()
    assert cp.count == REDUCE_COPIES, cp.count


def reduce_fast(gq, gk, gv, go, gi, gr, gvec):
    vm = pl.BlockSpec(memory_space=pltpu.VMEM)
    anyspace = pl.BlockSpec(memory_space=pl.ANY)
    square = (4, 2, TR, D)
    return pl.pallas_call(
        reduce_kernel,
        out_shape=tuple(jax.ShapeDtypeStruct((TR, D), F32) for _ in range(4))
        + (
            jax.ShapeDtypeStruct((TR, FF), F32),
            jax.ShapeDtypeStruct((FF // 8, D), F32),
            jax.ShapeDtypeStruct((8, D), F32),
        ),
        in_specs=[anyspace] * 6 + [vm],
        out_specs=(vm,) * 7,
        scratch_shapes=[
            pltpu.VMEM((3, 4, 4, TR, D), BF),
            pltpu.VMEM((3, 4, 4, TR, D), BF),
            pltpu.VMEM((3, 4, HR, D), BF),
            pltpu.VMEM((3, 4, HR, D), BF),
            pltpu.VMEM((3, 4, TR, D), BF),
            pltpu.VMEM((3, 4, TR, D), BF),
            pltpu.VMEM((3, 4, TR, D), BF),
            pltpu.VMEM((3, HR, D), BF),
            pltpu.VMEM((3, HR, D), BF),
            pltpu.VMEM((3, TR, D), BF),
            pltpu.VMEM((3, TR, D), BF),
            pltpu.VMEM((3, 4, TR, D), BF),
            pltpu.VMEM((4, 8, D), F32),
            pltpu.VMEM((4, 8, D), F32),
            pltpu.VMEM((4, 4, 8, D), F32),
            pltpu.VMEM((4, 8, D), F32),
            pltpu.SemaphoreType.DMA((REDUCE_COPIES,)),
            pltpu.SemaphoreType.DMA((REDUCE_COPIES,)),
            pltpu.SemaphoreType.DMA((6,)),
        ],
        compiler_params=pltpu.CompilerParams(
            collective_id=1, has_side_effects=True, vmem_limit_bytes=60 << 20
        ),
        name="reduce",
    )(
        gq.reshape(square), gk.reshape(square), gv.reshape(square), go.reshape(square),
        gi.reshape((4,) + square), gr.reshape((4, 2, 4, TR, D)), gvec.reshape((4, 2, 8, D)),
    )


NT = (((1,), (1,)), ((), ()))
TN = (((0,), (0,)), ((), ()))
NN = (((1,), (0,)), ((), ()))
EPS = 1e-06
RSQRT2 = 0.7071067811865476
RSQRT2PI = 0.3989422804014327


def mm(a, b, dims=NN):
    return lax.dot_general(a, b, dims, preferred_element_type=F32)


def rows_of(i, size):
    return pl.ds(pl.multiple_of(i * size, size), size)


def column_mask(kept, shape, width):
    return jnp.where(lax.broadcasted_iota(jnp.int32, shape, 1) < kept * width, 1.0, 0.0).astype(F32)


def mean_of(v):
    return jnp.sum(v, axis=1, keepdims=True) * (1.0 / D)


def norm_rows(total):
    centered = total - mean_of(total)
    inverse = lax.rsqrt(mean_of(centered * centered) + EPS)
    return centered * inverse, inverse


def norm_back(grad, normed, inverse):
    return inverse * (grad - mean_of(grad) - normed * mean_of(grad * normed))


def expand_vectors(fv, rows, binner):
    lane = lax.broadcasted_iota(jnp.int32, (128, D), 0)
    column = lax.broadcasted_iota(jnp.int32, (128, D), 1)
    total = jnp.zeros((16, D), F32)
    for s in range(8):
        pick = jnp.where((column == lane + TR * s) & (lane < TR), 1.0, 0.0).astype(BF)
        total = total + mm(fv[s], pick)
    rows[...] = total[0:8]
    for s in range(8):
        tile = fv[s].astype(F32)
        for r in range(3):
            binner[0:1, 128 * (3 * s + r) : 128 * (3 * s + r + 1)] = tile[8 + r : 9 + r]


def project(x, fa, rows, q, k, v, block=256):
    def one(i, _):
        at = rows_of(i, block)
        xb = x[at]
        q[at] = ((mm(xb, fa[0]) + rows[0:1]) * 0.125).astype(BF)
        k[at] = mm(xb, fa[1]).astype(BF)
        v[at] = (mm(xb, fa[2]) + rows[1:2]).astype(BF)
        return 0

    lax.fori_loop(0, x.shape[0] // block, one, 0)


def low_lanes(n):
    return lax.broadcasted_iota(jnp.int32, (n, 128), 1) < HEAD_DIM


def attend(i, qkv, segc, segr, kept, att, inv, ebuf, qb=512):
    q, k, v = qkv
    r, pair = lax.div(i, 6), lax.rem(i, 6)
    lanes = pl.ds(pl.multiple_of(pair * 128, 128), 128)
    rows = rows_of(r, SEQ)
    kp, vp = k[rows, lanes], v[rows, lanes]
    low = low_lanes(SEQ)
    ones = jnp.ones_like(vp)
    vs = (jnp.where(low, vp, ones), jnp.where(low, ones, vp))
    ids = segr[r]
    lowq = low_lanes(qb)
    for b in range(SEQ // qb):
        at = pl.ds(pl.multiple_of(r * SEQ + b * qb, qb), qb)
        qp = q[at, lanes]
        zero = jnp.zeros_like(qp)
        same = segc[r, b * qb : (b + 1) * qb] == ids
        out = []
        for h in range(2):
            qh = jnp.where(lowq, qp, zero) if h == 0 else jnp.where(lowq, zero, qp)
            scores = jnp.where(same, mm(qh, kp, NT), -1e30)
            top = jnp.max(scores, axis=1, keepdims=True)
            e = jnp.exp(scores - top).astype(BF)
            ebuf[h, b * qb : (b + 1) * qb] = e
            out.append(mm(e, vs[h]))
        inverse = 1.0 / pltpu.roll(jnp.where(lowq, out[1], out[0]), HEAD_DIM, 1)
        column = lax.broadcasted_iota(jnp.int32, (1, 128), 1) + pair * 128
        mask = jnp.where(column < kept * HEAD_DIM, 1.0, 0.0).astype(F32)
        att[at, lanes] = (jnp.where(lowq, out[0], out[1]) * (inverse * mask)).astype(BF)
        inv[at, lanes] = inverse


def branch_out(x, att, fa, rows, t1, block=256):
    def one(i, _):
        at = rows_of(i, block)
        t1[at] = x[at].astype(F32) + (mm(att[at], fa[3]) + rows[2:3])
        return 0

    lax.fori_loop(0, x.shape[0] // block, one, 0)


def feed_forward(t1, grad, rows, binner, wi, wr, wo, inv, kept, y, res, bg, dos, hl, act, ig, og, gp, sums, bsum, block=256):
    b_outer, gain_two, shift_two = rows[5:6], rows[6:7], rows[7:8]
    gain_one, shift_one = rows[3:4], rows[4:5]
    sums[...] = jnp.zeros_like(sums)
    bsum[...] = jnp.zeros_like(bsum)
    heads = column_mask(kept, (1, D), HEAD_DIM)

    def add(k, value):
        sums[k : k + 1] += jnp.sum(value, axis=0, keepdims=True)

    def one(i, _):
        at = rows_of(i, block)
        n1, inv1 = norm_rows(t1[at])
        hidden = n1 * gain_one + shift_one
        low = hidden.astype(BF)
        hl[at] = low
        outer = jnp.zeros((block, D), F32)
        for j in range(4):
            cols = slice(j * D, (j + 1) * D)
            inner = mm(low, wi[j]) + binner[:, cols]
            keep = column_mask(kept * 256 - j * D, (1, D), 1)
            phi = 0.5 + 0.5 * lax.erf(inner * RSQRT2)
            masked = inner * keep
            a = (masked * phi).astype(BF)
            gp[:, cols] = (keep * phi + masked * (RSQRT2PI * jnp.exp(-0.5 * (inner * inner)))).astype(BF)
            act[at, cols] = a
            outer = outer + mm(a, wr[cols])
        n2, inv2 = norm_rows(hidden + (outer + b_outer))
        y[at] = (n2 * gain_two + shift_two).astype(BF)
        top = grad[at].astype(F32)
        add(7, top)
        add(6, top * n2)
        res2 = norm_back(top * gain_two, n2, inv2)
        o = res2.astype(BF)
        og[at] = o
        add(5, o.astype(F32))
        hg = res2
        for j in range(4):
            cols = slice(j * D, (j + 1) * D)
            g = (mm(o, wr[cols], NT) * gp[:, cols].astype(F32)).astype(BF)
            ig[at, cols] = g
            bsum[:, cols] += jnp.sum(g.astype(F32), axis=0, keepdims=True)
            hg = hg + mm(g, wi[j], NT)
        add(4, hg)
        n1, inv1 = norm_rows(t1[at])
        add(3, hg * n1)
        res1 = norm_back(hg * gain_one, n1, inv1)
        res[at] = res1
        b = res1.astype(BF)
        bg[at] = b
        add(2, b.astype(F32))
        dos[at] = (mm(b, wo[...], NT) * (inv[at] * heads)).astype(BF)
        return 0

    lax.fori_loop(0, t1.shape[0] // block, one, 0)


def inner_grads(j, hl, ig, gi):
    cols = pl.ds(pl.multiple_of(j * D, D), D)
    gi[j] = mm(hl[...], ig[:, cols], TN).astype(BF)


def outer_grads(j, act, og, gr, block=512):
    cols = pl.ds(pl.multiple_of(j * block, block), block)
    gr[cols] = mm(act[:, cols], og[...], TN).astype(BF)


def attend_back(i, qkv, dos, att, ebuf, dq, dk, dv):
    q, k, v = qkv
    r, pair = lax.div(i, 6), lax.rem(i, 6)
    lanes = pl.ds(pl.multiple_of(pair * 128, 128), 128)
    rows = rows_of(r, SEQ)
    qp, kp, vp, dp = q[rows, lanes], k[rows, lanes], v[rows, lanes], dos[rows, lanes]
    low = low_lanes(SEQ)
    zero = jnp.zeros_like(qp)
    product = dp.astype(F32) * att[rows, lanes].astype(F32)
    gq = jnp.zeros((SEQ, 128), F32)
    gk = jnp.zeros((SEQ, 128), F32)
    gv = jnp.zeros((SEQ, 128), F32)
    for h in range(2):
        mine = low if h == 0 else jnp.logical_not(low)
        dh = jnp.where(mine, dp, zero)
        delta = jnp.sum(jnp.where(mine, product, 0.0), axis=1, keepdims=True)
        e = ebuf[h]
        ds = (e.astype(F32) * (mm(dh, vp, NT) - delta)).astype(BF)
        gv = gv + mm(e, dh, TN)
        gk = gk + mm(ds, jnp.where(mine, qp, zero), TN)
        gq = gq + mm(ds, jnp.where(mine, kp, zero))
    dq[rows, lanes] = (gq * 0.125).astype(BF)
    dk[rows, lanes] = gk.astype(BF)
    dv[rows, lanes] = gv.astype(BF)


def input_back(res, dq, dk, dv, fa, out, sums, block=256):
    sums[0:2] = jnp.zeros((2, D), F32)

    def one(i, _):
        at = rows_of(i, block)
        a, b, c = dq[at], dk[at], dv[at]
        out[at] = (res[at] + mm(a, fa[0], NT) + mm(b, fa[1], NT) + mm(c, fa[2], NT)).astype(BF)
        sums[0:1] += jnp.sum(a.astype(F32), axis=0, keepdims=True)
        sums[1:2] += jnp.sum(c.astype(F32), axis=0, keepdims=True)
        return 0

    lax.fori_loop(0, res.shape[0] // block, one, 0)


VM = pl.BlockSpec(memory_space=pltpu.VMEM)
SM = pl.BlockSpec(memory_space=pltpu.SMEM)
ANY = pl.BlockSpec(memory_space=pl.ANY)


def params(**more):
    return pltpu.CompilerParams(vmem_limit_bytes=62 << 20, **more)


def shape(*dims, dtype=BF):
    return jax.ShapeDtypeStruct(dims, dtype)


def forward_kernel(x, segc, segr, kept, fa, rows, q, k, v, att, inv, e_out, t1, ebuf, sem):
    project(x, fa, rows, q, k, v)
    keep = kept[0]

    def out_copy(i, slot):
        r, pair = lax.div(i, 6), lax.rem(i, 6)
        return pltpu.make_async_copy(ebuf.at[slot], e_out.at[r, pair], sem.at[slot])

    def one(i, _):
        slot = lax.rem(i, 2)

        @pl.when(i >= 2)
        def _():
            out_copy(i - 2, slot).wait()

        attend(i, (q, k, v), segc, segr, keep, att, inv, ebuf.at[slot])
        out_copy(i, slot).start()
        return 0

    n = 6 * (x.shape[0] // SEQ)
    lax.fori_loop(0, n, one, 0)
    branch_out(x, att, fa, rows, t1)
    out_copy(n - 2, (n - 2) % 2).wait()
    out_copy(n - 1, (n - 1) % 2).wait()


def forward_attention(x, segment_ids, kept, fa, rows):
    t = x.shape[0]
    n = t // SEQ
    return pl.pallas_call(
        forward_kernel,
        out_shape=(shape(t, D), shape(t, D), shape(t, D), shape(t, D), shape(t, D, dtype=F32),
                   shape(n, 6, 2, SEQ, SEQ), shape(t, D, dtype=F32)),
        in_specs=[VM, VM, VM, SM, VM, VM],
        out_specs=(VM, VM, VM, VM, VM, ANY, VM),
        scratch_shapes=[pltpu.VMEM((2, 2, SEQ, SEQ), BF), pltpu.SemaphoreType.DMA((2,))],
        compiler_params=params(),
        name="attention",
    )(x, segment_ids.reshape(n, SEQ, 1), segment_ids.reshape(n, 1, SEQ), kept, fa, rows)


def ffn_kernel(t1, grad, rows, binner, wi, wr, wo, inv, kept, y, res, bg, dos, gi, gr, sums, bsum, hl, act, ig, og, gp):
    feed_forward(t1, grad, rows, binner, wi, wr, wo, inv, kept[0], y, res, bg, dos, hl, act, ig, og, gp, sums, bsum)

    def one(j, _):
        inner_grads(j, hl, ig, gi)
        return 0

    lax.fori_loop(0, 4, one, 0)

    def two(j, _):
        outer_grads(j, act, og, gr)
        return 0

    lax.fori_loop(0, FF // 512, two, 0)


def ffn(t1, grad, rows, binner, wi, wr, wo, inv, kept):
    t = t1.shape[0]
    return pl.pallas_call(
        ffn_kernel,
        out_shape=(shape(t, D), shape(t, D, dtype=F32), shape(t, D), shape(t, D),
                   shape(4, D, D), shape(FF, D), shape(8, D, dtype=F32), shape(1, FF, dtype=F32)),
        in_specs=[VM] * 8 + [SM],
        out_specs=(VM,) * 8,
        scratch_shapes=[pltpu.VMEM((t, D), BF), pltpu.VMEM((t, FF), BF), pltpu.VMEM((t, FF), BF),
                        pltpu.VMEM((t, D), BF), pltpu.VMEM((256, FF), BF)],
        compiler_params=params(),
        name="ffn",
    )(t1, grad, rows, binner, wi, wr, wo, inv, kept)


def backward_kernel(x, q, k, v, e_in, att, dos, bg, res, fa, sums_in, out, gq, gk, gv, go, sums, dq, dk, dv, ebuf, sem):
    def in_copy(i, slot):
        r, pair = lax.div(i, 6), lax.rem(i, 6)
        return pltpu.make_async_copy(e_in.at[r, pair], ebuf.at[slot], sem.at[slot])

    n = 6 * (x.shape[0] // SEQ)
    in_copy(0, 0).start()
    sums[...] = sums_in[...]
    go[...] = mm(att[...], bg[...], TN).astype(BF)

    def one(i, _):
        slot = lax.rem(i, 2)

        @pl.when(i + 1 < n)
        def _():
            in_copy(i + 1, 1 - slot).start()

        in_copy(i, slot).wait()
        attend_back(i, (q, k, v), dos, att, ebuf.at[slot], dq, dk, dv)
        return 0

    lax.fori_loop(0, n, one, 0)
    gq[...] = mm(x[...], dq[...], TN).astype(BF)
    gk[...] = mm(x[...], dk[...], TN).astype(BF)
    gv[...] = mm(x[...], dv[...], TN).astype(BF)
    input_back(res, dq, dk, dv, fa, out, sums)


def backward_attention(x, q, k, v, e, att, dos, bg, res, fa, sums):
    t = x.shape[0]
    return pl.pallas_call(
        backward_kernel,
        out_shape=(shape(t, D), shape(D, D), shape(D, D), shape(D, D), shape(D, D), shape(8, D, dtype=F32)),
        in_specs=[VM] * 4 + [ANY] + [VM] * 6,
        out_specs=(VM,) * 6,
        scratch_shapes=[pltpu.VMEM((t, D), BF)] * 3 + [pltpu.VMEM((2, 2, SEQ, SEQ), BF), pltpu.SemaphoreType.DMA((2,))],
        compiler_params=params(),
        name="attention_back",
    )(x, q, k, v, e, att, dos, bg, res, fa, sums)

def kernels_fit():
    return lax.axis_size("width") == 4 and lax.axis_size("shard") == 8


def gather(wq, wk, wv, wo, wi, wr, eight, b_inner):
    if kernels_fit():
        vec = jnp.pad(
            jnp.stack([jnp.concatenate(eight), jnp.pad(b_inner, (0, D - FF // 8))]), ((0, 14), (0, 0))
        ).astype(BF)
        fa, fi, fo, fv = gather_fast(wq, wk, wv, wo, wi, wr, vec)
        fa, fi, fo = fa.reshape(4, D, D), fi.reshape(4, D, D), fo.reshape(FF, D)
        rows = fv[:, 0].reshape(8, 8, TR).astype(F32)
        rows = rows.transpose(1, 0, 2).reshape(8, D)
        return fa, fi, fo, rows, fv[:, 1, : FF // 8].reshape(1, FF).astype(F32)

    def whole(a):
        return lax.all_gather(a.astype(BF), "shard", axis=0, tiled=True)

    fi = whole(wi)
    fi = jnp.stack([fi[:, q * D : (q + 1) * D] for q in range(4)])
    vectors = tuple(whole(a).astype(F32) for a in eight)
    fa = jnp.stack([whole(wq), whole(wk), whole(wv), whole(wo)])
    return fa, fi, whole(wr), jnp.stack(vectors), whole(b_inner).astype(F32).reshape(1, FF)


def reduce(gq, gk, gv, go, gi, gr, eight, b_inner):
    if kernels_fit():
        first = jnp.stack([a.reshape(8, TR) for a in eight], axis=1).reshape(8, 1, D)
        second = jnp.pad(b_inner.reshape(8, 1, FF // 8), ((0, 0), (0, 0), (0, D - FF // 8)))
        vec = jnp.pad(jnp.concatenate([first, second], axis=1), ((0, 0), (0, 6), (0, 0)))
        *matrices, ovec = reduce_fast(gq, gk, gv, go, gi, gr, vec)
        vectors = tuple(ovec[0, k * TR : (k + 1) * TR] for k in range(8))
        return matrices, vectors, ovec[1, : FF // 8]

    def owned(a):
        a = lax.psum_scatter(a, "shard", scatter_dimension=0, tiled=True)
        return lax.psum(a.astype(BF), "width").astype(F32)

    gi = jnp.concatenate([gi[q] for q in range(4)], axis=1)
    matrices = tuple(owned(a.astype(F32)) for a in (gq, gk, gv, go, gi, gr))
    return matrices, tuple(owned(a) for a in eight), owned(b_inner)


def body(
    layer_input, segment_ids, group_heads,
    w_query, b_query, w_key, w_value, b_value, w_out, b_out, gain_one, shift_one,
    w_inner, b_inner, w_outer, b_outer, gain_two, shift_two, out_grad,
):
    eight = (b_query, b_value, b_out, gain_one, shift_one, b_outer, gain_two, shift_two)
    fa, fi, fo, rows, binner = gather(w_query, w_key, w_value, w_out, w_inner, w_outer, eight, b_inner)
    q, k, v, att, inv, e, t1 = forward_attention(layer_input, segment_ids, group_heads, fa, rows)
    y, res, bg, dos, gi, gr, sums, bsum = ffn(t1, out_grad, rows, binner, fi, fo, fa[3], inv, group_heads)
    input_grad, gq, gk, gv, go, sums = backward_attention(layer_input, q, k, v, e, att, dos, bg, res, fa, sums)
    matrices, vectors, b_inner_grad = reduce(gq, gk, gv, go, gi, gr, tuple(sums[i] for i in range(8)), bsum[0])
    return (
        y, input_grad, matrices[0], vectors[0], matrices[1], matrices[2], vectors[1], matrices[3], vectors[2],
        vectors[3], vectors[4], matrices[4], b_inner_grad, matrices[5], vectors[5], vectors[6], vectors[7],
    )


def solution(mesh):
    placed = (
        P(("width", "shard"), None),
        P(("width", "shard"), None),
        P("width"),
        P("shard", None),
        P("shard"),
        P("shard", None),
        P("shard", None),
        P("shard"),
        P("shard", None),
        P("shard"),
        P("shard"),
        P("shard"),
        P("shard", None),
        P("shard"),
        P("shard", None),
        P("shard"),
        P("shard"),
        P("shard"),
        P(("width", "shard"), None),
    )
    return jax.shard_map(
        body,
        mesh=mesh,
        in_specs=placed,
        out_specs=(
            P(("width", "shard"), None),
            P(("width", "shard"), None),
            P("shard", None),
            P("shard"),
            P("shard", None),
            P("shard", None),
            P("shard"),
            P("shard", None),
            P("shard"),
            P("shard"),
            P("shard"),
            P("shard", None),
            P("shard"),
            P("shard", None),
            P("shard"),
            P("shard"),
            P("shard"),
        ),
        check_vma=False,
    )
```

```python
import functools
import jax
import jax.numpy as jnp
from jax import lax
from jax.experimental import pallas as pl
from jax.experimental.pallas import tpu as pltpu
from jax.sharding import PartitionSpec as P

HEADS = 12
HEAD_DIM = 64
FF = 3072
D = 768
SEQ = 512
MESH = pl.DeviceIdType.MESH
BF = jnp.bfloat16
F32 = jnp.float32
TR = 96
CW = 256
NT = (((1,), (1,)), ((), ()))
TN = (((0,), (0,)), ((), ()))
NN = (((1,), (0,)), ((), ()))
EPS = 1e-06
RSQRT2 = 0.7071067811865476
RSQRT2PI = 0.3989422804014327
VM = pl.BlockSpec(memory_space=pltpu.VMEM)
SM = pl.BlockSpec(memory_space=pltpu.SMEM)
ANY = pl.BlockSpec(memory_space=pl.ANY)


def params(**more):
    return pltpu.CompilerParams(vmem_limit_bytes=62 << 20, **more)


def shape(*dims, dtype=BF):
    return jax.ShapeDtypeStruct(dims, dtype)


class Place:
    def __init__(self):
        self.w = w = lax.axis_index("width")
        self.s = s = lax.axis_index("shard")
        self.c = c = lax.rem(s, 2)
        self.z = lax.div(s, 2)
        xw, yw = w + 1 - 2 * lax.rem(w, 2), lax.rem(w + 2, 4)
        up, down = lax.rem(s + 2, 8), lax.rem(s + 6, 8)
        self.wa = jnp.where(c == 0, xw, yw)
        self.wb = jnp.where(c == 0, yw, xw)
        self.wd = 3 - w
        self.sa = jnp.where(c == 0, up, down)
        self.sb = jnp.where(c == 0, down, up)
        self.so = lax.rem(s + 4, 8)
        self.sib = (w, s + 1 - 2 * c)
        self.plane_a, self.plane_b = (self.wa, s), (self.wb, s)
        self.ring_a, self.ring_b = (w, self.sa), (w, self.sb)


def greet(p, devices):
    barrier = pltpu.get_barrier_semaphore()
    for device in devices:
        pl.semaphore_signal(barrier, inc=1, device_id=device, device_id_type=MESH)
    pl.semaphore_wait(barrier, len(devices))


def others(p):
    return [(p.wa, p.s), (p.wb, p.s), (p.wd, p.s)] + [(p.w, lax.rem(p.s + k, 8)) for k in range(1, 8)]


class Net:
    def __init__(self, send, recv):
        self.send, self.recv, self.made = send, recv, {}

    def define(self, name, make):
        assert name not in self.made
        self.made[name] = (len(self.made), make)

    def copy(self, name):
        k, make = self.made[name]
        src, dst, device = make()
        return pltpu.make_async_remote_copy(
            src_ref=src, dst_ref=dst, send_sem=self.send.at[k], recv_sem=self.recv.at[k],
            device_id=device, device_id_type=MESH,
        )

    def start(self, *names):
        for name in names:
            self.copy(name).start()

    def wait(self, *names):
        for name in names:
            self.copy(name).wait_recv()

    def finish(self):
        for name in self.made:
            self.copy(name).wait_send()


def quarter(w):
    return pl.ds(pl.multiple_of(48 * lax.rem(w, 2), 48), 48), pl.ds(pl.multiple_of(384 * lax.div(w, 2), 384), 384)


def mm(a, b, dims=NN):
    return lax.dot_general(a, b, dims, preferred_element_type=F32)


def rows_of(i, size):
    return pl.ds(pl.multiple_of(i * size, size), size)


def column_mask(kept, shape, width):
    return jnp.where(lax.broadcasted_iota(jnp.int32, shape, 1) < kept * width, 1.0, 0.0).astype(F32)


def mean_of(v):
    return jnp.sum(v, axis=1, keepdims=True) * (1.0 / D)


def norm_rows(total):
    centered = total - mean_of(total)
    inverse = lax.rsqrt(mean_of(centered * centered) + EPS)
    return centered * inverse, inverse


def norm_back(grad, normed, inverse):
    return inverse * (grad - mean_of(grad) - normed * mean_of(grad * normed))


def low_lanes(n):
    return lax.broadcasted_iota(jnp.int32, (n, 128), 1) < HEAD_DIM


def place_of(i):
    return lax.div(i, 4), lax.rem(i, 2), lax.rem(lax.div(i, 2), 2)


def pair_lanes(pair, part):
    return pl.ds(pl.multiple_of(part * CW + pair * 128, 128), 128)


def chunk_bias(rows, c):
    lanes = slice(c * CW, (c + 1) * CW)
    return jnp.concatenate([rows[0:1, lanes], jnp.zeros((1, CW), F32), rows[1:2, lanes]], axis=1)


def project(x, fa, rows, qkv, block=256):
    scale = jnp.where(lax.broadcasted_iota(jnp.int32, (1, D), 1) < CW, 0.125, 1.0)

    def one(i, _):
        at = rows_of(i, block)
        xb = x[at]
        for c in range(3):
            weight = fa[c].reshape(D, D)
            qkv[c, at] = ((mm(xb, weight) + chunk_bias(rows, c)) * scale).astype(BF)
        return 0

    lax.fori_loop(0, x.shape[0] // block, one, 0)


def turn_ids(seg, segt):
    for r in range(seg.shape[0]):
        row = seg[r : r + 1, :].astype(F32)
        segt[r] = jnp.broadcast_to(row, (128, SEQ)).T


def attend(i, qkv, seg, segt, kept, att, inv, ebuf, qb=512):
    c, r, pair = place_of(i)
    base = r * SEQ
    rows = pl.ds(pl.multiple_of(base, SEQ), SEQ)
    kp, vp = qkv[c, rows, pair_lanes(pair, 1)], qkv[c, rows, pair_lanes(pair, 2)]
    low = low_lanes(SEQ)
    ones = jnp.ones_like(vp)
    vs = (jnp.where(low, vp, ones), jnp.where(low, ones, vp))
    ids = seg[pl.ds(r, 1), :].astype(F32)
    lowq = low_lanes(qb)
    lanes = pl.ds(pl.multiple_of(c * CW + pair * 128, 128), 128)
    column = lax.broadcasted_iota(jnp.int32, (1, 128), 1) + (c * CW + pair * 128)
    mask = jnp.where(column < kept * HEAD_DIM, 1.0, 0.0).astype(F32)
    for b in range(SEQ // qb):
        at = pl.ds(pl.multiple_of(base + b * qb, qb), qb)
        qp = qkv[c, at, pair_lanes(pair, 0)]
        zero = jnp.zeros_like(qp)
        own = segt[r, b * qb : (b + 1) * qb]
        same = jnp.concatenate([own == ids[:, j * 128 : (j + 1) * 128] for j in range(4)], axis=1)
        out = []
        for h in range(2):
            qh = jnp.where(lowq, qp, zero) if h == 0 else jnp.where(lowq, zero, qp)
            scores = jnp.where(same, mm(qh, kp, NT), -1e30)
            top = jnp.max(scores, axis=1, keepdims=True)
            e = jnp.exp(scores - top).astype(BF)
            ebuf[h, b * qb : (b + 1) * qb] = e
            out.append(mm(e, vs[h]))
        inverse = 1.0 / pltpu.roll(jnp.where(lowq, out[1], out[0]), HEAD_DIM, 1)
        att[at, lanes] = (jnp.where(lowq, out[0], out[1]) * (inverse * mask)).astype(BF)
        inv[at, lanes] = inverse


def expand_vectors(fv, rows, binner):
    lane = lax.broadcasted_iota(jnp.int32, (128, D), 0)
    column = lax.broadcasted_iota(jnp.int32, (128, D), 1)
    total = jnp.zeros((16, D), F32)
    for s in range(8):
        pick = jnp.where((column == lane + TR * s) & (lane < TR), 1.0, 0.0).astype(BF)
        total = total + mm(fv[s], pick)
        tile = fv[s].astype(F32)
        for r in range(3):
            binner[0:1, 128 * (3 * s + r) : 128 * (3 * s + r + 1)] = tile[8 + r : 9 + r]
    rows[...] = total[0:8]


HIER = (True, False, True, False)
GATHER_COPIES = sum(16 if hier else 7 for hier in HIER) + 7


def gather_net(p, own, fa, fi, fo, vec, fv, ssem, rsem):
    net = Net(ssem, rsem)
    units = (slice(0, 3), slice(3, 4), slice(4, 8), slice(8, 12))
    every = (slice(None), slice(None))

    def piece(g, s, part):
        if g < 2:
            return fa.at[(units[g], s, *part)]
        return fi.at[(slice(None), s, *part)] if g == 2 else fo.at[(s, slice(None), *part)]

    for g in range(4):
        mine = quarter(p.w) if HIER[g] else every
        first = quarter(p.wa)

        def add(name, src, dst, device):
            net.define((g, *name), lambda: (src(), dst(), device))

        def same(name, g, s, part, device):
            add(name, lambda: piece(g, s, part), lambda: piece(g, s, part), device)

        add(("zb",), lambda g=g, mine=mine: own.at[(units[g], *mine)], lambda g=g, mine=mine: piece(g, p.s, mine), p.ring_a)
        add(("za",), lambda g=g, mine=mine: own.at[(units[g], *mine)], lambda g=g, mine=mine: piece(g, p.s, mine), p.ring_b)
        same(("zo",), g, p.sb, mine, p.ring_a)
        add(("own", "c"), lambda g=g: own.at[units[g]], lambda g=g: piece(g, p.s, every), p.sib)
        for name, s in (("zb", p.sb), ("za", p.sa), ("zo", p.so)):
            if HIER[g]:
                same((name, "xa"), g, s, mine, p.plane_a)
                same((name, "xb"), g, s, mine, p.plane_b)
                same((name, "xd"), g, s, first, p.plane_b)
            same((name, "c"), g, s, every, p.sib)
    for k in range(1, 8):
        net.define(("v", k), lambda k=k: (vec, fv.at[p.s], (p.w, lax.rem(p.s + k, 8))))
    assert len(net.made) == GATHER_COPIES
    return net


def forward_kernel(
    x, seg, kept, wq, wk, wv, wo, wi, wr, vec,
    fi, fo, fa_out, qkv_out, att_out, inv_out, e_out, t1_out, rows, binner,
    own, fa, fv, qkv, att, inv, t1, segt, ebuf, ssem, rsem, lsem, esem,
):
    p = Place()
    for c in range(3):
        for part, ref in enumerate((wq, wk, wv)):
            own[c, :, part * CW : (part + 1) * CW] = ref[:, c * CW : (c + 1) * CW].astype(BF)
    greet(p, others(p))
    net = gather_net(p, own, fa, fi, fo, vec, fv, ssem, rsem)
    names = ("zb", "za", "zo")
    net.start((0, "zb"), (0, "za"), (0, "own", "c"))
    own[3] = wo[...].astype(BF)
    for q in range(4):
        own[4 + q] = wi[:, q * D : (q + 1) * D].astype(BF)
        own[8 + q] = wr[q * TR : (q + 1) * TR, :].astype(BF)
    net.start(*[("v", k) for k in range(1, 8)])
    local = {}

    def put(name, k, src, dst):
        local[name] = lambda: pltpu.make_async_copy(src(), dst(), lsem.at[k])

    put("own a", 0, lambda: own.at[0:4], lambda: fa.at[:, p.s])
    put("own i", 1, lambda: own.at[4:8], lambda: fi.at[:, p.s])
    put("own o", 2, lambda: own.at[8:12], lambda: fo.at[p.s])
    put("vec", 3, lambda: vec, lambda: fv.at[p.s])
    put("qkv", 4, lambda: qkv, lambda: qkv_out)
    put("fa", 5, lambda: fa, lambda: fa_out)
    put("att", 6, lambda: att, lambda: att_out)
    put("inv", 7, lambda: inv, lambda: inv_out)
    put("t1", 8, lambda: t1, lambda: t1_out)
    for name in ("own a", "own i", "own o", "vec"):
        local[name]().start()

    def ring1(g):
        net.wait((g, "zb"))
        net.start((g, "zo"))
        if HIER[g]:
            net.start((g, "zb", "xa"), (g, "zb", "xb"))
        net.wait((g, "za"))
        if HIER[g]:
            net.start((g, "za", "xa"), (g, "za", "xb"))

    def ring2(g):
        net.wait((g, "zo"))
        if HIER[g]:
            net.start((g, "zo", "xa"), (g, "zo", "xb"))

    def relay(g, name):
        net.wait((g, name, "xa"))
        net.start((g, name, "xd"))

    def share(g, name):
        if HIER[g]:
            net.wait((g, name, "xb"), (g, name, "xd"))
        net.start((g, name, "c"))

    def landed(g):
        net.wait((g, "own", "c"), *[(g, name, "c") for name in names])

    ring1(0)
    net.start((2, "zb"), (2, "za"), (1, "zb"), (1, "za"), (1, "own", "c"), (2, "own", "c"), (3, "own", "c"))
    ring2(0)
    turn_ids(seg, segt)
    relay(0, "zb")
    relay(0, "za")
    share(0, "zb")
    net.start((3, "zb"), (3, "za"))
    relay(0, "zo")
    share(0, "za")
    net.wait(*[("v", k) for k in range(1, 8)])
    local["vec"]().wait()
    expand_vectors(fv, rows, binner)
    share(0, "zo")
    ring1(2)
    ring1(1)
    local["own a"]().wait()
    landed(0)

    project(x, fa, rows, qkv)
    local["qkv"]().start()
    ring2(2)
    ring2(1)
    for name in names:
        share(1, name)
    keep = kept[0]

    def out_copy(i, slot):
        c, r, pair = place_of(i)
        return pltpu.make_async_copy(ebuf.at[slot], e_out.at[c, r, pair], esem.at[slot])

    steps = {
        0: lambda: relay(2, "zb"),
        1: lambda: relay(2, "za"),
        2: lambda: (share(2, "zb"), ring1(3)),
        3: lambda: relay(2, "zo"),
        4: lambda: share(2, "za"),
        6: lambda: (share(2, "zo"), share(3, "zb"), share(3, "za")),
        9: lambda: (ring2(3), share(3, "zo")),
    }

    def one(i, _):
        slot = lax.rem(i, 2)

        @pl.when(i >= 2)
        def _():
            out_copy(i - 2, slot).wait()

        attend(i, qkv, seg, segt, keep, att, inv, ebuf.at[slot])
        out_copy(i, slot).start()
        for k, step in steps.items():
            @pl.when(i == k)
            def _(step=step):
                step()
        return 0

    n = 6 * (x.shape[0] // SEQ)
    lax.fori_loop(0, n, one, 0)
    local["att"]().start()
    local["inv"]().start()
    landed(1)
    local["fa"]().start()

    def last(i, _):
        at = rows_of(i, 256)
        t1[at] = x[at].astype(F32) + (mm(att[at], fa[3].reshape(D, D)) + rows[2:3])
        return 0

    lax.fori_loop(0, x.shape[0] // 256, last, 0)
    local["t1"]().start()
    out_copy(n - 2, (n - 2) % 2).wait()
    out_copy(n - 1, (n - 1) % 2).wait()
    landed(2)
    landed(3)
    for name in ("own i", "own o", "qkv", "fa", "att", "inv", "t1"):
        local[name]().wait()
    net.finish()


def forward(x, seg, kept, wq, wk, wv, wo, wi, wr, vec):
    t = x.shape[0]
    n = t // SEQ
    return pl.pallas_call(
        forward_kernel,
        out_shape=(
            shape(4, 8, TR, D), shape(8, 4, TR, D), shape(4, 8, TR, D), shape(3, t, D), shape(t, D), shape(t, D, dtype=F32),
            shape(3, n, 2, 2, SEQ, SEQ), shape(t, D, dtype=F32), shape(8, D, dtype=F32), shape(1, FF, dtype=F32),
        ),
        in_specs=[VM, VM, SM] + [VM] * 7,
        out_specs=(ANY,) * 8 + (VM, VM),
        scratch_shapes=[
            pltpu.VMEM((12, TR, D), BF),
            pltpu.VMEM((4, 8, TR, D), BF),
            pltpu.VMEM((8, 16, 128), BF),
            pltpu.VMEM((3, t, D), BF),
            pltpu.VMEM((t, D), BF),
            pltpu.VMEM((t, D), F32),
            pltpu.VMEM((t, D), F32),
            pltpu.VMEM((n, SEQ, 128), F32),
            pltpu.VMEM((2, 2, SEQ, SEQ), BF),
            pltpu.SemaphoreType.DMA((GATHER_COPIES,)),
            pltpu.SemaphoreType.DMA((GATHER_COPIES,)),
            pltpu.SemaphoreType.DMA((9,)),
            pltpu.SemaphoreType.DMA((2,)),
        ],
        compiler_params=params(collective_id=0, has_side_effects=True),
        name="forward",
    )(x, seg, kept, wq, wk, wv, wo, wi, wr, vec)


def ffn_kernel(
    t1, grad, rows, binner, kept, inv, fi, fo, fa,
    y, res, bg, dos, sums, bsum, g_out,
    wi, wr, wo, hl, act, ig, og, gp, gbuf, lsem, gsem, block=256,
):
    load = [
        pltpu.make_async_copy(fi, wi, lsem.at[0]),
        pltpu.make_async_copy(fo, wr, lsem.at[1]),
        pltpu.make_async_copy(fa.at[3], wo, lsem.at[2]),
    ]
    for copy in load:
        copy.start()
    keep_heads = kept[0]
    b_outer, gain_two, shift_two = rows[5:6], rows[6:7], rows[7:8]
    gain_one, shift_one = rows[3:4], rows[4:5]
    sums[...] = jnp.zeros_like(sums)
    bsum[...] = jnp.zeros_like(bsum)
    heads = column_mask(keep_heads, (1, D), HEAD_DIM)
    for copy in load:
        copy.wait()

    def add(k, value):
        sums[k : k + 1] += jnp.sum(value, axis=0, keepdims=True)

    def inner_weight(j):
        return wi[j].reshape(D, D)

    def outer_weight(j):
        return wr[2 * j : 2 * j + 2].reshape(D, D)

    def one(i, _):
        at = rows_of(i, block)
        n1, inv1 = norm_rows(t1[at])
        hidden = n1 * gain_one + shift_one
        low = hidden.astype(BF)
        hl[at] = low
        outer = jnp.zeros((block, D), F32)
        for j in range(4):
            cols = slice(j * D, (j + 1) * D)
            inner = mm(low, inner_weight(j)) + binner[:, cols]
            keep = column_mask(keep_heads * 256 - j * D, (1, D), 1)
            phi = 0.5 + 0.5 * lax.erf(inner * RSQRT2)
            masked = inner * keep
            a = (masked * phi).astype(BF)
            gp[:, cols] = (keep * phi + masked * (RSQRT2PI * jnp.exp(-0.5 * (inner * inner)))).astype(BF)
            act[at, cols] = a
            outer = outer + mm(a, outer_weight(j))
        n2, inv2 = norm_rows(hidden + (outer + b_outer))
        y[at] = (n2 * gain_two + shift_two).astype(BF)
        top = grad[at].astype(F32)
        add(7, top)
        add(6, top * n2)
        res2 = norm_back(top * gain_two, n2, inv2)
        o = res2.astype(BF)
        og[at] = o
        add(5, o.astype(F32))
        hg = res2
        for j in range(4):
            cols = slice(j * D, (j + 1) * D)
            g = (mm(o, outer_weight(j), NT) * gp[:, cols].astype(F32)).astype(BF)
            ig[at, cols] = g
            bsum[:, cols] += jnp.sum(g.astype(F32), axis=0, keepdims=True)
            hg = hg + mm(g, inner_weight(j), NT)
        add(4, hg)
        n1, inv1 = norm_rows(t1[at])
        add(3, hg * n1)
        res1 = norm_back(hg * gain_one, n1, inv1)
        res[at] = res1
        b = res1.astype(BF)
        bg[at] = b
        add(2, b.astype(F32))
        dos[at] = (mm(b, wo[...].reshape(D, D), NT) * (inv[at] * heads)).astype(BF)
        return 0

    lax.fori_loop(0, t1.shape[0] // block, one, 0)

    def outer_out(j):
        return pltpu.make_async_copy(gbuf.at[j], g_out.at[lax.div(j, 2), pl.ds(2 * lax.rem(j, 2), 2), 0:4], gsem.at[j])

    def inner_out(j):
        return pltpu.make_async_copy(gbuf.at[4 + j], g_out.at[:, :, 4 + j], gsem.at[4 + j])

    def two(j, _):
        cols = rows_of(j, D)
        gbuf[j] = mm(act[:, cols], og[...], TN).astype(BF).reshape(2, 4, TR, D)
        outer_out(j).start()
        return 0

    lax.fori_loop(0, 4, two, 0)

    def three(j, _):
        cols = rows_of(j, D)
        gbuf[4 + j] = mm(hl[...], ig[:, cols], TN).astype(BF).reshape(2, 4, TR, D)
        inner_out(j).start()
        return 0

    lax.fori_loop(0, 4, three, 0)
    for j in range(4):
        outer_out(j).wait()
        inner_out(j).wait()


def ffn(t1, grad, rows, binner, kept, inv, fi, fo, fa):
    t = t1.shape[0]
    return pl.pallas_call(
        ffn_kernel,
        out_shape=(
            shape(t, D), shape(t, D, dtype=F32), shape(t, D), shape(t, D),
            shape(8, D, dtype=F32), shape(1, FF, dtype=F32), shape(2, 4, 8, TR, D),
        ),
        in_specs=[VM] * 4 + [SM, VM] + [ANY] * 3,
        out_specs=(VM,) * 6 + (ANY,),
        scratch_shapes=[
            pltpu.VMEM((4, 8, TR, D), BF),
            pltpu.VMEM((8, 4, TR, D), BF),
            pltpu.VMEM((8, TR, D), BF),
            pltpu.VMEM((t, D), BF),
            pltpu.VMEM((t, FF), BF),
            pltpu.VMEM((t, FF), BF),
            pltpu.VMEM((t, D), BF),
            pltpu.VMEM((256, FF), BF),
            pltpu.VMEM((8, 2, 4, TR, D), BF),
            pltpu.SemaphoreType.DMA((3,)),
            pltpu.SemaphoreType.DMA((8,)),
        ],
        compiler_params=params(),
        name="ffn",
    )(t1, grad, rows, binner, kept, inv, fi, fo, fa)


def attend_back(i, qkv, dos, att, ebuf, dqkv):
    c, r, pair = place_of(i)
    rows = rows_of(r, SEQ)
    lanes = pl.ds(pl.multiple_of(c * CW + pair * 128, 128), 128)
    qp, kp, vp = (qkv[c, rows, pair_lanes(pair, part)] for part in range(3))
    dp = dos[rows, lanes]
    low = low_lanes(SEQ)
    zero = jnp.zeros_like(qp)
    product = dp.astype(F32) * att[rows, lanes].astype(F32)
    gq = jnp.zeros((SEQ, 128), F32)
    gk = jnp.zeros((SEQ, 128), F32)
    gv = jnp.zeros((SEQ, 128), F32)
    for h in range(2):
        mine = low if h == 0 else jnp.logical_not(low)
        dh = jnp.where(mine, dp, zero)
        delta = jnp.sum(jnp.where(mine, product, 0.0), axis=1, keepdims=True)
        e = ebuf[h]
        ds = (e.astype(F32) * (mm(dh, vp, NT) - delta)).astype(BF)
        gv = gv + mm(e, dh, TN)
        gk = gk + mm(ds, jnp.where(mine, qp, zero), TN)
        gq = gq + mm(ds, jnp.where(mine, kp, zero))
    dqkv[c, rows, pair_lanes(pair, 0)] = (gq * 0.125).astype(BF)
    dqkv[c, rows, pair_lanes(pair, 1)] = gk.astype(BF)
    dqkv[c, rows, pair_lanes(pair, 2)] = gv.astype(BF)


def chunk_grads(c, x, dqkv, gx, sums):
    gx[c] = mm(x[...], dqkv[c], TN).astype(BF).reshape(4, 2, 1, TR, D)
    part = dqkv[c].astype(F32)
    total = jnp.sum(part, axis=0, keepdims=True)
    lanes = pl.ds(pl.multiple_of(c * CW, CW), CW)
    sums[0:1, lanes] = total[:, 0:CW]
    sums[1:2, lanes] = total[:, 2 * CW :]


def input_back(res, dqkv, fa, out, block=256):
    def one(i, _):
        at = rows_of(i, block)
        total = res[at]
        for c in range(3):
            total = total + mm(dqkv[c, at], fa[c].reshape(D, D), NT)
        out[at] = total.astype(BF)
        return 0

    lax.fori_loop(0, res.shape[0] // block, one, 0)


JOBS = ((0, 4, True), (4, 4, False), (8, 1, True), (9, 1, False), (10, 1, True), (11, 1, False))
REDUCE_COPIES = 10 * len(JOBS) + 7
JOB_BUFFERS = 7


def job_shapes(units, ring_first):
    big, part, tile = (4, units, TR, D), (units, 48, 384), (units, TR, D)
    first = tile if ring_first else (4, *part)
    return [big, big, first, first, first, first, part, part, part]


class Job:
    def __init__(self, net, p, k, first, units, ring_first, source, bufs, result):
        self.net, self.p, self.k, self.ring_first = net, p, k, ring_first
        self.held, self.landed, self.d1, self.a1, self.b1, self.mid, self.d2, self.a2, self.b2 = bufs
        self.result = result
        self.units = slice(first, first + units)
        held, mid = self.held, self.mid
        z, za, zb, zo = p.z, lax.div(p.sa, 2), lax.div(p.sb, 2), lax.div(p.so, 2)
        self.z = z
        ring = (za, zb, zo, p.ring_a, p.ring_a, p.ring_b)
        plane = (p.wb, p.wa, p.wd, p.plane_a, p.plane_b, p.plane_a)

        def tile(t):
            return held, (t,)

        def plane_quarter(w):
            return held, (slice(None), slice(None), *quarter(w))

        def mid_quarter(w):
            return mid, (slice(None), *quarter(w))

        def mid_tile(t):
            return mid, (t,)

        one, two = (ring, plane) if ring_first else (plane, ring)
        self.at1, self.at2 = (tile, mid_quarter) if ring_first else (plane_quarter, mid_tile)
        self.one, self.two = one, two
        self.own1 = z if ring_first else p.w
        self.own2 = p.w if ring_first else z
        net.define((k, "c"), lambda: (source(1 - p.c), self.landed, p.sib))
        for stage, at, way, d, a, b in ((1, self.at1, one, self.d1, self.a1, self.b1), (2, self.at2, two, self.d2, self.a2, self.b2)):
            relayed, direct, opposite, dev_o, dev_r, dev_d = way

            def send(name, index, dst, device, at=at):
                def make():
                    ref, where = at(index)
                    return ref.at[where], dst, device

                net.define((k, name), make)

            send(("d", stage), opposite, d, dev_o)
            send(("b", stage), direct, b, dev_d)
            send(("a", stage), relayed, a, dev_r)

        def share(name, w, device):
            def make():
                ref = result.at[(self.units, *quarter(w))]
                return ref, ref, device

            net.define((k, name), make)

        share("ga", p.w, p.plane_a)
        share("gb", p.w, p.plane_b)
        share("gd", p.wa, p.plane_b)

    def start(self, *names):
        self.net.start(*[(self.k, name) for name in names])

    def wait(self, *names):
        self.net.wait(*[(self.k, name) for name in names])

    def send(self):
        self.start("c")

    def pair(self):
        self.wait("c")
        held, landed = self.held, self.landed

        def one(t, _):
            held[t] = (held[t].astype(F32) + landed[t].astype(F32)).astype(BF)
            return 0

        lax.fori_loop(0, 4, one, 0)
        self.start(("d", 1), ("b", 1))

    def relay(self, stage):
        at, way, d = (self.at1, self.one, self.d1) if stage == 1 else (self.at2, self.two, self.d2)
        self.wait(("d", stage))
        ref, where = at(way[0])
        ref[where] = (ref[where].astype(F32) + d[...].astype(F32)).astype(BF)
        self.start(("a", stage))

    def total(self, stage):
        at, own, a, b = (self.at1, self.own1, self.a1, self.b1) if stage == 1 else (self.at2, self.own2, self.a2, self.b2)
        self.wait(("a", stage), ("b", stage))
        ref, where = at(own)
        return (ref[where].astype(F32) + a[...].astype(F32) + b[...].astype(F32)).astype(BF)

    def turn(self):
        self.mid[...] = self.total(1)
        self.start(("d", 2), ("b", 2))

    def share(self):
        self.result[(self.units, *quarter(self.p.w))] = self.total(2)
        self.start("ga", "gb")

    def pass_on(self):
        self.wait("ga")
        self.start("gd")

    def end(self):
        self.wait("gb", "gd")


def backward_kernel(
    x, qkv_in, e_in, att_in, dos_in, bg_in, res_in, fa_in, g_in, sums_in, bsum,
    out, result, ovec,
    qkv, att, dos, bg, res, fa, dqkv, gx, go, ebuf, sums, vt, vheld, vrecv, vplane, vz, *rest,
):
    bufs, (ssem, rsem, lsem, esem) = rest[:-4], rest[-4:]
    p = Place()
    n = 6 * (x.shape[0] // SEQ)
    load = {}

    def get(name, k, src, dst):
        load[name] = pltpu.make_async_copy(src, dst, lsem.at[k])
        load[name].start()

    def in_copy(i, slot):
        c, r, pair = place_of(i)
        return pltpu.make_async_copy(e_in.at[c, r, pair], ebuf.at[slot], esem.at[slot])

    jobs = []
    net = Net(ssem, rsem)
    g4 = g_in
    per = 9
    for k, (first, units, ring_first) in enumerate(JOBS):
        if k < 2:
            source = lambda core, first=first, units=units: g4.at[:, core, first : first + units]
        elif k == 2:
            source = lambda core: go.at[:, core]
        else:
            source = lambda core, c=k - 3: gx.at[c, :, core]
        jobs.append(Job(net, p, k, first, units, ring_first, source, bufs[per * k : per * (k + 1)], result))
    get("att", 0, att_in, att)
    get("bg", 1, bg_in, bg)
    get("h0", 2, g4.at[:, p.c, 0:4], jobs[0].held)
    get("h1", 3, g4.at[:, p.c, 4:8], jobs[1].held)
    get("qkv", 4, qkv_in, qkv)
    get("dos", 5, dos_in, dos)
    in_copy(0, 0).start()
    get("res", 6, res_in, res)
    get("fa", 7, fa_in.at[0:3], fa)
    net.define(("v", "c"), lambda: (vt.at[:, 1 - p.c], vrecv, p.sib))
    for k, device in enumerate((p.plane_a, p.plane_b, (p.wd, p.s))):
        net.define(("v", "p", k), lambda device=device: (vheld.at[0], vplane.at[p.w], device))
    for k in range(1, 4):
        to = lax.rem(p.z + k, 4)
        net.define(("v", "z", k), lambda to=to: (vheld.at[1, to], vz.at[p.z], (p.w, 2 * to + p.c)))
    assert len(net.made) == REDUCE_COPIES, len(net.made)

    greet(p, others(p))
    jobs[0].send()
    jobs[1].send()
    sums[...] = sums_in[...]
    load["att"].wait()
    load["bg"].wait()
    go[...] = mm(att[...], bg[...], TN).astype(BF).reshape(4, 2, 1, TR, D)
    jobs[2].send()
    load["h0"].wait()
    jobs[0].pair()
    load["h1"].wait()
    jobs[1].pair()

    def own_half(k, source):
        jobs[k].held[...] = source[:, p.c]

    own_half(2, go)
    load["qkv"].wait()
    load["dos"].wait()
    jobs[2].pair()

    def begin(k):
        own_half(k, gx.at[k - 3])
        jobs[k].pair()

    a, b, w, c0, c1, c2 = jobs
    steps = {
        2: lambda: w.relay(1),
        3: lambda: c0.send(),
        4: lambda: (b.relay(1), begin(3), w.turn()),
        5: lambda: a.relay(1),
        6: lambda: (w.relay(2), c0.relay(1)),
        7: lambda: (c1.send(), w.share()),
        8: lambda: (b.turn(), begin(4), c0.turn()),
        9: lambda: (a.turn(), b.relay(2), w.pass_on()),
        10: lambda: (c1.relay(1), c0.relay(2), b.share()),
        11: lambda: (c2.send(), a.relay(2), c0.share(), c1.turn()),
    }

    def one(i, _):
        slot = lax.rem(i, 2)

        @pl.when(i + 1 < n)
        def _():
            in_copy(i + 1, 1 - slot).start()

        in_copy(i, slot).wait()
        attend_back(i, qkv, dos, att, ebuf.at[slot], dqkv)

        @pl.when(lax.rem(i, 4) == 3)
        def _():
            chunk_grads(lax.div(i, 4), x, dqkv, gx, sums)

        for k, step in steps.items():
            @pl.when(i == k)
            def _(step=step):
                step()
        return 0

    lax.fori_loop(0, n, one, 0)

    for s in range(8):
        vt[s // 2, s % 2] = jnp.zeros((16, 128), F32)
        vt[s // 2, s % 2, 0:8, 0:TR] = sums[:, TR * s : TR * (s + 1)]
        for r in range(3):
            vt[s // 2, s % 2, 8 + r : 9 + r] = bsum[0:1, 128 * (3 * s + r) : 128 * (3 * s + r + 1)]
    net.start(("v", "c"))
    begin(5)
    a.share()
    b.pass_on()
    c0.pass_on()
    c1.relay(2)
    net.wait(("v", "c"))
    vheld[0] = vt[:, p.c] + vrecv[...]
    vplane[p.w] = vheld[0]
    net.start(*[("v", "p", k) for k in range(3)])
    load["res"].wait()
    load["fa"].wait()
    c2.relay(1)

    def back(i):
        at = pl.ds(256 * i, 256)
        total = res[at]
        for c in range(3):
            total = total + mm(dqkv[c, at], fa[c].reshape(D, D), NT)
        out[at] = total.astype(BF)

    back(0)
    a.pass_on()
    c1.share()
    c2.turn()
    net.wait(*[("v", "p", k) for k in range(3)])
    vheld[1] = (vplane[0] + vplane[1]) + (vplane[2] + vplane[3])
    vz[p.z] = vheld[1, p.z]
    net.start(*[("v", "z", k) for k in range(1, 4)])
    back(1)
    c1.pass_on()
    c2.relay(2)
    back(2)
    c2.share()
    back(3)
    net.wait(*[("v", "z", k) for k in range(1, 4)])
    ovec[...] = (vz[0] + vz[1]) + (vz[2] + vz[3])
    c2.pass_on()
    for job in jobs:
        job.end()
    net.finish()


def backward(x, qkv, e, att, dos, bg, res, fa, g, sums, bsum):
    t = x.shape[0]
    job_scratch = [pltpu.VMEM(s, BF) for _, units, ring_first in JOBS for s in job_shapes(units, ring_first)]
    return pl.pallas_call(
        backward_kernel,
        out_shape=(shape(t, D), shape(12, TR, D), shape(16, 128, dtype=F32)),
        in_specs=[VM] + [ANY] * 8 + [VM, VM],
        out_specs=(VM,) * 3,
        scratch_shapes=[
            pltpu.VMEM((3, t, D), BF),
            pltpu.VMEM((t, D), BF),
            pltpu.VMEM((t, D), BF),
            pltpu.VMEM((t, D), BF),
            pltpu.VMEM((t, D), F32),
            pltpu.VMEM((3, 8, TR, D), BF),
            pltpu.VMEM((3, t, D), BF),
            pltpu.VMEM((3, 4, 2, 1, TR, D), BF),
            pltpu.VMEM((4, 2, 1, TR, D), BF),
            pltpu.VMEM((2, 2, SEQ, SEQ), BF),
            pltpu.VMEM((8, D), F32),
            pltpu.VMEM((4, 2, 16, 128), F32),
            pltpu.VMEM((2, 4, 16, 128), F32),
            pltpu.VMEM((4, 16, 128), F32),
            pltpu.VMEM((4, 4, 16, 128), F32),
            pltpu.VMEM((4, 16, 128), F32),
        ]
        + job_scratch
        + [
            pltpu.SemaphoreType.DMA((REDUCE_COPIES,)),
            pltpu.SemaphoreType.DMA((REDUCE_COPIES,)),
            pltpu.SemaphoreType.DMA((8,)),
            pltpu.SemaphoreType.DMA((2,)),
        ],
        compiler_params=params(collective_id=1, has_side_effects=True),
        name="backward",
    )(x, qkv, e, att, dos, bg, res, fa, g.reshape(4, 2, 8, TR, D), sums, bsum)


def finish_kernel(result, ovec, inp, oq, ok, ov, oo, oi, our, out, *vectors):
    for c in range(3):
        tile = result[9 + c].astype(F32)
        for part, ref in enumerate((oq, ok, ov)):
            ref[:, c * CW : (c + 1) * CW] = tile[:, part * CW : (part + 1) * CW]
    oo[...] = result[8].astype(F32)
    for q in range(4):
        oi[:, q * D : (q + 1) * D] = result[4 + q].astype(F32)
        our[q * TR : (q + 1) * TR, :] = result[q].astype(F32)
    out[...] = inp[...]
    for k in range(8):
        vectors[k][...] = ovec[k, 0:TR]
    for r in range(3):
        vectors[8][128 * r : 128 * (r + 1)] = ovec[8 + r]


def finish(result, ovec, inp):
    t = inp.shape[0]
    return pl.pallas_call(
        finish_kernel,
        out_shape=tuple(shape(TR, D, dtype=F32) for _ in range(4))
        + (shape(TR, FF, dtype=F32), shape(4 * TR, D, dtype=F32), shape(t, D))
        + tuple(shape(TR, dtype=F32) for _ in range(8))
        + (shape(4 * TR, dtype=F32),),
        in_specs=[VM] * 3,
        out_specs=(VM,) * 16,
        compiler_params=params(),
        name="finish",
    )(result, ovec, inp)


def forward_local_kernel(x, seg, kept, fa, rows, qkv, att, inv, e_out, t1, segt, ebuf, esem):
    turn_ids(seg, segt)
    project(x, fa, rows, qkv)
    keep = kept[0]

    def one(i, _):
        c, r, pair = place_of(i)
        attend(i, qkv, seg, segt, keep, att, inv, ebuf)
        copy = pltpu.make_async_copy(ebuf, e_out.at[c, r, pair], esem.at[0])
        copy.start()
        copy.wait()
        return 0

    lax.fori_loop(0, 6 * (x.shape[0] // SEQ), one, 0)
    t1[...] = x[...].astype(F32) + (mm(att[...], fa[3].reshape(D, D)) + rows[2:3])


def forward_local(x, seg, kept, fa, rows):
    t = x.shape[0]
    n = t // SEQ
    return pl.pallas_call(
        forward_local_kernel,
        out_shape=(shape(3, t, D), shape(t, D), shape(t, D, dtype=F32), shape(3, n, 2, 2, SEQ, SEQ), shape(t, D, dtype=F32)),
        in_specs=[VM, VM, SM, VM, VM],
        out_specs=(VM, VM, VM, ANY, VM),
        scratch_shapes=[
            pltpu.VMEM((n, SEQ, 128), F32), pltpu.VMEM((2, SEQ, SEQ), BF), pltpu.SemaphoreType.DMA((1,)),
        ],
        compiler_params=params(),
        name="forward_local",
    )(x, seg, kept, fa, rows)


def backward_local_kernel(x, qkv, e_in, att, dos, bg, res, fa, sums_in, out, gx, go, sums, dqkv, ebuf, esem):
    sums[...] = sums_in[...]
    go[...] = mm(att[...], bg[...], TN).astype(BF).reshape(4, 2, 1, TR, D)

    def one(i, _):
        c, r, pair = place_of(i)
        copy = pltpu.make_async_copy(e_in.at[c, r, pair], ebuf, esem.at[0])
        copy.start()
        copy.wait()
        attend_back(i, qkv, dos, att, ebuf, dqkv)

        @pl.when(lax.rem(i, 4) == 3)
        def _():
            chunk_grads(lax.div(i, 4), x, dqkv, gx, sums)

        return 0

    lax.fori_loop(0, 6 * (x.shape[0] // SEQ), one, 0)
    input_back(res, dqkv, fa, out)


def backward_local(x, qkv, e, att, dos, bg, res, fa, sums):
    t = x.shape[0]
    return pl.pallas_call(
        backward_local_kernel,
        out_shape=(shape(t, D), shape(3, 4, 2, 1, TR, D), shape(4, 2, 1, TR, D), shape(8, D, dtype=F32)),
        in_specs=[VM, VM, ANY] + [VM] * 6,
        out_specs=(VM,) * 4,
        scratch_shapes=[pltpu.VMEM((3, t, D), BF), pltpu.VMEM((2, SEQ, SEQ), BF), pltpu.SemaphoreType.DMA((1,))],
        compiler_params=params(),
        name="backward_local",
    )(x, qkv, e, att, dos, bg, res, fa, sums)


def gather_lax(wq, wk, wv, wo, wi, wr, eight, b_inner):
    def whole(a):
        return lax.all_gather(a.astype(BF), "shard", axis=0, tiled=True)

    wq, wk, wv, wo, wi, wr = (whole(a) for a in (wq, wk, wv, wo, wi, wr))
    chunks = [jnp.concatenate([a[:, c * CW : (c + 1) * CW] for a in (wq, wk, wv)], axis=1) for c in range(3)]
    fa = jnp.stack(chunks + [wo]).reshape(4, 8, TR, D)
    fi = jnp.stack([wi[:, q * D : (q + 1) * D] for q in range(4)]).reshape(4, 8, TR, D)
    rows = jnp.stack([whole(a) for a in eight]).astype(F32)
    return fa, fi, wr.reshape(8, 4, TR, D), rows, whole(b_inner).astype(F32).reshape(1, FF)


def reduce_lax(g, gx, go, sums, bsum):
    g = g.reshape(8, 8, TR, D)
    gr = g[:, 0:4].reshape(FF, D)
    gi = jnp.concatenate([g[:, 4 + j].reshape(D, D) for j in range(4)], axis=1)
    gx = gx.reshape(3, D, 3, CW)
    squares = [jnp.concatenate([gx[c, :, part] for c in range(3)], axis=1) for part in range(3)]

    def owned(a):
        a = lax.psum_scatter(a.astype(F32), "shard", scatter_dimension=0, tiled=True)
        return lax.psum(a.astype(BF), "width").astype(F32)

    matrices = [owned(a) for a in (*squares, go.reshape(D, D), gi, gr)]
    return matrices, [owned(sums[k]) for k in range(8)] + [owned(bsum[0])]


def body(
    layer_input, segment_ids, group_heads,
    w_query, b_query, w_key, w_value, b_value, w_out, b_out, gain_one, shift_one,
    w_inner, b_inner, w_outer, b_outer, gain_two, shift_two, out_grad,
):
    eight = (b_query, b_value, b_out, gain_one, shift_one, b_outer, gain_two, shift_two)
    weights = (w_query, w_key, w_value, w_out, w_inner, w_outer)
    own_kernels = lax.axis_size("width") == 4 and lax.axis_size("shard") == 8
    if own_kernels:
        vec = jnp.concatenate([jnp.stack(eight), jnp.zeros((8, 128 - TR), F32)], axis=1)
        vec = jnp.concatenate([vec, b_inner.reshape(3, 128), jnp.zeros((5, 128), F32)], axis=0).astype(BF)
        fi, fo, fa, qkv, att, inv, e, t1, rows, binner = forward(layer_input, segment_ids, group_heads, *weights, vec)
    else:
        fa, fi, fo, rows, binner = gather_lax(*weights, eight, b_inner)
        qkv, att, inv, e, t1 = forward_local(layer_input, segment_ids, group_heads, fa, rows)
    y, res, bg, dos, sums, bsum, g = ffn(t1, out_grad, rows, binner, group_heads, inv, fi, fo, fa)
    if own_kernels:
        input_grad, result, ovec = backward(layer_input, qkv, e, att, dos, bg, res, fa, g, sums, bsum)
        gq, gk, gv, go, gi, gr, input_grad, *vectors = finish(result, ovec, input_grad)
    else:
        input_grad, gx, go, sums = backward_local(layer_input, qkv, e, att, dos, bg, res, fa[0:3], sums)
        (gq, gk, gv, go, gi, gr), vectors = reduce_lax(g, gx, go, sums, bsum)
    return (
        y, input_grad, gq, vectors[0], gk, gv, vectors[1], go, vectors[2],
        vectors[3], vectors[4], gi, vectors[8], gr, vectors[5], vectors[6], vectors[7],
    )


def solution(mesh):
    placed = (
        P(("width", "shard"), None),
        P(("width", "shard"), None),
        P("width"),
        P("shard", None),
        P("shard"),
        P("shard", None),
        P("shard", None),
        P("shard"),
        P("shard", None),
        P("shard"),
        P("shard"),
        P("shard"),
        P("shard", None),
        P("shard"),
        P("shard", None),
        P("shard"),
        P("shard"),
        P("shard"),
        P(("width", "shard"), None),
    )
    return jax.shard_map(
        body,
        mesh=mesh,
        in_specs=placed,
        out_specs=(
            P(("width", "shard"), None),
            P(("width", "shard"), None),
            P("shard", None),
            P("shard"),
            P("shard", None),
            P("shard", None),
            P("shard"),
            P("shard", None),
            P("shard"),
            P("shard"),
            P("shard"),
            P("shard", None),
            P("shard"),
            P("shard", None),
            P("shard"),
            P("shard"),
            P("shard"),
        ),
        check_vma=False,
    )
```

```python
import functools
import jax
import jax.numpy as jnp
from jax import lax
from jax.experimental import pallas as pl
from jax.experimental.pallas import tpu as pltpu
from jax.sharding import PartitionSpec as P

HEADS = 12
HEAD_DIM = 64
FF = 3072
D = 768
SEQ = 512
MESH = pl.DeviceIdType.MESH
BF = jnp.bfloat16
F32 = jnp.float32
TR = 96
CW = 256
NT = (((1,), (1,)), ((), ()))
TN = (((0,), (0,)), ((), ()))
NN = (((1,), (0,)), ((), ()))
EPS = 1e-06
RSQRT2 = 0.7071067811865476
RSQRT2PI = 0.3989422804014327
VM = pl.BlockSpec(memory_space=pltpu.VMEM)
SM = pl.BlockSpec(memory_space=pltpu.SMEM)
ANY = pl.BlockSpec(memory_space=pl.ANY)


def params(**more):
    return pltpu.CompilerParams(vmem_limit_bytes=62 << 20, **more)


def shape(*dims, dtype=BF):
    return jax.ShapeDtypeStruct(dims, dtype)


class Place:
    def __init__(self):
        self.w = w = lax.axis_index("width")
        self.s = s = lax.axis_index("shard")
        self.c = c = lax.rem(s, 2)
        self.z = lax.div(s, 2)
        xw, yw = w + 1 - 2 * lax.rem(w, 2), lax.rem(w + 2, 4)
        up, down = lax.rem(s + 2, 8), lax.rem(s + 6, 8)
        self.wa = jnp.where(c == 0, xw, yw)
        self.wb = jnp.where(c == 0, yw, xw)
        self.wd = 3 - w
        self.sa = jnp.where(c == 0, up, down)
        self.sb = jnp.where(c == 0, down, up)
        self.so = lax.rem(s + 4, 8)
        self.sib = (w, s + 1 - 2 * c)
        self.plane_a, self.plane_b = (self.wa, s), (self.wb, s)
        self.ring_a, self.ring_b = (w, self.sa), (w, self.sb)


def call(devices):
    barrier = pltpu.get_barrier_semaphore()
    for device in devices:
        pl.semaphore_signal(barrier, inc=1, device_id=device, device_id_type=MESH)


def answer(devices):
    pl.semaphore_wait(pltpu.get_barrier_semaphore(), len(devices))


def others(p):
    return [(p.wa, p.s), (p.wb, p.s), (p.wd, p.s)] + [(p.w, lax.rem(p.s + k, 8)) for k in range(1, 8)]


class Net:
    def __init__(self, send, recv):
        self.send, self.recv, self.made, self.sent = send, recv, {}, set()

    def define(self, name, make):
        assert name not in self.made
        self.made[name] = (len(self.made), make)

    def copy(self, name):
        k, make = self.made[name]
        src, dst, device = make()
        return pltpu.make_async_remote_copy(
            src_ref=src, dst_ref=dst, send_sem=self.send.at[k], recv_sem=self.recv.at[k],
            device_id=device, device_id_type=MESH,
        )

    def start(self, *names):
        for name in names:
            self.copy(name).start()

    def wait(self, *names):
        for name in names:
            self.copy(name).wait_recv()

    def finish(self):
        for name in self.made:
            if name not in self.sent:
                self.copy(name).wait_send()


def quarter(w):
    return pl.ds(pl.multiple_of(48 * lax.rem(w, 2), 48), 48), pl.ds(pl.multiple_of(384 * lax.div(w, 2), 384), 384)


def mm(a, b, dims=NN):
    return lax.dot_general(a, b, dims, preferred_element_type=F32)


def rows_of(i, size):
    return pl.ds(pl.multiple_of(i * size, size), size)


def column_mask(kept, shape, width):
    return jnp.where(lax.broadcasted_iota(jnp.int32, shape, 1) < kept * width, 1.0, 0.0).astype(F32)


def mean_of(v):
    return jnp.sum(v, axis=1, keepdims=True) * (1.0 / D)


def norm_rows(total):
    centered = total - mean_of(total)
    inverse = lax.rsqrt(mean_of(centered * centered) + EPS)
    return centered * inverse, inverse


def norm_back(grad, normed, inverse):
    return inverse * (grad - mean_of(grad) - normed * mean_of(grad * normed))


def low_lanes(n):
    return lax.broadcasted_iota(jnp.int32, (n, 128), 1) < HEAD_DIM


def place_of(i):
    return lax.div(i, 4), lax.rem(i, 2), lax.rem(lax.div(i, 2), 2)


def pair_lanes(pair, part):
    return pl.ds(pl.multiple_of(part * CW + pair * 128, 128), 128)


def project(c, x, fa, rows, qkv, block=256):
    lanes = pl.ds(pl.multiple_of(c * CW, CW), CW)
    bias = jnp.concatenate([rows[0:1, lanes], jnp.zeros((1, CW), F32), rows[1:2, lanes]], axis=1)
    scale = jnp.where(lax.broadcasted_iota(jnp.int32, (1, D), 1) < CW, 0.125, 1.0)

    def one(i, _):
        at = rows_of(i, block)
        qkv[c, at] = ((mm(x[at], fa[c].reshape(D, D)) + bias) * scale).astype(BF)
        return 0

    lax.fori_loop(0, x.shape[0] // block, one, 0)


def turn_ids(seg, segt):
    for r in range(seg.shape[0]):
        row = seg[r : r + 1, :].astype(F32)
        segt[r] = jnp.broadcast_to(row, (128, SEQ)).T


def attend(i, qkv, seg, segt, kept, att, inv, ebuf, qb=512):
    c, r, pair = place_of(i)
    base = r * SEQ
    rows = pl.ds(pl.multiple_of(base, SEQ), SEQ)
    kp, vp = qkv[c, rows, pair_lanes(pair, 1)], qkv[c, rows, pair_lanes(pair, 2)]
    low = low_lanes(SEQ)
    ones = jnp.ones_like(vp)
    vs = (jnp.where(low, vp, ones), jnp.where(low, ones, vp))
    ids = seg[pl.ds(r, 1), :].astype(F32)
    lowq = low_lanes(qb)
    lanes = pl.ds(pl.multiple_of(c * CW + pair * 128, 128), 128)
    column = lax.broadcasted_iota(jnp.int32, (1, 128), 1) + (c * CW + pair * 128)
    mask = jnp.where(column < kept * HEAD_DIM, 1.0, 0.0).astype(F32)
    for b in range(SEQ // qb):
        at = pl.ds(pl.multiple_of(base + b * qb, qb), qb)
        qp = qkv[c, at, pair_lanes(pair, 0)]
        zero = jnp.zeros_like(qp)
        own = segt[r, b * qb : (b + 1) * qb]
        same = jnp.concatenate([own == ids[:, j * 128 : (j + 1) * 128] for j in range(4)], axis=1)
        out = []
        for h in range(2):
            qh = jnp.where(lowq, qp, zero) if h == 0 else jnp.where(lowq, zero, qp)
            scores = jnp.where(same, mm(qh, kp, NT), -1e30)
            top = jnp.max(scores, axis=1, keepdims=True)
            e = jnp.exp(scores - top).astype(BF)
            ebuf[h, b * qb : (b + 1) * qb] = e
            out.append(mm(e, vs[h]))
        inverse = 1.0 / pltpu.roll(jnp.where(lowq, out[1], out[0]), HEAD_DIM, 1)
        att[at, lanes] = (jnp.where(lowq, out[0], out[1]) * (inverse * mask)).astype(BF)
        inv[at, lanes] = inverse


def expand_vectors(fv, rows, binner):
    lane = lax.broadcasted_iota(jnp.int32, (128, D), 0)
    column = lax.broadcasted_iota(jnp.int32, (128, D), 1)
    total = jnp.zeros((16, D), F32)
    for s in range(8):
        pick = jnp.where((column == lane + TR * s) & (lane < TR), 1.0, 0.0).astype(BF)
        total = total + mm(fv[s], pick)
        tile = fv[s].astype(F32)
        for r in range(3):
            binner[0:1, 128 * (3 * s + r) : 128 * (3 * s + r + 1)] = tile[8 + r : 9 + r]
    rows[...] = total[0:8]


GROUPS = (slice(0, 1), slice(1, 2), slice(2, 3), slice(3, 4), slice(4, 8), slice(8, 12))
WO, INNER, OUTER = 3, 4, 5
GATHER_COPIES = 16 * len(GROUPS) + 7


def gather_net(p, own, fa, fi, fo, vec, fv, ssem, rsem):
    net = Net(ssem, rsem)
    every = (slice(None), slice(None))

    def piece(g, s, part):
        if g <= WO:
            return fa.at[(GROUPS[g], s, *part)]
        return fi.at[(slice(None), s, *part)] if g == INNER else fo.at[(s, slice(None), *part)]

    mine, first = quarter(p.w), quarter(p.wa)
    for g in range(len(GROUPS)):

        def add(name, src, dst, device):
            net.define((g, *name), lambda: (src(), dst(), device))

        def same(name, g, s, part, device):
            add(name, lambda: piece(g, s, part), lambda: piece(g, s, part), device)

        for name, device in (("zb", p.ring_a), ("za", p.ring_b)):
            add((name,), lambda g=g: own.at[(GROUPS[g], *mine)], lambda g=g: piece(g, p.s, mine), device)
        same(("zo",), g, p.sb, mine, p.ring_a)
        add(("own", "c"), lambda g=g: own.at[GROUPS[g]], lambda g=g: piece(g, p.s, every), p.sib)
        for name, s in (("zb", p.sb), ("za", p.sa), ("zo", p.so)):
            same((name, "xa"), g, s, mine, p.plane_a)
            same((name, "xb"), g, s, mine, p.plane_b)
            same((name, "xd"), g, s, first, p.plane_b)
            same((name, "c"), g, s, every, p.sib)
    for k in range(1, 8):
        net.define(("v", k), lambda k=k: (vec, fv.at[p.s], (p.w, lax.rem(p.s + k, 8))))
    assert len(net.made) == GATHER_COPIES
    return net


def ffn_inner(i, block, t1, rows, binner, kept, wi, hl, act, gp):
    at = rows_of(i, block)
    n1, _ = norm_rows(t1[at])
    low = (n1 * rows[3:4] + rows[4:5]).astype(BF)
    hl[at] = low
    for j in range(4):
        inner = mm(low, wi[j].reshape(D, D)) + binner[:, j * D : (j + 1) * D]
        keep = column_mask(kept * 256 - j * D, (1, D), 1)
        phi = 0.5 + 0.5 * lax.erf(inner * RSQRT2)
        masked = inner * keep
        act[j, at] = (masked * phi).astype(BF)
        gp[j, at] = (keep * phi + masked * (RSQRT2PI * jnp.exp(-0.5 * (inner * inner)))).astype(BF)


def ffn_outer(i, block, t1, grad, rows, kept, wi, wr, wo, inv, act, gp, y, bg, dos, og, sums, bsum):
    at = rows_of(i, block)

    def add(k, value):
        sums[k : k + 1] += jnp.sum(value, axis=0, keepdims=True)

    def outer_weight(j):
        return wr[2 * j : 2 * j + 2].reshape(D, D)

    outer = jnp.zeros((block, D), F32)
    for j in range(4):
        outer = outer + mm(act[j, at], outer_weight(j))
    n1, inv1 = norm_rows(t1[at])
    hidden = n1 * rows[3:4] + rows[4:5]
    n2, inv2 = norm_rows(hidden + (outer + rows[5:6]))
    y[at] = (n2 * rows[6:7] + rows[7:8]).astype(BF)
    top = grad[at].astype(F32)
    add(7, top)
    add(6, top * n2)
    res2 = norm_back(top * rows[6:7], n2, inv2)
    o = res2.astype(BF)
    og[at] = o
    add(5, o.astype(F32))
    hg = res2
    for j in range(4):
        cols = slice(j * D, (j + 1) * D)
        g = (mm(o, outer_weight(j), NT) * gp[j, at].astype(F32)).astype(BF)
        gp[j, at] = g
        bsum[:, cols] += jnp.sum(g.astype(F32), axis=0, keepdims=True)
        hg = hg + mm(g, wi[j].reshape(D, D), NT)
    add(4, hg)
    add(3, hg * n1)
    res1 = norm_back(hg * rows[3:4], n1, inv1)
    t1[at] = res1
    b = res1.astype(BF)
    bg[at] = b
    add(2, b.astype(F32))
    heads = column_mask(kept, (1, D), HEAD_DIM)
    dos[at] = (mm(b, wo, NT) * (inv[at] * heads)).astype(BF)


def forward_kernel(
    x, seg, kept, wq, wk, wv, wo, wi, wr, vec, grad_in,
    sums, bsum, fa_out, qkv_out, att_out, e_out, y_out, res_out, bg_out, dos_out, hl_out, og_out, ai_out,
    own, fa, fi, fo, fv, rows, binner, att, inv, t1, segt, ebuf, grad, y, bg, dos, hl, og, act, gp,
    ssem, rsem, lsem, esem,
):
    qkv = gp.at[0:3]
    p = Place()
    call(others(p))

    def cast(c):
        for part, ref in enumerate((wq, wk, wv)):
            own[c, :, part * CW : (part + 1) * CW] = ref[:, c * CW : (c + 1) * CW].astype(BF)

    cast(0)
    answer(others(p))
    net = gather_net(p, own, fa, fi, fo, vec, fv, ssem, rsem)
    names = ("zb", "za", "zo")

    def ring(g):
        net.start((g, "zb"), (g, "za"), (g, "own", "c"))

    def onward(g):
        net.wait((g, "zb"))
        net.start((g, "zo"))

    def plane(g, *which):
        for name in which or names:
            if name != "zb":
                net.wait((g, name))
            net.start((g, name, "xa"), (g, name, "xb"))

    def relay(g, *which):
        for name in which or names:
            net.wait((g, name, "xa"))
            net.start((g, name, "xd"))

    def share(g, *which):
        for name in which or names:
            net.wait((g, name, "xb"), (g, name, "xd"))
            net.start((g, name, "c"))

    def landed(g):
        net.wait((g, "own", "c"), *[(g, name, "c") for name in names])

    ring(0)
    cast(1)
    ring(1)
    cast(2)
    own[3] = wo[...].astype(BF)
    for q in range(4):
        own[4 + q] = wi[:, q * D : (q + 1) * D].astype(BF)
        own[8 + q] = wr[q * TR : (q + 1) * TR, :].astype(BF)
    net.start(*[("v", k) for k in range(1, 8)])
    local = {}

    def put(name, k, src, dst):
        local[name] = lambda: pltpu.make_async_copy(src(), dst(), lsem.at[k])

    pieces = (
        ("own a", lambda: own.at[0:4], lambda: fa.at[:, p.s]),
        ("own i", lambda: own.at[4:8], lambda: fi.at[:, p.s]),
        ("own o", lambda: own.at[8:12], lambda: fo.at[p.s]),
        ("vec", lambda: vec, lambda: fv.at[p.s]),
        ("grad", lambda: grad_in, lambda: grad),
        ("qkv", lambda: qkv, lambda: qkv_out),
        ("fa", lambda: fa.at[0:3], lambda: fa_out),
        ("att", lambda: att, lambda: att_out),
        ("hl", lambda: hl, lambda: hl_out),
        ("act", lambda: act, lambda: ai_out.at[0:4]),
        ("ig", lambda: gp, lambda: ai_out.at[4:8]),
        ("og", lambda: og, lambda: og_out),
        ("y", lambda: y, lambda: y_out),
        ("res", lambda: t1, lambda: res_out),
        ("bg", lambda: bg, lambda: bg_out),
        ("dos", lambda: dos, lambda: dos_out),
    )
    for k, (name, src, dst) in enumerate(pieces):
        put(name, k, src, dst)
    for name in ("own a", "own i", "own o", "vec", "grad"):
        local[name]().start()

    onward(0)
    plane(0, "zb", "za")
    onward(1)
    ring(2)
    plane(1, "zb", "za")
    plane(0, "zo")
    turn_ids(seg, segt)
    relay(0, "zb", "za")
    plane(1, "zo")
    relay(1, "zb")
    onward(2)
    ring(WO)
    relay(1, "za")
    plane(2, "zb", "za")
    relay(0, "zo")
    share(0, "zb", "za")
    relay(1, "zo")
    plane(2, "zo")
    share(1, "zb")
    relay(2, "zb")
    onward(WO)
    ring(INNER)
    share(1, "za")
    relay(2, "za")
    plane(WO, "zb")
    share(0, "zo")
    plane(WO, "za")
    share(1, "zo")
    relay(2, "zo")
    net.wait(*[("v", k) for k in range(1, 8)])
    local["vec"]().wait()
    expand_vectors(fv, rows, binner)
    share(2, "zb")
    plane(WO, "zo")
    local["own a"]().wait()
    keep = kept[0]

    def out_copy(i, slot):
        c, r, pair = place_of(i)
        return pltpu.make_async_copy(ebuf.at[slot], e_out.at[c, r, pair], esem.at[slot])

    before = {0: lambda: landed(0), 4: lambda: landed(1), 8: lambda: landed(2)}
    steps = {
        0: lambda: (share(2, "za", "zo"), relay(WO), onward(INNER), ring(OUTER), plane(INNER, "zb", "za"),),
        1: lambda: (share(WO),),
        2: lambda: (plane(INNER, "zo"),),
        3: lambda: (relay(INNER, "zb"),),
        4: lambda: (relay(INNER, "za"), onward(OUTER), plane(OUTER, "zb", "za"),),
        5: lambda: (relay(INNER, "zo"),),
        6: lambda: (share(INNER, "zb"),),
        7: lambda: (share(INNER, "za"), relay(OUTER, "zb"), plane(OUTER, "zo"),),
        8: lambda: (relay(OUTER, "za"),),
        9: lambda: (relay(OUTER, "zo"),),
        10: lambda: (share(INNER, "zo"),),
        11: lambda: (share(OUTER, "zb"),),
    }
    later = {
        0: lambda: (share(OUTER, "zo"),),
    }

    def after_residual():
        share(OUTER, "za")

    def at_step(i, table):
        for k, step in table.items():
            @pl.when(i == k)
            def _(step=step):
                step()

    def one(i, _):
        slot = lax.rem(i, 2)

        @pl.when(i >= 2)
        def _():
            out_copy(i - 2, slot).wait()

        at_step(i, before)

        @pl.when(lax.rem(i, 4) == 0)
        def _():
            project(lax.div(i, 4), x, fa, rows, qkv)

        attend(i, qkv, seg, segt, keep, att, inv, ebuf.at[slot])
        out_copy(i, slot).start()
        at_step(i, steps)
        return 0

    n = 6 * (x.shape[0] // SEQ)
    lax.fori_loop(0, n, one, 0)
    local["qkv"]().start()
    local["att"]().start()
    local["fa"]().start()
    sums[...] = jnp.zeros_like(sums)
    bsum[...] = jnp.zeros_like(bsum)
    landed(WO)
    block = 256
    blocks = x.shape[0] // block

    def residual(i, _):
        at = rows_of(i, block)
        t1[at] = x[at].astype(F32) + (mm(att[at], fa[3].reshape(D, D)) + rows[2:3])
        return 0

    lax.fori_loop(0, blocks, residual, 0)
    after_residual()
    landed(INNER)
    local["own i"]().wait()
    local["qkv"]().wait()

    def first(i, _):
        ffn_inner(i, block, t1, rows, binner, keep, fi, hl, act, gp)
        at_step(i, later)
        return 0

    lax.fori_loop(0, blocks, first, 0)
    local["hl"]().start()
    local["act"]().start()
    landed(OUTER)
    local["own o"]().wait()
    local["grad"]().wait()

    def second(i, _):
        ffn_outer(i, block, t1, grad, rows, keep, fi, fo, fa[3].reshape(D, D), inv, act, gp, y, bg, dos, og, sums, bsum)
        return 0

    lax.fori_loop(0, blocks, second, 0)
    for name in ("og", "ig", "dos", "bg", "res", "y"):
        local[name]().start()
    out_copy(n - 2, (n - 2) % 2).wait()
    out_copy(n - 1, (n - 1) % 2).wait()
    for name in ("fa", "att", "hl", "act", "og", "ig", "dos", "bg", "res", "y"):
        local[name]().wait()
    net.finish()


def forward(x, seg, kept, wq, wk, wv, wo, wi, wr, vec, grad):
    t = x.shape[0]
    n = t // SEQ
    return pl.pallas_call(
        forward_kernel,
        out_shape=(
            shape(8, D, dtype=F32), shape(1, FF, dtype=F32), shape(3, 8, TR, D), shape(3, t, D), shape(t, D),
            shape(3, n, 2, 2, SEQ, SEQ), shape(t, D), shape(t, D, dtype=F32), shape(t, D), shape(t, D), shape(t, D),
            shape(t, D), shape(8, t, D),
        ),
        in_specs=[VM, VM, SM] + [VM] * 7 + [ANY],
        out_specs=(VM, VM) + (ANY,) * 11,
        scratch_shapes=[
            pltpu.VMEM((12, TR, D), BF),
            pltpu.VMEM((4, 8, TR, D), BF),
            pltpu.VMEM((4, 8, TR, D), BF),
            pltpu.VMEM((8, 4, TR, D), BF),
            pltpu.VMEM((8, 16, 128), BF),
            pltpu.VMEM((8, D), F32),
            pltpu.VMEM((1, FF), F32),
            pltpu.VMEM((t, D), BF),
            pltpu.VMEM((t, D), F32),
            pltpu.VMEM((t, D), F32),
            pltpu.VMEM((n, SEQ, 128), F32),
            pltpu.VMEM((2, 2, SEQ, SEQ), BF),
        ]
        + [pltpu.VMEM((t, D), BF)] * 6
        + [pltpu.VMEM((4, t, D), BF)] * 2
        + [
            pltpu.SemaphoreType.DMA((GATHER_COPIES,)),
            pltpu.SemaphoreType.DMA((GATHER_COPIES,)),
            pltpu.SemaphoreType.DMA((16,)),
            pltpu.SemaphoreType.DMA((2,)),
        ],
        compiler_params=params(collective_id=0, has_side_effects=True),
        name="forward",
    )(x, seg, kept, wq, wk, wv, wo, wi, wr, vec, grad)


def attend_back(i, qkv, dos, att, ebuf, dqkv):
    c, r, pair = place_of(i)
    rows = rows_of(r, SEQ)
    lanes = pl.ds(pl.multiple_of(c * CW + pair * 128, 128), 128)
    qp, kp, vp = (qkv[c, rows, pair_lanes(pair, part)] for part in range(3))
    dp = dos[rows, lanes]
    low = low_lanes(SEQ)
    zero = jnp.zeros_like(qp)
    product = dp.astype(F32) * att[rows, lanes].astype(F32)
    gq = jnp.zeros((SEQ, 128), F32)
    gk = jnp.zeros((SEQ, 128), F32)
    gv = jnp.zeros((SEQ, 128), F32)
    for h in range(2):
        mine = low if h == 0 else jnp.logical_not(low)
        dh = jnp.where(mine, dp, zero)
        delta = jnp.sum(jnp.where(mine, product, 0.0), axis=1, keepdims=True)
        e = ebuf[h]
        ds = (e.astype(F32) * (mm(dh, vp, NT) - delta)).astype(BF)
        gv = gv + mm(e, dh, TN)
        gk = gk + mm(ds, jnp.where(mine, qp, zero), TN)
        gq = gq + mm(ds, jnp.where(mine, kp, zero))
    dqkv[c, rows, pair_lanes(pair, 0)] = (gq * 0.125).astype(BF)
    dqkv[c, rows, pair_lanes(pair, 1)] = gk.astype(BF)
    dqkv[c, rows, pair_lanes(pair, 2)] = gv.astype(BF)


def chunk_grads(c, x, dqkv, gx, sums):
    gx[c] = mm(x[...], dqkv[c], TN).astype(BF).reshape(4, 2, 1, TR, D)
    part = dqkv[c].astype(F32)
    total = jnp.sum(part, axis=0, keepdims=True)
    lanes = pl.ds(pl.multiple_of(c * CW, CW), CW)
    sums[0:1, lanes] = total[:, 0:CW]
    sums[1:2, lanes] = total[:, 2 * CW :]


def input_back(res, dqkv, fa, out, block=256):
    def one(i, _):
        at = rows_of(i, block)
        total = res[at]
        for c in range(3):
            total = total + mm(dqkv[c, at], fa[c].reshape(D, D), NT)
        out[at] = total.astype(BF)
        return 0

    lax.fori_loop(0, res.shape[0] // block, one, 0)


JOBS = ((0, 4, True), (4, 4, False), (8, 1, False), (9, 1, False), (10, 1, False), (11, 1, False))
REDUCE_COPIES = 9 * len(JOBS) + (4 + 4 + 4) + 7
JOB_BUFFERS = 7


def job_shapes(units, ring_first):
    big, part, tile = (4, units, TR, D), (units, 48, 384), (units, TR, D)
    first = tile if ring_first else (4, *part)
    return [big, big, first, first, first, first, part, part, part]


class Job:
    def __init__(self, net, p, k, first, units, ring_first, source, bufs, result):
        self.net, self.p, self.k, self.ring_first = net, p, k, ring_first
        self.held, self.landed, self.d1, self.a1, self.b1, self.mid, self.d2, self.a2, self.b2 = bufs
        self.result = result
        self.units = slice(first, first + units)
        held, mid = self.held, self.mid
        z, za, zb, zo = p.z, lax.div(p.sa, 2), lax.div(p.sb, 2), lax.div(p.so, 2)
        self.z = z
        ring = (za, zb, zo, p.ring_a, p.ring_a, p.ring_b)
        plane = (p.wb, p.wa, p.wd, p.plane_a, p.plane_b, p.plane_a)

        def tile(t):
            return held, (t,)

        def plane_quarter(w):
            return held, (slice(None), slice(None), *quarter(w))

        def mid_quarter(w):
            return mid, (slice(None), *quarter(w))

        def mid_tile(t):
            return mid, (t,)

        one, two = (ring, plane) if ring_first else (plane, ring)
        self.at1, self.at2 = (tile, mid_quarter) if ring_first else (plane_quarter, mid_tile)
        self.one, self.two = one, two
        self.own1 = z if ring_first else p.w
        self.own2 = p.w if ring_first else z
        self.parts = len(source)
        for j, make in enumerate(source):
            net.define((k, "c", j), lambda make=make: (*make(self.landed), p.sib))
        for stage, at, way, d, a, b in ((1, self.at1, one, self.d1, self.a1, self.b1), (2, self.at2, two, self.d2, self.a2, self.b2)):
            relayed, direct, opposite, dev_o, dev_r, dev_d = way

            def send(name, index, dst, device, at=at):
                def make():
                    ref, where = at(index)
                    return ref.at[where], dst, device

                net.define((k, *name), make)

            send(("d", stage), opposite, d, dev_o)
            send(("b", stage), direct, b, dev_d)
            send(("a", stage), relayed, a, dev_r)

        def share(name, w, device):
            def make():
                ref = result.at[(self.units, *quarter(w))]
                return ref, ref, device

            net.define((k, name), make)

        share("ga", p.w, p.plane_a)
        share("gb", p.w, p.plane_b)
        share("gd", p.wa, p.plane_b)

    def names(self, names):
        return [(self.k, *name) if isinstance(name, tuple) else (self.k, name) for name in names]

    def start(self, *names):
        self.net.start(*self.names(names))

    def wait(self, *names):
        self.net.wait(*self.names(names))

    def send(self, j=0):
        self.start(("c", j))

    def pair(self):
        self.wait(*[("c", j) for j in range(self.parts)])
        held, landed = self.held, self.landed

        def one(t, _):
            held[t] = (held[t].astype(F32) + landed[t].astype(F32)).astype(BF)
            return 0

        lax.fori_loop(0, 4, one, 0)
        self.start(("d", 1), ("b", 1))

    def relay(self, stage):
        at, way, d = (self.at1, self.one, self.d1) if stage == 1 else (self.at2, self.two, self.d2)
        self.wait(("d", stage))
        ref, where = at(way[0])
        ref[where] = (ref[where].astype(F32) + d[...].astype(F32)).astype(BF)
        self.start(("a", stage))

    def total(self, stage):
        at, own, a, b = (self.at1, self.own1, self.a1, self.b1) if stage == 1 else (self.at2, self.own2, self.a2, self.b2)
        self.wait(("a", stage), ("b", stage))
        ref, where = at(own)
        return (ref[where].astype(F32) + a[...].astype(F32) + b[...].astype(F32)).astype(BF)

    def turn(self):
        self.mid[...] = self.total(1)
        self.start(("d", 2), ("b", 2))

    def share(self):
        self.result[(self.units, *quarter(self.p.w))] = self.total(2)
        self.start("ga", "gb")

    def pass_on(self):
        self.wait("ga")
        self.start("gd")

    def end(self):
        self.wait("gb", "gd")


def backward_kernel(
    x, qkv_in, e_in, att_in, dos_in, bg_in, res_in, fa_in, hl_in, og_in, ai_in, sums_in, bsum,
    out, result, ovec,
    qkv, att, dos, bg, res, fa, dqkv, gx, go, ebuf, sums, vt, vheld, vrecv, vplane, vz, *rest,
):
    bufs, (ssem, rsem, lsem, esem) = rest[:-4], rest[-4:]
    p = Place()
    call(others(p))
    n = 6 * (x.shape[0] // SEQ)
    og, hl = dqkv.at[0], dqkv.at[1]
    loads = (
        ("og", lambda: og_in, lambda: og),
        ("hl", lambda: hl_in, lambda: hl),
        ("att", lambda: att_in, lambda: att),
        ("bg", lambda: bg_in, lambda: bg),
        ("qkv", lambda: qkv_in, lambda: qkv),
        ("dos", lambda: dos_in, lambda: dos),
        ("res", lambda: res_in, lambda: res),
        ("fa", lambda: fa_in, lambda: fa.at[0:3]),
    )
    load = {
        name: lambda k=k, src=src, dst=dst: pltpu.make_async_copy(src(), dst(), lsem.at[k])
        for k, (name, src, dst) in enumerate(loads)
    }

    def block_copy(j):
        return pltpu.make_async_copy(ai_in.at[j], qkv.at[j % 3], lsem.at[len(loads) + j % 3])

    def in_copy(i, slot):
        c, r, pair = place_of(i)
        return pltpu.make_async_copy(e_in.at[c, r, pair], ebuf.at[slot], esem.at[slot])

    load["og"]().start()
    block_copy(0).start()
    block_copy(1).start()
    load["hl"]().start()
    for name in ("att", "bg", "dos"):
        load[name]().start()
    in_copy(0, 0).start()
    load["res"]().start()

    def staged(k, j):
        return fa.at[2 * k + j // 2, 4 * (j % 2) : 4 * (j % 2) + 4]

    jobs = []
    net = Net(ssem, rsem)
    per = 9
    for k, (first, units, ring_first) in enumerate(JOBS):
        if k == 0:
            source = [lambda landed, j=j: (staged(0, j), landed.at[j]) for j in range(4)]
        elif k == 1:
            source = [lambda landed, j=j: (staged(1, j), landed.at[:, j]) for j in range(4)]
        elif k == 2:
            source = [lambda landed: (go.at[:, 1 - p.c], landed)]
        else:
            source = [lambda landed, c=k - 3: (gx.at[c, :, 1 - p.c], landed)]
        jobs.append(Job(net, p, k, first, units, ring_first, source, bufs[per * k : per * (k + 1)], result))
    net.define(("v", "c"), lambda: (vt.at[:, 1 - p.c], vrecv, p.sib))
    for k, device in enumerate((p.plane_a, p.plane_b, (p.wd, p.s))):
        net.define(("v", "p", k), lambda device=device: (vheld.at[0], vplane.at[p.w], device))
    for k in range(1, 4):
        to = lax.rem(p.z + k, 4)
        net.define(("v", "z", k), lambda to=to: (vheld.at[1, to], vz.at[p.z], (p.w, 2 * to + p.c)))
    assert len(net.made) == REDUCE_COPIES, len(net.made)

    first_core = p.c == 0
    for j in range(8):
        if j == 0:
            load["og"]().wait()
        if j == 4:
            load["hl"]().wait()
        if j + 2 < 8:
            block_copy(j + 2).start()
        block_copy(j).wait()
        block = qkv.at[j % 3]
        if j < 4:
            tiles = mm(block[...], og[...], TN).astype(BF).reshape(2, 4, TR, D)
            zero, one = tiles[0], tiles[1]
            jobs[0].held[j] = jnp.where(first_core, zero, one)
        else:
            tiles = mm(hl[...], block[...], TN).astype(BF).reshape(4, 2, TR, D)
            zero, one = tiles[:, 0], tiles[:, 1]
            jobs[1].held[:, j - 4] = jnp.where(first_core, zero, one)
        staged(j // 4, j % 4)[...] = jnp.where(first_core, one, zero)
        if j == 0:
            answer(others(p))
        jobs[j // 4].send(j % 4)
        if j == 4:
            jobs[0].pair()
    load["qkv"]().start()
    sums[...] = sums_in[...]
    load["att"]().wait()
    load["bg"]().wait()
    go[...] = mm(att[...], bg[...], TN).astype(BF).reshape(4, 2, 1, TR, D)
    jobs[2].send()
    jobs[1].pair()

    def own_half(k, source):
        jobs[k].held[...] = source[:, p.c]

    own_half(2, go)
    load["qkv"]().wait()
    load["dos"]().wait()
    jobs[2].pair()

    def begin(k):
        own_half(k, gx.at[k - 3])
        jobs[k].pair()

    a, b, w, c0, c1, c2 = jobs
    steps = {
        2: lambda: w.relay(1),
        3: lambda: c0.send(),
        4: lambda: (b.relay(1), begin(3), w.turn()),
        5: lambda: a.relay(1),
        6: lambda: (w.relay(2), c0.relay(1)),
        7: lambda: (c1.send(), w.share()),
        8: lambda: (b.turn(), begin(4), c0.turn()),
        9: lambda: (a.turn(), b.relay(2), w.pass_on()),
        10: lambda: (c1.relay(1), c0.relay(2), b.share()),
        11: lambda: (c2.send(), a.relay(2), c0.share(), c1.turn()),
    }

    def one(i, _):
        slot = lax.rem(i, 2)

        @pl.when(i + 1 < n)
        def _():
            in_copy(i + 1, 1 - slot).start()

        in_copy(i, slot).wait()
        attend_back(i, qkv, dos, att, ebuf.at[slot], dqkv)

        @pl.when(lax.rem(i, 4) == 3)
        def _():
            chunk_grads(lax.div(i, 4), x, dqkv, gx, sums)

        for k, step in steps.items():
            @pl.when(i == k)
            def _(step=step):
                step()
        return 0

    lax.fori_loop(0, n, one, 0)

    for k in range(2):
        for j in range(4):
            net.copy((k, "c", j)).wait_send()
            net.sent.add((k, "c", j))
    load["fa"]().start()

    for s in range(8):
        vt[s // 2, s % 2] = jnp.zeros((16, 128), F32)
        vt[s // 2, s % 2, 0:8, 0:TR] = sums[:, TR * s : TR * (s + 1)]
        for r in range(3):
            vt[s // 2, s % 2, 8 + r : 9 + r] = bsum[0:1, 128 * (3 * s + r) : 128 * (3 * s + r + 1)]
    net.start(("v", "c"))
    begin(5)
    a.share()
    b.pass_on()
    c0.pass_on()
    c1.relay(2)
    net.wait(("v", "c"))
    vheld[0] = vt[:, p.c] + vrecv[...]
    vplane[p.w] = vheld[0]
    net.start(*[("v", "p", k) for k in range(3)])
    load["res"]().wait()
    load["fa"]().wait()
    c2.relay(1)

    def back(i):
        at = pl.ds(256 * i, 256)
        total = res[at]
        for c in range(3):
            total = total + mm(dqkv[c, at], fa[c].reshape(D, D), NT)
        out[at] = total.astype(BF)

    back(0)
    a.pass_on()
    c1.share()
    c2.turn()
    net.wait(*[("v", "p", k) for k in range(3)])
    vheld[1] = (vplane[0] + vplane[1]) + (vplane[2] + vplane[3])
    vz[p.z] = vheld[1, p.z]
    net.start(*[("v", "z", k) for k in range(1, 4)])
    back(1)
    c1.pass_on()
    c2.relay(2)
    back(2)
    c2.share()
    back(3)
    net.wait(*[("v", "z", k) for k in range(1, 4)])
    ovec[...] = (vz[0] + vz[1]) + (vz[2] + vz[3])
    c2.pass_on()
    for job in jobs:
        job.end()
    net.finish()


def backward(x, qkv, e, att, dos, bg, res, fa, hl, og, ai, sums, bsum):
    t = x.shape[0]
    job_scratch = [pltpu.VMEM(s, BF) for _, units, ring_first in JOBS for s in job_shapes(units, ring_first)]
    return pl.pallas_call(
        backward_kernel,
        out_shape=(shape(t, D), shape(12, TR, D), shape(16, 128, dtype=F32)),
        in_specs=[VM] + [ANY] * 10 + [VM, VM],
        out_specs=(VM,) * 3,
        scratch_shapes=[
            pltpu.VMEM((3, t, D), BF),
            pltpu.VMEM((t, D), BF),
            pltpu.VMEM((t, D), BF),
            pltpu.VMEM((t, D), BF),
            pltpu.VMEM((t, D), F32),
            pltpu.VMEM((4, 8, TR, D), BF),
            pltpu.VMEM((3, t, D), BF),
            pltpu.VMEM((3, 4, 2, 1, TR, D), BF),
            pltpu.VMEM((4, 2, 1, TR, D), BF),
            pltpu.VMEM((2, 2, SEQ, SEQ), BF),
            pltpu.VMEM((8, D), F32),
            pltpu.VMEM((4, 2, 16, 128), F32),
            pltpu.VMEM((2, 4, 16, 128), F32),
            pltpu.VMEM((4, 16, 128), F32),
            pltpu.VMEM((4, 4, 16, 128), F32),
            pltpu.VMEM((4, 16, 128), F32),
        ]
        + job_scratch
        + [
            pltpu.SemaphoreType.DMA((REDUCE_COPIES,)),
            pltpu.SemaphoreType.DMA((REDUCE_COPIES,)),
            pltpu.SemaphoreType.DMA((11,)),
            pltpu.SemaphoreType.DMA((2,)),
        ],
        compiler_params=params(collective_id=1, has_side_effects=True),
        name="backward",
    )(x, qkv, e, att, dos, bg, res, fa, hl, og, ai, sums, bsum)


def finish_kernel(result, ovec, inp, oq, ok, ov, oo, oi, our, out, *vectors):
    for c in range(3):
        tile = result[9 + c].astype(F32)
        for part, ref in enumerate((oq, ok, ov)):
            ref[:, c * CW : (c + 1) * CW] = tile[:, part * CW : (part + 1) * CW]
    oo[...] = result[8].astype(F32)
    for q in range(4):
        oi[:, q * D : (q + 1) * D] = result[4 + q].astype(F32)
        our[q * TR : (q + 1) * TR, :] = result[q].astype(F32)
    out[...] = inp[...]
    for k in range(8):
        vectors[k][...] = ovec[k, 0:TR]
    for r in range(3):
        vectors[8][128 * r : 128 * (r + 1)] = ovec[8 + r]


def finish(result, ovec, inp):
    t = inp.shape[0]
    return pl.pallas_call(
        finish_kernel,
        out_shape=tuple(shape(TR, D, dtype=F32) for _ in range(4))
        + (shape(TR, FF, dtype=F32), shape(4 * TR, D, dtype=F32), shape(t, D))
        + tuple(shape(TR, dtype=F32) for _ in range(8))
        + (shape(4 * TR, dtype=F32),),
        in_specs=[VM] * 3,
        out_specs=(VM,) * 16,
        compiler_params=params(),
        name="finish",
    )(result, ovec, inp)


def forward_local_kernel(x, seg, kept, fa, rows, qkv, att, inv, e_out, t1, segt, ebuf, esem):
    turn_ids(seg, segt)
    for c in range(3):
        project(c, x, fa, rows, qkv)
    keep = kept[0]

    def one(i, _):
        c, r, pair = place_of(i)
        attend(i, qkv, seg, segt, keep, att, inv, ebuf)
        copy = pltpu.make_async_copy(ebuf, e_out.at[c, r, pair], esem.at[0])
        copy.start()
        copy.wait()
        return 0

    lax.fori_loop(0, 6 * (x.shape[0] // SEQ), one, 0)
    t1[...] = x[...].astype(F32) + (mm(att[...], fa[3].reshape(D, D)) + rows[2:3])


def forward_local(x, seg, kept, fa, rows):
    t = x.shape[0]
    n = t // SEQ
    return pl.pallas_call(
        forward_local_kernel,
        out_shape=(shape(3, t, D), shape(t, D), shape(t, D, dtype=F32), shape(3, n, 2, 2, SEQ, SEQ), shape(t, D, dtype=F32)),
        in_specs=[VM, VM, SM, VM, VM],
        out_specs=(VM, VM, VM, ANY, VM),
        scratch_shapes=[
            pltpu.VMEM((n, SEQ, 128), F32), pltpu.VMEM((2, SEQ, SEQ), BF), pltpu.SemaphoreType.DMA((1,)),
        ],
        compiler_params=params(),
        name="forward_local",
    )(x, seg, kept, fa, rows)


def ffn_local_kernel(
    t1, grad, rows, binner, kept, inv, fi, fo, fa, y, res, bg, dos, sums, bsum, g, hl, og, act, gp, t2, tile, gsem, block=256
):
    sums[...] = jnp.zeros_like(sums)
    bsum[...] = jnp.zeros_like(bsum)
    t2[...] = t1[...]
    blocks = t1.shape[0] // block

    def first(i, _):
        ffn_inner(i, block, t2, rows, binner, kept[0], fi, hl, act, gp)
        return 0

    def second(i, _):
        wo = fa[3].reshape(D, D)
        ffn_outer(i, block, t2, grad, rows, kept[0], fi, fo, wo, inv, act, gp, y, bg, dos, og, sums, bsum)
        return 0

    lax.fori_loop(0, blocks, first, 0)
    lax.fori_loop(0, blocks, second, 0)
    res[...] = t2[...]

    def one(j, _):
        tile[...] = mm(act[j], og[...], TN).astype(BF).reshape(2, 4, TR, D)
        copy = pltpu.make_async_copy(tile, g.at[lax.div(j, 2), pl.ds(2 * lax.rem(j, 2), 2), 0:4], gsem.at[0])
        copy.start()
        copy.wait()
        tile[...] = mm(hl[...], gp[j], TN).astype(BF).reshape(2, 4, TR, D)
        copy = pltpu.make_async_copy(tile, g.at[:, :, 4 + j], gsem.at[0])
        copy.start()
        copy.wait()
        return 0

    lax.fori_loop(0, 4, one, 0)


def ffn_local(t1, grad, rows, binner, kept, inv, fi, fo, fa):
    t = t1.shape[0]
    return pl.pallas_call(
        ffn_local_kernel,
        out_shape=(
            shape(t, D), shape(t, D, dtype=F32), shape(t, D), shape(t, D),
            shape(8, D, dtype=F32), shape(1, FF, dtype=F32), shape(2, 4, 8, TR, D),
        ),
        in_specs=[VM] * 4 + [SM] + [VM] * 4,
        out_specs=(VM,) * 6 + (ANY,),
        scratch_shapes=[
            pltpu.VMEM((t, D), BF), pltpu.VMEM((t, D), BF), pltpu.VMEM((4, t, D), BF), pltpu.VMEM((4, t, D), BF),
            pltpu.VMEM((t, D), F32), pltpu.VMEM((2, 4, TR, D), BF), pltpu.SemaphoreType.DMA((1,)),
        ],
        compiler_params=params(),
        name="ffn_local",
    )(t1, grad, rows, binner, kept, inv, fi, fo, fa)


def backward_local_kernel(x, qkv, e_in, att, dos, bg, res, fa, sums_in, out, gx, go, sums, dqkv, ebuf, esem):
    sums[...] = sums_in[...]
    go[...] = mm(att[...], bg[...], TN).astype(BF).reshape(4, 2, 1, TR, D)

    def one(i, _):
        c, r, pair = place_of(i)
        copy = pltpu.make_async_copy(e_in.at[c, r, pair], ebuf, esem.at[0])
        copy.start()
        copy.wait()
        attend_back(i, qkv, dos, att, ebuf, dqkv)

        @pl.when(lax.rem(i, 4) == 3)
        def _():
            chunk_grads(lax.div(i, 4), x, dqkv, gx, sums)

        return 0

    lax.fori_loop(0, 6 * (x.shape[0] // SEQ), one, 0)
    input_back(res, dqkv, fa, out)


def backward_local(x, qkv, e, att, dos, bg, res, fa, sums):
    t = x.shape[0]
    return pl.pallas_call(
        backward_local_kernel,
        out_shape=(shape(t, D), shape(3, 4, 2, 1, TR, D), shape(4, 2, 1, TR, D), shape(8, D, dtype=F32)),
        in_specs=[VM, VM, ANY] + [VM] * 6,
        out_specs=(VM,) * 4,
        scratch_shapes=[pltpu.VMEM((3, t, D), BF), pltpu.VMEM((2, SEQ, SEQ), BF), pltpu.SemaphoreType.DMA((1,))],
        compiler_params=params(),
        name="backward_local",
    )(x, qkv, e, att, dos, bg, res, fa, sums)


def gather_lax(wq, wk, wv, wo, wi, wr, eight, b_inner):
    def whole(a):
        return lax.all_gather(a.astype(BF), "shard", axis=0, tiled=True)

    wq, wk, wv, wo, wi, wr = (whole(a) for a in (wq, wk, wv, wo, wi, wr))
    chunks = [jnp.concatenate([a[:, c * CW : (c + 1) * CW] for a in (wq, wk, wv)], axis=1) for c in range(3)]
    fa = jnp.stack(chunks + [wo]).reshape(4, 8, TR, D)
    fi = jnp.stack([wi[:, q * D : (q + 1) * D] for q in range(4)]).reshape(4, 8, TR, D)
    rows = jnp.stack([whole(a) for a in eight]).astype(F32)
    return fa, fi, wr.reshape(8, 4, TR, D), rows, whole(b_inner).astype(F32).reshape(1, FF)


def reduce_lax(g, gx, go, sums, bsum):
    g = g.reshape(8, 8, TR, D)
    gr = g[:, 0:4].reshape(FF, D)
    gi = jnp.concatenate([g[:, 4 + j].reshape(D, D) for j in range(4)], axis=1)
    gx = gx.reshape(3, D, 3, CW)
    squares = [jnp.concatenate([gx[c, :, part] for c in range(3)], axis=1) for part in range(3)]

    def owned(a):
        a = lax.psum_scatter(a.astype(F32), "shard", scatter_dimension=0, tiled=True)
        return lax.psum(a.astype(BF), "width").astype(F32)

    matrices = [owned(a) for a in (*squares, go.reshape(D, D), gi, gr)]
    return matrices, [owned(sums[k]) for k in range(8)] + [owned(bsum[0])]


def body(
    layer_input, segment_ids, group_heads,
    w_query, b_query, w_key, w_value, b_value, w_out, b_out, gain_one, shift_one,
    w_inner, b_inner, w_outer, b_outer, gain_two, shift_two, out_grad,
):
    eight = (b_query, b_value, b_out, gain_one, shift_one, b_outer, gain_two, shift_two)
    weights = (w_query, w_key, w_value, w_out, w_inner, w_outer)
    own_kernels = lax.axis_size("width") == 4 and lax.axis_size("shard") == 8
    if own_kernels:
        vec = jnp.concatenate([jnp.stack(eight), jnp.zeros((8, 128 - TR), F32)], axis=1)
        vec = jnp.concatenate([vec, b_inner.reshape(3, 128), jnp.zeros((5, 128), F32)], axis=0).astype(BF)
        sums, bsum, fa, qkv, att, e, y, res, bg, dos, hl, og, ai = forward(
            layer_input, segment_ids, group_heads, *weights, vec, out_grad
        )
    else:
        fa, fi, fo, rows, binner = gather_lax(*weights, eight, b_inner)
        qkv, att, inv, e, t1 = forward_local(layer_input, segment_ids, group_heads, fa, rows)
        y, res, bg, dos, sums, bsum, g = ffn_local(t1, out_grad, rows, binner, group_heads, inv, fi, fo, fa)
    if own_kernels:
        input_grad, result, ovec = backward(layer_input, qkv, e, att, dos, bg, res, fa, hl, og, ai, sums, bsum)
        gq, gk, gv, go, gi, gr, input_grad, *vectors = finish(result, ovec, input_grad)
    else:
        input_grad, gx, go, sums = backward_local(layer_input, qkv, e, att, dos, bg, res, fa[0:3], sums)
        (gq, gk, gv, go, gi, gr), vectors = reduce_lax(g, gx, go, sums, bsum)
    return (
        y, input_grad, gq, vectors[0], gk, gv, vectors[1], go, vectors[2],
        vectors[3], vectors[4], gi, vectors[8], gr, vectors[5], vectors[6], vectors[7],
    )


def solution(mesh):
    placed = (
        P(("width", "shard"), None),
        P(("width", "shard"), None),
        P("width"),
        P("shard", None),
        P("shard"),
        P("shard", None),
        P("shard", None),
        P("shard"),
        P("shard", None),
        P("shard"),
        P("shard"),
        P("shard"),
        P("shard", None),
        P("shard"),
        P("shard", None),
        P("shard"),
        P("shard"),
        P("shard"),
        P(("width", "shard"), None),
    )
    return jax.shard_map(
        body,
        mesh=mesh,
        in_specs=placed,
        out_specs=(
            P(("width", "shard"), None),
            P(("width", "shard"), None),
            P("shard", None),
            P("shard"),
            P("shard", None),
            P("shard", None),
            P("shard"),
            P("shard", None),
            P("shard"),
            P("shard"),
            P("shard"),
            P("shard", None),
            P("shard"),
            P("shard", None),
            P("shard"),
            P("shard"),
            P("shard"),
        ),
        check_vma=False,
    )
```

```python
import functools
import jax
import jax.numpy as jnp
from jax import lax
from jax.experimental import pallas as pl
from jax.experimental.pallas import tpu as pltpu
from jax.sharding import PartitionSpec as P

HEADS = 12
HEAD_DIM = 64
FF = 3072
D = 768
SEQ = 512
MESH = pl.DeviceIdType.MESH
BF = jnp.bfloat16
F32 = jnp.float32
TR = 96
CW = 256
NT = (((1,), (1,)), ((), ()))
TN = (((0,), (0,)), ((), ()))
NN = (((1,), (0,)), ((), ()))
EPS = 1e-06
RSQRT2 = 0.7071067811865476
RSQRT2PI = 0.3989422804014327
VM = pl.BlockSpec(memory_space=pltpu.VMEM)
SM = pl.BlockSpec(memory_space=pltpu.SMEM)
ANY = pl.BlockSpec(memory_space=pl.ANY)


def params(**more):
    return pltpu.CompilerParams(vmem_limit_bytes=62 << 20, **more)


def shape(*dims, dtype=BF):
    return jax.ShapeDtypeStruct(dims, dtype)


class Place:
    def __init__(self):
        self.w = w = lax.axis_index("width")
        self.s = s = lax.axis_index("shard")
        self.c = c = lax.rem(s, 2)
        self.z = lax.div(s, 2)
        xw, yw = w + 1 - 2 * lax.rem(w, 2), lax.rem(w + 2, 4)
        up, down = lax.rem(s + 2, 8), lax.rem(s + 6, 8)
        self.wa = jnp.where(c == 0, xw, yw)
        self.wb = jnp.where(c == 0, yw, xw)
        self.wd = 3 - w
        self.sa = jnp.where(c == 0, up, down)
        self.sb = jnp.where(c == 0, down, up)
        self.so = lax.rem(s + 4, 8)
        self.sib = (w, s + 1 - 2 * c)
        self.plane_a, self.plane_b = (self.wa, s), (self.wb, s)
        self.ring_a, self.ring_b = (w, self.sa), (w, self.sb)


def call(devices):
    barrier = pltpu.get_barrier_semaphore()
    for device in devices:
        pl.semaphore_signal(barrier, inc=1, device_id=device, device_id_type=MESH)


def answer(devices):
    pl.semaphore_wait(pltpu.get_barrier_semaphore(), len(devices))


def others(p):
    return [(p.wa, p.s), (p.wb, p.s), (p.wd, p.s)] + [(p.w, lax.rem(p.s + k, 8)) for k in range(1, 8)]


class Net:
    def __init__(self, send, recv):
        self.send, self.recv, self.made, self.sent = send, recv, {}, set()

    def define(self, name, make):
        assert name not in self.made
        self.made[name] = (len(self.made), make)

    def copy(self, name):
        k, make = self.made[name]
        src, dst, device = make()
        return pltpu.make_async_remote_copy(
            src_ref=src, dst_ref=dst, send_sem=self.send.at[k], recv_sem=self.recv.at[k],
            device_id=device, device_id_type=MESH,
        )

    def start(self, *names):
        for name in names:
            self.copy(name).start()

    def wait(self, *names):
        for name in names:
            self.copy(name).wait_recv()

    def finish(self):
        for name in self.made:
            if name not in self.sent:
                self.copy(name).wait_send()


def quarter(w):
    return pl.ds(pl.multiple_of(48 * lax.rem(w, 2), 48), 48), pl.ds(pl.multiple_of(384 * lax.div(w, 2), 384), 384)


def mm(a, b, dims=NN):
    return lax.dot_general(a, b, dims, preferred_element_type=F32)


def rows_of(i, size):
    return pl.ds(pl.multiple_of(i * size, size), size)


def column_mask(kept, shape, width):
    return jnp.where(lax.broadcasted_iota(jnp.int32, shape, 1) < kept * width, 1.0, 0.0).astype(F32)


def mean_of(v):
    return jnp.sum(v, axis=1, keepdims=True) * (1.0 / D)


def norm_rows(total):
    centered = total - mean_of(total)
    inverse = lax.rsqrt(mean_of(centered * centered) + EPS)
    return centered * inverse, inverse


def norm_back(grad, normed, inverse):
    return inverse * (grad - mean_of(grad) - normed * mean_of(grad * normed))


def low_lanes(n):
    return lax.broadcasted_iota(jnp.int32, (n, 128), 1) < HEAD_DIM


def place_of(i):
    return lax.div(i, 4), lax.rem(i, 2), lax.rem(lax.div(i, 2), 2)


def pair_lanes(pair, part):
    return pl.ds(pl.multiple_of(part * CW + pair * 128, 128), 128)


def project(c, x, fa, rows, qkv, block=256):
    lanes = pl.ds(pl.multiple_of(c * CW, CW), CW)
    bias = jnp.concatenate([rows[0:1, lanes], jnp.zeros((1, CW), F32), rows[1:2, lanes]], axis=1)
    scale = jnp.where(lax.broadcasted_iota(jnp.int32, (1, D), 1) < CW, 0.125, 1.0)

    def one(i, _):
        at = rows_of(i, block)
        qkv[c, at] = ((mm(x[at], fa[c].reshape(D, D)) + bias) * scale).astype(BF)
        return 0

    lax.fori_loop(0, x.shape[0] // block, one, 0)


def turn_ids(seg, segt):
    for r in range(seg.shape[0]):
        row = seg[r : r + 1, :].astype(F32)
        segt[r] = jnp.broadcast_to(row, (128, SEQ)).T


def attend(i, qkv, seg, segt, kept, att, inv, ebuf, qb=512):
    c, r, pair = place_of(i)
    base = r * SEQ
    rows = pl.ds(pl.multiple_of(base, SEQ), SEQ)
    kp, vp = qkv[c, rows, pair_lanes(pair, 1)], qkv[c, rows, pair_lanes(pair, 2)]
    low = low_lanes(SEQ)
    ones = jnp.ones_like(vp)
    vs = (jnp.where(low, vp, ones), jnp.where(low, ones, vp))
    ids = seg[pl.ds(r, 1), :].astype(F32)
    lowq = low_lanes(qb)
    lanes = pl.ds(pl.multiple_of(c * CW + pair * 128, 128), 128)
    column = lax.broadcasted_iota(jnp.int32, (1, 128), 1) + (c * CW + pair * 128)
    mask = jnp.where(column < kept * HEAD_DIM, 1.0, 0.0).astype(F32)
    for b in range(SEQ // qb):
        at = pl.ds(pl.multiple_of(base + b * qb, qb), qb)
        qp = qkv[c, at, pair_lanes(pair, 0)]
        zero = jnp.zeros_like(qp)
        own = segt[r, b * qb : (b + 1) * qb]
        same = jnp.concatenate([own == ids[:, j * 128 : (j + 1) * 128] for j in range(4)], axis=1)
        out = []
        for h in range(2):
            qh = jnp.where(lowq, qp, zero) if h == 0 else jnp.where(lowq, zero, qp)
            scores = jnp.where(same, mm(qh, kp, NT), -1e30)
            top = jnp.max(scores, axis=1, keepdims=True)
            e = jnp.exp(scores - top).astype(BF)
            ebuf[h, b * qb : (b + 1) * qb] = e
            out.append(mm(e, vs[h]))
        inverse = 1.0 / pltpu.roll(jnp.where(lowq, out[1], out[0]), HEAD_DIM, 1)
        att[at, lanes] = (jnp.where(lowq, out[0], out[1]) * (inverse * mask)).astype(BF)
        inv[at, lanes] = inverse


def expand_vectors(fv, rows, binner):
    lane = lax.broadcasted_iota(jnp.int32, (128, D), 0)
    column = lax.broadcasted_iota(jnp.int32, (128, D), 1)
    total = jnp.zeros((16, D), F32)
    for s in range(8):
        pick = jnp.where((column == lane + TR * s) & (lane < TR), 1.0, 0.0).astype(BF)
        total = total + mm(fv[s], pick)
        tile = fv[s].astype(F32)
        for r in range(3):
            binner[0:1, 128 * (3 * s + r) : 128 * (3 * s + r + 1)] = tile[8 + r : 9 + r]
    rows[...] = total[0:8]


GROUPS = (slice(0, 1), slice(1, 2), slice(2, 3), slice(3, 4), slice(4, 8), slice(8, 12))
WO, INNER, OUTER = 3, 4, 5
GATHER_COPIES = 16 * len(GROUPS) + 7


def gather_net(p, own, fa, fi, fo, vec, fv, ssem, rsem):
    net = Net(ssem, rsem)
    every = (slice(None), slice(None))

    def piece(g, s, part):
        if g <= WO:
            return fa.at[(GROUPS[g], s, *part)]
        return fi.at[(slice(None), s, *part)] if g == INNER else fo.at[(s, slice(None), *part)]

    mine, first = quarter(p.w), quarter(p.wa)
    for g in range(len(GROUPS)):

        def add(name, src, dst, device):
            net.define((g, *name), lambda: (src(), dst(), device))

        def same(name, g, s, part, device):
            add(name, lambda: piece(g, s, part), lambda: piece(g, s, part), device)

        for name, device in (("zb", p.ring_a), ("za", p.ring_b)):
            add((name,), lambda g=g: own.at[(GROUPS[g], *mine)], lambda g=g: piece(g, p.s, mine), device)
        same(("zo",), g, p.sb, mine, p.ring_a)
        add(("own", "c"), lambda g=g: own.at[GROUPS[g]], lambda g=g: piece(g, p.s, every), p.sib)
        for name, s in (("zb", p.sb), ("za", p.sa), ("zo", p.so)):
            same((name, "xa"), g, s, mine, p.plane_a)
            same((name, "xb"), g, s, mine, p.plane_b)
            same((name, "xd"), g, s, first, p.plane_b)
            same((name, "c"), g, s, every, p.sib)
    for k in range(1, 8):
        net.define(("v", k), lambda k=k: (vec, fv.at[p.s], (p.w, lax.rem(p.s + k, 8))))
    assert len(net.made) == GATHER_COPIES
    return net


def ffn_inner(i, block, t1, rows, binner, kept, wi, hl, act, gp):
    at = rows_of(i, block)
    n1, _ = norm_rows(t1[at])
    low = (n1 * rows[3:4] + rows[4:5]).astype(BF)
    hl[at] = low
    for j in range(4):
        inner = mm(low, wi[j].reshape(D, D)) + binner[:, j * D : (j + 1) * D]
        keep = column_mask(kept * 256 - j * D, (1, D), 1)
        phi = 0.5 + 0.5 * lax.erf(inner * RSQRT2)
        masked = inner * keep
        act[j, at] = (masked * phi).astype(BF)
        gp[j, at] = (keep * phi + masked * (RSQRT2PI * jnp.exp(-0.5 * (inner * inner)))).astype(BF)


def ffn_outer(i, block, t1, grad, rows, kept, wi, wr, wo, inv, act, gp, y, bg, dos, og, sums, bsum):
    at = rows_of(i, block)

    def add(k, value):
        sums[k : k + 1] += jnp.sum(value, axis=0, keepdims=True)

    def outer_weight(j):
        return wr[2 * j : 2 * j + 2].reshape(D, D)

    outer = jnp.zeros((block, D), F32)
    for j in range(4):
        outer = outer + mm(act[j, at], outer_weight(j))
    n1, inv1 = norm_rows(t1[at])
    hidden = n1 * rows[3:4] + rows[4:5]
    n2, inv2 = norm_rows(hidden + (outer + rows[5:6]))
    y[at] = (n2 * rows[6:7] + rows[7:8]).astype(BF)
    top = grad[at].astype(F32)
    add(7, top)
    add(6, top * n2)
    res2 = norm_back(top * rows[6:7], n2, inv2)
    o = res2.astype(BF)
    og[at] = o
    add(5, o.astype(F32))
    hg = res2
    for j in range(4):
        cols = slice(j * D, (j + 1) * D)
        g = (mm(o, outer_weight(j), NT) * gp[j, at].astype(F32)).astype(BF)
        gp[j, at] = g
        bsum[:, cols] += jnp.sum(g.astype(F32), axis=0, keepdims=True)
        hg = hg + mm(g, wi[j].reshape(D, D), NT)
    add(4, hg)
    add(3, hg * n1)
    res1 = norm_back(hg * rows[3:4], n1, inv1)
    t1[at] = res1
    b = res1.astype(BF)
    bg[at] = b
    add(2, b.astype(F32))
    heads = column_mask(kept, (1, D), HEAD_DIM)
    dos[at] = (mm(b, wo, NT) * (inv[at] * heads)).astype(BF)


def forward_kernel(
    x, seg, kept, wq, wk, wv, wo, wi, wr, vec, grad_in,
    sums, bsum, fa_out, qkv_out, att_out, e_out, y_out, res_out, bg_out, dos_out, hl_out, og_out, ai_out,
    own, fa, fi, fo, fv, rows, binner, att, inv, t1, segt, ebuf, grad, y, bg, dos, hl, og, act, gp,
    ssem, rsem, lsem, esem,
):
    qkv = gp.at[0:3]
    p = Place()
    call(others(p))

    def cast(c):
        for part, ref in enumerate((wq, wk, wv)):
            own[c, :, part * CW : (part + 1) * CW] = ref[:, c * CW : (c + 1) * CW].astype(BF)

    cast(0)
    answer(others(p))
    net = gather_net(p, own, fa, fi, fo, vec, fv, ssem, rsem)
    names = ("zb", "za", "zo")

    def ring(g):
        net.start((g, "zb"), (g, "za"), (g, "own", "c"))

    def onward(g):
        net.wait((g, "zb"))
        net.start((g, "zo"))

    def plane(g, *which):
        for name in which or names:
            if name != "zb":
                net.wait((g, name))
            net.start((g, name, "xa"), (g, name, "xb"))

    def relay(g, *which):
        for name in which or names:
            net.wait((g, name, "xa"))
            net.start((g, name, "xd"))

    def share(g, *which):
        for name in which or names:
            net.wait((g, name, "xb"), (g, name, "xd"))
            net.start((g, name, "c"))

    def landed(g):
        net.wait((g, "own", "c"), *[(g, name, "c") for name in names])

    ring(0)
    cast(1)
    ring(1)
    cast(2)
    own[3] = wo[...].astype(BF)
    for q in range(4):
        own[4 + q] = wi[:, q * D : (q + 1) * D].astype(BF)
        own[8 + q] = wr[q * TR : (q + 1) * TR, :].astype(BF)
    net.start(*[("v", k) for k in range(1, 8)])
    local = {}

    def put(name, k, src, dst):
        local[name] = lambda: pltpu.make_async_copy(src(), dst(), lsem.at[k])

    pieces = (
        ("own a", lambda: own.at[0:4], lambda: fa.at[:, p.s]),
        ("own i", lambda: own.at[4:8], lambda: fi.at[:, p.s]),
        ("own o", lambda: own.at[8:12], lambda: fo.at[p.s]),
        ("vec", lambda: vec, lambda: fv.at[p.s]),
        ("grad", lambda: grad_in, lambda: grad),
        ("qkv", lambda: qkv, lambda: qkv_out),
        ("fa", lambda: fa.at[0:3], lambda: fa_out),
        ("att", lambda: att, lambda: att_out),
        ("hl", lambda: hl, lambda: hl_out),
        ("act", lambda: act, lambda: ai_out.at[0:4]),
        ("ig", lambda: gp, lambda: ai_out.at[4:8]),
        ("og", lambda: og, lambda: og_out),
        ("y", lambda: y, lambda: y_out),
        ("res", lambda: t1, lambda: res_out),
        ("bg", lambda: bg, lambda: bg_out),
        ("dos", lambda: dos, lambda: dos_out),
    )
    for k, (name, src, dst) in enumerate(pieces):
        put(name, k, src, dst)
    for name in ("own a", "own i", "own o", "vec", "grad"):
        local[name]().start()

    onward(0)
    plane(0, "zb", "za")
    onward(1)
    ring(2)
    plane(1, "zb", "za")
    plane(0, "zo")
    turn_ids(seg, segt)
    relay(0, "zb", "za")
    plane(1, "zo")
    relay(1, "zb")
    onward(2)
    ring(INNER)
    relay(1, "za")
    plane(2, "zb", "za")
    relay(0, "zo")
    share(0, "zb", "za")
    relay(1, "zo")
    share(1, "zb")
    plane(2, "zo")
    share(1, "za")
    relay(2, "zb", "za")
    share(0, "zo")
    onward(INNER)
    ring(WO)
    share(1, "zo")
    plane(INNER, "zb")
    relay(2, "zo")
    net.wait(*[("v", k) for k in range(1, 8)])
    local["vec"]().wait()
    expand_vectors(fv, rows, binner)
    share(2, "zb", "za")
    plane(INNER, "za")
    local["own a"]().wait()
    keep = kept[0]

    def out_copy(i, slot):
        c, r, pair = place_of(i)
        return pltpu.make_async_copy(ebuf.at[slot], e_out.at[c, r, pair], esem.at[slot])

    before = {0: lambda: landed(0), 4: lambda: landed(1), 8: lambda: landed(2)}
    steps = {
        1: lambda: (plane(INNER, "zo"), relay(INNER, "zb"), onward(WO), ring(OUTER), share(2, "zo"), plane(WO, "zb", "za"),),
        2: lambda: (relay(INNER, "za"),),
        4: lambda: (relay(INNER, "zo"), plane(WO, "zo"), relay(WO, "zb"),),
        5: lambda: (relay(WO, "za"), onward(OUTER), plane(OUTER, "zb"),),
        6: lambda: (share(INNER, "zb"),),
        7: lambda: (relay(WO, "zo"), plane(OUTER, "za"),),
        8: lambda: (share(INNER, "za"),),
        9: lambda: (share(INNER, "zo"), relay(OUTER, "zb"), plane(OUTER, "zo"),),
        10: lambda: (share(WO, "zb", "za"),),
        11: lambda: (relay(OUTER, "za"), share(WO, "zo"), relay(OUTER, "zo"),),
    }
    later = {
        1: lambda: (share(OUTER, "za", "zo"),),
    }

    def after_residual():
        share(OUTER, "zb")

    def at_step(i, table):
        for k, step in table.items():
            @pl.when(i == k)
            def _(step=step):
                step()

    def one(i, _):
        slot = lax.rem(i, 2)

        @pl.when(i >= 2)
        def _():
            out_copy(i - 2, slot).wait()

        at_step(i, before)

        @pl.when(lax.rem(i, 4) == 0)
        def _():
            project(lax.div(i, 4), x, fa, rows, qkv)

        attend(i, qkv, seg, segt, keep, att, inv, ebuf.at[slot])
        out_copy(i, slot).start()
        at_step(i, steps)
        return 0

    n = 6 * (x.shape[0] // SEQ)
    lax.fori_loop(0, n, one, 0)
    local["qkv"]().start()
    local["att"]().start()
    local["fa"]().start()
    sums[...] = jnp.zeros_like(sums)
    bsum[...] = jnp.zeros_like(bsum)
    landed(WO)
    block = 256
    blocks = x.shape[0] // block

    def residual(i, _):
        at = rows_of(i, block)
        t1[at] = x[at].astype(F32) + (mm(att[at], fa[3].reshape(D, D)) + rows[2:3])
        return 0

    lax.fori_loop(0, blocks, residual, 0)
    after_residual()
    landed(INNER)
    local["own i"]().wait()
    local["qkv"]().wait()

    def first(i, _):
        ffn_inner(i, block, t1, rows, binner, keep, fi, hl, act, gp)
        at_step(i, later)
        return 0

    lax.fori_loop(0, blocks, first, 0)
    local["hl"]().start()
    local["act"]().start()
    landed(OUTER)
    local["own o"]().wait()
    local["grad"]().wait()

    def second(i, _):
        ffn_outer(i, block, t1, grad, rows, keep, fi, fo, fa[3].reshape(D, D), inv, act, gp, y, bg, dos, og, sums, bsum)
        return 0

    lax.fori_loop(0, blocks, second, 0)
    for name in ("og", "ig", "dos", "bg", "res", "y"):
        local[name]().start()
    out_copy(n - 2, (n - 2) % 2).wait()
    out_copy(n - 1, (n - 1) % 2).wait()
    for name in ("fa", "att", "hl", "act", "og", "ig", "dos", "bg", "res", "y"):
        local[name]().wait()
    net.finish()


def forward(x, seg, kept, wq, wk, wv, wo, wi, wr, vec, grad):
    t = x.shape[0]
    n = t // SEQ
    return pl.pallas_call(
        forward_kernel,
        out_shape=(
            shape(8, D, dtype=F32), shape(1, FF, dtype=F32), shape(3, 8, TR, D), shape(3, t, D), shape(t, D),
            shape(3, n, 2, 2, SEQ, SEQ), shape(t, D), shape(t, D, dtype=F32), shape(t, D), shape(t, D), shape(t, D),
            shape(t, D), shape(8, t, D),
        ),
        in_specs=[VM, VM, SM] + [VM] * 7 + [ANY],
        out_specs=(VM, VM) + (ANY,) * 11,
        scratch_shapes=[
            pltpu.VMEM((12, TR, D), BF),
            pltpu.VMEM((4, 8, TR, D), BF),
            pltpu.VMEM((4, 8, TR, D), BF),
            pltpu.VMEM((8, 4, TR, D), BF),
            pltpu.VMEM((8, 16, 128), BF),
            pltpu.VMEM((8, D), F32),
            pltpu.VMEM((1, FF), F32),
            pltpu.VMEM((t, D), BF),
            pltpu.VMEM((t, D), F32),
            pltpu.VMEM((t, D), F32),
            pltpu.VMEM((n, SEQ, 128), F32),
            pltpu.VMEM((2, 2, SEQ, SEQ), BF),
        ]
        + [pltpu.VMEM((t, D), BF)] * 6
        + [pltpu.VMEM((4, t, D), BF)] * 2
        + [
            pltpu.SemaphoreType.DMA((GATHER_COPIES,)),
            pltpu.SemaphoreType.DMA((GATHER_COPIES,)),
            pltpu.SemaphoreType.DMA((16,)),
            pltpu.SemaphoreType.DMA((2,)),
        ],
        compiler_params=params(collective_id=0, has_side_effects=True),
        name="forward",
    )(x, seg, kept, wq, wk, wv, wo, wi, wr, vec, grad)


def attend_back(i, qkv, dos, att, ebuf, dqkv):
    c, r, pair = place_of(i)
    rows = rows_of(r, SEQ)
    lanes = pl.ds(pl.multiple_of(c * CW + pair * 128, 128), 128)
    qp, kp, vp = (qkv[c, rows, pair_lanes(pair, part)] for part in range(3))
    dp = dos[rows, lanes]
    low = low_lanes(SEQ)
    zero = jnp.zeros_like(qp)
    product = dp.astype(F32) * att[rows, lanes].astype(F32)
    gq = jnp.zeros((SEQ, 128), F32)
    gk = jnp.zeros((SEQ, 128), F32)
    gv = jnp.zeros((SEQ, 128), F32)
    for h in range(2):
        mine = low if h == 0 else jnp.logical_not(low)
        dh = jnp.where(mine, dp, zero)
        delta = jnp.sum(jnp.where(mine, product, 0.0), axis=1, keepdims=True)
        e = ebuf[h]
        ds = (e.astype(F32) * (mm(dh, vp, NT) - delta)).astype(BF)
        gv = gv + mm(e, dh, TN)
        gk = gk + mm(ds, jnp.where(mine, qp, zero), TN)
        gq = gq + mm(ds, jnp.where(mine, kp, zero))
    dqkv[c, rows, pair_lanes(pair, 0)] = (gq * 0.125).astype(BF)
    dqkv[c, rows, pair_lanes(pair, 1)] = gk.astype(BF)
    dqkv[c, rows, pair_lanes(pair, 2)] = gv.astype(BF)


def chunk_grads(c, x, dqkv, gx, sums):
    gx[c] = mm(x[...], dqkv[c], TN).astype(BF).reshape(4, 2, 1, TR, D)
    part = dqkv[c].astype(F32)
    total = jnp.sum(part, axis=0, keepdims=True)
    lanes = pl.ds(pl.multiple_of(c * CW, CW), CW)
    sums[0:1, lanes] = total[:, 0:CW]
    sums[1:2, lanes] = total[:, 2 * CW :]


def input_back(res, dqkv, fa, out, block=256):
    def one(i, _):
        at = rows_of(i, block)
        total = res[at]
        for c in range(3):
            total = total + mm(dqkv[c, at], fa[c].reshape(D, D), NT)
        out[at] = total.astype(BF)
        return 0

    lax.fori_loop(0, res.shape[0] // block, one, 0)


JOBS = (
    (4, 1, False),
    (5, 1, True),
    (6, 1, True),
    (7, 1, False),
    (0, 2, True),
    (2, 2, False),
    (8, 1, False),
    (9, 1, False),
    (10, 1, False),
    (11, 1, False),
)
OUTER_UNITS = 4
REDUCE_COPIES = 9 * len(JOBS) + sum(first >= OUTER_UNITS for first, _, _ in JOBS) + 4 + 7


def job_shapes(units, ring_first):
    part, tile = (units, 48, 384), (units, TR, D)
    first = tile if ring_first else (4, *part)
    return [first, first, first, first, part, part, part]


class Job:
    def __init__(self, net, p, k, first, units, ring_first, held, landed, arrivals, bufs, result):
        self.net, self.p, self.k = net, p, k
        self.held, self.landed, self.arrivals = held, landed, arrivals
        self.d1, self.a1, self.b1, self.mid, self.d2, self.a2, self.b2 = bufs
        self.result = result
        self.units = slice(first, first + units)
        held, mid = self.held, self.mid
        z, za, zb, zo = p.z, lax.div(p.sa, 2), lax.div(p.sb, 2), lax.div(p.so, 2)
        self.z = z
        ring = (za, zb, zo, p.ring_a, p.ring_a, p.ring_b)
        plane = (p.wb, p.wa, p.wd, p.plane_a, p.plane_b, p.plane_a)

        def tile(t):
            return held, (t,)

        def plane_quarter(w):
            return held, (slice(None), slice(None), *quarter(w))

        def mid_quarter(w):
            return mid, (slice(None), *quarter(w))

        def mid_tile(t):
            return mid, (t,)

        one, two = (ring, plane) if ring_first else (plane, ring)
        self.at1, self.at2 = (tile, mid_quarter) if ring_first else (plane_quarter, mid_tile)
        self.one, self.two = one, two
        self.own1 = z if ring_first else p.w
        self.own2 = p.w if ring_first else z
        for stage, at, way, d, a, b in ((1, self.at1, one, self.d1, self.a1, self.b1), (2, self.at2, two, self.d2, self.a2, self.b2)):
            relayed, direct, opposite, dev_o, dev_r, dev_d = way

            def send(name, index, dst, device, at=at):
                def make():
                    ref, where = at(index)
                    return ref.at[where], dst, device

                net.define((k, *name), make)

            send(("d", stage), opposite, d, dev_o)
            send(("b", stage), direct, b, dev_d)
            send(("a", stage), relayed, a, dev_r)

        def share(name, w, device):
            def make():
                ref = result.at[(self.units, *quarter(w))]
                return ref, ref, device

            net.define((k, name), make)

        share("ga", p.w, p.plane_a)
        share("gb", p.w, p.plane_b)
        share("gd", p.wa, p.plane_b)

    def names(self, names):
        return [(self.k, *name) if isinstance(name, tuple) else (self.k, name) for name in names]

    def start(self, *names):
        self.net.start(*self.names(names))

    def wait(self, *names):
        self.net.wait(*self.names(names))

    def send(self):
        self.net.start(*self.arrivals)

    def pair(self):
        self.net.wait(*self.arrivals)
        held, landed = self.held, self.landed

        def one(t, _):
            held[t] = (held[t].astype(F32) + landed[t].astype(F32)).astype(BF)
            return 0

        lax.fori_loop(0, 4, one, 0)
        self.start(("d", 1), ("b", 1))

    def relay(self, stage):
        at, way, d = (self.at1, self.one, self.d1) if stage == 1 else (self.at2, self.two, self.d2)
        self.wait(("d", stage))
        ref, where = at(way[0])
        ref[where] = (ref[where].astype(F32) + d[...].astype(F32)).astype(BF)
        self.start(("a", stage))

    def total(self, stage):
        at, own, a, b = (self.at1, self.own1, self.a1, self.b1) if stage == 1 else (self.at2, self.own2, self.a2, self.b2)
        self.wait(("a", stage), ("b", stage))
        ref, where = at(own)
        return (ref[where].astype(F32) + a[...].astype(F32) + b[...].astype(F32)).astype(BF)

    def turn(self):
        self.mid[...] = self.total(1)
        self.start(("d", 2), ("b", 2))

    def share(self):
        self.result[(self.units, *quarter(self.p.w))] = self.total(2)
        self.start("ga", "gb")

    def pass_on(self):
        self.wait("ga")
        self.start("gd")

    def end(self):
        self.wait("gb", "gd")


def backward_kernel(
    x, qkv_in, e_in, att_in, dos_in, bg_in, res_in, fa_in, hl_in, og_in, ai_in, sums_in, bsum,
    out, result, ovec,
    qkv, att, dos, bg, res, fa, dqkv, gx, go, ebuf, sums, vt, vheld, vrecv, vplane, vz, *rest,
):
    bufs, (ssem, rsem, lsem, esem) = rest[:-4], rest[-4:]
    p = Place()
    call(others(p))
    n = 6 * (x.shape[0] // SEQ)
    og, hl = dqkv.at[0], dqkv.at[1]
    loads = (
        ("og", lambda: og_in, lambda: og),
        ("hl", lambda: hl_in, lambda: hl),
        ("att", lambda: att_in, lambda: att),
        ("bg", lambda: bg_in, lambda: bg),
        ("qkv", lambda: qkv_in, lambda: qkv),
        ("dos", lambda: dos_in, lambda: dos),
        ("res", lambda: res_in, lambda: res),
        ("fa", lambda: fa_in, lambda: fa.at[0:3]),
    )
    load = {
        name: lambda k=k, src=src, dst=dst: pltpu.make_async_copy(src(), dst(), lsem.at[k])
        for k, (name, src, dst) in enumerate(loads)
    }

    def block_copy(j):
        return pltpu.make_async_copy(ai_in.at[(j + 4) % 8], qkv.at[j % 3], lsem.at[len(loads) + j % 3])

    def in_copy(i, slot):
        c, r, pair = place_of(i)
        return pltpu.make_async_copy(e_in.at[c, r, pair], ebuf.at[slot], esem.at[slot])

    load["hl"]().start()
    block_copy(0).start()
    block_copy(1).start()
    load["og"]().start()
    for name in ("att", "bg", "dos"):
        load[name]().start()
    in_copy(0, 0).start()
    load["res"]().start()

    def staged(j):
        return fa.at[j // 2, 4 * (j % 2) : 4 * (j % 2) + 4]

    net = Net(ssem, rsem)
    held_outer, landed_outer, held_rest, landed_rest = bufs[0:4]
    jobs = []
    per = 7
    outer_arrivals = [("o", j) for j in range(4)]
    for j in range(4):
        net.define(("o", j), lambda j=j: (staged(4 + j), landed_outer.at[j], p.sib))
    for k, (first, units, ring_first) in enumerate(JOBS):
        if first < OUTER_UNITS:
            held, landed = held_outer.at[:, first : first + units], landed_outer.at[:, first : first + units]
            arrivals = outer_arrivals
            outer_arrivals = []
        else:
            r = first - OUTER_UNITS
            held, landed = held_rest.at[r], landed_rest.at[r]
            arrivals = [(k, "c")]
            if r < 4:
                source = lambda r=r: staged(r)
            elif r == 4:
                source = lambda: go.at[:, 1 - p.c, 0]
            else:
                source = lambda c=r - 5: gx.at[c, :, 1 - p.c, 0]
            net.define((k, "c"), lambda source=source, landed=landed: (source(), landed.at[:, 0], p.sib))
        job_bufs = bufs[4 + per * k : 4 + per * (k + 1)]
        jobs.append(Job(net, p, k, first, units, ring_first, held, landed, arrivals, job_bufs, result))
    net.define(("v", "c"), lambda: (vt.at[:, 1 - p.c], vrecv, p.sib))
    for k, device in enumerate((p.plane_a, p.plane_b, (p.wd, p.s))):
        net.define(("v", "p", k), lambda device=device: (vheld.at[0], vplane.at[p.w], device))
    for k in range(1, 4):
        to = lax.rem(p.z + k, 4)
        net.define(("v", "z", k), lambda to=to: (vheld.at[1, to], vz.at[p.z], (p.w, 2 * to + p.c)))
    assert len(net.made) == REDUCE_COPIES, len(net.made)

    def own_half(k, source):
        jobs[k].held[...] = source[:, p.c]

    def begin(k):
        first = JOBS[k][0]
        if first == 8:
            own_half(k, go)
        elif first > 8:
            own_half(k, gx.at[first - 9])
        jobs[k].pair()

    first_core = p.c == 0
    after = {
        0: lambda: (jobs[0].send(),),
        1: lambda: (jobs[1].send(),),
        2: lambda: (jobs[2].send(),),
        3: lambda: (jobs[3].send(), begin(0),),
        4: lambda: (net.start(("o", 0)), begin(1),),
        5: lambda: (net.start(("o", 1)), begin(2),),
        6: lambda: (net.start(("o", 2)), jobs[0].relay(1), begin(3),),
        7: lambda: (net.start(("o", 3)),),
    }
    for j in range(8):
        if j == 0:
            load["hl"]().wait()
        if j == 4:
            load["og"]().wait()
        if j + 2 < 8:
            block_copy(j + 2).start()
        block_copy(j).wait()
        block = qkv.at[j % 3]
        if j < 4:
            tiles = mm(hl[...], block[...], TN).astype(BF).reshape(4, 2, TR, D)
            zero, one = tiles[:, 0], tiles[:, 1]
            held_rest[j, :, 0] = jnp.where(first_core, zero, one)
        else:
            tiles = mm(block[...], og[...], TN).astype(BF).reshape(2, 4, TR, D)
            zero, one = tiles[0], tiles[1]
            held_outer[j - 4] = jnp.where(first_core, zero, one)
        staged(j)[...] = jnp.where(first_core, one, zero)
        if j == 0:
            answer(others(p))
        if j in after:
            after[j]()
    load["qkv"]().start()
    sums[...] = sums_in[...]
    load["att"]().wait()
    load["bg"]().wait()
    go[...] = mm(att[...], bg[...], TN).astype(BF).reshape(4, 2, 1, TR, D)
    jobs[6].send()
    load["qkv"]().wait()
    load["dos"]().wait()
    steps = {
        1: lambda: (jobs[0].turn(), jobs[1].relay(1), jobs[3].relay(1), begin(4), begin(5),),
        2: lambda: (begin(6),),
        3: lambda: (jobs[7].send(), jobs[2].relay(1), jobs[0].relay(2), jobs[3].turn(),),
        5: lambda: (jobs[5].relay(1),),
        6: lambda: (begin(7),),
        7: lambda: (jobs[8].send(), jobs[1].turn(),),
        8: lambda: (jobs[6].relay(1),),
    }

    def one(i, _):
        slot = lax.rem(i, 2)

        @pl.when(i + 1 < n)
        def _():
            in_copy(i + 1, 1 - slot).start()

        in_copy(i, slot).wait()
        attend_back(i, qkv, dos, att, ebuf.at[slot], dqkv)

        @pl.when(lax.rem(i, 4) == 3)
        def _():
            chunk_grads(lax.div(i, 4), x, dqkv, gx, sums)

        for k, step in steps.items():
            @pl.when(i == k)
            def _(step=step):
                step()
        return 0

    lax.fori_loop(0, n, one, 0)
    jobs[9].send()
    jobs[5].turn()
    jobs[7].relay(1)
    begin(8)
    jobs[4].relay(1)
    jobs[6].turn()
    staged_names = [(k, "c") for k, job in enumerate(JOBS) if 4 <= job[0] < 8] + [("o", j) for j in range(4)]
    for name in staged_names:
        net.copy(name).wait_send()
        net.sent.add(name)
    load["fa"]().start()

    for s in range(8):
        vt[s // 2, s % 2] = jnp.zeros((16, 128), F32)
        vt[s // 2, s % 2, 0:8, 0:TR] = sums[:, TR * s : TR * (s + 1)]
        for r in range(3):
            vt[s // 2, s % 2, 8 + r : 9 + r] = bsum[0:1, 128 * (3 * s + r) : 128 * (3 * s + r + 1)]
    net.start(("v", "c"))
    load["res"]().wait()

    def back(i):
        at = pl.ds(256 * i, 256)
        total = res[at]
        for c in range(3):
            total = total + mm(dqkv[c, at], fa[c].reshape(D, D), NT)
        out[at] = total.astype(BF)

    load["fa"]().wait()
    back(0)
    jobs[1].relay(2)
    net.wait(("v", "c"))
    vheld[0] = vt[:, p.c] + vrecv[...]
    vplane[p.w] = vheld[0]
    net.start(*[("v", "p", k) for k in range(3)])
    back(1)
    jobs[2].turn()
    back(2)
    jobs[0].share()
    begin(9)
    net.wait(*[("v", "p", k) for k in range(3)])
    vheld[1] = (vplane[0] + vplane[1]) + (vplane[2] + vplane[3])
    vz[p.z] = vheld[1, p.z]
    net.start(*[("v", "z", k) for k in range(1, 4)])
    back(3)
    jobs[3].relay(2)
    jobs[7].turn()
    jobs[8].relay(1)
    jobs[1].share()
    jobs[5].relay(2)
    jobs[2].relay(2)
    jobs[0].pass_on()
    jobs[9].relay(1)
    jobs[8].turn()
    jobs[2].share()
    jobs[4].turn()
    jobs[6].relay(2)
    jobs[1].pass_on()
    jobs[3].share()
    jobs[7].relay(2)
    jobs[9].turn()
    jobs[2].pass_on()
    jobs[5].share()
    jobs[4].relay(2)
    jobs[8].relay(2)
    jobs[6].share()
    jobs[7].share()
    jobs[3].pass_on()
    jobs[9].relay(2)
    jobs[5].pass_on()
    jobs[8].share()
    jobs[6].pass_on()
    jobs[4].share()
    jobs[7].pass_on()
    net.wait(*[("v", "z", k) for k in range(1, 4)])
    ovec[...] = (vz[0] + vz[1]) + (vz[2] + vz[3])
    jobs[9].share()
    jobs[8].pass_on()
    jobs[4].pass_on()
    jobs[9].pass_on()
    for job in jobs:
        job.end()
    net.finish()


def backward(x, qkv, e, att, dos, bg, res, fa, hl, og, ai, sums, bsum):
    t = x.shape[0]
    job_scratch = [pltpu.VMEM(s, BF) for s in ((4, 4, TR, D),) * 2 + ((8, 4, 1, TR, D),) * 2]
    job_scratch += [pltpu.VMEM(s, BF) for _, units, ring_first in JOBS for s in job_shapes(units, ring_first)]
    return pl.pallas_call(
        backward_kernel,
        out_shape=(shape(t, D), shape(12, TR, D), shape(16, 128, dtype=F32)),
        in_specs=[VM] + [ANY] * 10 + [VM, VM],
        out_specs=(VM,) * 3,
        scratch_shapes=[
            pltpu.VMEM((3, t, D), BF),
            pltpu.VMEM((t, D), BF),
            pltpu.VMEM((t, D), BF),
            pltpu.VMEM((t, D), BF),
            pltpu.VMEM((t, D), F32),
            pltpu.VMEM((4, 8, TR, D), BF),
            pltpu.VMEM((3, t, D), BF),
            pltpu.VMEM((3, 4, 2, 1, TR, D), BF),
            pltpu.VMEM((4, 2, 1, TR, D), BF),
            pltpu.VMEM((2, 2, SEQ, SEQ), BF),
            pltpu.VMEM((8, D), F32),
            pltpu.VMEM((4, 2, 16, 128), F32),
            pltpu.VMEM((2, 4, 16, 128), F32),
            pltpu.VMEM((4, 16, 128), F32),
            pltpu.VMEM((4, 4, 16, 128), F32),
            pltpu.VMEM((4, 16, 128), F32),
        ]
        + job_scratch
        + [
            pltpu.SemaphoreType.DMA((REDUCE_COPIES,)),
            pltpu.SemaphoreType.DMA((REDUCE_COPIES,)),
            pltpu.SemaphoreType.DMA((11,)),
            pltpu.SemaphoreType.DMA((2,)),
        ],
        compiler_params=params(collective_id=1, has_side_effects=True),
        name="backward",
    )(x, qkv, e, att, dos, bg, res, fa, hl, og, ai, sums, bsum)


def finish_kernel(result, ovec, inp, oq, ok, ov, oo, oi, our, out, *vectors):
    for c in range(3):
        tile = result[9 + c].astype(F32)
        for part, ref in enumerate((oq, ok, ov)):
            ref[:, c * CW : (c + 1) * CW] = tile[:, part * CW : (part + 1) * CW]
    oo[...] = result[8].astype(F32)
    for q in range(4):
        oi[:, q * D : (q + 1) * D] = result[4 + q].astype(F32)
        our[q * TR : (q + 1) * TR, :] = result[q].astype(F32)
    out[...] = inp[...]
    for k in range(8):
        vectors[k][...] = ovec[k, 0:TR]
    for r in range(3):
        vectors[8][128 * r : 128 * (r + 1)] = ovec[8 + r]


def finish(result, ovec, inp):
    t = inp.shape[0]
    return pl.pallas_call(
        finish_kernel,
        out_shape=tuple(shape(TR, D, dtype=F32) for _ in range(4))
        + (shape(TR, FF, dtype=F32), shape(4 * TR, D, dtype=F32), shape(t, D))
        + tuple(shape(TR, dtype=F32) for _ in range(8))
        + (shape(4 * TR, dtype=F32),),
        in_specs=[VM] * 3,
        out_specs=(VM,) * 16,
        compiler_params=params(),
        name="finish",
    )(result, ovec, inp)


def forward_local_kernel(x, seg, kept, fa, rows, qkv, att, inv, e_out, t1, segt, ebuf, esem):
    turn_ids(seg, segt)
    for c in range(3):
        project(c, x, fa, rows, qkv)
    keep = kept[0]

    def one(i, _):
        c, r, pair = place_of(i)
        attend(i, qkv, seg, segt, keep, att, inv, ebuf)
        copy = pltpu.make_async_copy(ebuf, e_out.at[c, r, pair], esem.at[0])
        copy.start()
        copy.wait()
        return 0

    lax.fori_loop(0, 6 * (x.shape[0] // SEQ), one, 0)
    t1[...] = x[...].astype(F32) + (mm(att[...], fa[3].reshape(D, D)) + rows[2:3])


def forward_local(x, seg, kept, fa, rows):
    t = x.shape[0]
    n = t // SEQ
    return pl.pallas_call(
        forward_local_kernel,
        out_shape=(shape(3, t, D), shape(t, D), shape(t, D, dtype=F32), shape(3, n, 2, 2, SEQ, SEQ), shape(t, D, dtype=F32)),
        in_specs=[VM, VM, SM, VM, VM],
        out_specs=(VM, VM, VM, ANY, VM),
        scratch_shapes=[
            pltpu.VMEM((n, SEQ, 128), F32), pltpu.VMEM((2, SEQ, SEQ), BF), pltpu.SemaphoreType.DMA((1,)),
        ],
        compiler_params=params(),
        name="forward_local",
    )(x, seg, kept, fa, rows)


def ffn_local_kernel(
    t1, grad, rows, binner, kept, inv, fi, fo, fa, y, res, bg, dos, sums, bsum, g, hl, og, act, gp, t2, tile, gsem, block=256
):
    sums[...] = jnp.zeros_like(sums)
    bsum[...] = jnp.zeros_like(bsum)
    t2[...] = t1[...]
    blocks = t1.shape[0] // block

    def first(i, _):
        ffn_inner(i, block, t2, rows, binner, kept[0], fi, hl, act, gp)
        return 0

    def second(i, _):
        wo = fa[3].reshape(D, D)
        ffn_outer(i, block, t2, grad, rows, kept[0], fi, fo, wo, inv, act, gp, y, bg, dos, og, sums, bsum)
        return 0

    lax.fori_loop(0, blocks, first, 0)
    lax.fori_loop(0, blocks, second, 0)
    res[...] = t2[...]

    def one(j, _):
        tile[...] = mm(act[j], og[...], TN).astype(BF).reshape(2, 4, TR, D)
        copy = pltpu.make_async_copy(tile, g.at[lax.div(j, 2), pl.ds(2 * lax.rem(j, 2), 2), 0:4], gsem.at[0])
        copy.start()
        copy.wait()
        tile[...] = mm(hl[...], gp[j], TN).astype(BF).reshape(2, 4, TR, D)
        copy = pltpu.make_async_copy(tile, g.at[:, :, 4 + j], gsem.at[0])
        copy.start()
        copy.wait()
        return 0

    lax.fori_loop(0, 4, one, 0)


def ffn_local(t1, grad, rows, binner, kept, inv, fi, fo, fa):
    t = t1.shape[0]
    return pl.pallas_call(
        ffn_local_kernel,
        out_shape=(
            shape(t, D), shape(t, D, dtype=F32), shape(t, D), shape(t, D),
            shape(8, D, dtype=F32), shape(1, FF, dtype=F32), shape(2, 4, 8, TR, D),
        ),
        in_specs=[VM] * 4 + [SM] + [VM] * 4,
        out_specs=(VM,) * 6 + (ANY,),
        scratch_shapes=[
            pltpu.VMEM((t, D), BF), pltpu.VMEM((t, D), BF), pltpu.VMEM((4, t, D), BF), pltpu.VMEM((4, t, D), BF),
            pltpu.VMEM((t, D), F32), pltpu.VMEM((2, 4, TR, D), BF), pltpu.SemaphoreType.DMA((1,)),
        ],
        compiler_params=params(),
        name="ffn_local",
    )(t1, grad, rows, binner, kept, inv, fi, fo, fa)


def backward_local_kernel(x, qkv, e_in, att, dos, bg, res, fa, sums_in, out, gx, go, sums, dqkv, ebuf, esem):
    sums[...] = sums_in[...]
    go[...] = mm(att[...], bg[...], TN).astype(BF).reshape(4, 2, 1, TR, D)

    def one(i, _):
        c, r, pair = place_of(i)
        copy = pltpu.make_async_copy(e_in.at[c, r, pair], ebuf, esem.at[0])
        copy.start()
        copy.wait()
        attend_back(i, qkv, dos, att, ebuf, dqkv)

        @pl.when(lax.rem(i, 4) == 3)
        def _():
            chunk_grads(lax.div(i, 4), x, dqkv, gx, sums)

        return 0

    lax.fori_loop(0, 6 * (x.shape[0] // SEQ), one, 0)
    input_back(res, dqkv, fa, out)


def backward_local(x, qkv, e, att, dos, bg, res, fa, sums):
    t = x.shape[0]
    return pl.pallas_call(
        backward_local_kernel,
        out_shape=(shape(t, D), shape(3, 4, 2, 1, TR, D), shape(4, 2, 1, TR, D), shape(8, D, dtype=F32)),
        in_specs=[VM, VM, ANY] + [VM] * 6,
        out_specs=(VM,) * 4,
        scratch_shapes=[pltpu.VMEM((3, t, D), BF), pltpu.VMEM((2, SEQ, SEQ), BF), pltpu.SemaphoreType.DMA((1,))],
        compiler_params=params(),
        name="backward_local",
    )(x, qkv, e, att, dos, bg, res, fa, sums)


def gather_lax(wq, wk, wv, wo, wi, wr, eight, b_inner):
    def whole(a):
        return lax.all_gather(a.astype(BF), "shard", axis=0, tiled=True)

    wq, wk, wv, wo, wi, wr = (whole(a) for a in (wq, wk, wv, wo, wi, wr))
    chunks = [jnp.concatenate([a[:, c * CW : (c + 1) * CW] for a in (wq, wk, wv)], axis=1) for c in range(3)]
    fa = jnp.stack(chunks + [wo]).reshape(4, 8, TR, D)
    fi = jnp.stack([wi[:, q * D : (q + 1) * D] for q in range(4)]).reshape(4, 8, TR, D)
    rows = jnp.stack([whole(a) for a in eight]).astype(F32)
    return fa, fi, wr.reshape(8, 4, TR, D), rows, whole(b_inner).astype(F32).reshape(1, FF)


def reduce_lax(g, gx, go, sums, bsum):
    g = g.reshape(8, 8, TR, D)
    gr = g[:, 0:4].reshape(FF, D)
    gi = jnp.concatenate([g[:, 4 + j].reshape(D, D) for j in range(4)], axis=1)
    gx = gx.reshape(3, D, 3, CW)
    squares = [jnp.concatenate([gx[c, :, part] for c in range(3)], axis=1) for part in range(3)]

    def owned(a):
        a = lax.psum_scatter(a.astype(F32), "shard", scatter_dimension=0, tiled=True)
        return lax.psum(a.astype(BF), "width").astype(F32)

    matrices = [owned(a) for a in (*squares, go.reshape(D, D), gi, gr)]
    return matrices, [owned(sums[k]) for k in range(8)] + [owned(bsum[0])]


def body(
    layer_input, segment_ids, group_heads,
    w_query, b_query, w_key, w_value, b_value, w_out, b_out, gain_one, shift_one,
    w_inner, b_inner, w_outer, b_outer, gain_two, shift_two, out_grad,
):
    eight = (b_query, b_value, b_out, gain_one, shift_one, b_outer, gain_two, shift_two)
    weights = (w_query, w_key, w_value, w_out, w_inner, w_outer)
    own_kernels = lax.axis_size("width") == 4 and lax.axis_size("shard") == 8
    if own_kernels:
        vec = jnp.concatenate([jnp.stack(eight), jnp.zeros((8, 128 - TR), F32)], axis=1)
        vec = jnp.concatenate([vec, b_inner.reshape(3, 128), jnp.zeros((5, 128), F32)], axis=0).astype(BF)
        sums, bsum, fa, qkv, att, e, y, res, bg, dos, hl, og, ai = forward(
            layer_input, segment_ids, group_heads, *weights, vec, out_grad
        )
    else:
        fa, fi, fo, rows, binner = gather_lax(*weights, eight, b_inner)
        qkv, att, inv, e, t1 = forward_local(layer_input, segment_ids, group_heads, fa, rows)
        y, res, bg, dos, sums, bsum, g = ffn_local(t1, out_grad, rows, binner, group_heads, inv, fi, fo, fa)
    if own_kernels:
        input_grad, result, ovec = backward(layer_input, qkv, e, att, dos, bg, res, fa, hl, og, ai, sums, bsum)
        gq, gk, gv, go, gi, gr, input_grad, *vectors = finish(result, ovec, input_grad)
    else:
        input_grad, gx, go, sums = backward_local(layer_input, qkv, e, att, dos, bg, res, fa[0:3], sums)
        (gq, gk, gv, go, gi, gr), vectors = reduce_lax(g, gx, go, sums, bsum)
    return (
        y, input_grad, gq, vectors[0], gk, gv, vectors[1], go, vectors[2],
        vectors[3], vectors[4], gi, vectors[8], gr, vectors[5], vectors[6], vectors[7],
    )


def solution(mesh):
    placed = (
        P(("width", "shard"), None),
        P(("width", "shard"), None),
        P("width"),
        P("shard", None),
        P("shard"),
        P("shard", None),
        P("shard", None),
        P("shard"),
        P("shard", None),
        P("shard"),
        P("shard"),
        P("shard"),
        P("shard", None),
        P("shard"),
        P("shard", None),
        P("shard"),
        P("shard"),
        P("shard"),
        P(("width", "shard"), None),
    )
    return jax.shard_map(
        body,
        mesh=mesh,
        in_specs=placed,
        out_specs=(
            P(("width", "shard"), None),
            P(("width", "shard"), None),
            P("shard", None),
            P("shard"),
            P("shard", None),
            P("shard", None),
            P("shard"),
            P("shard", None),
            P("shard"),
            P("shard"),
            P("shard"),
            P("shard", None),
            P("shard"),
            P("shard", None),
            P("shard"),
            P("shard"),
            P("shard"),
        ),
        check_vma=False,
    )
```

```python
import functools
import jax
import jax.numpy as jnp
from jax import lax
from jax.experimental import pallas as pl
from jax.experimental.pallas import tpu as pltpu
from jax.sharding import PartitionSpec as P

HEADS = 12
HEAD_DIM = 64
FF = 3072
D = 768
SEQ = 512
MESH = pl.DeviceIdType.MESH
BF = jnp.bfloat16
F32 = jnp.float32
TR = 96
CW = 256
NT = (((1,), (1,)), ((), ()))
TN = (((0,), (0,)), ((), ()))
NN = (((1,), (0,)), ((), ()))
EPS = 1e-06
RSQRT2 = 0.7071067811865476
RSQRT2PI = 0.3989422804014327
VM = pl.BlockSpec(memory_space=pltpu.VMEM)
SM = pl.BlockSpec(memory_space=pltpu.SMEM)
ANY = pl.BlockSpec(memory_space=pl.ANY)


def params(**more):
    return pltpu.CompilerParams(vmem_limit_bytes=62 << 20, **more)


def shape(*dims, dtype=BF):
    return jax.ShapeDtypeStruct(dims, dtype)


class Place:
    def __init__(self):
        self.w = w = lax.axis_index("width")
        self.s = s = lax.axis_index("shard")
        self.c = c = lax.rem(s, 2)
        self.z = lax.div(s, 2)
        xw, yw = w + 1 - 2 * lax.rem(w, 2), lax.rem(w + 2, 4)
        up, down = lax.rem(s + 2, 8), lax.rem(s + 6, 8)
        self.wa = jnp.where(c == 0, xw, yw)
        self.wb = jnp.where(c == 0, yw, xw)
        self.wd = 3 - w
        self.sa = jnp.where(c == 0, up, down)
        self.sb = jnp.where(c == 0, down, up)
        self.so = lax.rem(s + 4, 8)
        self.sib = (w, s + 1 - 2 * c)
        self.plane_a, self.plane_b = (self.wa, s), (self.wb, s)
        self.ring_a, self.ring_b = (w, self.sa), (w, self.sb)


def call(devices):
    barrier = pltpu.get_barrier_semaphore()
    for device in devices:
        pl.semaphore_signal(barrier, inc=1, device_id=device, device_id_type=MESH)


def answer(devices):
    pl.semaphore_wait(pltpu.get_barrier_semaphore(), len(devices))


def others(p):
    return [(p.wa, p.s), (p.wb, p.s), (p.wd, p.s)] + [(p.w, lax.rem(p.s + k, 8)) for k in range(1, 8)]


class Net:
    def __init__(self, send, recv):
        self.send, self.recv, self.made, self.sent = send, recv, {}, set()

    def define(self, name, make):
        assert name not in self.made
        self.made[name] = (len(self.made), make)

    def copy(self, name):
        k, make = self.made[name]
        src, dst, device = make()
        return pltpu.make_async_remote_copy(
            src_ref=src, dst_ref=dst, send_sem=self.send.at[k], recv_sem=self.recv.at[k],
            device_id=device, device_id_type=MESH,
        )

    def start(self, *names):
        for name in names:
            self.copy(name).start()

    def wait(self, *names):
        for name in names:
            self.copy(name).wait_recv()

    def finish(self):
        for name in self.made:
            if name not in self.sent:
                self.copy(name).wait_send()


def quarter(w):
    return pl.ds(pl.multiple_of(48 * lax.rem(w, 2), 48), 48), pl.ds(pl.multiple_of(384 * lax.div(w, 2), 384), 384)


def mm(a, b, dims=NN):
    return lax.dot_general(a, b, dims, preferred_element_type=F32)


def rows_of(i, size):
    return pl.ds(pl.multiple_of(i * size, size), size)


def column_mask(kept, shape, width):
    return jnp.where(lax.broadcasted_iota(jnp.int32, shape, 1) < kept * width, 1.0, 0.0).astype(F32)


def mean_of(v):
    return jnp.sum(v, axis=1, keepdims=True) * (1.0 / D)


def norm_rows(total):
    centered = total - mean_of(total)
    inverse = lax.rsqrt(mean_of(centered * centered) + EPS)
    return centered * inverse, inverse


def norm_back(grad, normed, inverse):
    return inverse * (grad - mean_of(grad) - normed * mean_of(grad * normed))


def low_lanes(n):
    return lax.broadcasted_iota(jnp.int32, (n, 128), 1) < HEAD_DIM


def place_of(i):
    return lax.div(i, 4), lax.rem(i, 2), lax.rem(lax.div(i, 2), 2)


def pair_lanes(pair, part):
    return pl.ds(pl.multiple_of(part * CW + pair * 128, 128), 128)


def project(c, x, fa, rows, qkv, block=256):
    lanes = pl.ds(pl.multiple_of(c * CW, CW), CW)
    bias = jnp.concatenate([rows[0:1, lanes], jnp.zeros((1, CW), F32), rows[1:2, lanes]], axis=1)
    scale = jnp.where(lax.broadcasted_iota(jnp.int32, (1, D), 1) < CW, 0.125, 1.0)

    def one(i, _):
        at = rows_of(i, block)
        qkv[c, at] = ((mm(x[at], fa[c].reshape(D, D)) + bias) * scale).astype(BF)
        return 0

    lax.fori_loop(0, x.shape[0] // block, one, 0)


def turn_ids(seg, segt):
    for r in range(seg.shape[0]):
        row = seg[r : r + 1, :].astype(F32)
        segt[r] = jnp.broadcast_to(row, (128, SEQ)).T


def attend(i, qkv, seg, segt, kept, att, inv, ebuf, qb=512):
    c, r, pair = place_of(i)
    base = r * SEQ
    rows = pl.ds(pl.multiple_of(base, SEQ), SEQ)
    kp, vp = qkv[c, rows, pair_lanes(pair, 1)], qkv[c, rows, pair_lanes(pair, 2)]
    low = low_lanes(SEQ)
    ones = jnp.ones_like(vp)
    vs = (jnp.where(low, vp, ones), jnp.where(low, ones, vp))
    ids = seg[pl.ds(r, 1), :].astype(F32)
    lowq = low_lanes(qb)
    lanes = pl.ds(pl.multiple_of(c * CW + pair * 128, 128), 128)
    column = lax.broadcasted_iota(jnp.int32, (1, 128), 1) + (c * CW + pair * 128)
    mask = jnp.where(column < kept * HEAD_DIM, 1.0, 0.0).astype(F32)
    for b in range(SEQ // qb):
        at = pl.ds(pl.multiple_of(base + b * qb, qb), qb)
        qp = qkv[c, at, pair_lanes(pair, 0)]
        zero = jnp.zeros_like(qp)
        own = segt[r, b * qb : (b + 1) * qb]
        same = jnp.concatenate([own == ids[:, j * 128 : (j + 1) * 128] for j in range(4)], axis=1)
        out = []
        for h in range(2):
            qh = jnp.where(lowq, qp, zero) if h == 0 else jnp.where(lowq, zero, qp)
            scores = jnp.where(same, mm(qh, kp, NT), -1e30)
            top = jnp.max(scores, axis=1, keepdims=True)
            e = jnp.exp(scores - top).astype(BF)
            ebuf[h, b * qb : (b + 1) * qb] = e
            out.append(mm(e, vs[h]))
        inverse = 1.0 / pltpu.roll(jnp.where(lowq, out[1], out[0]), HEAD_DIM, 1)
        att[at, lanes] = (jnp.where(lowq, out[0], out[1]) * (inverse * mask)).astype(BF)
        inv[at, lanes] = inverse


def expand_vectors(fv, rows, binner):
    lane = lax.broadcasted_iota(jnp.int32, (128, D), 0)
    column = lax.broadcasted_iota(jnp.int32, (128, D), 1)
    total = jnp.zeros((16, D), F32)
    for s in range(8):
        pick = jnp.where((column == lane + TR * s) & (lane < TR), 1.0, 0.0).astype(BF)
        total = total + mm(fv[s], pick)
        tile = fv[s].astype(F32)
        for r in range(3):
            binner[0:1, 128 * (3 * s + r) : 128 * (3 * s + r + 1)] = tile[8 + r : 9 + r]
    rows[...] = total[0:8]


GROUPS = (slice(0, 1), slice(1, 2), slice(2, 3), slice(3, 4), slice(4, 8), slice(8, 12))
WO, INNER, OUTER = 3, 4, 5
GATHER_COPIES = 16 * len(GROUPS) + 7


def gather_net(p, own, fa, fi, fo, vec, fv, ssem, rsem):
    net = Net(ssem, rsem)
    every = (slice(None), slice(None))

    def piece(g, s, part):
        if g <= WO:
            return fa.at[(GROUPS[g], s, *part)]
        return fi.at[(slice(None), s, *part)] if g == INNER else fo.at[(s, slice(None), *part)]

    mine, first = quarter(p.w), quarter(p.wa)
    for g in range(len(GROUPS)):

        def add(name, src, dst, device):
            net.define((g, *name), lambda: (src(), dst(), device))

        def same(name, g, s, part, device):
            add(name, lambda: piece(g, s, part), lambda: piece(g, s, part), device)

        for name, device in (("zb", p.ring_a), ("za", p.ring_b)):
            add((name,), lambda g=g: own.at[(GROUPS[g], *mine)], lambda g=g: piece(g, p.s, mine), device)
        same(("zo",), g, p.sb, mine, p.ring_a)
        add(("own", "c"), lambda g=g: own.at[GROUPS[g]], lambda g=g: piece(g, p.s, every), p.sib)
        for name, s in (("zb", p.sb), ("za", p.sa), ("zo", p.so)):
            same((name, "xa"), g, s, mine, p.plane_a)
            same((name, "xb"), g, s, mine, p.plane_b)
            same((name, "xd"), g, s, first, p.plane_b)
            same((name, "c"), g, s, every, p.sib)
    for k in range(1, 8):
        net.define(("v", k), lambda k=k: (vec, fv.at[p.s], (p.w, lax.rem(p.s + k, 8))))
    assert len(net.made) == GATHER_COPIES
    return net


def ffn_inner(i, block, t1, rows, binner, kept, wi, hl, act, gp):
    at = rows_of(i, block)
    n1, _ = norm_rows(t1[at])
    low = (n1 * rows[3:4] + rows[4:5]).astype(BF)
    hl[at] = low
    for j in range(4):
        inner = mm(low, wi[j].reshape(D, D)) + binner[:, j * D : (j + 1) * D]
        keep = column_mask(kept * 256 - j * D, (1, D), 1)
        phi = 0.5 + 0.5 * lax.erf(inner * RSQRT2)
        masked = inner * keep
        act[j, at] = (masked * phi).astype(BF)
        gp[j, at] = (keep * phi + masked * (RSQRT2PI * jnp.exp(-0.5 * (inner * inner)))).astype(BF)


def outer_product(i, block, wr, act, ob):
    at = rows_of(i, block)
    outer = jnp.zeros((block, D), F32)
    for j in range(4):
        outer = outer + mm(act[j, at], wr[2 * j : 2 * j + 2].reshape(D, D))
    ob[...] = outer


def ffn_outer(i, block, blocks, t1, grad, rows, kept, wi, wr, wo, inv, act, gp, ob, y, bg, dos, og, sums, bsum):
    at = rows_of(i, block)

    def add(k, value):
        sums[k : k + 1] += jnp.sum(value, axis=0, keepdims=True)

    def outer_weight(j):
        return wr[2 * j : 2 * j + 2].reshape(D, D)

    n1, inv1 = norm_rows(t1[at])
    hidden = n1 * rows[3:4] + rows[4:5]
    n2, inv2 = norm_rows(hidden + (ob[...] + rows[5:6]))
    outer_product(jnp.minimum(i + 1, blocks - 1), block, wr, act, ob)
    y[at] = (n2 * rows[6:7] + rows[7:8]).astype(BF)
    top = grad[at].astype(F32)
    add(7, top)
    add(6, top * n2)
    res2 = norm_back(top * rows[6:7], n2, inv2)
    o = res2.astype(BF)
    og[at] = o
    add(5, o.astype(F32))
    hg = res2
    for j in range(4):
        cols = slice(j * D, (j + 1) * D)
        g = (mm(o, outer_weight(j), NT) * gp[j, at].astype(F32)).astype(BF)
        gp[j, at] = g
        bsum[:, cols] += jnp.sum(g.astype(F32), axis=0, keepdims=True)
        hg = hg + mm(g, wi[j].reshape(D, D), NT)
    add(4, hg)
    add(3, hg * n1)
    res1 = norm_back(hg * rows[3:4], n1, inv1)
    t1[at] = res1
    b = res1.astype(BF)
    bg[at] = b
    add(2, b.astype(F32))
    heads = column_mask(kept, (1, D), HEAD_DIM)
    dos[at] = (mm(b, wo, NT) * (inv[at] * heads)).astype(BF)


def forward_kernel(
    x, seg, kept, wq, wk, wv, wo, wi, wr, v0, v1, v2, v3, v4, v5, v6, v7, v_inner, grad_in,
    sums, bsum, fa_out, qkv_out, att_out, e_out, y_out, res_out, bg_out, dos_out, hl_out, og_out, ai_out,
    own, vtile, vec, fa, fi, fo, fv, rows, binner, att, inv, t1, segt, ebuf, grad, y, bg, dos, hl, og, act, gp, ob,
    ssem, rsem, lsem, esem, fsem,
):
    qkv = gp.at[0:3]
    p = Place()
    call(others(p))

    def cast(c):
        for part, ref in enumerate((wq, wk, wv)):
            own[c, :, part * CW : (part + 1) * CW] = ref[:, c * CW : (c + 1) * CW].astype(BF)

    cast(0)
    vtile[...] = jnp.zeros_like(vtile)
    for k, ref in enumerate((v0, v1, v2, v3, v4, v5, v6, v7)):
        vtile[k : k + 1, 0:TR] = ref[...]
    for r in range(3):
        vtile[8 + r : 9 + r] = v_inner[128 * r : 128 * (r + 1)].reshape(1, 128)
    vec[...] = vtile[...].astype(BF)
    answer(others(p))
    net = gather_net(p, own, fa, fi, fo, vec, fv, ssem, rsem)
    names = ("zb", "za", "zo")

    def ring(g):
        net.start((g, "zb"), (g, "za"), (g, "own", "c"))

    def onward(g):
        net.wait((g, "zb"))
        net.start((g, "zo"))

    def plane(g, *which):
        for name in which or names:
            if name != "zb":
                net.wait((g, name))
            net.start((g, name, "xa"), (g, name, "xb"))

    def relay(g, *which):
        for name in which or names:
            net.wait((g, name, "xa"))
            net.start((g, name, "xd"))

    def share(g, *which):
        for name in which or names:
            net.wait((g, name, "xb"), (g, name, "xd"))
            net.start((g, name, "c"))

    def landed(g):
        net.wait((g, "own", "c"), *[(g, name, "c") for name in names])

    ring(0)
    cast(1)
    ring(1)
    cast(2)
    own[3] = wo[...].astype(BF)
    for q in range(4):
        own[4 + q] = wi[:, q * D : (q + 1) * D].astype(BF)
        own[8 + q] = wr[q * TR : (q + 1) * TR, :].astype(BF)
    net.start(*[("v", k) for k in range(1, 8)])
    local = {}

    def put(name, k, src, dst):
        local[name] = lambda: pltpu.make_async_copy(src(), dst(), lsem.at[k])

    pieces = (
        ("own a", lambda: own.at[0:4], lambda: fa.at[:, p.s]),
        ("own i", lambda: own.at[4:8], lambda: fi.at[:, p.s]),
        ("own o", lambda: own.at[8:12], lambda: fo.at[p.s]),
        ("vec", lambda: vec, lambda: fv.at[p.s]),
        ("grad", lambda: grad_in, lambda: grad),
        ("qkv", lambda: qkv, lambda: qkv_out),
        ("fa", lambda: fa.at[0:3], lambda: fa_out),
        ("att", lambda: att, lambda: att_out),
        ("hl", lambda: hl, lambda: hl_out),
        ("act", lambda: act, lambda: ai_out.at[0:4]),
    )
    for k, (name, src, dst) in enumerate(pieces):
        put(name, k, src, dst)
    for name in ("own a", "own i", "own o", "vec", "grad"):
        local[name]().start()

    onward(0)
    plane(0, "zb", "za")
    onward(1)
    ring(2)
    plane(1, "zb", "za")
    plane(0, "zo")
    turn_ids(seg, segt)
    relay(0, "zb", "za")
    plane(1, "zo")
    relay(1, "zb")
    onward(2)
    ring(INNER)
    relay(1, "za")
    plane(2, "zb", "za")
    relay(0, "zo")
    share(0, "zb", "za")
    relay(1, "zo")
    share(1, "zb")
    plane(2, "zo")
    share(1, "za")
    relay(2, "zb", "za")
    share(0, "zo")
    onward(INNER)
    ring(WO)
    share(1, "zo")
    plane(INNER, "zb")
    relay(2, "zo")
    net.wait(*[("v", k) for k in range(1, 8)])
    local["vec"]().wait()
    expand_vectors(fv, rows, binner)
    share(2, "zb", "za")
    plane(INNER, "za")
    local["own a"]().wait()
    keep = kept[0]

    def out_copy(i, slot):
        c, r, pair = place_of(i)
        return pltpu.make_async_copy(ebuf.at[slot], e_out.at[c, r, pair], esem.at[slot])

    before = {0: lambda: landed(0), 4: lambda: landed(1), 8: lambda: landed(2)}
    steps = {
        1: lambda: (plane(INNER, "zo"), relay(INNER, "zb"), onward(WO), ring(OUTER), share(2, "zo"), plane(WO, "zb", "za"),),
        2: lambda: (relay(INNER, "za"),),
        4: lambda: (relay(INNER, "zo"), plane(WO, "zo"), relay(WO, "zb"),),
        5: lambda: (relay(WO, "za"), onward(OUTER), plane(OUTER, "zb"),),
        6: lambda: (share(INNER, "zb"),),
        7: lambda: (relay(WO, "zo"), plane(OUTER, "za"),),
        8: lambda: (share(INNER, "za"),),
        9: lambda: (share(INNER, "zo"), relay(OUTER, "zb"), plane(OUTER, "zo"),),
        10: lambda: (share(WO, "zb", "za"),),
        11: lambda: (relay(OUTER, "za"), share(WO, "zo"), relay(OUTER, "zo"),),
    }
    later = {
        1: lambda: (share(OUTER, "za", "zo"),),
    }

    def after_residual():
        share(OUTER, "zb")

    def at_step(i, table):
        for k, step in table.items():
            @pl.when(i == k)
            def _(step=step):
                step()

    def one(i, _):
        slot = lax.rem(i, 2)

        @pl.when(i >= 2)
        def _():
            out_copy(i - 2, slot).wait()

        at_step(i, before)

        @pl.when(lax.rem(i, 4) == 0)
        def _():
            project(lax.div(i, 4), x, fa, rows, qkv)

        attend(i, qkv, seg, segt, keep, att, inv, ebuf.at[slot])
        out_copy(i, slot).start()
        at_step(i, steps)
        return 0

    n = 6 * (x.shape[0] // SEQ)
    lax.fori_loop(0, n, one, 0)
    local["qkv"]().start()
    local["att"]().start()
    local["fa"]().start()
    sums[...] = jnp.zeros_like(sums)
    bsum[...] = jnp.zeros_like(bsum)
    landed(WO)
    block = 256
    blocks = x.shape[0] // block

    def residual(i, _):
        at = rows_of(i, block)
        t1[at] = x[at].astype(F32) + (mm(att[at], fa[3].reshape(D, D)) + rows[2:3])
        return 0

    lax.fori_loop(0, blocks, residual, 0)
    after_residual()
    landed(INNER)
    local["own i"]().wait()
    local["qkv"]().wait()

    def first(i, _):
        ffn_inner(i, block, t1, rows, binner, keep, fi, hl, act, gp)
        at_step(i, later)
        return 0

    lax.fori_loop(0, blocks, first, 0)
    local["hl"]().start()
    local["act"]().start()
    landed(OUTER)
    local["own o"]().wait()
    local["grad"]().wait()

    def flush(i):
        at = rows_of(i, block)
        pairs = (
            (gp.at[:, at], ai_out.at[4:8, at]), (og.at[at], og_out.at[at]), (dos.at[at], dos_out.at[at]),
            (bg.at[at], bg_out.at[at]), (t1.at[at], res_out.at[at]), (y.at[at], y_out.at[at]),
        )
        return [pltpu.make_async_copy(src, dst, fsem.at[i, k]) for k, (src, dst) in enumerate(pairs)]

    def second(i, _):
        wo = fa[3].reshape(D, D)
        ffn_outer(i, block, blocks, t1, grad, rows, keep, fi, fo, wo, inv, act, gp, ob, y, bg, dos, og, sums, bsum)
        for copy in flush(i):
            copy.start()
        return 0

    outer_product(0, block, fo, act, ob)
    lax.fori_loop(0, blocks, second, 0)
    out_copy(n - 2, (n - 2) % 2).wait()
    out_copy(n - 1, (n - 1) % 2).wait()
    for name in ("fa", "att", "hl", "act"):
        local[name]().wait()
    for i in range(blocks):
        for copy in flush(i):
            copy.wait()
    net.finish()


def forward(x, seg, kept, wq, wk, wv, wo, wi, wr, eight, b_inner, grad):
    t = x.shape[0]
    n = t // SEQ
    return pl.pallas_call(
        forward_kernel,
        out_shape=(
            shape(8, D, dtype=F32), shape(1, FF, dtype=F32), shape(3, 8, TR, D), shape(3, t, D), shape(t, D),
            shape(3, n, 2, 2, SEQ, SEQ), shape(t, D), shape(t, D, dtype=F32), shape(t, D), shape(t, D), shape(t, D),
            shape(t, D), shape(8, t, D),
        ),
        in_specs=[VM, VM, SM] + [VM] * 15 + [ANY],
        out_specs=(VM, VM) + (ANY,) * 11,
        scratch_shapes=[
            pltpu.VMEM((12, TR, D), BF),
            pltpu.VMEM((16, 128), F32),
            pltpu.VMEM((16, 128), BF),
            pltpu.VMEM((4, 8, TR, D), BF),
            pltpu.VMEM((4, 8, TR, D), BF),
            pltpu.VMEM((8, 4, TR, D), BF),
            pltpu.VMEM((8, 16, 128), BF),
            pltpu.VMEM((8, D), F32),
            pltpu.VMEM((1, FF), F32),
            pltpu.VMEM((t, D), BF),
            pltpu.VMEM((t, D), F32),
            pltpu.VMEM((t, D), F32),
            pltpu.VMEM((n, SEQ, 128), F32),
            pltpu.VMEM((2, 2, SEQ, SEQ), BF),
        ]
        + [pltpu.VMEM((t, D), BF)] * 6
        + [pltpu.VMEM((4, t, D), BF)] * 2
        + [
            pltpu.VMEM((256, D), F32),
            pltpu.SemaphoreType.DMA((GATHER_COPIES,)),
            pltpu.SemaphoreType.DMA((GATHER_COPIES,)),
            pltpu.SemaphoreType.DMA((10,)),
            pltpu.SemaphoreType.DMA((2,)),
            pltpu.SemaphoreType.DMA((t // 256, 6)),
        ],
        compiler_params=params(collective_id=0, has_side_effects=True),
        name="forward",
    )(x, seg, kept, wq, wk, wv, wo, wi, wr, *(a.reshape(1, TR) for a in eight), b_inner, grad)


def attend_back(i, qkv, dos, att, ebuf, dqkv):
    c, r, pair = place_of(i)
    rows = rows_of(r, SEQ)
    lanes = pl.ds(pl.multiple_of(c * CW + pair * 128, 128), 128)
    qp, kp, vp = (qkv[c, rows, pair_lanes(pair, part)] for part in range(3))
    dp = dos[rows, lanes]
    low = low_lanes(SEQ)
    zero = jnp.zeros_like(qp)
    product = dp.astype(F32) * att[rows, lanes].astype(F32)
    gq = jnp.zeros((SEQ, 128), F32)
    gk = jnp.zeros((SEQ, 128), F32)
    gv = jnp.zeros((SEQ, 128), F32)
    for h in range(2):
        mine = low if h == 0 else jnp.logical_not(low)
        dh = jnp.where(mine, dp, zero)
        delta = jnp.sum(jnp.where(mine, product, 0.0), axis=1, keepdims=True)
        e = ebuf[h]
        ds = (e.astype(F32) * (mm(dh, vp, NT) - delta)).astype(BF)
        gv = gv + mm(e, dh, TN)
        gk = gk + mm(ds, jnp.where(mine, qp, zero), TN)
        gq = gq + mm(ds, jnp.where(mine, kp, zero))
    dqkv[c, rows, pair_lanes(pair, 0)] = (gq * 0.125).astype(BF)
    dqkv[c, rows, pair_lanes(pair, 1)] = gk.astype(BF)
    dqkv[c, rows, pair_lanes(pair, 2)] = gv.astype(BF)


def chunk_grads(c, x, dqkv, gx, sums):
    gx[c] = mm(x[...], dqkv[c], TN).astype(BF).reshape(4, 2, 1, TR, D)
    part = dqkv[c].astype(F32)
    total = jnp.sum(part, axis=0, keepdims=True)
    lanes = pl.ds(pl.multiple_of(c * CW, CW), CW)
    sums[0:1, lanes] = total[:, 0:CW]
    sums[1:2, lanes] = total[:, 2 * CW :]


def input_back(res, dqkv, fa, out, block=256):
    def one(i, _):
        at = rows_of(i, block)
        total = res[at]
        for c in range(3):
            total = total + mm(dqkv[c, at], fa[c].reshape(D, D), NT)
        out[at] = total.astype(BF)
        return 0

    lax.fori_loop(0, res.shape[0] // block, one, 0)


JOBS = (
    (4, 1, False),
    (5, 1, True),
    (6, 1, True),
    (7, 1, False),
    (0, 2, True),
    (2, 2, False),
    (8, 1, False),
    (9, 1, False),
    (10, 1, False),
    (11, 1, False),
)
OUTER_UNITS = 4
REDUCE_COPIES = 9 * len(JOBS) + sum(first >= OUTER_UNITS for first, _, _ in JOBS) + 4 + 7


def job_shapes(units, ring_first):
    part, tile = (units, 48, 384), (units, TR, D)
    first = tile if ring_first else (4, *part)
    return [first, first, first, first, part, part, part]


class Job:
    def __init__(self, net, p, k, first, units, ring_first, held, landed, arrivals, bufs, result):
        self.net, self.p, self.k = net, p, k
        self.held, self.landed, self.arrivals = held, landed, arrivals
        self.d1, self.a1, self.b1, self.mid, self.d2, self.a2, self.b2 = bufs
        self.result = result
        self.units = slice(first, first + units)
        held, mid = self.held, self.mid
        z, za, zb, zo = p.z, lax.div(p.sa, 2), lax.div(p.sb, 2), lax.div(p.so, 2)
        self.z = z
        ring = (za, zb, zo, p.ring_a, p.ring_a, p.ring_b)
        plane = (p.wb, p.wa, p.wd, p.plane_a, p.plane_b, p.plane_a)

        def tile(t):
            return held, (t,)

        def plane_quarter(w):
            return held, (slice(None), slice(None), *quarter(w))

        def mid_quarter(w):
            return mid, (slice(None), *quarter(w))

        def mid_tile(t):
            return mid, (t,)

        one, two = (ring, plane) if ring_first else (plane, ring)
        self.at1, self.at2 = (tile, mid_quarter) if ring_first else (plane_quarter, mid_tile)
        self.one, self.two = one, two
        self.own1 = z if ring_first else p.w
        self.own2 = p.w if ring_first else z
        for stage, at, way, d, a, b in ((1, self.at1, one, self.d1, self.a1, self.b1), (2, self.at2, two, self.d2, self.a2, self.b2)):
            relayed, direct, opposite, dev_o, dev_r, dev_d = way

            def send(name, index, dst, device, at=at):
                def make():
                    ref, where = at(index)
                    return ref.at[where], dst, device

                net.define((k, *name), make)

            send(("d", stage), opposite, d, dev_o)
            send(("b", stage), direct, b, dev_d)
            send(("a", stage), relayed, a, dev_r)

        def share(name, w, device):
            def make():
                ref = result.at[(self.units, *quarter(w))]
                return ref, ref, device

            net.define((k, name), make)

        share("ga", p.w, p.plane_a)
        share("gb", p.w, p.plane_b)
        share("gd", p.wa, p.plane_b)

    def names(self, names):
        return [(self.k, *name) if isinstance(name, tuple) else (self.k, name) for name in names]

    def start(self, *names):
        self.net.start(*self.names(names))

    def wait(self, *names):
        self.net.wait(*self.names(names))

    def send(self):
        self.net.start(*self.arrivals)

    def pair(self):
        self.net.wait(*self.arrivals)
        held, landed = self.held, self.landed

        def one(t, _):
            held[t] = (held[t].astype(F32) + landed[t].astype(F32)).astype(BF)
            return 0

        lax.fori_loop(0, 4, one, 0)
        self.start(("d", 1), ("b", 1))

    def relay(self, stage):
        at, way, d = (self.at1, self.one, self.d1) if stage == 1 else (self.at2, self.two, self.d2)
        self.wait(("d", stage))
        ref, where = at(way[0])
        ref[where] = (ref[where].astype(F32) + d[...].astype(F32)).astype(BF)
        self.start(("a", stage))

    def total(self, stage):
        at, own, a, b = (self.at1, self.own1, self.a1, self.b1) if stage == 1 else (self.at2, self.own2, self.a2, self.b2)
        self.wait(("a", stage), ("b", stage))
        ref, where = at(own)
        return (ref[where].astype(F32) + a[...].astype(F32) + b[...].astype(F32)).astype(BF)

    def turn(self):
        self.mid[...] = self.total(1)
        self.start(("d", 2), ("b", 2))

    def share(self):
        self.result[(self.units, *quarter(self.p.w))] = self.total(2)
        self.start("ga", "gb")

    def pass_on(self):
        self.wait("ga")
        self.start("gd")

    def end(self):
        self.wait("gb", "gd")


def backward_kernel(
    x, qkv_in, e_in, att_in, dos_in, bg_in, res_in, fa_in, hl_in, og_in, ai_in, sums_in, bsum,
    out, result, ovec,
    qkv, att, dos, bg, res, fa, dqkv, gx, go, ebuf, sums, vt, vheld, vrecv, vplane, vz, *rest,
):
    bufs, (ssem, rsem, lsem, esem) = rest[:-4], rest[-4:]
    p = Place()
    call(others(p))
    n = 6 * (x.shape[0] // SEQ)
    og, hl = dqkv.at[0], dqkv.at[1]
    loads = (
        ("og", lambda: og_in, lambda: og),
        ("hl", lambda: hl_in, lambda: hl),
        ("att", lambda: att_in, lambda: att),
        ("bg", lambda: bg_in, lambda: bg),
        ("qkv", lambda: qkv_in, lambda: qkv),
        ("dos", lambda: dos_in, lambda: dos),
        ("res", lambda: res_in, lambda: res),
        ("fa", lambda: fa_in, lambda: fa.at[0:3]),
    )
    load = {
        name: lambda k=k, src=src, dst=dst: pltpu.make_async_copy(src(), dst(), lsem.at[k])
        for k, (name, src, dst) in enumerate(loads)
    }

    def block_copy(j):
        return pltpu.make_async_copy(ai_in.at[(j + 4) % 8], qkv.at[j % 3], lsem.at[len(loads) + j % 3])

    def in_copy(i, slot):
        c, r, pair = place_of(i)
        return pltpu.make_async_copy(e_in.at[c, r, pair], ebuf.at[slot], esem.at[slot])

    load["hl"]().start()
    block_copy(0).start()
    block_copy(1).start()
    load["og"]().start()
    for name in ("att", "bg", "dos"):
        load[name]().start()
    in_copy(0, 0).start()
    load["res"]().start()

    def staged(j):
        return fa.at[j // 2, 4 * (j % 2) : 4 * (j % 2) + 4]

    net = Net(ssem, rsem)
    held_outer, landed_outer, held_rest, landed_rest = bufs[0:4]
    jobs = []
    per = 7
    outer_arrivals = [("o", j) for j in range(4)]
    for j in range(4):
        net.define(("o", j), lambda j=j: (staged(4 + j), landed_outer.at[j], p.sib))
    for k, (first, units, ring_first) in enumerate(JOBS):
        if first < OUTER_UNITS:
            held, landed = held_outer.at[:, first : first + units], landed_outer.at[:, first : first + units]
            arrivals = outer_arrivals
            outer_arrivals = []
        else:
            r = first - OUTER_UNITS
            held, landed = held_rest.at[r], landed_rest.at[r]
            arrivals = [(k, "c")]
            if r < 4:
                source = lambda r=r: staged(r)
            elif r == 4:
                source = lambda: go.at[:, 1 - p.c, 0]
            else:
                source = lambda c=r - 5: gx.at[c, :, 1 - p.c, 0]
            net.define((k, "c"), lambda source=source, landed=landed: (source(), landed.at[:, 0], p.sib))
        job_bufs = bufs[4 + per * k : 4 + per * (k + 1)]
        jobs.append(Job(net, p, k, first, units, ring_first, held, landed, arrivals, job_bufs, result))
    net.define(("v", "c"), lambda: (vt.at[:, 1 - p.c], vrecv, p.sib))
    for k, device in enumerate((p.plane_a, p.plane_b, (p.wd, p.s))):
        net.define(("v", "p", k), lambda device=device: (vheld.at[0], vplane.at[p.w], device))
    for k in range(1, 4):
        to = lax.rem(p.z + k, 4)
        net.define(("v", "z", k), lambda to=to: (vheld.at[1, to], vz.at[p.z], (p.w, 2 * to + p.c)))
    assert len(net.made) == REDUCE_COPIES, len(net.made)

    def own_half(k, source):
        jobs[k].held[...] = source[:, p.c]

    def begin(k):
        first = JOBS[k][0]
        if first == 8:
            own_half(k, go)
        elif first > 8:
            own_half(k, gx.at[first - 9])
        jobs[k].pair()

    first_core = p.c == 0
    after = {
        0: lambda: (jobs[0].send(),),
        1: lambda: (jobs[1].send(),),
        2: lambda: (jobs[2].send(),),
        3: lambda: (jobs[3].send(), begin(0),),
        4: lambda: (net.start(("o", 0)), begin(1),),
        5: lambda: (net.start(("o", 1)), begin(2),),
        6: lambda: (net.start(("o", 2)), jobs[0].relay(1), begin(3),),
        7: lambda: (net.start(("o", 3)),),
    }
    for j in range(8):
        if j == 0:
            load["hl"]().wait()
        if j == 4:
            load["og"]().wait()
        if j + 2 < 8:
            block_copy(j + 2).start()
        block_copy(j).wait()
        block = qkv.at[j % 3]
        if j < 4:
            tiles = mm(hl[...], block[...], TN).astype(BF).reshape(4, 2, TR, D)
            zero, one = tiles[:, 0], tiles[:, 1]
            held_rest[j, :, 0] = jnp.where(first_core, zero, one)
        else:
            tiles = mm(block[...], og[...], TN).astype(BF).reshape(2, 4, TR, D)
            zero, one = tiles[0], tiles[1]
            held_outer[j - 4] = jnp.where(first_core, zero, one)
        staged(j)[...] = jnp.where(first_core, one, zero)
        if j == 0:
            answer(others(p))
        if j in after:
            after[j]()
    load["qkv"]().start()
    sums[...] = sums_in[...]
    load["att"]().wait()
    load["bg"]().wait()
    go[...] = mm(att[...], bg[...], TN).astype(BF).reshape(4, 2, 1, TR, D)
    jobs[6].send()
    load["qkv"]().wait()
    load["dos"]().wait()
    steps = {
        1: lambda: (jobs[0].turn(), jobs[1].relay(1), jobs[3].relay(1), begin(4), begin(5),),
        2: lambda: (begin(6),),
        3: lambda: (jobs[7].send(), jobs[2].relay(1), jobs[0].relay(2), jobs[3].turn(),),
        5: lambda: (jobs[5].relay(1),),
        6: lambda: (begin(7),),
        7: lambda: (jobs[8].send(), jobs[1].turn(),),
        8: lambda: (jobs[6].relay(1),),
    }

    def one(i, _):
        slot = lax.rem(i, 2)

        @pl.when(i + 1 < n)
        def _():
            in_copy(i + 1, 1 - slot).start()

        in_copy(i, slot).wait()
        attend_back(i, qkv, dos, att, ebuf.at[slot], dqkv)

        @pl.when(lax.rem(i, 4) == 3)
        def _():
            chunk_grads(lax.div(i, 4), x, dqkv, gx, sums)

        for k, step in steps.items():
            @pl.when(i == k)
            def _(step=step):
                step()
        return 0

    lax.fori_loop(0, n, one, 0)
    jobs[9].send()
    jobs[5].turn()
    jobs[7].relay(1)
    begin(8)
    jobs[4].relay(1)
    jobs[6].turn()
    staged_names = [(k, "c") for k, job in enumerate(JOBS) if 4 <= job[0] < 8] + [("o", j) for j in range(4)]
    for name in staged_names:
        net.copy(name).wait_send()
        net.sent.add(name)
    load["fa"]().start()

    for s in range(8):
        vt[s // 2, s % 2] = jnp.zeros((16, 128), F32)
        vt[s // 2, s % 2, 0:8, 0:TR] = sums[:, TR * s : TR * (s + 1)]
        for r in range(3):
            vt[s // 2, s % 2, 8 + r : 9 + r] = bsum[0:1, 128 * (3 * s + r) : 128 * (3 * s + r + 1)]
    net.start(("v", "c"))
    load["res"]().wait()

    def back(i):
        at = pl.ds(256 * i, 256)
        total = res[at]
        for c in range(3):
            total = total + mm(dqkv[c, at], fa[c].reshape(D, D), NT)
        out[at] = total.astype(BF)

    load["fa"]().wait()
    back(0)
    jobs[1].relay(2)
    net.wait(("v", "c"))
    vheld[0] = vt[:, p.c] + vrecv[...]
    vplane[p.w] = vheld[0]
    net.start(*[("v", "p", k) for k in range(3)])
    back(1)
    jobs[2].turn()
    back(2)
    jobs[0].share()
    begin(9)
    net.wait(*[("v", "p", k) for k in range(3)])
    vheld[1] = (vplane[0] + vplane[1]) + (vplane[2] + vplane[3])
    vz[p.z] = vheld[1, p.z]
    net.start(*[("v", "z", k) for k in range(1, 4)])
    back(3)
    jobs[3].relay(2)
    jobs[7].turn()
    jobs[8].relay(1)
    jobs[1].share()
    jobs[5].relay(2)
    jobs[2].relay(2)
    jobs[0].pass_on()
    jobs[9].relay(1)
    jobs[8].turn()
    jobs[2].share()
    jobs[4].turn()
    jobs[6].relay(2)
    jobs[1].pass_on()
    jobs[3].share()
    jobs[7].relay(2)
    jobs[9].turn()
    jobs[2].pass_on()
    jobs[5].share()
    jobs[4].relay(2)
    jobs[8].relay(2)
    jobs[6].share()
    jobs[7].share()
    jobs[3].pass_on()
    jobs[9].relay(2)
    jobs[5].pass_on()
    jobs[8].share()
    jobs[6].pass_on()
    jobs[4].share()
    jobs[7].pass_on()
    net.wait(*[("v", "z", k) for k in range(1, 4)])
    ovec[...] = (vz[0] + vz[1]) + (vz[2] + vz[3])
    jobs[9].share()
    jobs[8].pass_on()
    jobs[4].pass_on()
    jobs[9].pass_on()
    for job in jobs:
        job.end()
    net.finish()


def backward(x, qkv, e, att, dos, bg, res, fa, hl, og, ai, sums, bsum):
    t = x.shape[0]
    job_scratch = [pltpu.VMEM(s, BF) for s in ((4, 4, TR, D),) * 2 + ((8, 4, 1, TR, D),) * 2]
    job_scratch += [pltpu.VMEM(s, BF) for _, units, ring_first in JOBS for s in job_shapes(units, ring_first)]
    return pl.pallas_call(
        backward_kernel,
        out_shape=(shape(t, D), shape(12, TR, D), shape(16, 128, dtype=F32)),
        in_specs=[VM] + [ANY] * 10 + [VM, VM],
        out_specs=(VM,) * 3,
        scratch_shapes=[
            pltpu.VMEM((3, t, D), BF),
            pltpu.VMEM((t, D), BF),
            pltpu.VMEM((t, D), BF),
            pltpu.VMEM((t, D), BF),
            pltpu.VMEM((t, D), F32),
            pltpu.VMEM((4, 8, TR, D), BF),
            pltpu.VMEM((3, t, D), BF),
            pltpu.VMEM((3, 4, 2, 1, TR, D), BF),
            pltpu.VMEM((4, 2, 1, TR, D), BF),
            pltpu.VMEM((2, 2, SEQ, SEQ), BF),
            pltpu.VMEM((8, D), F32),
            pltpu.VMEM((4, 2, 16, 128), F32),
            pltpu.VMEM((2, 4, 16, 128), F32),
            pltpu.VMEM((4, 16, 128), F32),
            pltpu.VMEM((4, 4, 16, 128), F32),
            pltpu.VMEM((4, 16, 128), F32),
        ]
        + job_scratch
        + [
            pltpu.SemaphoreType.DMA((REDUCE_COPIES,)),
            pltpu.SemaphoreType.DMA((REDUCE_COPIES,)),
            pltpu.SemaphoreType.DMA((11,)),
            pltpu.SemaphoreType.DMA((2,)),
        ],
        compiler_params=params(collective_id=1, has_side_effects=True),
        name="backward",
    )(x, qkv, e, att, dos, bg, res, fa, hl, og, ai, sums, bsum)


def finish_kernel(result, ovec, inp, y, oq, ok, ov, oo, oi, our, out, y_out, *vectors):
    for c in range(3):
        tile = result[9 + c].astype(F32)
        for part, ref in enumerate((oq, ok, ov)):
            ref[:, c * CW : (c + 1) * CW] = tile[:, part * CW : (part + 1) * CW]
    oo[...] = result[8].astype(F32)
    for q in range(4):
        oi[:, q * D : (q + 1) * D] = result[4 + q].astype(F32)
        our[q] = result[q].astype(F32)
    out[...] = inp[...]
    y_out[...] = y[...]
    for k in range(8):
        vectors[k][...] = ovec[k, 0:TR]
    for r in range(3):
        vectors[8][128 * r : 128 * (r + 1)] = ovec[8 + r]


def finish(result, ovec, inp, y):
    t = inp.shape[0]
    steps = 2
    rows = TR // steps

    def part(*dims):
        at = len(dims) - 2
        return pl.BlockSpec(dims, lambda h: tuple(h if k == at else 0 for k in range(len(dims))))

    def vector(n):
        return pl.BlockSpec((n,), lambda h: (0,))

    *outs, gr, out, y, v0, v1, v2, v3, v4, v5, v6, v7, v8 = pl.pallas_call(
        finish_kernel,
        grid=(steps,),
        out_shape=tuple(shape(TR, D, dtype=F32) for _ in range(4))
        + (shape(TR, FF, dtype=F32), shape(4, TR, D, dtype=F32), shape(t, D), shape(t, D))
        + tuple(shape(TR, dtype=F32) for _ in range(8))
        + (shape(4 * TR, dtype=F32),),
        in_specs=[part(12, rows, D), pl.BlockSpec((16, 128), lambda h: (0, 0)), part(t // steps, D), part(t // steps, D)],
        out_specs=(part(rows, D),) * 4
        + (part(rows, FF), part(4, rows, D), part(t // steps, D), part(t // steps, D))
        + (vector(TR),) * 8
        + (vector(4 * TR),),
        compiler_params=params(),
        name="finish",
    )(result, ovec, inp, y)
    return *outs, gr.reshape(4 * TR, D), out, y, v0, v1, v2, v3, v4, v5, v6, v7, v8


def forward_local_kernel(x, seg, kept, fa, rows, qkv, att, inv, e_out, t1, segt, ebuf, esem):
    turn_ids(seg, segt)
    for c in range(3):
        project(c, x, fa, rows, qkv)
    keep = kept[0]

    def one(i, _):
        c, r, pair = place_of(i)
        attend(i, qkv, seg, segt, keep, att, inv, ebuf)
        copy = pltpu.make_async_copy(ebuf, e_out.at[c, r, pair], esem.at[0])
        copy.start()
        copy.wait()
        return 0

    lax.fori_loop(0, 6 * (x.shape[0] // SEQ), one, 0)
    t1[...] = x[...].astype(F32) + (mm(att[...], fa[3].reshape(D, D)) + rows[2:3])


def forward_local(x, seg, kept, fa, rows):
    t = x.shape[0]
    n = t // SEQ
    return pl.pallas_call(
        forward_local_kernel,
        out_shape=(shape(3, t, D), shape(t, D), shape(t, D, dtype=F32), shape(3, n, 2, 2, SEQ, SEQ), shape(t, D, dtype=F32)),
        in_specs=[VM, VM, SM, VM, VM],
        out_specs=(VM, VM, VM, ANY, VM),
        scratch_shapes=[
            pltpu.VMEM((n, SEQ, 128), F32), pltpu.VMEM((2, SEQ, SEQ), BF), pltpu.SemaphoreType.DMA((1,)),
        ],
        compiler_params=params(),
        name="forward_local",
    )(x, seg, kept, fa, rows)


def ffn_local_kernel(
    t1, grad, rows, binner, kept, inv, fi, fo, fa, y, res, bg, dos, sums, bsum, g, hl, og, act, gp, t2, ob, tile, gsem, block=256
):
    sums[...] = jnp.zeros_like(sums)
    bsum[...] = jnp.zeros_like(bsum)
    t2[...] = t1[...]
    blocks = t1.shape[0] // block

    def first(i, _):
        ffn_inner(i, block, t2, rows, binner, kept[0], fi, hl, act, gp)
        return 0

    def second(i, _):
        wo = fa[3].reshape(D, D)
        ffn_outer(i, block, blocks, t2, grad, rows, kept[0], fi, fo, wo, inv, act, gp, ob, y, bg, dos, og, sums, bsum)
        return 0

    lax.fori_loop(0, blocks, first, 0)
    outer_product(0, block, fo, act, ob)
    lax.fori_loop(0, blocks, second, 0)
    res[...] = t2[...]

    def one(j, _):
        tile[...] = mm(act[j], og[...], TN).astype(BF).reshape(2, 4, TR, D)
        copy = pltpu.make_async_copy(tile, g.at[lax.div(j, 2), pl.ds(2 * lax.rem(j, 2), 2), 0:4], gsem.at[0])
        copy.start()
        copy.wait()
        tile[...] = mm(hl[...], gp[j], TN).astype(BF).reshape(2, 4, TR, D)
        copy = pltpu.make_async_copy(tile, g.at[:, :, 4 + j], gsem.at[0])
        copy.start()
        copy.wait()
        return 0

    lax.fori_loop(0, 4, one, 0)


def ffn_local(t1, grad, rows, binner, kept, inv, fi, fo, fa):
    t = t1.shape[0]
    return pl.pallas_call(
        ffn_local_kernel,
        out_shape=(
            shape(t, D), shape(t, D, dtype=F32), shape(t, D), shape(t, D),
            shape(8, D, dtype=F32), shape(1, FF, dtype=F32), shape(2, 4, 8, TR, D),
        ),
        in_specs=[VM] * 4 + [SM] + [VM] * 4,
        out_specs=(VM,) * 6 + (ANY,),
        scratch_shapes=[
            pltpu.VMEM((t, D), BF), pltpu.VMEM((t, D), BF), pltpu.VMEM((4, t, D), BF), pltpu.VMEM((4, t, D), BF),
            pltpu.VMEM((t, D), F32), pltpu.VMEM((256, D), F32), pltpu.VMEM((2, 4, TR, D), BF),
            pltpu.SemaphoreType.DMA((1,)),
        ],
        compiler_params=params(),
        name="ffn_local",
    )(t1, grad, rows, binner, kept, inv, fi, fo, fa)


def backward_local_kernel(x, qkv, e_in, att, dos, bg, res, fa, sums_in, out, gx, go, sums, dqkv, ebuf, esem):
    sums[...] = sums_in[...]
    go[...] = mm(att[...], bg[...], TN).astype(BF).reshape(4, 2, 1, TR, D)

    def one(i, _):
        c, r, pair = place_of(i)
        copy = pltpu.make_async_copy(e_in.at[c, r, pair], ebuf, esem.at[0])
        copy.start()
        copy.wait()
        attend_back(i, qkv, dos, att, ebuf, dqkv)

        @pl.when(lax.rem(i, 4) == 3)
        def _():
            chunk_grads(lax.div(i, 4), x, dqkv, gx, sums)

        return 0

    lax.fori_loop(0, 6 * (x.shape[0] // SEQ), one, 0)
    input_back(res, dqkv, fa, out)


def backward_local(x, qkv, e, att, dos, bg, res, fa, sums):
    t = x.shape[0]
    return pl.pallas_call(
        backward_local_kernel,
        out_shape=(shape(t, D), shape(3, 4, 2, 1, TR, D), shape(4, 2, 1, TR, D), shape(8, D, dtype=F32)),
        in_specs=[VM, VM, ANY] + [VM] * 6,
        out_specs=(VM,) * 4,
        scratch_shapes=[pltpu.VMEM((3, t, D), BF), pltpu.VMEM((2, SEQ, SEQ), BF), pltpu.SemaphoreType.DMA((1,))],
        compiler_params=params(),
        name="backward_local",
    )(x, qkv, e, att, dos, bg, res, fa, sums)


def gather_lax(wq, wk, wv, wo, wi, wr, eight, b_inner):
    def whole(a):
        return lax.all_gather(a.astype(BF), "shard", axis=0, tiled=True)

    wq, wk, wv, wo, wi, wr = (whole(a) for a in (wq, wk, wv, wo, wi, wr))
    chunks = [jnp.concatenate([a[:, c * CW : (c + 1) * CW] for a in (wq, wk, wv)], axis=1) for c in range(3)]
    fa = jnp.stack(chunks + [wo]).reshape(4, 8, TR, D)
    fi = jnp.stack([wi[:, q * D : (q + 1) * D] for q in range(4)]).reshape(4, 8, TR, D)
    rows = jnp.stack([whole(a) for a in eight]).astype(F32)
    return fa, fi, wr.reshape(8, 4, TR, D), rows, whole(b_inner).astype(F32).reshape(1, FF)


def reduce_lax(g, gx, go, sums, bsum):
    g = g.reshape(8, 8, TR, D)
    gr = g[:, 0:4].reshape(FF, D)
    gi = jnp.concatenate([g[:, 4 + j].reshape(D, D) for j in range(4)], axis=1)
    gx = gx.reshape(3, D, 3, CW)
    squares = [jnp.concatenate([gx[c, :, part] for c in range(3)], axis=1) for part in range(3)]

    def owned(a):
        a = lax.psum_scatter(a.astype(F32), "shard", scatter_dimension=0, tiled=True)
        return lax.psum(a.astype(BF), "width").astype(F32)

    matrices = [owned(a) for a in (*squares, go.reshape(D, D), gi, gr)]
    return matrices, [owned(sums[k]) for k in range(8)] + [owned(bsum[0])]


def body(
    layer_input, segment_ids, group_heads,
    w_query, b_query, w_key, w_value, b_value, w_out, b_out, gain_one, shift_one,
    w_inner, b_inner, w_outer, b_outer, gain_two, shift_two, out_grad,
):
    eight = (b_query, b_value, b_out, gain_one, shift_one, b_outer, gain_two, shift_two)
    weights = (w_query, w_key, w_value, w_out, w_inner, w_outer)
    own_kernels = lax.axis_size("width") == 4 and lax.axis_size("shard") == 8
    if own_kernels:
        sums, bsum, fa, qkv, att, e, y, res, bg, dos, hl, og, ai = forward(
            layer_input, segment_ids, group_heads, *weights, eight, b_inner, out_grad
        )
    else:
        fa, fi, fo, rows, binner = gather_lax(*weights, eight, b_inner)
        qkv, att, inv, e, t1 = forward_local(layer_input, segment_ids, group_heads, fa, rows)
        y, res, bg, dos, sums, bsum, g = ffn_local(t1, out_grad, rows, binner, group_heads, inv, fi, fo, fa)
    if own_kernels:
        input_grad, result, ovec = backward(layer_input, qkv, e, att, dos, bg, res, fa, hl, og, ai, sums, bsum)
        gq, gk, gv, go, gi, gr, input_grad, y, *vectors = finish(result, ovec, input_grad, y)
    else:
        input_grad, gx, go, sums = backward_local(layer_input, qkv, e, att, dos, bg, res, fa[0:3], sums)
        (gq, gk, gv, go, gi, gr), vectors = reduce_lax(g, gx, go, sums, bsum)
    return (
        y, input_grad, gq, vectors[0], gk, gv, vectors[1], go, vectors[2],
        vectors[3], vectors[4], gi, vectors[8], gr, vectors[5], vectors[6], vectors[7],
    )


def solution(mesh):
    placed = (
        P(("width", "shard"), None),
        P(("width", "shard"), None),
        P("width"),
        P("shard", None),
        P("shard"),
        P("shard", None),
        P("shard", None),
        P("shard"),
        P("shard", None),
        P("shard"),
        P("shard"),
        P("shard"),
        P("shard", None),
        P("shard"),
        P("shard", None),
        P("shard"),
        P("shard"),
        P("shard"),
        P(("width", "shard"), None),
    )
    return jax.shard_map(
        body,
        mesh=mesh,
        in_specs=placed,
        out_specs=(
            P(("width", "shard"), None),
            P(("width", "shard"), None),
            P("shard", None),
            P("shard"),
            P("shard", None),
            P("shard", None),
            P("shard"),
            P("shard", None),
            P("shard"),
            P("shard"),
            P("shard"),
            P("shard", None),
            P("shard"),
            P("shard", None),
            P("shard"),
            P("shard"),
            P("shard"),
        ),
        check_vma=False,
    )
```

```python
import functools
import jax
import jax.numpy as jnp
from jax import lax
from jax.experimental import pallas as pl
from jax.experimental.pallas import tpu as pltpu
from jax.sharding import PartitionSpec as P

HEADS = 12
HEAD_DIM = 64
FF = 3072
D = 768
SEQ = 512
MESH = pl.DeviceIdType.MESH
BF = jnp.bfloat16
F32 = jnp.float32
TR = 96
CW = 256
NT = (((1,), (1,)), ((), ()))
TN = (((0,), (0,)), ((), ()))
NN = (((1,), (0,)), ((), ()))
EPS = 1e-06
RSQRT2 = 0.7071067811865476
RSQRT2PI = 0.3989422804014327
VM = pl.BlockSpec(memory_space=pltpu.VMEM)
SM = pl.BlockSpec(memory_space=pltpu.SMEM)
ANY = pl.BlockSpec(memory_space=pl.ANY)


def params(**more):
    return pltpu.CompilerParams(vmem_limit_bytes=62 << 20, **more)


def shape(*dims, dtype=BF):
    return jax.ShapeDtypeStruct(dims, dtype)


class Place:
    def __init__(self):
        self.w = w = lax.axis_index("width")
        self.s = s = lax.axis_index("shard")
        self.c = c = lax.rem(s, 2)
        self.z = lax.div(s, 2)
        xw, yw = w + 1 - 2 * lax.rem(w, 2), lax.rem(w + 2, 4)
        up, down = lax.rem(s + 2, 8), lax.rem(s + 6, 8)
        self.wa = jnp.where(c == 0, xw, yw)
        self.wb = jnp.where(c == 0, yw, xw)
        self.wd = 3 - w
        self.sa = jnp.where(c == 0, up, down)
        self.sb = jnp.where(c == 0, down, up)
        self.so = lax.rem(s + 4, 8)
        self.sib = (w, s + 1 - 2 * c)
        self.plane_a, self.plane_b = (self.wa, s), (self.wb, s)
        self.ring_a, self.ring_b = (w, self.sa), (w, self.sb)


def call(devices):
    barrier = pltpu.get_barrier_semaphore()
    for device in devices:
        pl.semaphore_signal(barrier, inc=1, device_id=device, device_id_type=MESH)


def answer(devices):
    pl.semaphore_wait(pltpu.get_barrier_semaphore(), len(devices))


def others(p):
    return [(p.wa, p.s), (p.wb, p.s), (p.wd, p.s)] + [(p.w, lax.rem(p.s + k, 8)) for k in range(1, 8)]


class Net:
    def __init__(self, send, recv):
        self.send, self.recv, self.made, self.sent = send, recv, {}, set()

    def define(self, name, make):
        assert name not in self.made
        self.made[name] = (len(self.made), make)

    def copy(self, name):
        k, make = self.made[name]
        src, dst, device = make()
        return pltpu.make_async_remote_copy(
            src_ref=src, dst_ref=dst, send_sem=self.send.at[k], recv_sem=self.recv.at[k],
            device_id=device, device_id_type=MESH,
        )

    def start(self, *names):
        for name in names:
            self.copy(name).start()

    def wait(self, *names):
        for name in names:
            self.copy(name).wait_recv()

    def finish(self):
        for name in self.made:
            if name not in self.sent:
                self.copy(name).wait_send()


def quarter(w):
    return pl.ds(pl.multiple_of(48 * lax.rem(w, 2), 48), 48), pl.ds(pl.multiple_of(384 * lax.div(w, 2), 384), 384)


def mm(a, b, dims=NN):
    return lax.dot_general(a, b, dims, preferred_element_type=F32)


def rows_of(i, size):
    return pl.ds(pl.multiple_of(i * size, size), size)


def column_mask(kept, shape, width):
    return jnp.where(lax.broadcasted_iota(jnp.int32, shape, 1) < kept * width, 1.0, 0.0).astype(F32)


def mean_of(v):
    return jnp.sum(v, axis=1, keepdims=True) * (1.0 / D)


def norm_rows(total):
    centered = total - mean_of(total)
    inverse = lax.rsqrt(mean_of(centered * centered) + EPS)
    return centered * inverse, inverse


def norm_back(grad, normed, inverse):
    return inverse * (grad - mean_of(grad) - normed * mean_of(grad * normed))


def low_lanes(n):
    return lax.broadcasted_iota(jnp.int32, (n, 128), 1) < HEAD_DIM


def place_of(i):
    return lax.div(i, 4), lax.rem(i, 2), lax.rem(lax.div(i, 2), 2)


def pair_lanes(pair, part):
    return pl.ds(pl.multiple_of(part * CW + pair * 128, 128), 128)


def project(c, x, fa, rows, qkv, block=256):
    lanes = pl.ds(pl.multiple_of(c * CW, CW), CW)
    bias = jnp.concatenate([rows[0:1, lanes], jnp.zeros((1, CW), F32), rows[1:2, lanes]], axis=1)
    scale = jnp.where(lax.broadcasted_iota(jnp.int32, (1, D), 1) < CW, 0.125, 1.0)

    def one(i, _):
        at = rows_of(i, block)
        qkv[c, at] = ((mm(x[at], fa[c].reshape(D, D)) + bias) * scale).astype(BF)
        return 0

    lax.fori_loop(0, x.shape[0] // block, one, 0)


def turn_ids(seg, segt):
    for r in range(seg.shape[0]):
        row = seg[r : r + 1, :].astype(F32)
        segt[r] = jnp.broadcast_to(row, (128, SEQ)).T


def attend(i, qkv, seg, segt, kept, att, inv, ebuf, qb=512):
    c, r, pair = place_of(i)
    base = r * SEQ
    rows = pl.ds(pl.multiple_of(base, SEQ), SEQ)
    kp, vp = qkv[c, rows, pair_lanes(pair, 1)], qkv[c, rows, pair_lanes(pair, 2)]
    low = low_lanes(SEQ)
    ones = jnp.ones_like(vp)
    vs = (jnp.where(low, vp, ones), jnp.where(low, ones, vp))
    ids = seg[pl.ds(r, 1), :].astype(F32)
    lowq = low_lanes(qb)
    lanes = pl.ds(pl.multiple_of(c * CW + pair * 128, 128), 128)
    column = lax.broadcasted_iota(jnp.int32, (1, 128), 1) + (c * CW + pair * 128)
    mask = jnp.where(column < kept * HEAD_DIM, 1.0, 0.0).astype(F32)
    for b in range(SEQ // qb):
        at = pl.ds(pl.multiple_of(base + b * qb, qb), qb)
        qp = qkv[c, at, pair_lanes(pair, 0)]
        zero = jnp.zeros_like(qp)
        own = segt[r, b * qb : (b + 1) * qb]
        same = jnp.concatenate([own == ids[:, j * 128 : (j + 1) * 128] for j in range(4)], axis=1)
        out = []
        for h in range(2):
            qh = jnp.where(lowq, qp, zero) if h == 0 else jnp.where(lowq, zero, qp)
            scores = jnp.where(same, mm(qh, kp, NT), -1e30)
            top = jnp.max(scores, axis=1, keepdims=True)
            e = jnp.exp(scores - top).astype(BF)
            ebuf[h, b * qb : (b + 1) * qb] = e
            out.append(mm(e, vs[h]))
        inverse = 1.0 / pltpu.roll(jnp.where(lowq, out[1], out[0]), HEAD_DIM, 1)
        att[at, lanes] = (jnp.where(lowq, out[0], out[1]) * (inverse * mask)).astype(BF)
        inv[at, lanes] = inverse


def expand_vectors(fv, rows, binner):
    lane = lax.broadcasted_iota(jnp.int32, (128, D), 0)
    column = lax.broadcasted_iota(jnp.int32, (128, D), 1)
    total = jnp.zeros((16, D), F32)
    for s in range(8):
        pick = jnp.where((column == lane + TR * s) & (lane < TR), 1.0, 0.0).astype(BF)
        total = total + mm(fv[s], pick)
        tile = fv[s].astype(F32)
        for r in range(3):
            binner[0:1, 128 * (3 * s + r) : 128 * (3 * s + r + 1)] = tile[8 + r : 9 + r]
    rows[...] = total[0:8]


GROUPS = (slice(0, 1), slice(1, 2), slice(2, 3), slice(3, 4), slice(4, 8), slice(8, 12))
WO, INNER, OUTER = 3, 4, 5
GATHER_COPIES = 16 * len(GROUPS) + 7


def gather_net(p, own, fa, fi, fo, vec, fv, ssem, rsem):
    net = Net(ssem, rsem)
    every = (slice(None), slice(None))

    def piece(g, s, part):
        if g <= WO:
            return fa.at[(GROUPS[g], s, *part)]
        return fi.at[(slice(None), s, *part)] if g == INNER else fo.at[(s, slice(None), *part)]

    mine, first = quarter(p.w), quarter(p.wa)
    for g in range(len(GROUPS)):

        def add(name, src, dst, device):
            net.define((g, *name), lambda: (src(), dst(), device))

        def same(name, g, s, part, device):
            add(name, lambda: piece(g, s, part), lambda: piece(g, s, part), device)

        for name, device in (("zb", p.ring_a), ("za", p.ring_b)):
            add((name,), lambda g=g: own.at[(GROUPS[g], *mine)], lambda g=g: piece(g, p.s, mine), device)
        same(("zo",), g, p.sb, mine, p.ring_a)
        add(("own", "c"), lambda g=g: own.at[GROUPS[g]], lambda g=g: piece(g, p.s, every), p.sib)
        for name, s in (("zb", p.sb), ("za", p.sa), ("zo", p.so)):
            same((name, "xa"), g, s, mine, p.plane_a)
            same((name, "xb"), g, s, mine, p.plane_b)
            same((name, "xd"), g, s, first, p.plane_b)
            same((name, "c"), g, s, every, p.sib)
    for k in range(1, 8):
        net.define(("v", k), lambda k=k: (vec, fv.at[p.s], (p.w, lax.rem(p.s + k, 8))))
    assert len(net.made) == GATHER_COPIES
    return net


def ffn_inner(i, block, t1, rows, binner, kept, wi, hl, act, gp):
    at = rows_of(i, block)
    n1, _ = norm_rows(t1[at])
    low = (n1 * rows[3:4] + rows[4:5]).astype(BF)
    hl[at] = low
    for j in range(4):
        inner = mm(low, wi[j].reshape(D, D)) + binner[:, j * D : (j + 1) * D]
        keep = column_mask(kept * 256 - j * D, (1, D), 1)
        phi = 0.5 + 0.5 * lax.erf(inner * RSQRT2)
        masked = inner * keep
        act[j, at] = (masked * phi).astype(BF)
        gp[j, at] = (keep * phi + masked * (RSQRT2PI * jnp.exp(-0.5 * (inner * inner)))).astype(BF)


def outer_product(i, block, wr, act, ob):
    at = rows_of(i, block)
    outer = jnp.zeros((block, D), F32)
    for j in range(4):
        outer = outer + mm(act[j, at], wr[2 * j : 2 * j + 2].reshape(D, D))
    ob[...] = outer


def ffn_outer(i, block, blocks, t1, grad, rows, kept, wi, wr, wo, inv, act, gp, ob, y, bg, dos, og, sums, bsum):
    at = rows_of(i, block)

    def add(k, value):
        sums[k : k + 1] += jnp.sum(value, axis=0, keepdims=True)

    def outer_weight(j):
        return wr[2 * j : 2 * j + 2].reshape(D, D)

    n1, inv1 = norm_rows(t1[at])
    hidden = n1 * rows[3:4] + rows[4:5]
    n2, inv2 = norm_rows(hidden + (ob[...] + rows[5:6]))
    outer_product(jnp.minimum(i + 1, blocks - 1), block, wr, act, ob)
    y[at] = (n2 * rows[6:7] + rows[7:8]).astype(BF)
    top = grad[at].astype(F32)
    add(7, top)
    add(6, top * n2)
    res2 = norm_back(top * rows[6:7], n2, inv2)
    o = res2.astype(BF)
    og[at] = o
    add(5, o.astype(F32))
    hg = res2
    for j in range(4):
        cols = slice(j * D, (j + 1) * D)
        g = (mm(o, outer_weight(j), NT) * gp[j, at].astype(F32)).astype(BF)
        gp[j, at] = g
        bsum[:, cols] += jnp.sum(g.astype(F32), axis=0, keepdims=True)
        hg = hg + mm(g, wi[j].reshape(D, D), NT)
    add(4, hg)
    add(3, hg * n1)
    res1 = norm_back(hg * rows[3:4], n1, inv1)
    t1[at] = res1
    b = res1.astype(BF)
    bg[at] = b
    add(2, b.astype(F32))
    heads = column_mask(kept, (1, D), HEAD_DIM)
    dos[at] = (mm(b, wo, NT) * (inv[at] * heads)).astype(BF)


def forward_kernel(
    x_in, seg, kept, wq_in, wk_in, wv_in, wo_in, wi_in, wr_in, v0, v1, v2, v3, v4, v5, v6, v7, v_inner, grad_in,
    sums, bsum, fa_out, qkv_out, att_out, e_out, y_out, res_out, bg_out, dos_out, hl_out, og_out, ai_out,
    own, vtile, vec, fa, fi, fo, fv, rows, binner, att, inv, t1, segt, ebuf, grad, y, bg, dos, hl, og, act, gp, ob,
    x, wq, wk, wv, wo, wi, wr, ssem, rsem, lsem, esem, fsem, isem,
):
    qkv = gp.at[0:3]
    p = Place()
    call(others(p))
    arriving = [
        pltpu.make_async_copy(src, dst, isem.at[k])
        for k, (src, dst) in enumerate(
            ((wq_in, wq), (wk_in, wk), (wv_in, wv), (wo_in, wo), (wi_in, wi), (wr_in, wr), (x_in, x))
        )
    ]
    for copy in arriving:
        copy.start()

    def cast(c):
        for part, ref in enumerate((wq, wk, wv)):
            own[c, :, part * CW : (part + 1) * CW] = ref[:, c * CW : (c + 1) * CW].astype(BF)

    for copy in arriving[0:3]:
        copy.wait()
    cast(0)
    vtile[...] = jnp.zeros_like(vtile)
    for k, ref in enumerate((v0, v1, v2, v3, v4, v5, v6, v7)):
        vtile[k : k + 1, 0:TR] = ref[...]
    for r in range(3):
        vtile[8 + r : 9 + r] = v_inner[128 * r : 128 * (r + 1)].reshape(1, 128)
    vec[...] = vtile[...].astype(BF)
    answer(others(p))
    net = gather_net(p, own, fa, fi, fo, vec, fv, ssem, rsem)
    names = ("zb", "za", "zo")

    def ring(g):
        net.start((g, "zb"), (g, "za"), (g, "own", "c"))

    def onward(g):
        net.wait((g, "zb"))
        net.start((g, "zo"))

    def plane(g, *which):
        for name in which or names:
            if name != "zb":
                net.wait((g, name))
            net.start((g, name, "xa"), (g, name, "xb"))

    def relay(g, *which):
        for name in which or names:
            net.wait((g, name, "xa"))
            net.start((g, name, "xd"))

    def share(g, *which):
        for name in which or names:
            net.wait((g, name, "xb"), (g, name, "xd"))
            net.start((g, name, "c"))

    def landed(g):
        net.wait((g, "own", "c"), *[(g, name, "c") for name in names])

    ring(0)
    cast(1)
    ring(1)
    cast(2)
    for copy in arriving[3:]:
        copy.wait()
    own[3] = wo[...].astype(BF)
    for q in range(4):
        own[4 + q] = wi[:, q * D : (q + 1) * D].astype(BF)
        own[8 + q] = wr[q * TR : (q + 1) * TR, :].astype(BF)
    net.start(*[("v", k) for k in range(1, 8)])
    local = {}

    def put(name, k, src, dst):
        local[name] = lambda: pltpu.make_async_copy(src(), dst(), lsem.at[k])

    pieces = (
        ("own a", lambda: own.at[0:4], lambda: fa.at[:, p.s]),
        ("own i", lambda: own.at[4:8], lambda: fi.at[:, p.s]),
        ("own o", lambda: own.at[8:12], lambda: fo.at[p.s]),
        ("vec", lambda: vec, lambda: fv.at[p.s]),
        ("grad", lambda: grad_in, lambda: grad),
        ("qkv", lambda: qkv, lambda: qkv_out),
        ("fa", lambda: fa.at[0:3], lambda: fa_out),
        ("att", lambda: att, lambda: att_out),
        ("hl", lambda: hl, lambda: hl_out),
        ("act", lambda: act, lambda: ai_out.at[0:4]),
    )
    for k, (name, src, dst) in enumerate(pieces):
        put(name, k, src, dst)
    for name in ("own a", "own i", "own o", "vec", "grad"):
        local[name]().start()

    onward(0)
    plane(0, "zb", "za")
    onward(1)
    ring(2)
    plane(1, "zb", "za")
    plane(0, "zo")
    turn_ids(seg, segt)
    relay(0, "zb", "za")
    plane(1, "zo")
    relay(1, "zb")
    onward(2)
    ring(INNER)
    relay(1, "za")
    plane(2, "zb", "za")
    relay(0, "zo")
    share(0, "zb", "za")
    relay(1, "zo")
    share(1, "zb")
    plane(2, "zo")
    share(1, "za")
    relay(2, "zb", "za")
    share(0, "zo")
    onward(INNER)
    ring(WO)
    share(1, "zo")
    plane(INNER, "zb")
    relay(2, "zo")
    net.wait(*[("v", k) for k in range(1, 8)])
    local["vec"]().wait()
    expand_vectors(fv, rows, binner)
    share(2, "zb", "za")
    plane(INNER, "za")
    local["own a"]().wait()
    keep = kept[0]

    def out_copy(i, slot):
        c, r, pair = place_of(i)
        return pltpu.make_async_copy(ebuf.at[slot], e_out.at[c, r, pair], esem.at[slot])

    before = {0: lambda: landed(0), 4: lambda: landed(1), 8: lambda: landed(2)}
    steps = {
        1: lambda: (plane(INNER, "zo"), relay(INNER, "zb"), onward(WO), ring(OUTER), share(2, "zo"), plane(WO, "zb", "za"),),
        2: lambda: (relay(INNER, "za"),),
        4: lambda: (relay(INNER, "zo"), plane(WO, "zo"), relay(WO, "zb"),),
        5: lambda: (relay(WO, "za"), onward(OUTER), plane(OUTER, "zb"),),
        6: lambda: (share(INNER, "zb"),),
        7: lambda: (relay(WO, "zo"), plane(OUTER, "za"),),
        8: lambda: (share(INNER, "za"),),
        9: lambda: (share(INNER, "zo"), relay(OUTER, "zb"), plane(OUTER, "zo"),),
        10: lambda: (share(WO, "zb", "za"),),
        11: lambda: (relay(OUTER, "za"), share(WO, "zo"), relay(OUTER, "zo"),),
    }
    later = {
        1: lambda: (share(OUTER, "za", "zo"),),
    }

    def after_residual():
        share(OUTER, "zb")

    def at_step(i, table):
        for k, step in table.items():
            @pl.when(i == k)
            def _(step=step):
                step()

    def one(i, _):
        slot = lax.rem(i, 2)

        @pl.when(i >= 2)
        def _():
            out_copy(i - 2, slot).wait()

        at_step(i, before)

        @pl.when(lax.rem(i, 4) == 0)
        def _():
            project(lax.div(i, 4), x, fa, rows, qkv)

        attend(i, qkv, seg, segt, keep, att, inv, ebuf.at[slot])
        out_copy(i, slot).start()
        at_step(i, steps)
        return 0

    n = 6 * (x.shape[0] // SEQ)
    lax.fori_loop(0, n, one, 0)
    local["qkv"]().start()
    local["att"]().start()
    local["fa"]().start()
    sums[...] = jnp.zeros_like(sums)
    bsum[...] = jnp.zeros_like(bsum)
    landed(WO)
    block = 256
    blocks = x.shape[0] // block

    def residual(i, _):
        at = rows_of(i, block)
        t1[at] = x[at].astype(F32) + (mm(att[at], fa[3].reshape(D, D)) + rows[2:3])
        return 0

    lax.fori_loop(0, blocks, residual, 0)
    after_residual()
    landed(INNER)
    local["own i"]().wait()
    local["qkv"]().wait()

    def first(i, _):
        ffn_inner(i, block, t1, rows, binner, keep, fi, hl, act, gp)
        at_step(i, later)
        return 0

    lax.fori_loop(0, blocks, first, 0)
    local["hl"]().start()
    local["act"]().start()
    landed(OUTER)
    local["own o"]().wait()
    local["grad"]().wait()

    def flush(i):
        at = rows_of(i, block)
        pairs = (
            (gp.at[:, at], ai_out.at[4:8, at]), (og.at[at], og_out.at[at]), (dos.at[at], dos_out.at[at]),
            (bg.at[at], bg_out.at[at]), (t1.at[at], res_out.at[at]), (y.at[at], y_out.at[at]),
        )
        return [pltpu.make_async_copy(src, dst, fsem.at[i, k]) for k, (src, dst) in enumerate(pairs)]

    def second(i, _):
        wo = fa[3].reshape(D, D)
        ffn_outer(i, block, blocks, t1, grad, rows, keep, fi, fo, wo, inv, act, gp, ob, y, bg, dos, og, sums, bsum)
        for copy in flush(i):
            copy.start()
        return 0

    outer_product(0, block, fo, act, ob)
    lax.fori_loop(0, blocks, second, 0)
    out_copy(n - 2, (n - 2) % 2).wait()
    out_copy(n - 1, (n - 1) % 2).wait()
    for name in ("fa", "att", "hl", "act"):
        local[name]().wait()
    for i in range(blocks):
        for copy in flush(i):
            copy.wait()
    net.finish()


def forward(x, seg, kept, wq, wk, wv, wo, wi, wr, eight, b_inner, grad):
    t = x.shape[0]
    n = t // SEQ
    return pl.pallas_call(
        forward_kernel,
        out_shape=(
            shape(8, D, dtype=F32), shape(1, FF, dtype=F32), shape(3, 8, TR, D), shape(3, t, D), shape(t, D),
            shape(3, n, 2, 2, SEQ, SEQ), shape(t, D), shape(t, D, dtype=F32), shape(t, D), shape(t, D), shape(t, D),
            shape(t, D), shape(8, t, D),
        ),
        in_specs=[ANY, VM, SM] + [ANY] * 6 + [VM] * 9 + [ANY],
        out_specs=(VM, VM) + (ANY,) * 11,
        scratch_shapes=[
            pltpu.VMEM((12, TR, D), BF),
            pltpu.VMEM((16, 128), F32),
            pltpu.VMEM((16, 128), BF),
            pltpu.VMEM((4, 8, TR, D), BF),
            pltpu.VMEM((4, 8, TR, D), BF),
            pltpu.VMEM((8, 4, TR, D), BF),
            pltpu.VMEM((8, 16, 128), BF),
            pltpu.VMEM((8, D), F32),
            pltpu.VMEM((1, FF), F32),
            pltpu.VMEM((t, D), BF),
            pltpu.VMEM((t, D), F32),
            pltpu.VMEM((t, D), F32),
            pltpu.VMEM((n, SEQ, 128), F32),
            pltpu.VMEM((2, 2, SEQ, SEQ), BF),
        ]
        + [pltpu.VMEM((t, D), BF)] * 6
        + [pltpu.VMEM((4, t, D), BF)] * 2
        + [
            pltpu.VMEM((256, D), F32),
            pltpu.VMEM((t, D), BF),
            *[pltpu.VMEM((TR, D), F32)] * 4,
            pltpu.VMEM((TR, FF), F32),
            pltpu.VMEM((4 * TR, D), F32),
            pltpu.SemaphoreType.DMA((GATHER_COPIES,)),
            pltpu.SemaphoreType.DMA((GATHER_COPIES,)),
            pltpu.SemaphoreType.DMA((10,)),
            pltpu.SemaphoreType.DMA((2,)),
            pltpu.SemaphoreType.DMA((t // 256, 6)),
            pltpu.SemaphoreType.DMA((7,)),
        ],
        compiler_params=params(collective_id=0, has_side_effects=True),
        name="forward",
    )(x, seg, kept, wq, wk, wv, wo, wi, wr, *(a.reshape(1, TR) for a in eight), b_inner, grad)


def attend_back(i, qkv, dos, att, ebuf, dqkv):
    c, r, pair = place_of(i)
    rows = rows_of(r, SEQ)
    lanes = pl.ds(pl.multiple_of(c * CW + pair * 128, 128), 128)
    qp, kp, vp = (qkv[c, rows, pair_lanes(pair, part)] for part in range(3))
    dp = dos[rows, lanes]
    low = low_lanes(SEQ)
    zero = jnp.zeros_like(qp)
    product = dp.astype(F32) * att[rows, lanes].astype(F32)
    gq = jnp.zeros((SEQ, 128), F32)
    gk = jnp.zeros((SEQ, 128), F32)
    gv = jnp.zeros((SEQ, 128), F32)
    for h in range(2):
        mine = low if h == 0 else jnp.logical_not(low)
        dh = jnp.where(mine, dp, zero)
        delta = jnp.sum(jnp.where(mine, product, 0.0), axis=1, keepdims=True)
        e = ebuf[h]
        ds = (e.astype(F32) * (mm(dh, vp, NT) - delta)).astype(BF)
        gv = gv + mm(e, dh, TN)
        gk = gk + mm(ds, jnp.where(mine, qp, zero), TN)
        gq = gq + mm(ds, jnp.where(mine, kp, zero))
    dqkv[c, rows, pair_lanes(pair, 0)] = (gq * 0.125).astype(BF)
    dqkv[c, rows, pair_lanes(pair, 1)] = gk.astype(BF)
    dqkv[c, rows, pair_lanes(pair, 2)] = gv.astype(BF)


def chunk_grads(c, x, dqkv, gx, sums):
    gx[c] = mm(x[...], dqkv[c], TN).astype(BF).reshape(4, 2, 1, TR, D)
    part = dqkv[c].astype(F32)
    total = jnp.sum(part, axis=0, keepdims=True)
    lanes = pl.ds(pl.multiple_of(c * CW, CW), CW)
    sums[0:1, lanes] = total[:, 0:CW]
    sums[1:2, lanes] = total[:, 2 * CW :]


def input_back(res, dqkv, fa, out, block=256):
    def one(i, _):
        at = rows_of(i, block)
        total = res[at]
        for c in range(3):
            total = total + mm(dqkv[c, at], fa[c].reshape(D, D), NT)
        out[at] = total.astype(BF)
        return 0

    lax.fori_loop(0, res.shape[0] // block, one, 0)


JOBS = (
    (4, 1, False),
    (5, 1, True),
    (6, 1, True),
    (7, 1, False),
    (0, 2, True),
    (2, 2, False),
    (8, 1, False),
    (9, 1, False),
    (10, 1, False),
    (11, 1, False),
)
OUTER_UNITS = 4
REDUCE_COPIES = 9 * len(JOBS) + sum(first >= OUTER_UNITS for first, _, _ in JOBS) + 4 + 7


def job_shapes(units, ring_first):
    part, tile = (units, 48, 384), (units, TR, D)
    first = tile if ring_first else (4, *part)
    return [first, first, first, first, part, part, part]


class Job:
    def __init__(self, net, p, k, first, units, ring_first, held, landed, arrivals, bufs, result):
        self.net, self.p, self.k = net, p, k
        self.held, self.landed, self.arrivals = held, landed, arrivals
        self.d1, self.a1, self.b1, self.mid, self.d2, self.a2, self.b2 = bufs
        self.result = result
        self.units = slice(first, first + units)
        held, mid = self.held, self.mid
        z, za, zb, zo = p.z, lax.div(p.sa, 2), lax.div(p.sb, 2), lax.div(p.so, 2)
        self.z = z
        ring = (za, zb, zo, p.ring_a, p.ring_a, p.ring_b)
        plane = (p.wb, p.wa, p.wd, p.plane_a, p.plane_b, p.plane_a)

        def tile(t):
            return held, (t,)

        def plane_quarter(w):
            return held, (slice(None), slice(None), *quarter(w))

        def mid_quarter(w):
            return mid, (slice(None), *quarter(w))

        def mid_tile(t):
            return mid, (t,)

        one, two = (ring, plane) if ring_first else (plane, ring)
        self.at1, self.at2 = (tile, mid_quarter) if ring_first else (plane_quarter, mid_tile)
        self.one, self.two = one, two
        self.own1 = z if ring_first else p.w
        self.own2 = p.w if ring_first else z
        for stage, at, way, d, a, b in ((1, self.at1, one, self.d1, self.a1, self.b1), (2, self.at2, two, self.d2, self.a2, self.b2)):
            relayed, direct, opposite, dev_o, dev_r, dev_d = way

            def send(name, index, dst, device, at=at):
                def make():
                    ref, where = at(index)
                    return ref.at[where], dst, device

                net.define((k, *name), make)

            send(("d", stage), opposite, d, dev_o)
            send(("b", stage), direct, b, dev_d)
            send(("a", stage), relayed, a, dev_r)

        def share(name, w, device):
            def make():
                ref = result.at[(self.units, *quarter(w))]
                return ref, ref, device

            net.define((k, name), make)

        share("ga", p.w, p.plane_a)
        share("gb", p.w, p.plane_b)
        share("gd", p.wa, p.plane_b)

    def names(self, names):
        return [(self.k, *name) if isinstance(name, tuple) else (self.k, name) for name in names]

    def start(self, *names):
        self.net.start(*self.names(names))

    def wait(self, *names):
        self.net.wait(*self.names(names))

    def send(self):
        self.net.start(*self.arrivals)

    def pair(self):
        self.net.wait(*self.arrivals)
        held, landed = self.held, self.landed

        def one(t, _):
            held[t] = (held[t].astype(F32) + landed[t].astype(F32)).astype(BF)
            return 0

        lax.fori_loop(0, 4, one, 0)
        self.start(("d", 1), ("b", 1))

    def relay(self, stage):
        at, way, d = (self.at1, self.one, self.d1) if stage == 1 else (self.at2, self.two, self.d2)
        self.wait(("d", stage))
        ref, where = at(way[0])
        ref[where] = (ref[where].astype(F32) + d[...].astype(F32)).astype(BF)
        self.start(("a", stage))

    def total(self, stage):
        at, own, a, b = (self.at1, self.own1, self.a1, self.b1) if stage == 1 else (self.at2, self.own2, self.a2, self.b2)
        self.wait(("a", stage), ("b", stage))
        ref, where = at(own)
        return (ref[where].astype(F32) + a[...].astype(F32) + b[...].astype(F32)).astype(BF)

    def turn(self):
        self.mid[...] = self.total(1)
        self.start(("d", 2), ("b", 2))

    def share(self):
        self.result[(self.units, *quarter(self.p.w))] = self.total(2)
        self.start("ga", "gb")

    def pass_on(self):
        self.wait("ga")
        self.start("gd")

    def end(self):
        self.wait("gb", "gd")


def backward_kernel(
    x_in, qkv_in, e_in, att_in, dos_in, bg_in, res_in, fa_in, hl_in, og_in, ai_in, sums_in, bsum,
    out, result, ovec,
    x, qkv, att, dos, bg, res, fa, dqkv, gx, go, ebuf, sums, vt, vheld, vrecv, vplane, vz, *rest,
):
    bufs, (ssem, rsem, lsem, esem) = rest[:-4], rest[-4:]
    p = Place()
    call(others(p))
    n = 6 * (x.shape[0] // SEQ)
    og, hl = dqkv.at[0], dqkv.at[1]
    loads = (
        ("og", lambda: og_in, lambda: og),
        ("hl", lambda: hl_in, lambda: hl),
        ("att", lambda: att_in, lambda: att),
        ("bg", lambda: bg_in, lambda: bg),
        ("qkv", lambda: qkv_in, lambda: qkv),
        ("dos", lambda: dos_in, lambda: dos),
        ("res", lambda: res_in, lambda: res),
        ("fa", lambda: fa_in, lambda: fa.at[0:3]),
        ("x", lambda: x_in, lambda: x),
    )
    load = {
        name: lambda k=k, src=src, dst=dst: pltpu.make_async_copy(src(), dst(), lsem.at[k])
        for k, (name, src, dst) in enumerate(loads)
    }

    def block_copy(j):
        return pltpu.make_async_copy(ai_in.at[(j + 4) % 8], qkv.at[j % 3], lsem.at[len(loads) + j % 3])

    def in_copy(i, slot):
        c, r, pair = place_of(i)
        return pltpu.make_async_copy(e_in.at[c, r, pair], ebuf.at[slot], esem.at[slot])

    load["hl"]().start()
    block_copy(0).start()
    block_copy(1).start()
    load["og"]().start()
    for name in ("att", "bg", "dos"):
        load[name]().start()
    in_copy(0, 0).start()
    load["res"]().start()
    load["x"]().start()

    def staged(j):
        return fa.at[j // 2, 4 * (j % 2) : 4 * (j % 2) + 4]

    net = Net(ssem, rsem)
    held_outer, landed_outer, held_rest, landed_rest = bufs[0:4]
    jobs = []
    per = 7
    outer_arrivals = [("o", j) for j in range(4)]
    for j in range(4):
        net.define(("o", j), lambda j=j: (staged(4 + j), landed_outer.at[j], p.sib))
    for k, (first, units, ring_first) in enumerate(JOBS):
        if first < OUTER_UNITS:
            held, landed = held_outer.at[:, first : first + units], landed_outer.at[:, first : first + units]
            arrivals = outer_arrivals
            outer_arrivals = []
        else:
            r = first - OUTER_UNITS
            held, landed = held_rest.at[r], landed_rest.at[r]
            arrivals = [(k, "c")]
            if r < 4:
                source = lambda r=r: staged(r)
            elif r == 4:
                source = lambda: go.at[:, 1 - p.c, 0]
            else:
                source = lambda c=r - 5: gx.at[c, :, 1 - p.c, 0]
            net.define((k, "c"), lambda source=source, landed=landed: (source(), landed.at[:, 0], p.sib))
        job_bufs = bufs[4 + per * k : 4 + per * (k + 1)]
        jobs.append(Job(net, p, k, first, units, ring_first, held, landed, arrivals, job_bufs, result))
    net.define(("v", "c"), lambda: (vt.at[:, 1 - p.c], vrecv, p.sib))
    for k, device in enumerate((p.plane_a, p.plane_b, (p.wd, p.s))):
        net.define(("v", "p", k), lambda device=device: (vheld.at[0], vplane.at[p.w], device))
    for k in range(1, 4):
        to = lax.rem(p.z + k, 4)
        net.define(("v", "z", k), lambda to=to: (vheld.at[1, to], vz.at[p.z], (p.w, 2 * to + p.c)))
    assert len(net.made) == REDUCE_COPIES, len(net.made)

    def own_half(k, source):
        jobs[k].held[...] = source[:, p.c]

    def begin(k):
        first = JOBS[k][0]
        if first == 8:
            own_half(k, go)
        elif first > 8:
            own_half(k, gx.at[first - 9])
        jobs[k].pair()

    first_core = p.c == 0
    after = {
        0: lambda: (jobs[0].send(),),
        1: lambda: (jobs[1].send(),),
        2: lambda: (jobs[2].send(),),
        3: lambda: (jobs[3].send(), begin(0),),
        4: lambda: (net.start(("o", 0)), begin(1),),
        5: lambda: (net.start(("o", 1)), begin(2),),
        6: lambda: (net.start(("o", 2)), jobs[0].relay(1), begin(3),),
        7: lambda: (net.start(("o", 3)),),
    }
    for j in range(8):
        if j == 0:
            load["hl"]().wait()
        if j == 4:
            load["og"]().wait()
        if j + 2 < 8:
            block_copy(j + 2).start()
        block_copy(j).wait()
        block = qkv.at[j % 3]
        if j < 4:
            tiles = mm(hl[...], block[...], TN).astype(BF).reshape(4, 2, TR, D)
            zero, one = tiles[:, 0], tiles[:, 1]
            held_rest[j, :, 0] = jnp.where(first_core, zero, one)
        else:
            tiles = mm(block[...], og[...], TN).astype(BF).reshape(2, 4, TR, D)
            zero, one = tiles[0], tiles[1]
            held_outer[j - 4] = jnp.where(first_core, zero, one)
        staged(j)[...] = jnp.where(first_core, one, zero)
        if j == 0:
            answer(others(p))
        if j in after:
            after[j]()
    load["qkv"]().start()
    sums[...] = sums_in[...]
    load["att"]().wait()
    load["bg"]().wait()
    go[...] = mm(att[...], bg[...], TN).astype(BF).reshape(4, 2, 1, TR, D)
    jobs[6].send()
    load["qkv"]().wait()
    load["dos"]().wait()
    load["x"]().wait()
    steps = {
        1: lambda: (jobs[0].turn(), jobs[1].relay(1), jobs[3].relay(1), begin(4), begin(5),),
        2: lambda: (begin(6),),
        3: lambda: (jobs[7].send(), jobs[2].relay(1), jobs[0].relay(2), jobs[3].turn(),),
        5: lambda: (jobs[5].relay(1),),
        6: lambda: (begin(7),),
        7: lambda: (jobs[8].send(), jobs[1].turn(),),
        8: lambda: (jobs[6].relay(1),),
    }

    def one(i, _):
        slot = lax.rem(i, 2)

        @pl.when(i + 1 < n)
        def _():
            in_copy(i + 1, 1 - slot).start()

        in_copy(i, slot).wait()
        attend_back(i, qkv, dos, att, ebuf.at[slot], dqkv)

        @pl.when(lax.rem(i, 4) == 3)
        def _():
            chunk_grads(lax.div(i, 4), x, dqkv, gx, sums)

        for k, step in steps.items():
            @pl.when(i == k)
            def _(step=step):
                step()
        return 0

    lax.fori_loop(0, n, one, 0)
    jobs[9].send()
    jobs[5].turn()
    jobs[7].relay(1)
    begin(8)
    jobs[4].relay(1)
    jobs[6].turn()
    staged_names = [(k, "c") for k, job in enumerate(JOBS) if 4 <= job[0] < 8] + [("o", j) for j in range(4)]
    for name in staged_names:
        net.copy(name).wait_send()
        net.sent.add(name)
    load["fa"]().start()

    for s in range(8):
        vt[s // 2, s % 2] = jnp.zeros((16, 128), F32)
        vt[s // 2, s % 2, 0:8, 0:TR] = sums[:, TR * s : TR * (s + 1)]
        for r in range(3):
            vt[s // 2, s % 2, 8 + r : 9 + r] = bsum[0:1, 128 * (3 * s + r) : 128 * (3 * s + r + 1)]
    net.start(("v", "c"))
    load["res"]().wait()

    def back(i):
        at = pl.ds(256 * i, 256)
        total = res[at]
        for c in range(3):
            total = total + mm(dqkv[c, at], fa[c].reshape(D, D), NT)
        out[at] = total.astype(BF)

    load["fa"]().wait()
    back(0)
    jobs[1].relay(2)
    net.wait(("v", "c"))
    vheld[0] = vt[:, p.c] + vrecv[...]
    vplane[p.w] = vheld[0]
    net.start(*[("v", "p", k) for k in range(3)])
    back(1)
    jobs[2].turn()
    back(2)
    jobs[0].share()
    begin(9)
    net.wait(*[("v", "p", k) for k in range(3)])
    vheld[1] = (vplane[0] + vplane[1]) + (vplane[2] + vplane[3])
    vz[p.z] = vheld[1, p.z]
    net.start(*[("v", "z", k) for k in range(1, 4)])
    back(3)
    jobs[3].relay(2)
    jobs[7].turn()
    jobs[8].relay(1)
    jobs[1].share()
    jobs[5].relay(2)
    jobs[2].relay(2)
    jobs[0].pass_on()
    jobs[9].relay(1)
    jobs[8].turn()
    jobs[2].share()
    jobs[4].turn()
    jobs[6].relay(2)
    jobs[1].pass_on()
    jobs[3].share()
    jobs[7].relay(2)
    jobs[9].turn()
    jobs[2].pass_on()
    jobs[5].share()
    jobs[4].relay(2)
    jobs[8].relay(2)
    jobs[6].share()
    jobs[7].share()
    jobs[3].pass_on()
    jobs[9].relay(2)
    jobs[5].pass_on()
    jobs[8].share()
    jobs[6].pass_on()
    jobs[4].share()
    jobs[7].pass_on()
    net.wait(*[("v", "z", k) for k in range(1, 4)])
    ovec[...] = (vz[0] + vz[1]) + (vz[2] + vz[3])
    jobs[9].share()
    jobs[8].pass_on()
    jobs[4].pass_on()
    jobs[9].pass_on()
    for job in jobs:
        job.end()
    net.finish()


def backward(x, qkv, e, att, dos, bg, res, fa, hl, og, ai, sums, bsum):
    t = x.shape[0]
    job_scratch = [pltpu.VMEM(s, BF) for s in ((4, 4, TR, D),) * 2 + ((8, 4, 1, TR, D),) * 2]
    job_scratch += [pltpu.VMEM(s, BF) for _, units, ring_first in JOBS for s in job_shapes(units, ring_first)]
    return pl.pallas_call(
        backward_kernel,
        out_shape=(shape(t, D), shape(12, TR, D), shape(16, 128, dtype=F32)),
        in_specs=[ANY] * 11 + [VM, VM],
        out_specs=(VM,) * 3,
        scratch_shapes=[
            pltpu.VMEM((t, D), BF),
            pltpu.VMEM((3, t, D), BF),
            pltpu.VMEM((t, D), BF),
            pltpu.VMEM((t, D), BF),
            pltpu.VMEM((t, D), BF),
            pltpu.VMEM((t, D), F32),
            pltpu.VMEM((4, 8, TR, D), BF),
            pltpu.VMEM((3, t, D), BF),
            pltpu.VMEM((3, 4, 2, 1, TR, D), BF),
            pltpu.VMEM((4, 2, 1, TR, D), BF),
            pltpu.VMEM((2, 2, SEQ, SEQ), BF),
            pltpu.VMEM((8, D), F32),
            pltpu.VMEM((4, 2, 16, 128), F32),
            pltpu.VMEM((2, 4, 16, 128), F32),
            pltpu.VMEM((4, 16, 128), F32),
            pltpu.VMEM((4, 4, 16, 128), F32),
            pltpu.VMEM((4, 16, 128), F32),
        ]
        + job_scratch
        + [
            pltpu.SemaphoreType.DMA((REDUCE_COPIES,)),
            pltpu.SemaphoreType.DMA((REDUCE_COPIES,)),
            pltpu.SemaphoreType.DMA((12,)),
            pltpu.SemaphoreType.DMA((2,)),
        ],
        compiler_params=params(collective_id=1, has_side_effects=True),
        name="backward",
    )(x, qkv, e, att, dos, bg, res, fa, hl, og, ai, sums, bsum)


def finish_kernel(result, ovec, inp, y, oq, ok, ov, oo, oi, our, out, y_out, *vectors):
    for c in range(3):
        tile = result[9 + c].astype(F32)
        for part, ref in enumerate((oq, ok, ov)):
            ref[:, c * CW : (c + 1) * CW] = tile[:, part * CW : (part + 1) * CW]
    oo[...] = result[8].astype(F32)
    for q in range(4):
        oi[:, q * D : (q + 1) * D] = result[4 + q].astype(F32)
        our[q] = result[q].astype(F32)
    out[...] = inp[...]
    y_out[...] = y[...]
    for k in range(8):
        vectors[k][...] = ovec[k, 0:TR]
    for r in range(3):
        vectors[8][128 * r : 128 * (r + 1)] = ovec[8 + r]


def finish(result, ovec, inp, y):
    t = inp.shape[0]
    steps = 2
    rows = TR // steps

    def part(*dims):
        at = len(dims) - 2
        return pl.BlockSpec(dims, lambda h: tuple(h if k == at else 0 for k in range(len(dims))))

    def vector(n):
        return pl.BlockSpec((n,), lambda h: (0,))

    *outs, gr, out, y, v0, v1, v2, v3, v4, v5, v6, v7, v8 = pl.pallas_call(
        finish_kernel,
        grid=(steps,),
        out_shape=tuple(shape(TR, D, dtype=F32) for _ in range(4))
        + (shape(TR, FF, dtype=F32), shape(4, TR, D, dtype=F32), shape(t, D), shape(t, D))
        + tuple(shape(TR, dtype=F32) for _ in range(8))
        + (shape(4 * TR, dtype=F32),),
        in_specs=[part(12, rows, D), pl.BlockSpec((16, 128), lambda h: (0, 0)), part(t // steps, D), part(t // steps, D)],
        out_specs=(part(rows, D),) * 4
        + (part(rows, FF), part(4, rows, D), part(t // steps, D), part(t // steps, D))
        + (vector(TR),) * 8
        + (vector(4 * TR),),
        compiler_params=params(),
        name="finish",
    )(result, ovec, inp, y)
    return *outs, gr.reshape(4 * TR, D), out, y, v0, v1, v2, v3, v4, v5, v6, v7, v8


def forward_local_kernel(x, seg, kept, fa, rows, qkv, att, inv, e_out, t1, segt, ebuf, esem):
    turn_ids(seg, segt)
    for c in range(3):
        project(c, x, fa, rows, qkv)
    keep = kept[0]

    def one(i, _):
        c, r, pair = place_of(i)
        attend(i, qkv, seg, segt, keep, att, inv, ebuf)
        copy = pltpu.make_async_copy(ebuf, e_out.at[c, r, pair], esem.at[0])
        copy.start()
        copy.wait()
        return 0

    lax.fori_loop(0, 6 * (x.shape[0] // SEQ), one, 0)
    t1[...] = x[...].astype(F32) + (mm(att[...], fa[3].reshape(D, D)) + rows[2:3])


def forward_local(x, seg, kept, fa, rows):
    t = x.shape[0]
    n = t // SEQ
    return pl.pallas_call(
        forward_local_kernel,
        out_shape=(shape(3, t, D), shape(t, D), shape(t, D, dtype=F32), shape(3, n, 2, 2, SEQ, SEQ), shape(t, D, dtype=F32)),
        in_specs=[VM, VM, SM, VM, VM],
        out_specs=(VM, VM, VM, ANY, VM),
        scratch_shapes=[
            pltpu.VMEM((n, SEQ, 128), F32), pltpu.VMEM((2, SEQ, SEQ), BF), pltpu.SemaphoreType.DMA((1,)),
        ],
        compiler_params=params(),
        name="forward_local",
    )(x, seg, kept, fa, rows)


def ffn_local_kernel(
    t1, grad, rows, binner, kept, inv, fi, fo, fa, y, res, bg, dos, sums, bsum, g, hl, og, act, gp, t2, ob, tile, gsem, block=256
):
    sums[...] = jnp.zeros_like(sums)
    bsum[...] = jnp.zeros_like(bsum)
    t2[...] = t1[...]
    blocks = t1.shape[0] // block

    def first(i, _):
        ffn_inner(i, block, t2, rows, binner, kept[0], fi, hl, act, gp)
        return 0

    def second(i, _):
        wo = fa[3].reshape(D, D)
        ffn_outer(i, block, blocks, t2, grad, rows, kept[0], fi, fo, wo, inv, act, gp, ob, y, bg, dos, og, sums, bsum)
        return 0

    lax.fori_loop(0, blocks, first, 0)
    outer_product(0, block, fo, act, ob)
    lax.fori_loop(0, blocks, second, 0)
    res[...] = t2[...]

    def one(j, _):
        tile[...] = mm(act[j], og[...], TN).astype(BF).reshape(2, 4, TR, D)
        copy = pltpu.make_async_copy(tile, g.at[lax.div(j, 2), pl.ds(2 * lax.rem(j, 2), 2), 0:4], gsem.at[0])
        copy.start()
        copy.wait()
        tile[...] = mm(hl[...], gp[j], TN).astype(BF).reshape(2, 4, TR, D)
        copy = pltpu.make_async_copy(tile, g.at[:, :, 4 + j], gsem.at[0])
        copy.start()
        copy.wait()
        return 0

    lax.fori_loop(0, 4, one, 0)


def ffn_local(t1, grad, rows, binner, kept, inv, fi, fo, fa):
    t = t1.shape[0]
    return pl.pallas_call(
        ffn_local_kernel,
        out_shape=(
            shape(t, D), shape(t, D, dtype=F32), shape(t, D), shape(t, D),
            shape(8, D, dtype=F32), shape(1, FF, dtype=F32), shape(2, 4, 8, TR, D),
        ),
        in_specs=[VM] * 4 + [SM] + [VM] * 4,
        out_specs=(VM,) * 6 + (ANY,),
        scratch_shapes=[
            pltpu.VMEM((t, D), BF), pltpu.VMEM((t, D), BF), pltpu.VMEM((4, t, D), BF), pltpu.VMEM((4, t, D), BF),
            pltpu.VMEM((t, D), F32), pltpu.VMEM((256, D), F32), pltpu.VMEM((2, 4, TR, D), BF),
            pltpu.SemaphoreType.DMA((1,)),
        ],
        compiler_params=params(),
        name="ffn_local",
    )(t1, grad, rows, binner, kept, inv, fi, fo, fa)


def backward_local_kernel(x, qkv, e_in, att, dos, bg, res, fa, sums_in, out, gx, go, sums, dqkv, ebuf, esem):
    sums[...] = sums_in[...]
    go[...] = mm(att[...], bg[...], TN).astype(BF).reshape(4, 2, 1, TR, D)

    def one(i, _):
        c, r, pair = place_of(i)
        copy = pltpu.make_async_copy(e_in.at[c, r, pair], ebuf, esem.at[0])
        copy.start()
        copy.wait()
        attend_back(i, qkv, dos, att, ebuf, dqkv)

        @pl.when(lax.rem(i, 4) == 3)
        def _():
            chunk_grads(lax.div(i, 4), x, dqkv, gx, sums)

        return 0

    lax.fori_loop(0, 6 * (x.shape[0] // SEQ), one, 0)
    input_back(res, dqkv, fa, out)


def backward_local(x, qkv, e, att, dos, bg, res, fa, sums):
    t = x.shape[0]
    return pl.pallas_call(
        backward_local_kernel,
        out_shape=(shape(t, D), shape(3, 4, 2, 1, TR, D), shape(4, 2, 1, TR, D), shape(8, D, dtype=F32)),
        in_specs=[VM, VM, ANY] + [VM] * 6,
        out_specs=(VM,) * 4,
        scratch_shapes=[pltpu.VMEM((3, t, D), BF), pltpu.VMEM((2, SEQ, SEQ), BF), pltpu.SemaphoreType.DMA((1,))],
        compiler_params=params(),
        name="backward_local",
    )(x, qkv, e, att, dos, bg, res, fa, sums)


def gather_lax(wq, wk, wv, wo, wi, wr, eight, b_inner):
    def whole(a):
        return lax.all_gather(a.astype(BF), "shard", axis=0, tiled=True)

    wq, wk, wv, wo, wi, wr = (whole(a) for a in (wq, wk, wv, wo, wi, wr))
    chunks = [jnp.concatenate([a[:, c * CW : (c + 1) * CW] for a in (wq, wk, wv)], axis=1) for c in range(3)]
    fa = jnp.stack(chunks + [wo]).reshape(4, 8, TR, D)
    fi = jnp.stack([wi[:, q * D : (q + 1) * D] for q in range(4)]).reshape(4, 8, TR, D)
    rows = jnp.stack([whole(a) for a in eight]).astype(F32)
    return fa, fi, wr.reshape(8, 4, TR, D), rows, whole(b_inner).astype(F32).reshape(1, FF)


def reduce_lax(g, gx, go, sums, bsum):
    g = g.reshape(8, 8, TR, D)
    gr = g[:, 0:4].reshape(FF, D)
    gi = jnp.concatenate([g[:, 4 + j].reshape(D, D) for j in range(4)], axis=1)
    gx = gx.reshape(3, D, 3, CW)
    squares = [jnp.concatenate([gx[c, :, part] for c in range(3)], axis=1) for part in range(3)]

    def owned(a):
        a = lax.psum_scatter(a.astype(F32), "shard", scatter_dimension=0, tiled=True)
        return lax.psum(a.astype(BF), "width").astype(F32)

    matrices = [owned(a) for a in (*squares, go.reshape(D, D), gi, gr)]
    return matrices, [owned(sums[k]) for k in range(8)] + [owned(bsum[0])]


def body(
    layer_input, segment_ids, group_heads,
    w_query, b_query, w_key, w_value, b_value, w_out, b_out, gain_one, shift_one,
    w_inner, b_inner, w_outer, b_outer, gain_two, shift_two, out_grad,
):
    eight = (b_query, b_value, b_out, gain_one, shift_one, b_outer, gain_two, shift_two)
    weights = (w_query, w_key, w_value, w_out, w_inner, w_outer)
    own_kernels = lax.axis_size("width") == 4 and lax.axis_size("shard") == 8
    if own_kernels:
        sums, bsum, fa, qkv, att, e, y, res, bg, dos, hl, og, ai = forward(
            layer_input, segment_ids, group_heads, *weights, eight, b_inner, out_grad
        )
    else:
        fa, fi, fo, rows, binner = gather_lax(*weights, eight, b_inner)
        qkv, att, inv, e, t1 = forward_local(layer_input, segment_ids, group_heads, fa, rows)
        y, res, bg, dos, sums, bsum, g = ffn_local(t1, out_grad, rows, binner, group_heads, inv, fi, fo, fa)
    if own_kernels:
        input_grad, result, ovec = backward(layer_input, qkv, e, att, dos, bg, res, fa, hl, og, ai, sums, bsum)
        gq, gk, gv, go, gi, gr, input_grad, y, *vectors = finish(result, ovec, input_grad, y)
    else:
        input_grad, gx, go, sums = backward_local(layer_input, qkv, e, att, dos, bg, res, fa[0:3], sums)
        (gq, gk, gv, go, gi, gr), vectors = reduce_lax(g, gx, go, sums, bsum)
    return (
        y, input_grad, gq, vectors[0], gk, gv, vectors[1], go, vectors[2],
        vectors[3], vectors[4], gi, vectors[8], gr, vectors[5], vectors[6], vectors[7],
    )


def solution(mesh):
    placed = (
        P(("width", "shard"), None),
        P(("width", "shard"), None),
        P("width"),
        P("shard", None),
        P("shard"),
        P("shard", None),
        P("shard", None),
        P("shard"),
        P("shard", None),
        P("shard"),
        P("shard"),
        P("shard"),
        P("shard", None),
        P("shard"),
        P("shard", None),
        P("shard"),
        P("shard"),
        P("shard"),
        P(("width", "shard"), None),
    )
    return jax.shard_map(
        body,
        mesh=mesh,
        in_specs=placed,
        out_specs=(
            P(("width", "shard"), None),
            P(("width", "shard"), None),
            P("shard", None),
            P("shard"),
            P("shard", None),
            P("shard", None),
            P("shard"),
            P("shard", None),
            P("shard"),
            P("shard"),
            P("shard"),
            P("shard", None),
            P("shard"),
            P("shard", None),
            P("shard"),
            P("shard"),
            P("shard"),
        ),
        check_vma=False,
    )
```

```python
import functools
import jax
import jax.numpy as jnp
from jax import lax
from jax.experimental import pallas as pl
from jax.experimental.pallas import tpu as pltpu
from jax.sharding import PartitionSpec as P

HEADS = 12
HEAD_DIM = 64
FF = 3072
D = 768
SEQ = 512
MESH = pl.DeviceIdType.MESH
BF = jnp.bfloat16
F32 = jnp.float32
TR = 96
CW = 256
NT = (((1,), (1,)), ((), ()))
TN = (((0,), (0,)), ((), ()))
NN = (((1,), (0,)), ((), ()))
EPS = 1e-06
RSQRT2 = 0.7071067811865476
RSQRT2PI = 0.3989422804014327
VM = pl.BlockSpec(memory_space=pltpu.VMEM)
SM = pl.BlockSpec(memory_space=pltpu.SMEM)
ANY = pl.BlockSpec(memory_space=pl.ANY)


def params(**more):
    return pltpu.CompilerParams(vmem_limit_bytes=62 << 20, **more)


def shape(*dims, dtype=BF):
    return jax.ShapeDtypeStruct(dims, dtype)


class Place:
    def __init__(self):
        self.w = w = lax.axis_index("width")
        self.s = s = lax.axis_index("shard")
        self.c = c = lax.rem(s, 2)
        self.z = lax.div(s, 2)
        xw, yw = w + 1 - 2 * lax.rem(w, 2), lax.rem(w + 2, 4)
        up, down = lax.rem(s + 2, 8), lax.rem(s + 6, 8)
        self.wa = jnp.where(c == 0, xw, yw)
        self.wb = jnp.where(c == 0, yw, xw)
        self.wd = 3 - w
        self.sa = jnp.where(c == 0, up, down)
        self.sb = jnp.where(c == 0, down, up)
        self.so = lax.rem(s + 4, 8)
        self.sib = (w, s + 1 - 2 * c)
        self.plane_a, self.plane_b = (self.wa, s), (self.wb, s)
        self.ring_a, self.ring_b = (w, self.sa), (w, self.sb)


def call(devices):
    barrier = pltpu.get_barrier_semaphore()
    for device in devices:
        pl.semaphore_signal(barrier, inc=1, device_id=device, device_id_type=MESH)


def answer(devices):
    pl.semaphore_wait(pltpu.get_barrier_semaphore(), len(devices))


def others(p):
    return [(p.wa, p.s), (p.wb, p.s), (p.wd, p.s)] + [(p.w, lax.rem(p.s + k, 8)) for k in range(1, 8)]


class Net:
    def __init__(self, send, recv):
        self.send, self.recv, self.made, self.sent = send, recv, {}, set()

    def define(self, name, make):
        assert name not in self.made
        self.made[name] = (len(self.made), make)

    def copy(self, name):
        k, make = self.made[name]
        src, dst, device = make()
        return pltpu.make_async_remote_copy(
            src_ref=src, dst_ref=dst, send_sem=self.send.at[k], recv_sem=self.recv.at[k],
            device_id=device, device_id_type=MESH,
        )

    def start(self, *names):
        for name in names:
            self.copy(name).start()

    def wait(self, *names):
        for name in names:
            self.copy(name).wait_recv()

    def finish(self):
        for name in self.made:
            if name not in self.sent:
                self.copy(name).wait_send()


def quarter(w):
    return pl.ds(pl.multiple_of(48 * lax.rem(w, 2), 48), 48), pl.ds(pl.multiple_of(384 * lax.div(w, 2), 384), 384)


def mm(a, b, dims=NN):
    return lax.dot_general(a, b, dims, preferred_element_type=F32)


def rows_of(i, size):
    return pl.ds(pl.multiple_of(i * size, size), size)


def column_mask(kept, shape, width):
    return jnp.where(lax.broadcasted_iota(jnp.int32, shape, 1) < kept * width, 1.0, 0.0).astype(F32)


def mean_of(v):
    return jnp.sum(v, axis=1, keepdims=True) * (1.0 / D)


def norm_rows(total):
    centered = total - mean_of(total)
    inverse = lax.rsqrt(mean_of(centered * centered) + EPS)
    return centered * inverse, inverse


def norm_back(grad, normed, inverse):
    return inverse * (grad - mean_of(grad) - normed * mean_of(grad * normed))


def low_lanes(n):
    return lax.broadcasted_iota(jnp.int32, (n, 128), 1) < HEAD_DIM


def place_of(i):
    return lax.div(i, 4), lax.rem(i, 2), lax.rem(lax.div(i, 2), 2)


def pair_lanes(pair, part):
    return pl.ds(pl.multiple_of(part * CW + pair * 128, 128), 128)


def project(c, x, fa, rows, qkv, block=256):
    lanes = pl.ds(pl.multiple_of(c * CW, CW), CW)
    bias = jnp.concatenate([rows[0:1, lanes], jnp.zeros((1, CW), F32), rows[1:2, lanes]], axis=1)
    scale = jnp.where(lax.broadcasted_iota(jnp.int32, (1, D), 1) < CW, 0.125, 1.0)

    def one(i, _):
        at = rows_of(i, block)
        qkv[c, at] = ((mm(x[at], fa[c].reshape(D, D)) + bias) * scale).astype(BF)
        return 0

    lax.fori_loop(0, x.shape[0] // block, one, 0)


def turn_ids(seg, segt):
    for r in range(seg.shape[0]):
        row = seg[r : r + 1, :].astype(F32)
        segt[r] = jnp.broadcast_to(row, (128, SEQ)).T


def attend(i, qkv, seg, segt, kept, att, inv, ebuf, qb=512):
    c, r, pair = place_of(i)
    base = r * SEQ
    rows = pl.ds(pl.multiple_of(base, SEQ), SEQ)
    kp, vp = qkv[c, rows, pair_lanes(pair, 1)], qkv[c, rows, pair_lanes(pair, 2)]
    low = low_lanes(SEQ)
    ones = jnp.ones_like(vp)
    vs = (jnp.where(low, vp, ones), jnp.where(low, ones, vp))
    ids = seg[pl.ds(r, 1), :].astype(F32)
    lowq = low_lanes(qb)
    lanes = pl.ds(pl.multiple_of(c * CW + pair * 128, 128), 128)
    column = lax.broadcasted_iota(jnp.int32, (1, 128), 1) + (c * CW + pair * 128)
    mask = jnp.where(column < kept * HEAD_DIM, 1.0, 0.0).astype(F32)
    for b in range(SEQ // qb):
        at = pl.ds(pl.multiple_of(base + b * qb, qb), qb)
        qp = qkv[c, at, pair_lanes(pair, 0)]
        zero = jnp.zeros_like(qp)
        own = segt[r, b * qb : (b + 1) * qb]
        same = jnp.concatenate([own == ids[:, j * 128 : (j + 1) * 128] for j in range(4)], axis=1)
        out = []
        for h in range(2):
            qh = jnp.where(lowq, qp, zero) if h == 0 else jnp.where(lowq, zero, qp)
            scores = jnp.where(same, mm(qh, kp, NT), -1e30)
            top = jnp.max(scores, axis=1, keepdims=True)
            e = jnp.exp(scores - top).astype(BF)
            ebuf[h, b * qb : (b + 1) * qb] = e
            out.append(mm(e, vs[h]))
        inverse = 1.0 / pltpu.roll(jnp.where(lowq, out[1], out[0]), HEAD_DIM, 1)
        att[at, lanes] = (jnp.where(lowq, out[0], out[1]) * (inverse * mask)).astype(BF)
        inv[at, lanes] = inverse


def expand_vectors(fv, rows, binner):
    lane = lax.broadcasted_iota(jnp.int32, (128, D), 0)
    column = lax.broadcasted_iota(jnp.int32, (128, D), 1)
    total = jnp.zeros((16, D), F32)
    for s in range(8):
        pick = jnp.where((column == lane + TR * s) & (lane < TR), 1.0, 0.0).astype(BF)
        total = total + mm(fv[s], pick)
        tile = fv[s].astype(F32)
        for r in range(3):
            binner[0:1, 128 * (3 * s + r) : 128 * (3 * s + r + 1)] = tile[8 + r : 9 + r]
    rows[...] = total[0:8]


GROUPS = (slice(0, 1), slice(1, 2), slice(2, 3), slice(3, 4), slice(4, 8), slice(8, 12))
WO, INNER, OUTER = 3, 4, 5
GATHER_COPIES = 16 * len(GROUPS) + 7


def gather_net(p, own, fa, fi, fo, vec, fv, ssem, rsem):
    net = Net(ssem, rsem)
    every = (slice(None), slice(None))

    def piece(g, s, part):
        if g <= WO:
            return fa.at[(GROUPS[g], s, *part)]
        return fi.at[(slice(None), s, *part)] if g == INNER else fo.at[(s, slice(None), *part)]

    mine, first = quarter(p.w), quarter(p.wa)
    for g in range(len(GROUPS)):

        def add(name, src, dst, device):
            net.define((g, *name), lambda: (src(), dst(), device))

        def same(name, g, s, part, device):
            add(name, lambda: piece(g, s, part), lambda: piece(g, s, part), device)

        for name, device in (("zb", p.ring_a), ("za", p.ring_b)):
            add((name,), lambda g=g: own.at[(GROUPS[g], *mine)], lambda g=g: piece(g, p.s, mine), device)
        same(("zo",), g, p.sb, mine, p.ring_a)
        add(("own", "c"), lambda g=g: own.at[GROUPS[g]], lambda g=g: piece(g, p.s, every), p.sib)
        for name, s in (("zb", p.sb), ("za", p.sa), ("zo", p.so)):
            same((name, "xa"), g, s, mine, p.plane_a)
            same((name, "xb"), g, s, mine, p.plane_b)
            same((name, "xd"), g, s, first, p.plane_b)
            same((name, "c"), g, s, every, p.sib)
    for k in range(1, 8):
        net.define(("v", k), lambda k=k: (vec, fv.at[p.s], (p.w, lax.rem(p.s + k, 8))))
    assert len(net.made) == GATHER_COPIES
    return net


def ffn_inner(i, block, t1, rows, binner, kept, wi, hl, act, gp):
    at = rows_of(i, block)
    n1, _ = norm_rows(t1[at])
    low = (n1 * rows[3:4] + rows[4:5]).astype(BF)
    hl[at] = low
    for j in range(4):
        inner = mm(low, wi[j].reshape(D, D)) + binner[:, j * D : (j + 1) * D]
        keep = column_mask(kept * 256 - j * D, (1, D), 1)
        phi = 0.5 + 0.5 * lax.erf(inner * RSQRT2)
        masked = inner * keep
        act[j, at] = (masked * phi).astype(BF)
        gp[j, at] = (keep * phi + masked * (RSQRT2PI * jnp.exp(-0.5 * (inner * inner)))).astype(BF)


def outer_product(i, block, wr, act, ob):
    at = rows_of(i, block)
    outer = jnp.zeros((block, D), F32)
    for j in range(4):
        outer = outer + mm(act[j, at], wr[2 * j : 2 * j + 2].reshape(D, D))
    ob[...] = outer


def ffn_outer(i, block, blocks, t1, grad, rows, kept, wi, wr, wo, inv, act, gp, ob, y, bg, dos, og, sums, bsum):
    at = rows_of(i, block)

    def add(k, value):
        sums[k : k + 1] += jnp.sum(value, axis=0, keepdims=True)

    def outer_weight(j):
        return wr[2 * j : 2 * j + 2].reshape(D, D)

    n1, inv1 = norm_rows(t1[at])
    hidden = n1 * rows[3:4] + rows[4:5]
    n2, inv2 = norm_rows(hidden + (ob[...] + rows[5:6]))
    outer_product(jnp.minimum(i + 1, blocks - 1), block, wr, act, ob)
    y[at] = (n2 * rows[6:7] + rows[7:8]).astype(BF)
    top = grad[at].astype(F32)
    add(7, top)
    add(6, top * n2)
    res2 = norm_back(top * rows[6:7], n2, inv2)
    o = res2.astype(BF)
    og[at] = o
    add(5, o.astype(F32))
    hg = res2
    for j in range(4):
        cols = slice(j * D, (j + 1) * D)
        g = (mm(o, outer_weight(j), NT) * gp[j, at].astype(F32)).astype(BF)
        gp[j, at] = g
        bsum[:, cols] += jnp.sum(g.astype(F32), axis=0, keepdims=True)
        hg = hg + mm(g, wi[j].reshape(D, D), NT)
    add(4, hg)
    add(3, hg * n1)
    res1 = norm_back(hg * rows[3:4], n1, inv1)
    t1[at] = res1
    b = res1.astype(BF)
    bg[at] = b
    add(2, b.astype(F32))
    heads = column_mask(kept, (1, D), HEAD_DIM)
    dos[at] = (mm(b, wo, NT) * (inv[at] * heads)).astype(BF)


def forward_kernel(
    x_in, seg, kept, wq_in, wk_in, wv_in, wo_in, wi_in, wr_in, v0, v1, v2, v3, v4, v5, v6, v7, v_inner, grad_in,
    sums, bsum, fa_out, qkv_out, att_out, e_out, y_out, res_out, bg_out, dos_out, hl_out, og_out, ai_out,
    own, vtile, vec, fa, fi, fo, fv, rows, binner, att, inv, t1, segt, ebuf, grad, y, bg, dos, hl, og, act, gp, ob,
    x, wq, wk, wv, wo, wi, wr, ssem, rsem, lsem, esem, fsem, isem,
):
    qkv = gp.at[0:3]
    p = Place()
    call(others(p))
    arriving = [
        pltpu.make_async_copy(src, dst, isem.at[k])
        for k, (src, dst) in enumerate(
            ((wq_in, wq), (wk_in, wk), (wv_in, wv), (wo_in, wo), (wi_in, wi), (wr_in, wr), (x_in, x))
        )
    ]
    for copy in arriving:
        copy.start()

    def cast(c):
        for part, ref in enumerate((wq, wk, wv)):
            own[c, :, part * CW : (part + 1) * CW] = ref[:, c * CW : (c + 1) * CW].astype(BF)

    for copy in arriving[0:3]:
        copy.wait()
    cast(0)
    vtile[...] = jnp.zeros_like(vtile)
    for k, ref in enumerate((v0, v1, v2, v3, v4, v5, v6, v7)):
        vtile[k : k + 1, 0:TR] = ref[...]
    for r in range(3):
        vtile[8 + r : 9 + r] = v_inner[128 * r : 128 * (r + 1)].reshape(1, 128)
    vec[...] = vtile[...].astype(BF)
    answer(others(p))
    net = gather_net(p, own, fa, fi, fo, vec, fv, ssem, rsem)
    names = ("zb", "za", "zo")

    def ring(g):
        net.start((g, "zb"), (g, "za"), (g, "own", "c"))

    def onward(g):
        net.wait((g, "zb"))
        net.start((g, "zo"))

    def plane(g, *which):
        for name in which or names:
            if name != "zb":
                net.wait((g, name))
            net.start((g, name, "xa"), (g, name, "xb"))

    def relay(g, *which):
        for name in which or names:
            net.wait((g, name, "xa"))
            net.start((g, name, "xd"))

    def share(g, *which):
        for name in which or names:
            net.wait((g, name, "xb"), (g, name, "xd"))
            net.start((g, name, "c"))

    def landed(g):
        net.wait((g, "own", "c"), *[(g, name, "c") for name in names])

    ring(0)
    cast(1)
    ring(1)
    cast(2)
    for copy in arriving[3:]:
        copy.wait()
    own[3] = wo[...].astype(BF)
    for q in range(4):
        own[4 + q] = wi[:, q * D : (q + 1) * D].astype(BF)
        own[8 + q] = wr[q * TR : (q + 1) * TR, :].astype(BF)
    net.start(*[("v", k) for k in range(1, 8)])
    local = {}

    def put(name, k, src, dst):
        local[name] = lambda: pltpu.make_async_copy(src(), dst(), lsem.at[k])

    pieces = (
        ("own a", lambda: own.at[0:4], lambda: fa.at[:, p.s]),
        ("own i", lambda: own.at[4:8], lambda: fi.at[:, p.s]),
        ("own o", lambda: own.at[8:12], lambda: fo.at[p.s]),
        ("vec", lambda: vec, lambda: fv.at[p.s]),
        ("grad", lambda: grad_in, lambda: grad),
        ("qkv", lambda: qkv, lambda: qkv_out),
        ("fa", lambda: fa.at[0:3], lambda: fa_out),
        ("att", lambda: att, lambda: att_out),
        ("hl", lambda: hl, lambda: hl_out),
        ("act", lambda: act, lambda: ai_out.at[0:4]),
    )
    for k, (name, src, dst) in enumerate(pieces):
        put(name, k, src, dst)
    for name in ("own a", "own i", "own o", "vec", "grad"):
        local[name]().start()

    onward(0)
    plane(0, "zb", "za")
    onward(1)
    ring(2)
    plane(1, "zb", "za")
    plane(0, "zo")
    turn_ids(seg, segt)
    relay(0, "zb", "za")
    plane(1, "zo")
    relay(1, "zb")
    onward(2)
    ring(WO)
    relay(1, "za")
    plane(2, "zb", "za")
    relay(0, "zo")
    share(0, "zb", "za")
    relay(1, "zo")
    share(1, "zb")
    plane(2, "zo")
    share(1, "za")
    relay(2, "zb")
    onward(WO)
    ring(INNER)
    relay(2, "za")
    share(0, "zo")
    plane(WO, "zb", "za")
    share(1, "zo")
    relay(2, "zo")
    net.wait(*[("v", k) for k in range(1, 8)])
    local["vec"]().wait()
    expand_vectors(fv, rows, binner)
    share(2, "zb")
    plane(WO, "zo")
    local["own a"]().wait()
    keep = kept[0]

    def out_copy(i, slot):
        c, r, pair = place_of(i)
        return pltpu.make_async_copy(ebuf.at[slot], e_out.at[c, r, pair], esem.at[slot])

    before = {0: lambda: landed(0), 4: lambda: landed(1), 8: lambda: landed(2)}
    steps = {
        0: lambda: (share(2, "za", "zo"), relay(WO), onward(INNER), ring(OUTER), plane(INNER, "zb"),),
        1: lambda: (plane(INNER, "za"),),
        2: lambda: (share(WO),),
        4: lambda: (relay(INNER, "zb"), plane(INNER, "zo"),),
        5: lambda: (onward(OUTER), plane(OUTER, "zb"),),
        6: lambda: (relay(INNER, "za"),),
        8: lambda: (share(INNER, "zb"), relay(INNER, "zo"), plane(OUTER, "za"),),
        9: lambda: (plane(OUTER, "zo"),),
        10: lambda: (relay(OUTER, "zb"),),
    }
    later = {
        0: lambda: (share(OUTER, "zb"),),
        1: lambda: (share(OUTER, "za", "zo"),),
    }

    def after_residual():
        relay(OUTER, "za")
        share(INNER, "za")
        relay(OUTER, "zo")
        share(INNER, "zo")

    def at_step(i, table):
        for k, step in table.items():
            @pl.when(i == k)
            def _(step=step):
                step()

    def one(i, _):
        slot = lax.rem(i, 2)

        @pl.when(i >= 2)
        def _():
            out_copy(i - 2, slot).wait()

        at_step(i, before)

        @pl.when(lax.rem(i, 4) == 0)
        def _():
            project(lax.div(i, 4), x, fa, rows, qkv)

        attend(i, qkv, seg, segt, keep, att, inv, ebuf.at[slot])
        out_copy(i, slot).start()
        at_step(i, steps)
        return 0

    n = 6 * (x.shape[0] // SEQ)
    lax.fori_loop(0, n, one, 0)
    local["qkv"]().start()
    local["att"]().start()
    local["fa"]().start()
    sums[...] = jnp.zeros_like(sums)
    bsum[...] = jnp.zeros_like(bsum)
    landed(WO)
    block = 256
    blocks = x.shape[0] // block

    def residual(i, _):
        at = rows_of(i, block)
        t1[at] = x[at].astype(F32) + (mm(att[at], fa[3].reshape(D, D)) + rows[2:3])
        return 0

    lax.fori_loop(0, blocks, residual, 0)
    after_residual()
    landed(INNER)
    local["own i"]().wait()
    local["qkv"]().wait()

    def first(i, _):
        ffn_inner(i, block, t1, rows, binner, keep, fi, hl, act, gp)
        at_step(i, later)
        return 0

    lax.fori_loop(0, blocks, first, 0)
    local["hl"]().start()
    local["act"]().start()
    landed(OUTER)
    local["own o"]().wait()
    local["grad"]().wait()

    def flush(i):
        at = rows_of(i, block)
        pairs = (
            (gp.at[:, at], ai_out.at[4:8, at]), (og.at[at], og_out.at[at]), (dos.at[at], dos_out.at[at]),
            (bg.at[at], bg_out.at[at]), (t1.at[at], res_out.at[at]), (y.at[at], y_out.at[at]),
        )
        return [pltpu.make_async_copy(src, dst, fsem.at[i, k]) for k, (src, dst) in enumerate(pairs)]

    def second(i, _):
        wo = fa[3].reshape(D, D)
        ffn_outer(i, block, blocks, t1, grad, rows, keep, fi, fo, wo, inv, act, gp, ob, y, bg, dos, og, sums, bsum)
        for copy in flush(i):
            copy.start()
        return 0

    outer_product(0, block, fo, act, ob)
    lax.fori_loop(0, blocks, second, 0)
    out_copy(n - 2, (n - 2) % 2).wait()
    out_copy(n - 1, (n - 1) % 2).wait()
    for name in ("fa", "att", "hl", "act"):
        local[name]().wait()
    for i in range(blocks):
        for copy in flush(i):
            copy.wait()
    net.finish()


def forward(x, seg, kept, wq, wk, wv, wo, wi, wr, eight, b_inner, grad):
    t = x.shape[0]
    n = t // SEQ
    return pl.pallas_call(
        forward_kernel,
        out_shape=(
            shape(8, D, dtype=F32), shape(1, FF, dtype=F32), shape(3, 8, TR, D), shape(3, t, D), shape(t, D),
            shape(3, n, 2, 2, SEQ, SEQ), shape(t, D), shape(t, D, dtype=F32), shape(t, D), shape(t, D), shape(t, D),
            shape(t, D), shape(8, t, D),
        ),
        in_specs=[ANY, VM, SM] + [ANY] * 6 + [VM] * 9 + [ANY],
        out_specs=(VM, VM) + (ANY,) * 11,
        scratch_shapes=[
            pltpu.VMEM((12, TR, D), BF),
            pltpu.VMEM((16, 128), F32),
            pltpu.VMEM((16, 128), BF),
            pltpu.VMEM((4, 8, TR, D), BF),
            pltpu.VMEM((4, 8, TR, D), BF),
            pltpu.VMEM((8, 4, TR, D), BF),
            pltpu.VMEM((8, 16, 128), BF),
            pltpu.VMEM((8, D), F32),
            pltpu.VMEM((1, FF), F32),
            pltpu.VMEM((t, D), BF),
            pltpu.VMEM((t, D), F32),
            pltpu.VMEM((t, D), F32),
            pltpu.VMEM((n, SEQ, 128), F32),
            pltpu.VMEM((2, 2, SEQ, SEQ), BF),
        ]
        + [pltpu.VMEM((t, D), BF)] * 6
        + [pltpu.VMEM((4, t, D), BF)] * 2
        + [
            pltpu.VMEM((256, D), F32),
            pltpu.VMEM((t, D), BF),
            *[pltpu.VMEM((TR, D), F32)] * 4,
            pltpu.VMEM((TR, FF), F32),
            pltpu.VMEM((4 * TR, D), F32),
            pltpu.SemaphoreType.DMA((GATHER_COPIES,)),
            pltpu.SemaphoreType.DMA((GATHER_COPIES,)),
            pltpu.SemaphoreType.DMA((10,)),
            pltpu.SemaphoreType.DMA((2,)),
            pltpu.SemaphoreType.DMA((t // 256, 6)),
            pltpu.SemaphoreType.DMA((7,)),
        ],
        compiler_params=params(collective_id=0, has_side_effects=True),
        name="forward",
    )(x, seg, kept, wq, wk, wv, wo, wi, wr, *(a.reshape(1, TR) for a in eight), b_inner, grad)


def attend_back(i, qkv, dos, att, ebuf, dqkv):
    c, r, pair = place_of(i)
    rows = rows_of(r, SEQ)
    lanes = pl.ds(pl.multiple_of(c * CW + pair * 128, 128), 128)
    qp, kp, vp = (qkv[c, rows, pair_lanes(pair, part)] for part in range(3))
    dp = dos[rows, lanes]
    low = low_lanes(SEQ)
    zero = jnp.zeros_like(qp)
    product = dp.astype(F32) * att[rows, lanes].astype(F32)
    gq = jnp.zeros((SEQ, 128), F32)
    gk = jnp.zeros((SEQ, 128), F32)
    gv = jnp.zeros((SEQ, 128), F32)
    for h in range(2):
        mine = low if h == 0 else jnp.logical_not(low)
        dh = jnp.where(mine, dp, zero)
        delta = jnp.sum(jnp.where(mine, product, 0.0), axis=1, keepdims=True)
        e = ebuf[h]
        ds = (e.astype(F32) * (mm(dh, vp, NT) - delta)).astype(BF)
        gv = gv + mm(e, dh, TN)
        gk = gk + mm(ds, jnp.where(mine, qp, zero), TN)
        gq = gq + mm(ds, jnp.where(mine, kp, zero))
    dqkv[c, rows, pair_lanes(pair, 0)] = (gq * 0.125).astype(BF)
    dqkv[c, rows, pair_lanes(pair, 1)] = gk.astype(BF)
    dqkv[c, rows, pair_lanes(pair, 2)] = gv.astype(BF)


def chunk_grads(c, x, dqkv, gx, sums):
    gx[c] = mm(x[...], dqkv[c], TN).astype(BF).reshape(4, 2, 1, TR, D)
    part = dqkv[c].astype(F32)
    total = jnp.sum(part, axis=0, keepdims=True)
    lanes = pl.ds(pl.multiple_of(c * CW, CW), CW)
    sums[0:1, lanes] = total[:, 0:CW]
    sums[1:2, lanes] = total[:, 2 * CW :]


def input_back(res, dqkv, fa, out, block=256):
    def one(i, _):
        at = rows_of(i, block)
        total = res[at]
        for c in range(3):
            total = total + mm(dqkv[c, at], fa[c].reshape(D, D), NT)
        out[at] = total.astype(BF)
        return 0

    lax.fori_loop(0, res.shape[0] // block, one, 0)


JOBS = (
    (4, 1, False),
    (5, 1, True),
    (6, 1, True),
    (7, 1, False),
    (0, 2, True),
    (2, 2, False),
    (8, 1, False),
    (9, 1, False),
    (10, 1, False),
    (11, 1, False),
)
OUTER_UNITS = 4
REDUCE_COPIES = 9 * len(JOBS) + sum(first >= OUTER_UNITS for first, _, _ in JOBS) + 4 + 7


def job_shapes(units, ring_first):
    part, tile = (units, 48, 384), (units, TR, D)
    first = tile if ring_first else (4, *part)
    return [first, first, first, first, part, part, part]


class Job:
    def __init__(self, net, p, k, first, units, ring_first, held, landed, arrivals, bufs, result):
        self.net, self.p, self.k = net, p, k
        self.held, self.landed, self.arrivals = held, landed, arrivals
        self.d1, self.a1, self.b1, self.mid, self.d2, self.a2, self.b2 = bufs
        self.result = result
        self.units = slice(first, first + units)
        held, mid = self.held, self.mid
        z, za, zb, zo = p.z, lax.div(p.sa, 2), lax.div(p.sb, 2), lax.div(p.so, 2)
        self.z = z
        ring = (za, zb, zo, p.ring_a, p.ring_a, p.ring_b)
        plane = (p.wb, p.wa, p.wd, p.plane_a, p.plane_b, p.plane_a)

        def tile(t):
            return held, (t,)

        def plane_quarter(w):
            return held, (slice(None), slice(None), *quarter(w))

        def mid_quarter(w):
            return mid, (slice(None), *quarter(w))

        def mid_tile(t):
            return mid, (t,)

        one, two = (ring, plane) if ring_first else (plane, ring)
        self.at1, self.at2 = (tile, mid_quarter) if ring_first else (plane_quarter, mid_tile)
        self.one, self.two = one, two
        self.own1 = z if ring_first else p.w
        self.own2 = p.w if ring_first else z
        for stage, at, way, d, a, b in ((1, self.at1, one, self.d1, self.a1, self.b1), (2, self.at2, two, self.d2, self.a2, self.b2)):
            relayed, direct, opposite, dev_o, dev_r, dev_d = way

            def send(name, index, dst, device, at=at):
                def make():
                    ref, where = at(index)
                    return ref.at[where], dst, device

                net.define((k, *name), make)

            send(("d", stage), opposite, d, dev_o)
            send(("b", stage), direct, b, dev_d)
            send(("a", stage), relayed, a, dev_r)

        def share(name, w, device):
            def make():
                ref = result.at[(self.units, *quarter(w))]
                return ref, ref, device

            net.define((k, name), make)

        share("ga", p.w, p.plane_a)
        share("gb", p.w, p.plane_b)
        share("gd", p.wa, p.plane_b)

    def names(self, names):
        return [(self.k, *name) if isinstance(name, tuple) else (self.k, name) for name in names]

    def start(self, *names):
        self.net.start(*self.names(names))

    def wait(self, *names):
        self.net.wait(*self.names(names))

    def send(self):
        self.net.start(*self.arrivals)

    def pair(self):
        self.net.wait(*self.arrivals)
        held, landed = self.held, self.landed

        def one(t, _):
            held[t] = (held[t].astype(F32) + landed[t].astype(F32)).astype(BF)
            return 0

        lax.fori_loop(0, 4, one, 0)
        self.start(("d", 1), ("b", 1))

    def relay(self, stage):
        at, way, d = (self.at1, self.one, self.d1) if stage == 1 else (self.at2, self.two, self.d2)
        self.wait(("d", stage))
        ref, where = at(way[0])
        ref[where] = (ref[where].astype(F32) + d[...].astype(F32)).astype(BF)
        self.start(("a", stage))

    def total(self, stage):
        at, own, a, b = (self.at1, self.own1, self.a1, self.b1) if stage == 1 else (self.at2, self.own2, self.a2, self.b2)
        self.wait(("a", stage), ("b", stage))
        ref, where = at(own)
        return (ref[where].astype(F32) + a[...].astype(F32) + b[...].astype(F32)).astype(BF)

    def turn(self):
        self.mid[...] = self.total(1)
        self.start(("d", 2), ("b", 2))

    def share(self):
        self.result[(self.units, *quarter(self.p.w))] = self.total(2)
        self.start("ga", "gb")

    def pass_on(self):
        self.wait("ga")
        self.start("gd")

    def end(self):
        self.wait("gb", "gd")


def backward_kernel(
    x_in, qkv_in, e_in, att_in, dos_in, bg_in, res_in, fa_in, hl_in, og_in, ai_in, sums_in, bsum,
    out, result, ovec,
    x, qkv, att, dos, bg, res, fa, dqkv, gx, go, ebuf, sums, vt, vheld, vrecv, vplane, vz, *rest,
):
    bufs, (ssem, rsem, lsem, esem) = rest[:-4], rest[-4:]
    p = Place()
    call(others(p))
    n = 6 * (x.shape[0] // SEQ)
    og, hl = dqkv.at[0], dqkv.at[1]
    loads = (
        ("og", lambda: og_in, lambda: og),
        ("hl", lambda: hl_in, lambda: hl),
        ("att", lambda: att_in, lambda: att),
        ("bg", lambda: bg_in, lambda: bg),
        ("qkv", lambda: qkv_in, lambda: qkv),
        ("dos", lambda: dos_in, lambda: dos),
        ("res", lambda: res_in, lambda: res),
        ("fa", lambda: fa_in, lambda: fa.at[0:3]),
        ("x", lambda: x_in, lambda: x),
    )
    load = {
        name: lambda k=k, src=src, dst=dst: pltpu.make_async_copy(src(), dst(), lsem.at[k])
        for k, (name, src, dst) in enumerate(loads)
    }

    def block_copy(j):
        return pltpu.make_async_copy(ai_in.at[(j + 4) % 8], qkv.at[j % 3], lsem.at[len(loads) + j % 3])

    def in_copy(i, slot):
        c, r, pair = place_of(i)
        return pltpu.make_async_copy(e_in.at[c, r, pair], ebuf.at[slot], esem.at[slot])

    load["hl"]().start()
    block_copy(0).start()
    block_copy(1).start()
    load["og"]().start()
    for name in ("att", "bg", "dos"):
        load[name]().start()
    in_copy(0, 0).start()
    load["res"]().start()
    load["x"]().start()

    def staged(j):
        return fa.at[j // 2, 4 * (j % 2) : 4 * (j % 2) + 4]

    net = Net(ssem, rsem)
    held_outer, landed_outer, held_rest, landed_rest = bufs[0:4]
    jobs = []
    per = 7
    outer_arrivals = [("o", j) for j in range(4)]
    for j in range(4):
        net.define(("o", j), lambda j=j: (staged(4 + j), landed_outer.at[j], p.sib))
    for k, (first, units, ring_first) in enumerate(JOBS):
        if first < OUTER_UNITS:
            held, landed = held_outer.at[:, first : first + units], landed_outer.at[:, first : first + units]
            arrivals = outer_arrivals
            outer_arrivals = []
        else:
            r = first - OUTER_UNITS
            held, landed = held_rest.at[r], landed_rest.at[r]
            arrivals = [(k, "c")]
            if r < 4:
                source = lambda r=r: staged(r)
            elif r == 4:
                source = lambda: go.at[:, 1 - p.c, 0]
            else:
                source = lambda c=r - 5: gx.at[c, :, 1 - p.c, 0]
            net.define((k, "c"), lambda source=source, landed=landed: (source(), landed.at[:, 0], p.sib))
        job_bufs = bufs[4 + per * k : 4 + per * (k + 1)]
        jobs.append(Job(net, p, k, first, units, ring_first, held, landed, arrivals, job_bufs, result))
    net.define(("v", "c"), lambda: (vt.at[:, 1 - p.c], vrecv, p.sib))
    for k, device in enumerate((p.plane_a, p.plane_b, (p.wd, p.s))):
        net.define(("v", "p", k), lambda device=device: (vheld.at[0], vplane.at[p.w], device))
    for k in range(1, 4):
        to = lax.rem(p.z + k, 4)
        net.define(("v", "z", k), lambda to=to: (vheld.at[1, to], vz.at[p.z], (p.w, 2 * to + p.c)))
    assert len(net.made) == REDUCE_COPIES, len(net.made)

    def own_half(k, source):
        jobs[k].held[...] = source[:, p.c]

    def begin(k):
        first = JOBS[k][0]
        if first == 8:
            own_half(k, go)
        elif first > 8:
            own_half(k, gx.at[first - 9])
        jobs[k].pair()

    first_core = p.c == 0
    after = {
        0: lambda: (jobs[0].send(),),
        1: lambda: (jobs[1].send(),),
        2: lambda: (jobs[2].send(),),
        3: lambda: (jobs[3].send(), begin(0),),
        4: lambda: (net.start(("o", 0)), begin(1),),
        5: lambda: (net.start(("o", 1)), begin(2),),
        6: lambda: (net.start(("o", 2)), jobs[0].relay(1), begin(3),),
        7: lambda: (net.start(("o", 3)),),
    }
    for j in range(8):
        if j == 0:
            load["hl"]().wait()
        if j == 4:
            load["og"]().wait()
        if j + 2 < 8:
            block_copy(j + 2).start()
        block_copy(j).wait()
        block = qkv.at[j % 3]
        if j < 4:
            tiles = mm(hl[...], block[...], TN).astype(BF).reshape(4, 2, TR, D)
            zero, one = tiles[:, 0], tiles[:, 1]
            held_rest[j, :, 0] = jnp.where(first_core, zero, one)
        else:
            tiles = mm(block[...], og[...], TN).astype(BF).reshape(2, 4, TR, D)
            zero, one = tiles[0], tiles[1]
            held_outer[j - 4] = jnp.where(first_core, zero, one)
        staged(j)[...] = jnp.where(first_core, one, zero)
        if j == 0:
            answer(others(p))
        if j in after:
            after[j]()
    load["qkv"]().start()
    sums[...] = sums_in[...]
    load["att"]().wait()
    load["bg"]().wait()
    go[...] = mm(att[...], bg[...], TN).astype(BF).reshape(4, 2, 1, TR, D)
    jobs[6].send()
    load["qkv"]().wait()
    load["dos"]().wait()
    load["x"]().wait()
    steps = {
        1: lambda: (jobs[0].turn(), jobs[1].relay(1), jobs[3].relay(1), begin(4), begin(5),),
        2: lambda: (begin(6),),
        3: lambda: (jobs[7].send(), jobs[2].relay(1), jobs[0].relay(2), jobs[3].turn(),),
        5: lambda: (jobs[5].relay(1),),
        6: lambda: (begin(7),),
        7: lambda: (jobs[8].send(), jobs[1].turn(),),
        8: lambda: (jobs[6].relay(1),),
    }

    def one(i, _):
        slot = lax.rem(i, 2)

        @pl.when(i + 1 < n)
        def _():
            in_copy(i + 1, 1 - slot).start()

        in_copy(i, slot).wait()
        attend_back(i, qkv, dos, att, ebuf.at[slot], dqkv)

        @pl.when(lax.rem(i, 4) == 3)
        def _():
            chunk_grads(lax.div(i, 4), x, dqkv, gx, sums)

        for k, step in steps.items():
            @pl.when(i == k)
            def _(step=step):
                step()
        return 0

    lax.fori_loop(0, n, one, 0)
    jobs[9].send()
    jobs[5].turn()
    jobs[7].relay(1)
    begin(8)
    jobs[4].relay(1)
    jobs[6].turn()
    staged_names = [(k, "c") for k, job in enumerate(JOBS) if 4 <= job[0] < 8] + [("o", j) for j in range(4)]
    for name in staged_names:
        net.copy(name).wait_send()
        net.sent.add(name)
    load["fa"]().start()

    for s in range(8):
        vt[s // 2, s % 2] = jnp.zeros((16, 128), F32)
        vt[s // 2, s % 2, 0:8, 0:TR] = sums[:, TR * s : TR * (s + 1)]
        for r in range(3):
            vt[s // 2, s % 2, 8 + r : 9 + r] = bsum[0:1, 128 * (3 * s + r) : 128 * (3 * s + r + 1)]
    net.start(("v", "c"))
    load["res"]().wait()

    def back(i):
        at = pl.ds(256 * i, 256)
        total = res[at]
        for c in range(3):
            total = total + mm(dqkv[c, at], fa[c].reshape(D, D), NT)
        out[at] = total.astype(BF)

    load["fa"]().wait()
    back(0)
    jobs[1].relay(2)
    net.wait(("v", "c"))
    vheld[0] = vt[:, p.c] + vrecv[...]
    vplane[p.w] = vheld[0]
    net.start(*[("v", "p", k) for k in range(3)])
    back(1)
    jobs[2].turn()
    back(2)
    jobs[0].share()
    begin(9)
    net.wait(*[("v", "p", k) for k in range(3)])
    vheld[1] = (vplane[0] + vplane[1]) + (vplane[2] + vplane[3])
    vz[p.z] = vheld[1, p.z]
    net.start(*[("v", "z", k) for k in range(1, 4)])
    back(3)
    jobs[3].relay(2)
    jobs[7].turn()
    jobs[8].relay(1)
    jobs[1].share()
    jobs[5].relay(2)
    jobs[2].relay(2)
    jobs[0].pass_on()
    jobs[9].relay(1)
    jobs[8].turn()
    jobs[2].share()
    jobs[4].turn()
    jobs[6].relay(2)
    jobs[1].pass_on()
    jobs[3].share()
    jobs[7].relay(2)
    jobs[9].turn()
    jobs[2].pass_on()
    jobs[5].share()
    jobs[4].relay(2)
    jobs[8].relay(2)
    jobs[6].share()
    jobs[7].share()
    jobs[3].pass_on()
    jobs[9].relay(2)
    jobs[5].pass_on()
    jobs[8].share()
    jobs[6].pass_on()
    jobs[4].share()
    jobs[7].pass_on()
    net.wait(*[("v", "z", k) for k in range(1, 4)])
    ovec[...] = (vz[0] + vz[1]) + (vz[2] + vz[3])
    jobs[9].share()
    jobs[8].pass_on()
    jobs[4].pass_on()
    jobs[9].pass_on()
    for job in jobs:
        job.end()
    net.finish()


def backward(x, qkv, e, att, dos, bg, res, fa, hl, og, ai, sums, bsum):
    t = x.shape[0]
    job_scratch = [pltpu.VMEM(s, BF) for s in ((4, 4, TR, D),) * 2 + ((8, 4, 1, TR, D),) * 2]
    job_scratch += [pltpu.VMEM(s, BF) for _, units, ring_first in JOBS for s in job_shapes(units, ring_first)]
    return pl.pallas_call(
        backward_kernel,
        out_shape=(shape(t, D), shape(12, TR, D), shape(16, 128, dtype=F32)),
        in_specs=[ANY] * 11 + [VM, VM],
        out_specs=(VM,) * 3,
        scratch_shapes=[
            pltpu.VMEM((t, D), BF),
            pltpu.VMEM((3, t, D), BF),
            pltpu.VMEM((t, D), BF),
            pltpu.VMEM((t, D), BF),
            pltpu.VMEM((t, D), BF),
            pltpu.VMEM((t, D), F32),
            pltpu.VMEM((4, 8, TR, D), BF),
            pltpu.VMEM((3, t, D), BF),
            pltpu.VMEM((3, 4, 2, 1, TR, D), BF),
            pltpu.VMEM((4, 2, 1, TR, D), BF),
            pltpu.VMEM((2, 2, SEQ, SEQ), BF),
            pltpu.VMEM((8, D), F32),
            pltpu.VMEM((4, 2, 16, 128), F32),
            pltpu.VMEM((2, 4, 16, 128), F32),
            pltpu.VMEM((4, 16, 128), F32),
            pltpu.VMEM((4, 4, 16, 128), F32),
            pltpu.VMEM((4, 16, 128), F32),
        ]
        + job_scratch
        + [
            pltpu.SemaphoreType.DMA((REDUCE_COPIES,)),
            pltpu.SemaphoreType.DMA((REDUCE_COPIES,)),
            pltpu.SemaphoreType.DMA((12,)),
            pltpu.SemaphoreType.DMA((2,)),
        ],
        compiler_params=params(collective_id=1, has_side_effects=True),
        name="backward",
    )(x, qkv, e, att, dos, bg, res, fa, hl, og, ai, sums, bsum)


def finish_kernel(result, ovec, inp, y, oq, ok, ov, oo, oi, our, out, y_out, *vectors):
    for c in range(3):
        tile = result[9 + c].astype(F32)
        for part, ref in enumerate((oq, ok, ov)):
            ref[:, c * CW : (c + 1) * CW] = tile[:, part * CW : (part + 1) * CW]
    oo[...] = result[8].astype(F32)
    for q in range(4):
        oi[:, q * D : (q + 1) * D] = result[4 + q].astype(F32)
        our[q] = result[q].astype(F32)
    out[...] = inp[...]
    y_out[...] = y[...]
    for k in range(8):
        vectors[k][...] = ovec[k, 0:TR]
    for r in range(3):
        vectors[8][128 * r : 128 * (r + 1)] = ovec[8 + r]


def finish(result, ovec, inp, y):
    t = inp.shape[0]
    steps = 2
    rows = TR // steps

    def part(*dims):
        at = len(dims) - 2
        return pl.BlockSpec(dims, lambda h: tuple(h if k == at else 0 for k in range(len(dims))))

    def vector(n):
        return pl.BlockSpec((n,), lambda h: (0,))

    *outs, gr, out, y, v0, v1, v2, v3, v4, v5, v6, v7, v8 = pl.pallas_call(
        finish_kernel,
        grid=(steps,),
        out_shape=tuple(shape(TR, D, dtype=F32) for _ in range(4))
        + (shape(TR, FF, dtype=F32), shape(4, TR, D, dtype=F32), shape(t, D), shape(t, D))
        + tuple(shape(TR, dtype=F32) for _ in range(8))
        + (shape(4 * TR, dtype=F32),),
        in_specs=[part(12, rows, D), pl.BlockSpec((16, 128), lambda h: (0, 0)), part(t // steps, D), part(t // steps, D)],
        out_specs=(part(rows, D),) * 4
        + (part(rows, FF), part(4, rows, D), part(t // steps, D), part(t // steps, D))
        + (vector(TR),) * 8
        + (vector(4 * TR),),
        compiler_params=params(),
        name="finish",
    )(result, ovec, inp, y)
    return *outs, gr.reshape(4 * TR, D), out, y, v0, v1, v2, v3, v4, v5, v6, v7, v8


def forward_local_kernel(x, seg, kept, fa, rows, qkv, att, inv, e_out, t1, segt, ebuf, esem):
    turn_ids(seg, segt)
    for c in range(3):
        project(c, x, fa, rows, qkv)
    keep = kept[0]

    def one(i, _):
        c, r, pair = place_of(i)
        attend(i, qkv, seg, segt, keep, att, inv, ebuf)
        copy = pltpu.make_async_copy(ebuf, e_out.at[c, r, pair], esem.at[0])
        copy.start()
        copy.wait()
        return 0

    lax.fori_loop(0, 6 * (x.shape[0] // SEQ), one, 0)
    t1[...] = x[...].astype(F32) + (mm(att[...], fa[3].reshape(D, D)) + rows[2:3])


def forward_local(x, seg, kept, fa, rows):
    t = x.shape[0]
    n = t // SEQ
    return pl.pallas_call(
        forward_local_kernel,
        out_shape=(shape(3, t, D), shape(t, D), shape(t, D, dtype=F32), shape(3, n, 2, 2, SEQ, SEQ), shape(t, D, dtype=F32)),
        in_specs=[VM, VM, SM, VM, VM],
        out_specs=(VM, VM, VM, ANY, VM),
        scratch_shapes=[
            pltpu.VMEM((n, SEQ, 128), F32), pltpu.VMEM((2, SEQ, SEQ), BF), pltpu.SemaphoreType.DMA((1,)),
        ],
        compiler_params=params(),
        name="forward_local",
    )(x, seg, kept, fa, rows)


def ffn_local_kernel(
    t1, grad, rows, binner, kept, inv, fi, fo, fa, y, res, bg, dos, sums, bsum, g, hl, og, act, gp, t2, ob, tile, gsem, block=256
):
    sums[...] = jnp.zeros_like(sums)
    bsum[...] = jnp.zeros_like(bsum)
    t2[...] = t1[...]
    blocks = t1.shape[0] // block

    def first(i, _):
        ffn_inner(i, block, t2, rows, binner, kept[0], fi, hl, act, gp)
        return 0

    def second(i, _):
        wo = fa[3].reshape(D, D)
        ffn_outer(i, block, blocks, t2, grad, rows, kept[0], fi, fo, wo, inv, act, gp, ob, y, bg, dos, og, sums, bsum)
        return 0

    lax.fori_loop(0, blocks, first, 0)
    outer_product(0, block, fo, act, ob)
    lax.fori_loop(0, blocks, second, 0)
    res[...] = t2[...]

    def one(j, _):
        tile[...] = mm(act[j], og[...], TN).astype(BF).reshape(2, 4, TR, D)
        copy = pltpu.make_async_copy(tile, g.at[lax.div(j, 2), pl.ds(2 * lax.rem(j, 2), 2), 0:4], gsem.at[0])
        copy.start()
        copy.wait()
        tile[...] = mm(hl[...], gp[j], TN).astype(BF).reshape(2, 4, TR, D)
        copy = pltpu.make_async_copy(tile, g.at[:, :, 4 + j], gsem.at[0])
        copy.start()
        copy.wait()
        return 0

    lax.fori_loop(0, 4, one, 0)


def ffn_local(t1, grad, rows, binner, kept, inv, fi, fo, fa):
    t = t1.shape[0]
    return pl.pallas_call(
        ffn_local_kernel,
        out_shape=(
            shape(t, D), shape(t, D, dtype=F32), shape(t, D), shape(t, D),
            shape(8, D, dtype=F32), shape(1, FF, dtype=F32), shape(2, 4, 8, TR, D),
        ),
        in_specs=[VM] * 4 + [SM] + [VM] * 4,
        out_specs=(VM,) * 6 + (ANY,),
        scratch_shapes=[
            pltpu.VMEM((t, D), BF), pltpu.VMEM((t, D), BF), pltpu.VMEM((4, t, D), BF), pltpu.VMEM((4, t, D), BF),
            pltpu.VMEM((t, D), F32), pltpu.VMEM((256, D), F32), pltpu.VMEM((2, 4, TR, D), BF),
            pltpu.SemaphoreType.DMA((1,)),
        ],
        compiler_params=params(),
        name="ffn_local",
    )(t1, grad, rows, binner, kept, inv, fi, fo, fa)


def backward_local_kernel(x, qkv, e_in, att, dos, bg, res, fa, sums_in, out, gx, go, sums, dqkv, ebuf, esem):
    sums[...] = sums_in[...]
    go[...] = mm(att[...], bg[...], TN).astype(BF).reshape(4, 2, 1, TR, D)

    def one(i, _):
        c, r, pair = place_of(i)
        copy = pltpu.make_async_copy(e_in.at[c, r, pair], ebuf, esem.at[0])
        copy.start()
        copy.wait()
        attend_back(i, qkv, dos, att, ebuf, dqkv)

        @pl.when(lax.rem(i, 4) == 3)
        def _():
            chunk_grads(lax.div(i, 4), x, dqkv, gx, sums)

        return 0

    lax.fori_loop(0, 6 * (x.shape[0] // SEQ), one, 0)
    input_back(res, dqkv, fa, out)


def backward_local(x, qkv, e, att, dos, bg, res, fa, sums):
    t = x.shape[0]
    return pl.pallas_call(
        backward_local_kernel,
        out_shape=(shape(t, D), shape(3, 4, 2, 1, TR, D), shape(4, 2, 1, TR, D), shape(8, D, dtype=F32)),
        in_specs=[VM, VM, ANY] + [VM] * 6,
        out_specs=(VM,) * 4,
        scratch_shapes=[pltpu.VMEM((3, t, D), BF), pltpu.VMEM((2, SEQ, SEQ), BF), pltpu.SemaphoreType.DMA((1,))],
        compiler_params=params(),
        name="backward_local",
    )(x, qkv, e, att, dos, bg, res, fa, sums)


def gather_lax(wq, wk, wv, wo, wi, wr, eight, b_inner):
    def whole(a):
        return lax.all_gather(a.astype(BF), "shard", axis=0, tiled=True)

    wq, wk, wv, wo, wi, wr = (whole(a) for a in (wq, wk, wv, wo, wi, wr))
    chunks = [jnp.concatenate([a[:, c * CW : (c + 1) * CW] for a in (wq, wk, wv)], axis=1) for c in range(3)]
    fa = jnp.stack(chunks + [wo]).reshape(4, 8, TR, D)
    fi = jnp.stack([wi[:, q * D : (q + 1) * D] for q in range(4)]).reshape(4, 8, TR, D)
    rows = jnp.stack([whole(a) for a in eight]).astype(F32)
    return fa, fi, wr.reshape(8, 4, TR, D), rows, whole(b_inner).astype(F32).reshape(1, FF)


def reduce_lax(g, gx, go, sums, bsum):
    g = g.reshape(8, 8, TR, D)
    gr = g[:, 0:4].reshape(FF, D)
    gi = jnp.concatenate([g[:, 4 + j].reshape(D, D) for j in range(4)], axis=1)
    gx = gx.reshape(3, D, 3, CW)
    squares = [jnp.concatenate([gx[c, :, part] for c in range(3)], axis=1) for part in range(3)]

    def owned(a):
        a = lax.psum_scatter(a.astype(F32), "shard", scatter_dimension=0, tiled=True)
        return lax.psum(a.astype(BF), "width").astype(F32)

    matrices = [owned(a) for a in (*squares, go.reshape(D, D), gi, gr)]
    return matrices, [owned(sums[k]) for k in range(8)] + [owned(bsum[0])]


def body(
    layer_input, segment_ids, group_heads,
    w_query, b_query, w_key, w_value, b_value, w_out, b_out, gain_one, shift_one,
    w_inner, b_inner, w_outer, b_outer, gain_two, shift_two, out_grad,
):
    eight = (b_query, b_value, b_out, gain_one, shift_one, b_outer, gain_two, shift_two)
    weights = (w_query, w_key, w_value, w_out, w_inner, w_outer)
    own_kernels = lax.axis_size("width") == 4 and lax.axis_size("shard") == 8
    if own_kernels:
        sums, bsum, fa, qkv, att, e, y, res, bg, dos, hl, og, ai = forward(
            layer_input, segment_ids, group_heads, *weights, eight, b_inner, out_grad
        )
    else:
        fa, fi, fo, rows, binner = gather_lax(*weights, eight, b_inner)
        qkv, att, inv, e, t1 = forward_local(layer_input, segment_ids, group_heads, fa, rows)
        y, res, bg, dos, sums, bsum, g = ffn_local(t1, out_grad, rows, binner, group_heads, inv, fi, fo, fa)
    if own_kernels:
        input_grad, result, ovec = backward(layer_input, qkv, e, att, dos, bg, res, fa, hl, og, ai, sums, bsum)
        gq, gk, gv, go, gi, gr, input_grad, y, *vectors = finish(result, ovec, input_grad, y)
    else:
        input_grad, gx, go, sums = backward_local(layer_input, qkv, e, att, dos, bg, res, fa[0:3], sums)
        (gq, gk, gv, go, gi, gr), vectors = reduce_lax(g, gx, go, sums, bsum)
    return (
        y, input_grad, gq, vectors[0], gk, gv, vectors[1], go, vectors[2],
        vectors[3], vectors[4], gi, vectors[8], gr, vectors[5], vectors[6], vectors[7],
    )


def solution(mesh):
    placed = (
        P(("width", "shard"), None),
        P(("width", "shard"), None),
        P("width"),
        P("shard", None),
        P("shard"),
        P("shard", None),
        P("shard", None),
        P("shard"),
        P("shard", None),
        P("shard"),
        P("shard"),
        P("shard"),
        P("shard", None),
        P("shard"),
        P("shard", None),
        P("shard"),
        P("shard"),
        P("shard"),
        P(("width", "shard"), None),
    )
    return jax.shard_map(
        body,
        mesh=mesh,
        in_specs=placed,
        out_specs=(
            P(("width", "shard"), None),
            P(("width", "shard"), None),
            P("shard", None),
            P("shard"),
            P("shard", None),
            P("shard", None),
            P("shard"),
            P("shard", None),
            P("shard"),
            P("shard"),
            P("shard"),
            P("shard", None),
            P("shard"),
            P("shard", None),
            P("shard"),
            P("shard"),
            P("shard"),
        ),
        check_vma=False,
    )
```

```python
import functools
import jax
import jax.numpy as jnp
from jax import lax
from jax.experimental import pallas as pl
from jax.experimental.pallas import tpu as pltpu
from jax.sharding import PartitionSpec as P

HEADS = 12
HEAD_DIM = 64
FF = 3072
D = 768
SEQ = 512
MESH = pl.DeviceIdType.MESH
BF = jnp.bfloat16
F32 = jnp.float32
TR = 96
CW = 256
NT = (((1,), (1,)), ((), ()))
TN = (((0,), (0,)), ((), ()))
NN = (((1,), (0,)), ((), ()))
EPS = 1e-06
RSQRT2 = 0.7071067811865476
RSQRT2PI = 0.3989422804014327
VM = pl.BlockSpec(memory_space=pltpu.VMEM)
SM = pl.BlockSpec(memory_space=pltpu.SMEM)
ANY = pl.BlockSpec(memory_space=pl.ANY)


def params(**more):
    return pltpu.CompilerParams(vmem_limit_bytes=62 << 20, **more)


def shape(*dims, dtype=BF):
    return jax.ShapeDtypeStruct(dims, dtype)


class Place:
    def __init__(self):
        self.w = w = lax.axis_index("width")
        self.s = s = lax.axis_index("shard")
        self.c = c = lax.rem(s, 2)
        self.z = lax.div(s, 2)
        xw, yw = w + 1 - 2 * lax.rem(w, 2), lax.rem(w + 2, 4)
        up, down = lax.rem(s + 2, 8), lax.rem(s + 6, 8)
        self.wa = jnp.where(c == 0, xw, yw)
        self.wb = jnp.where(c == 0, yw, xw)
        self.wd = 3 - w
        self.sa = jnp.where(c == 0, up, down)
        self.sb = jnp.where(c == 0, down, up)
        self.so = lax.rem(s + 4, 8)
        self.sib = (w, s + 1 - 2 * c)
        self.plane_a, self.plane_b = (self.wa, s), (self.wb, s)
        self.ring_a, self.ring_b = (w, self.sa), (w, self.sb)


def call(devices):
    barrier = pltpu.get_barrier_semaphore()
    for device in devices:
        pl.semaphore_signal(barrier, inc=1, device_id=device, device_id_type=MESH)


def answer(devices):
    pl.semaphore_wait(pltpu.get_barrier_semaphore(), len(devices))


def others(p):
    return [(p.wa, p.s), (p.wb, p.s), (p.wd, p.s)] + [(p.w, lax.rem(p.s + k, 8)) for k in range(1, 8)]


class Net:
    def __init__(self, send, recv):
        self.send, self.recv, self.made, self.sent = send, recv, {}, set()

    def define(self, name, make):
        assert name not in self.made
        self.made[name] = (len(self.made), make)

    def copy(self, name):
        k, make = self.made[name]
        src, dst, device = make()
        return pltpu.make_async_remote_copy(
            src_ref=src, dst_ref=dst, send_sem=self.send.at[k], recv_sem=self.recv.at[k],
            device_id=device, device_id_type=MESH,
        )

    def start(self, *names):
        for name in names:
            self.copy(name).start()

    def wait(self, *names):
        for name in names:
            self.copy(name).wait_recv()

    def finish(self):
        for name in self.made:
            if name not in self.sent:
                self.copy(name).wait_send()


def quarter(w):
    return pl.ds(pl.multiple_of(48 * lax.rem(w, 2), 48), 48), pl.ds(pl.multiple_of(384 * lax.div(w, 2), 384), 384)


def mm(a, b, dims=NN):
    return lax.dot_general(a, b, dims, preferred_element_type=F32)


def rows_of(i, size):
    return pl.ds(pl.multiple_of(i * size, size), size)


def column_mask(kept, shape, width):
    return jnp.where(lax.broadcasted_iota(jnp.int32, shape, 1) < kept * width, 1.0, 0.0).astype(F32)


def mean_of(v):
    return jnp.sum(v, axis=1, keepdims=True) * (1.0 / D)


def norm_rows(total):
    centered = total - mean_of(total)
    inverse = lax.rsqrt(mean_of(centered * centered) + EPS)
    return centered * inverse, inverse


def norm_back(grad, normed, inverse):
    return inverse * (grad - mean_of(grad) - normed * mean_of(grad * normed))


def low_lanes(n):
    return lax.broadcasted_iota(jnp.int32, (n, 128), 1) < HEAD_DIM


def place_of(i):
    return lax.div(i, 4), lax.rem(i, 2), lax.rem(lax.div(i, 2), 2)


def pair_lanes(pair, part):
    return pl.ds(pl.multiple_of(part * CW + pair * 128, 128), 128)


def project(c, x, fa, rows, qkv, block=256):
    lanes = pl.ds(pl.multiple_of(c * CW, CW), CW)
    bias = jnp.concatenate([rows[0:1, lanes], jnp.zeros((1, CW), F32), rows[1:2, lanes]], axis=1)
    scale = jnp.where(lax.broadcasted_iota(jnp.int32, (1, D), 1) < CW, 0.125, 1.0)

    def one(i, _):
        at = rows_of(i, block)
        qkv[c, at] = ((mm(x[at], fa[c].reshape(D, D)) + bias) * scale).astype(BF)
        return 0

    lax.fori_loop(0, x.shape[0] // block, one, 0)


def turn_ids(seg, segt):
    for r in range(seg.shape[0]):
        row = seg[r : r + 1, :].astype(F32)
        segt[r] = jnp.broadcast_to(row, (128, SEQ)).T


def attend(i, qkv, seg, segt, kept, att, inv, ebuf, qb=512):
    c, r, pair = place_of(i)
    base = r * SEQ
    rows = pl.ds(pl.multiple_of(base, SEQ), SEQ)
    kp, vp = qkv[c, rows, pair_lanes(pair, 1)], qkv[c, rows, pair_lanes(pair, 2)]
    low = low_lanes(SEQ)
    ones = jnp.ones_like(vp)
    vs = (jnp.where(low, vp, ones), jnp.where(low, ones, vp))
    ids = seg[pl.ds(r, 1), :].astype(F32)
    lowq = low_lanes(qb)
    lanes = pl.ds(pl.multiple_of(c * CW + pair * 128, 128), 128)
    column = lax.broadcasted_iota(jnp.int32, (1, 128), 1) + (c * CW + pair * 128)
    mask = jnp.where(column < kept * HEAD_DIM, 1.0, 0.0).astype(F32)
    for b in range(SEQ // qb):
        at = pl.ds(pl.multiple_of(base + b * qb, qb), qb)
        qp = qkv[c, at, pair_lanes(pair, 0)]
        zero = jnp.zeros_like(qp)
        own = segt[r, b * qb : (b + 1) * qb]
        same = jnp.concatenate([own == ids[:, j * 128 : (j + 1) * 128] for j in range(4)], axis=1)
        out = []
        for h in range(2):
            qh = jnp.where(lowq, qp, zero) if h == 0 else jnp.where(lowq, zero, qp)
            scores = jnp.where(same, mm(qh, kp, NT), -1e30)
            top = jnp.max(scores, axis=1, keepdims=True)
            e = jnp.exp(scores - top).astype(BF)
            ebuf[h, b * qb : (b + 1) * qb] = e
            out.append(mm(e, vs[h]))
        inverse = 1.0 / pltpu.roll(jnp.where(lowq, out[1], out[0]), HEAD_DIM, 1)
        att[at, lanes] = (jnp.where(lowq, out[0], out[1]) * (inverse * mask)).astype(BF)
        inv[at, lanes] = inverse


def expand_vectors(fv, rows, binner):
    lane = lax.broadcasted_iota(jnp.int32, (128, D), 0)
    column = lax.broadcasted_iota(jnp.int32, (128, D), 1)
    total = jnp.zeros((16, D), F32)
    for s in range(8):
        pick = jnp.where((column == lane + TR * s) & (lane < TR), 1.0, 0.0).astype(BF)
        total = total + mm(fv[s], pick)
        tile = fv[s].astype(F32)
        for r in range(3):
            binner[0:1, 128 * (3 * s + r) : 128 * (3 * s + r + 1)] = tile[8 + r : 9 + r]
    rows[...] = total[0:8]


GROUPS = (slice(0, 1), slice(1, 2), slice(2, 3), slice(3, 4), slice(4, 8), slice(8, 12))
WO, INNER, OUTER = 3, 4, 5
GATHER_COPIES = 16 * len(GROUPS) + 7


def gather_net(p, own, fa, fi, fo, vec, fv, ssem, rsem):
    net = Net(ssem, rsem)
    every = (slice(None), slice(None))

    def piece(g, s, part):
        if g <= WO:
            return fa.at[(GROUPS[g], s, *part)]
        return fi.at[(slice(None), s, *part)] if g == INNER else fo.at[(s, slice(None), *part)]

    mine, first = quarter(p.w), quarter(p.wa)
    for g in range(len(GROUPS)):

        def add(name, src, dst, device):
            net.define((g, *name), lambda: (src(), dst(), device))

        def same(name, g, s, part, device):
            add(name, lambda: piece(g, s, part), lambda: piece(g, s, part), device)

        for name, device in (("zb", p.ring_a), ("za", p.ring_b)):
            add((name,), lambda g=g: own.at[(GROUPS[g], *mine)], lambda g=g: piece(g, p.s, mine), device)
        same(("zo",), g, p.sb, mine, p.ring_a)
        add(("own", "c"), lambda g=g: own.at[GROUPS[g]], lambda g=g: piece(g, p.s, every), p.sib)
        for name, s in (("zb", p.sb), ("za", p.sa), ("zo", p.so)):
            same((name, "xa"), g, s, mine, p.plane_a)
            same((name, "xb"), g, s, mine, p.plane_b)
            same((name, "xd"), g, s, first, p.plane_b)
            same((name, "c"), g, s, every, p.sib)
    for k in range(1, 8):
        net.define(("v", k), lambda k=k: (vec, fv.at[p.s], (p.w, lax.rem(p.s + k, 8))))
    assert len(net.made) == GATHER_COPIES
    return net


def ffn_inner(i, block, t1, rows, binner, kept, wi, hl, act, gp):
    at = rows_of(i, block)
    n1, _ = norm_rows(t1[at])
    low = (n1 * rows[3:4] + rows[4:5]).astype(BF)
    hl[at] = low
    for j in range(4):
        inner = mm(low, wi[j].reshape(D, D)) + binner[:, j * D : (j + 1) * D]
        keep = column_mask(kept * 256 - j * D, (1, D), 1)
        phi = 0.5 + 0.5 * lax.erf(inner * RSQRT2)
        masked = inner * keep
        act[j, at] = (masked * phi).astype(BF)
        gp[j, at] = (keep * phi + masked * (RSQRT2PI * jnp.exp(-0.5 * (inner * inner)))).astype(BF)


def outer_product(i, block, wr, act, ob):
    at = rows_of(i, block)
    outer = jnp.zeros((block, D), F32)
    for j in range(4):
        outer = outer + mm(act[j, at], wr[2 * j : 2 * j + 2].reshape(D, D))
    ob[...] = outer


def ffn_outer(i, block, blocks, t1, grad, rows, kept, wi, wr, wo, inv, act, gp, ob, y, bg, dos, og, sums, bsum):
    at = rows_of(i, block)

    def add(k, value):
        sums[k : k + 1] += jnp.sum(value, axis=0, keepdims=True)

    def outer_weight(j):
        return wr[2 * j : 2 * j + 2].reshape(D, D)

    n1, inv1 = norm_rows(t1[at])
    hidden = n1 * rows[3:4] + rows[4:5]
    n2, inv2 = norm_rows(hidden + (ob[...] + rows[5:6]))
    outer_product(jnp.minimum(i + 1, blocks - 1), block, wr, act, ob)
    y[at] = (n2 * rows[6:7] + rows[7:8]).astype(BF)
    top = grad[at].astype(F32)
    add(7, top)
    add(6, top * n2)
    res2 = norm_back(top * rows[6:7], n2, inv2)
    o = res2.astype(BF)
    og[at] = o
    add(5, o.astype(F32))
    hg = res2
    for j in range(4):
        cols = slice(j * D, (j + 1) * D)
        g = (mm(o, outer_weight(j), NT) * gp[j, at].astype(F32)).astype(BF)
        gp[j, at] = g
        bsum[:, cols] += jnp.sum(g.astype(F32), axis=0, keepdims=True)
        hg = hg + mm(g, wi[j].reshape(D, D), NT)
    add(4, hg)
    add(3, hg * n1)
    res1 = norm_back(hg * rows[3:4], n1, inv1)
    t1[at] = res1
    b = res1.astype(BF)
    bg[at] = b
    add(2, b.astype(F32))
    heads = column_mask(kept, (1, D), HEAD_DIM)
    dos[at] = (mm(b, wo, NT) * (inv[at] * heads)).astype(BF)


def forward_kernel(
    x_in, seg, kept, wq_in, wk_in, wv_in, wo_in, wi_in, wr_in, v0, v1, v2, v3, v4, v5, v6, v7, v_inner, grad_in,
    sums, bsum, fa_out, qkv_out, att_out, e_out, y_out, res_out, bg_out, dos_out, hl_out, og_out, ai_out,
    own, vtile, vec, fa, fi, fo, fv, rows, binner, att, inv, t1, segt, ebuf, grad, y, bg, dos, hl, og, act, gp, ob,
    x, wq, wk, wv, wo, wi, wr, ssem, rsem, lsem, esem, fsem, isem,
):
    qkv = gp.at[0:3]
    p = Place()
    call(others(p))
    arriving = [
        pltpu.make_async_copy(src, dst, isem.at[k])
        for k, (src, dst) in enumerate(
            ((wq_in, wq), (wk_in, wk), (wv_in, wv), (wo_in, wo), (wi_in, wi), (wr_in, wr), (x_in, x))
        )
    ]
    for copy in arriving[0:3]:
        copy.start()

    def cast(c):
        for part, ref in enumerate((wq, wk, wv)):
            own[c, :, part * CW : (part + 1) * CW] = ref[:, c * CW : (c + 1) * CW].astype(BF)

    for copy in arriving[0:3]:
        copy.wait()
    for copy in arriving[3:]:
        copy.start()
    cast(0)
    vtile[...] = jnp.zeros_like(vtile)
    for k, ref in enumerate((v0, v1, v2, v3, v4, v5, v6, v7)):
        vtile[k : k + 1, 0:TR] = ref[...]
    for r in range(3):
        vtile[8 + r : 9 + r] = v_inner[128 * r : 128 * (r + 1)].reshape(1, 128)
    vec[...] = vtile[...].astype(BF)
    answer(others(p))
    net = gather_net(p, own, fa, fi, fo, vec, fv, ssem, rsem)
    names = ("zb", "za", "zo")

    def ring(g):
        net.start((g, "zb"), (g, "za"), (g, "own", "c"))

    def onward(g):
        net.wait((g, "zb"))
        net.start((g, "zo"))

    def plane(g, *which):
        for name in which or names:
            if name != "zb":
                net.wait((g, name))
            net.start((g, name, "xa"), (g, name, "xb"))

    def relay(g, *which):
        for name in which or names:
            net.wait((g, name, "xa"))
            net.start((g, name, "xd"))

    def share(g, *which):
        for name in which or names:
            net.wait((g, name, "xb"), (g, name, "xd"))
            net.start((g, name, "c"))

    def landed(g):
        net.wait((g, "own", "c"), *[(g, name, "c") for name in names])

    ring(0)
    cast(1)
    ring(1)
    cast(2)
    for copy in arriving[3:]:
        copy.wait()
    own[3] = wo[...].astype(BF)
    for q in range(4):
        own[4 + q] = wi[:, q * D : (q + 1) * D].astype(BF)
        own[8 + q] = wr[q * TR : (q + 1) * TR, :].astype(BF)
    net.start(*[("v", k) for k in range(1, 8)])
    local = {}

    def put(name, k, src, dst):
        local[name] = lambda: pltpu.make_async_copy(src(), dst(), lsem.at[k])

    pieces = (
        ("own a", lambda: own.at[0:4], lambda: fa.at[:, p.s]),
        ("own i", lambda: own.at[4:8], lambda: fi.at[:, p.s]),
        ("own o", lambda: own.at[8:12], lambda: fo.at[p.s]),
        ("vec", lambda: vec, lambda: fv.at[p.s]),
        ("grad", lambda: grad_in, lambda: grad),
        ("qkv", lambda: qkv, lambda: qkv_out),
        ("fa", lambda: fa.at[0:3], lambda: fa_out),
        ("att", lambda: att, lambda: att_out),
        ("hl", lambda: hl, lambda: hl_out),
        ("act", lambda: act, lambda: ai_out.at[0:4]),
    )
    for k, (name, src, dst) in enumerate(pieces):
        put(name, k, src, dst)
    for name in ("own a", "own i", "own o", "vec", "grad"):
        local[name]().start()

    onward(0)
    plane(0, "zb", "za")
    onward(1)
    ring(2)
    plane(1, "zb", "za")
    plane(0, "zo")
    turn_ids(seg, segt)
    relay(0, "zb", "za")
    plane(1, "zo")
    relay(1, "zb")
    onward(2)
    ring(WO)
    relay(1, "za")
    plane(2, "zb", "za")
    relay(0, "zo")
    share(0, "zb", "za")
    relay(1, "zo")
    share(1, "zb")
    plane(2, "zo")
    share(1, "za")
    relay(2, "zb")
    onward(WO)
    ring(INNER)
    relay(2, "za")
    share(0, "zo")
    plane(WO, "zb", "za")
    share(1, "zo")
    relay(2, "zo")
    net.wait(*[("v", k) for k in range(1, 8)])
    local["vec"]().wait()
    expand_vectors(fv, rows, binner)
    share(2, "zb")
    plane(WO, "zo")
    local["own a"]().wait()
    keep = kept[0]

    def out_copy(i, slot):
        c, r, pair = place_of(i)
        return pltpu.make_async_copy(ebuf.at[slot], e_out.at[c, r, pair], esem.at[slot])

    before = {0: lambda: landed(0), 4: lambda: landed(1), 8: lambda: landed(2)}
    steps = {
        0: lambda: (share(2, "za", "zo"), relay(WO), onward(INNER), ring(OUTER), plane(INNER, "zb"),),
        1: lambda: (plane(INNER, "za"),),
        2: lambda: (share(WO),),
        4: lambda: (relay(INNER, "zb"), plane(INNER, "zo"),),
        5: lambda: (onward(OUTER), plane(OUTER, "zb"),),
        6: lambda: (relay(INNER, "za"),),
        8: lambda: (share(INNER, "zb"), relay(INNER, "zo"), plane(OUTER, "za"),),
        9: lambda: (plane(OUTER, "zo"),),
        10: lambda: (relay(OUTER, "zb"),),
    }
    later = {
        0: lambda: (share(OUTER, "zb"),),
        1: lambda: (share(OUTER, "za", "zo"),),
    }

    def after_residual():
        relay(OUTER, "za")
        share(INNER, "za")
        relay(OUTER, "zo")
        share(INNER, "zo")

    def at_step(i, table):
        for k, step in table.items():
            @pl.when(i == k)
            def _(step=step):
                step()

    def one(i, _):
        slot = lax.rem(i, 2)

        @pl.when(i >= 2)
        def _():
            out_copy(i - 2, slot).wait()

        at_step(i, before)

        @pl.when(lax.rem(i, 4) == 0)
        def _():
            project(lax.div(i, 4), x, fa, rows, qkv)

        attend(i, qkv, seg, segt, keep, att, inv, ebuf.at[slot])
        out_copy(i, slot).start()
        at_step(i, steps)
        return 0

    n = 6 * (x.shape[0] // SEQ)
    lax.fori_loop(0, n, one, 0)
    local["qkv"]().start()
    local["att"]().start()
    local["fa"]().start()
    sums[...] = jnp.zeros_like(sums)
    bsum[...] = jnp.zeros_like(bsum)
    landed(WO)
    block = 256
    blocks = x.shape[0] // block

    def residual(i, _):
        at = rows_of(i, block)
        t1[at] = x[at].astype(F32) + (mm(att[at], fa[3].reshape(D, D)) + rows[2:3])
        return 0

    lax.fori_loop(0, blocks, residual, 0)
    after_residual()
    landed(INNER)
    local["own i"]().wait()
    local["qkv"]().wait()

    def first(i, _):
        ffn_inner(i, block, t1, rows, binner, keep, fi, hl, act, gp)
        at_step(i, later)
        return 0

    lax.fori_loop(0, blocks, first, 0)
    local["hl"]().start()
    local["act"]().start()
    landed(OUTER)
    local["own o"]().wait()
    local["grad"]().wait()

    def flush(i):
        at = rows_of(i, block)
        pairs = (
            (gp.at[:, at], ai_out.at[4:8, at]), (og.at[at], og_out.at[at]), (dos.at[at], dos_out.at[at]),
            (bg.at[at], bg_out.at[at]), (t1.at[at], res_out.at[at]), (y.at[at], y_out.at[at]),
        )
        return [pltpu.make_async_copy(src, dst, fsem.at[i, k]) for k, (src, dst) in enumerate(pairs)]

    def second(i, _):
        wo = fa[3].reshape(D, D)
        ffn_outer(i, block, blocks, t1, grad, rows, keep, fi, fo, wo, inv, act, gp, ob, y, bg, dos, og, sums, bsum)
        for copy in flush(i):
            copy.start()
        return 0

    outer_product(0, block, fo, act, ob)
    lax.fori_loop(0, blocks, second, 0)
    out_copy(n - 2, (n - 2) % 2).wait()
    out_copy(n - 1, (n - 1) % 2).wait()
    for name in ("fa", "att", "hl", "act"):
        local[name]().wait()
    for i in range(blocks):
        for copy in flush(i):
            copy.wait()
    net.finish()


def forward(x, seg, kept, wq, wk, wv, wo, wi, wr, eight, b_inner, grad):
    t = x.shape[0]
    n = t // SEQ
    return pl.pallas_call(
        forward_kernel,
        out_shape=(
            shape(8, D, dtype=F32), shape(1, FF, dtype=F32), shape(3, 8, TR, D), shape(3, t, D), shape(t, D),
            shape(3, n, 2, 2, SEQ, SEQ), shape(t, D), shape(t, D, dtype=F32), shape(t, D), shape(t, D), shape(t, D),
            shape(t, D), shape(8, t, D),
        ),
        in_specs=[ANY, VM, SM] + [ANY] * 6 + [VM] * 9 + [ANY],
        out_specs=(VM, VM) + (ANY,) * 11,
        scratch_shapes=[
            pltpu.VMEM((12, TR, D), BF),
            pltpu.VMEM((16, 128), F32),
            pltpu.VMEM((16, 128), BF),
            pltpu.VMEM((4, 8, TR, D), BF),
            pltpu.VMEM((4, 8, TR, D), BF),
            pltpu.VMEM((8, 4, TR, D), BF),
            pltpu.VMEM((8, 16, 128), BF),
            pltpu.VMEM((8, D), F32),
            pltpu.VMEM((1, FF), F32),
            pltpu.VMEM((t, D), BF),
            pltpu.VMEM((t, D), F32),
            pltpu.VMEM((t, D), F32),
            pltpu.VMEM((n, SEQ, 128), F32),
            pltpu.VMEM((2, 2, SEQ, SEQ), BF),
        ]
        + [pltpu.VMEM((t, D), BF)] * 6
        + [pltpu.VMEM((4, t, D), BF)] * 2
        + [
            pltpu.VMEM((256, D), F32),
            pltpu.VMEM((t, D), BF),
            *[pltpu.VMEM((TR, D), F32)] * 4,
            pltpu.VMEM((TR, FF), F32),
            pltpu.VMEM((4 * TR, D), F32),
            pltpu.SemaphoreType.DMA((GATHER_COPIES,)),
            pltpu.SemaphoreType.DMA((GATHER_COPIES,)),
            pltpu.SemaphoreType.DMA((10,)),
            pltpu.SemaphoreType.DMA((2,)),
            pltpu.SemaphoreType.DMA((t // 256, 6)),
            pltpu.SemaphoreType.DMA((7,)),
        ],
        compiler_params=params(collective_id=0, has_side_effects=True),
        name="forward",
    )(x, seg, kept, wq, wk, wv, wo, wi, wr, *(a.reshape(1, TR) for a in eight), b_inner, grad)


def attend_back(i, qkv, dos, att, ebuf, dqkv):
    c, r, pair = place_of(i)
    rows = rows_of(r, SEQ)
    lanes = pl.ds(pl.multiple_of(c * CW + pair * 128, 128), 128)
    qp, kp, vp = (qkv[c, rows, pair_lanes(pair, part)] for part in range(3))
    dp = dos[rows, lanes]
    low = low_lanes(SEQ)
    zero = jnp.zeros_like(qp)
    product = dp.astype(F32) * att[rows, lanes].astype(F32)
    gq = jnp.zeros((SEQ, 128), F32)
    gk = jnp.zeros((SEQ, 128), F32)
    gv = jnp.zeros((SEQ, 128), F32)
    for h in range(2):
        mine = low if h == 0 else jnp.logical_not(low)
        dh = jnp.where(mine, dp, zero)
        delta = jnp.sum(jnp.where(mine, product, 0.0), axis=1, keepdims=True)
        e = ebuf[h]
        ds = (e.astype(F32) * (mm(dh, vp, NT) - delta)).astype(BF)
        gv = gv + mm(e, dh, TN)
        gk = gk + mm(ds, jnp.where(mine, qp, zero), TN)
        gq = gq + mm(ds, jnp.where(mine, kp, zero))
    dqkv[c, rows, pair_lanes(pair, 0)] = (gq * 0.125).astype(BF)
    dqkv[c, rows, pair_lanes(pair, 1)] = gk.astype(BF)
    dqkv[c, rows, pair_lanes(pair, 2)] = gv.astype(BF)


def chunk_grads(c, x, dqkv, gx, sums):
    gx[c] = mm(x[...], dqkv[c], TN).astype(BF).reshape(4, 2, 1, TR, D)
    part = dqkv[c].astype(F32)
    total = jnp.sum(part, axis=0, keepdims=True)
    lanes = pl.ds(pl.multiple_of(c * CW, CW), CW)
    sums[0:1, lanes] = total[:, 0:CW]
    sums[1:2, lanes] = total[:, 2 * CW :]


def input_back(res, dqkv, fa, out, block=256):
    def one(i, _):
        at = rows_of(i, block)
        total = res[at]
        for c in range(3):
            total = total + mm(dqkv[c, at], fa[c].reshape(D, D), NT)
        out[at] = total.astype(BF)
        return 0

    lax.fori_loop(0, res.shape[0] // block, one, 0)


JOBS = (
    (4, 1, False),
    (5, 1, True),
    (6, 1, True),
    (7, 1, False),
    (0, 2, True),
    (2, 2, False),
    (8, 1, False),
    (9, 1, False),
    (10, 1, False),
    (11, 1, False),
)
OUTER_UNITS = 4
REDUCE_COPIES = 9 * len(JOBS) + sum(first >= OUTER_UNITS for first, _, _ in JOBS) + 4 + 7


def job_shapes(units, ring_first):
    part, tile = (units, 48, 384), (units, TR, D)
    first = tile if ring_first else (4, *part)
    return [first, first, first, first, part, part, part]


class Job:
    def __init__(self, net, p, k, first, units, ring_first, held, landed, arrivals, bufs, result):
        self.net, self.p, self.k = net, p, k
        self.held, self.landed, self.arrivals = held, landed, arrivals
        self.d1, self.a1, self.b1, self.mid, self.d2, self.a2, self.b2 = bufs
        self.result = result
        self.units = slice(first, first + units)
        held, mid = self.held, self.mid
        z, za, zb, zo = p.z, lax.div(p.sa, 2), lax.div(p.sb, 2), lax.div(p.so, 2)
        self.z = z
        ring = (za, zb, zo, p.ring_a, p.ring_a, p.ring_b)
        plane = (p.wb, p.wa, p.wd, p.plane_a, p.plane_b, p.plane_a)

        def tile(t):
            return held, (t,)

        def plane_quarter(w):
            return held, (slice(None), slice(None), *quarter(w))

        def mid_quarter(w):
            return mid, (slice(None), *quarter(w))

        def mid_tile(t):
            return mid, (t,)

        one, two = (ring, plane) if ring_first else (plane, ring)
        self.at1, self.at2 = (tile, mid_quarter) if ring_first else (plane_quarter, mid_tile)
        self.one, self.two = one, two
        self.own1 = z if ring_first else p.w
        self.own2 = p.w if ring_first else z
        for stage, at, way, d, a, b in ((1, self.at1, one, self.d1, self.a1, self.b1), (2, self.at2, two, self.d2, self.a2, self.b2)):
            relayed, direct, opposite, dev_o, dev_r, dev_d = way

            def send(name, index, dst, device, at=at):
                def make():
                    ref, where = at(index)
                    return ref.at[where], dst, device

                net.define((k, *name), make)

            send(("d", stage), opposite, d, dev_o)
            send(("b", stage), direct, b, dev_d)
            send(("a", stage), relayed, a, dev_r)

        def share(name, w, device):
            def make():
                ref = result.at[(self.units, *quarter(w))]
                return ref, ref, device

            net.define((k, name), make)

        share("ga", p.w, p.plane_a)
        share("gb", p.w, p.plane_b)
        share("gd", p.wa, p.plane_b)

    def names(self, names):
        return [(self.k, *name) if isinstance(name, tuple) else (self.k, name) for name in names]

    def start(self, *names):
        self.net.start(*self.names(names))

    def wait(self, *names):
        self.net.wait(*self.names(names))

    def send(self):
        self.net.start(*self.arrivals)

    def pair(self):
        self.net.wait(*self.arrivals)
        held, landed = self.held, self.landed

        def one(t, _):
            held[t] = (held[t].astype(F32) + landed[t].astype(F32)).astype(BF)
            return 0

        lax.fori_loop(0, 4, one, 0)
        self.start(("d", 1), ("b", 1))

    def relay(self, stage):
        at, way, d = (self.at1, self.one, self.d1) if stage == 1 else (self.at2, self.two, self.d2)
        self.wait(("d", stage))
        ref, where = at(way[0])
        ref[where] = (ref[where].astype(F32) + d[...].astype(F32)).astype(BF)
        self.start(("a", stage))

    def total(self, stage):
        at, own, a, b = (self.at1, self.own1, self.a1, self.b1) if stage == 1 else (self.at2, self.own2, self.a2, self.b2)
        self.wait(("a", stage), ("b", stage))
        ref, where = at(own)
        return (ref[where].astype(F32) + a[...].astype(F32) + b[...].astype(F32)).astype(BF)

    def turn(self):
        self.mid[...] = self.total(1)
        self.start(("d", 2), ("b", 2))

    def share(self):
        self.result[(self.units, *quarter(self.p.w))] = self.total(2)
        self.start("ga", "gb")

    def pass_on(self):
        self.wait("ga")
        self.start("gd")

    def end(self):
        self.wait("gb", "gd")


def backward_kernel(
    x_in, qkv_in, e_in, att_in, dos_in, bg_in, res_in, fa_in, hl_in, og_in, ai_in, sums_in, bsum,
    out, result, ovec,
    x, qkv, att, dos, bg, res, fa, dqkv, gx, go, ebuf, sums, vt, vheld, vrecv, vplane, vz, *rest,
):
    bufs, (ssem, rsem, lsem, esem) = rest[:-4], rest[-4:]
    p = Place()
    call(others(p))
    n = 6 * (x.shape[0] // SEQ)
    og, hl = dqkv.at[0], dqkv.at[1]
    loads = (
        ("og", lambda: og_in, lambda: og),
        ("hl", lambda: hl_in, lambda: hl),
        ("att", lambda: att_in, lambda: att),
        ("bg", lambda: bg_in, lambda: bg),
        ("qkv", lambda: qkv_in, lambda: qkv),
        ("dos", lambda: dos_in, lambda: dos),
        ("res", lambda: res_in, lambda: res),
        ("fa", lambda: fa_in, lambda: fa.at[0:3]),
        ("x", lambda: x_in, lambda: x),
    )
    load = {
        name: lambda k=k, src=src, dst=dst: pltpu.make_async_copy(src(), dst(), lsem.at[k])
        for k, (name, src, dst) in enumerate(loads)
    }

    def block_copy(j):
        return pltpu.make_async_copy(ai_in.at[(j + 4) % 8], qkv.at[j % 3], lsem.at[len(loads) + j % 3])

    def in_copy(i, slot):
        c, r, pair = place_of(i)
        return pltpu.make_async_copy(e_in.at[c, r, pair], ebuf.at[slot], esem.at[slot])

    load["hl"]().start()
    block_copy(0).start()
    block_copy(1).start()
    load["og"]().start()

    def staged(j):
        return fa.at[j // 2, 4 * (j % 2) : 4 * (j % 2) + 4]

    net = Net(ssem, rsem)
    held_outer, landed_outer, held_rest, landed_rest = bufs[0:4]
    jobs = []
    per = 7
    outer_arrivals = [("o", j) for j in range(4)]
    for j in range(4):
        net.define(("o", j), lambda j=j: (staged(4 + j), landed_outer.at[j], p.sib))
    for k, (first, units, ring_first) in enumerate(JOBS):
        if first < OUTER_UNITS:
            held, landed = held_outer.at[:, first : first + units], landed_outer.at[:, first : first + units]
            arrivals = outer_arrivals
            outer_arrivals = []
        else:
            r = first - OUTER_UNITS
            held, landed = held_rest.at[r], landed_rest.at[r]
            arrivals = [(k, "c")]
            if r < 4:
                source = lambda r=r: staged(r)
            elif r == 4:
                source = lambda: go.at[:, 1 - p.c, 0]
            else:
                source = lambda c=r - 5: gx.at[c, :, 1 - p.c, 0]
            net.define((k, "c"), lambda source=source, landed=landed: (source(), landed.at[:, 0], p.sib))
        job_bufs = bufs[4 + per * k : 4 + per * (k + 1)]
        jobs.append(Job(net, p, k, first, units, ring_first, held, landed, arrivals, job_bufs, result))
    net.define(("v", "c"), lambda: (vt.at[:, 1 - p.c], vrecv, p.sib))
    for k, device in enumerate((p.plane_a, p.plane_b, (p.wd, p.s))):
        net.define(("v", "p", k), lambda device=device: (vheld.at[0], vplane.at[p.w], device))
    for k in range(1, 4):
        to = lax.rem(p.z + k, 4)
        net.define(("v", "z", k), lambda to=to: (vheld.at[1, to], vz.at[p.z], (p.w, 2 * to + p.c)))
    assert len(net.made) == REDUCE_COPIES, len(net.made)

    def own_half(k, source):
        jobs[k].held[...] = source[:, p.c]

    def begin(k):
        first = JOBS[k][0]
        if first == 8:
            own_half(k, go)
        elif first > 8:
            own_half(k, gx.at[first - 9])
        jobs[k].pair()

    first_core = p.c == 0
    after = {
        0: lambda: (jobs[0].send(),),
        1: lambda: (jobs[1].send(),),
        2: lambda: (jobs[2].send(),),
        3: lambda: (jobs[3].send(), begin(0),),
        4: lambda: (net.start(("o", 0)), begin(1),),
        5: lambda: (net.start(("o", 1)), begin(2),),
        6: lambda: (net.start(("o", 2)), jobs[0].relay(1), begin(3),),
        7: lambda: (net.start(("o", 3)),),
    }
    for j in range(8):
        if j == 0:
            load["hl"]().wait()
        if j == 4:
            load["og"]().wait()
        block_copy(j).wait()
        if j + 2 < 8:
            block_copy(j + 2).start()
        if j == 2:
            for name in ("att", "bg", "dos"):
                load[name]().start()
            in_copy(0, 0).start()
        if j == 4:
            load["res"]().start()
            load["x"]().start()
        block = qkv.at[j % 3]
        if j < 4:
            tiles = mm(hl[...], block[...], TN).astype(BF).reshape(4, 2, TR, D)
            zero, one = tiles[:, 0], tiles[:, 1]
            held_rest[j, :, 0] = jnp.where(first_core, zero, one)
        else:
            tiles = mm(block[...], og[...], TN).astype(BF).reshape(2, 4, TR, D)
            zero, one = tiles[0], tiles[1]
            held_outer[j - 4] = jnp.where(first_core, zero, one)
        staged(j)[...] = jnp.where(first_core, one, zero)
        if j == 0:
            answer(others(p))
        if j in after:
            after[j]()
    load["qkv"]().start()
    sums[...] = sums_in[...]
    load["att"]().wait()
    load["bg"]().wait()
    go[...] = mm(att[...], bg[...], TN).astype(BF).reshape(4, 2, 1, TR, D)
    jobs[6].send()
    load["qkv"]().wait()
    load["dos"]().wait()
    load["x"]().wait()
    steps = {
        1: lambda: (jobs[0].turn(), jobs[1].relay(1), jobs[3].relay(1), begin(4), begin(5),),
        2: lambda: (begin(6),),
        3: lambda: (jobs[7].send(), jobs[2].relay(1), jobs[0].relay(2), jobs[3].turn(),),
        5: lambda: (jobs[5].relay(1),),
        6: lambda: (begin(7),),
        7: lambda: (jobs[8].send(), jobs[1].turn(),),
        8: lambda: (jobs[6].relay(1),),
    }

    def one(i, _):
        slot = lax.rem(i, 2)

        @pl.when(i + 1 < n)
        def _():
            in_copy(i + 1, 1 - slot).start()

        in_copy(i, slot).wait()
        attend_back(i, qkv, dos, att, ebuf.at[slot], dqkv)

        @pl.when(lax.rem(i, 4) == 3)
        def _():
            chunk_grads(lax.div(i, 4), x, dqkv, gx, sums)

        for k, step in steps.items():
            @pl.when(i == k)
            def _(step=step):
                step()
        return 0

    lax.fori_loop(0, n, one, 0)
    jobs[9].send()
    jobs[5].turn()
    jobs[7].relay(1)
    begin(8)
    jobs[4].relay(1)
    jobs[6].turn()
    staged_names = [(k, "c") for k, job in enumerate(JOBS) if 4 <= job[0] < 8] + [("o", j) for j in range(4)]
    for name in staged_names:
        net.copy(name).wait_send()
        net.sent.add(name)
    load["fa"]().start()

    for s in range(8):
        vt[s // 2, s % 2] = jnp.zeros((16, 128), F32)
        vt[s // 2, s % 2, 0:8, 0:TR] = sums[:, TR * s : TR * (s + 1)]
        for r in range(3):
            vt[s // 2, s % 2, 8 + r : 9 + r] = bsum[0:1, 128 * (3 * s + r) : 128 * (3 * s + r + 1)]
    net.start(("v", "c"))
    load["res"]().wait()

    def back(i):
        at = pl.ds(256 * i, 256)
        total = res[at]
        for c in range(3):
            total = total + mm(dqkv[c, at], fa[c].reshape(D, D), NT)
        out[at] = total.astype(BF)

    load["fa"]().wait()
    back(0)
    jobs[1].relay(2)
    net.wait(("v", "c"))
    vheld[0] = vt[:, p.c] + vrecv[...]
    vplane[p.w] = vheld[0]
    net.start(*[("v", "p", k) for k in range(3)])
    back(1)
    jobs[2].turn()
    back(2)
    jobs[0].share()
    begin(9)
    net.wait(*[("v", "p", k) for k in range(3)])
    vheld[1] = (vplane[0] + vplane[1]) + (vplane[2] + vplane[3])
    vz[p.z] = vheld[1, p.z]
    net.start(*[("v", "z", k) for k in range(1, 4)])
    back(3)
    jobs[3].relay(2)
    jobs[7].turn()
    jobs[8].relay(1)
    jobs[1].share()
    jobs[5].relay(2)
    jobs[2].relay(2)
    jobs[0].pass_on()
    jobs[9].relay(1)
    jobs[8].turn()
    jobs[2].share()
    jobs[4].turn()
    jobs[6].relay(2)
    jobs[1].pass_on()
    jobs[3].share()
    jobs[7].relay(2)
    jobs[9].turn()
    jobs[2].pass_on()
    jobs[5].share()
    jobs[4].relay(2)
    jobs[8].relay(2)
    jobs[6].share()
    jobs[7].share()
    jobs[3].pass_on()
    jobs[9].relay(2)
    jobs[5].pass_on()
    jobs[8].share()
    jobs[6].pass_on()
    jobs[4].share()
    jobs[7].pass_on()
    net.wait(*[("v", "z", k) for k in range(1, 4)])
    ovec[...] = (vz[0] + vz[1]) + (vz[2] + vz[3])
    jobs[9].share()
    jobs[8].pass_on()
    jobs[4].pass_on()
    jobs[9].pass_on()
    for job in jobs:
        job.end()
    net.finish()


def backward(x, qkv, e, att, dos, bg, res, fa, hl, og, ai, sums, bsum):
    t = x.shape[0]
    job_scratch = [pltpu.VMEM(s, BF) for s in ((4, 4, TR, D),) * 2 + ((8, 4, 1, TR, D),) * 2]
    job_scratch += [pltpu.VMEM(s, BF) for _, units, ring_first in JOBS for s in job_shapes(units, ring_first)]
    return pl.pallas_call(
        backward_kernel,
        out_shape=(shape(t, D), shape(12, TR, D), shape(16, 128, dtype=F32)),
        in_specs=[ANY] * 11 + [VM, VM],
        out_specs=(VM,) * 3,
        scratch_shapes=[
            pltpu.VMEM((t, D), BF),
            pltpu.VMEM((3, t, D), BF),
            pltpu.VMEM((t, D), BF),
            pltpu.VMEM((t, D), BF),
            pltpu.VMEM((t, D), BF),
            pltpu.VMEM((t, D), F32),
            pltpu.VMEM((4, 8, TR, D), BF),
            pltpu.VMEM((3, t, D), BF),
            pltpu.VMEM((3, 4, 2, 1, TR, D), BF),
            pltpu.VMEM((4, 2, 1, TR, D), BF),
            pltpu.VMEM((2, 2, SEQ, SEQ), BF),
            pltpu.VMEM((8, D), F32),
            pltpu.VMEM((4, 2, 16, 128), F32),
            pltpu.VMEM((2, 4, 16, 128), F32),
            pltpu.VMEM((4, 16, 128), F32),
            pltpu.VMEM((4, 4, 16, 128), F32),
            pltpu.VMEM((4, 16, 128), F32),
        ]
        + job_scratch
        + [
            pltpu.SemaphoreType.DMA((REDUCE_COPIES,)),
            pltpu.SemaphoreType.DMA((REDUCE_COPIES,)),
            pltpu.SemaphoreType.DMA((12,)),
            pltpu.SemaphoreType.DMA((2,)),
        ],
        compiler_params=params(collective_id=1, has_side_effects=True),
        name="backward",
    )(x, qkv, e, att, dos, bg, res, fa, hl, og, ai, sums, bsum)


def finish_kernel(result, ovec, inp, y, oq, ok, ov, oo, oi, our, out, y_out, *vectors):
    for c in range(3):
        tile = result[9 + c].astype(F32)
        for part, ref in enumerate((oq, ok, ov)):
            ref[:, c * CW : (c + 1) * CW] = tile[:, part * CW : (part + 1) * CW]
    oo[...] = result[8].astype(F32)
    for q in range(4):
        oi[:, q * D : (q + 1) * D] = result[4 + q].astype(F32)
        our[q] = result[q].astype(F32)
    out[...] = inp[...]
    y_out[...] = y[...]
    for k in range(8):
        vectors[k][...] = ovec[k, 0:TR]
    for r in range(3):
        vectors[8][128 * r : 128 * (r + 1)] = ovec[8 + r]


def finish(result, ovec, inp, y):
    t = inp.shape[0]
    steps = 2
    rows = TR // steps

    def part(*dims):
        at = len(dims) - 2
        return pl.BlockSpec(dims, lambda h: tuple(h if k == at else 0 for k in range(len(dims))))

    def vector(n):
        return pl.BlockSpec((n,), lambda h: (0,))

    *outs, gr, out, y, v0, v1, v2, v3, v4, v5, v6, v7, v8 = pl.pallas_call(
        finish_kernel,
        grid=(steps,),
        out_shape=tuple(shape(TR, D, dtype=F32) for _ in range(4))
        + (shape(TR, FF, dtype=F32), shape(4, TR, D, dtype=F32), shape(t, D), shape(t, D))
        + tuple(shape(TR, dtype=F32) for _ in range(8))
        + (shape(4 * TR, dtype=F32),),
        in_specs=[part(12, rows, D), pl.BlockSpec((16, 128), lambda h: (0, 0)), part(t // steps, D), part(t // steps, D)],
        out_specs=(part(rows, D),) * 4
        + (part(rows, FF), part(4, rows, D), part(t // steps, D), part(t // steps, D))
        + (vector(TR),) * 8
        + (vector(4 * TR),),
        compiler_params=params(),
        name="finish",
    )(result, ovec, inp, y)
    return *outs, gr.reshape(4 * TR, D), out, y, v0, v1, v2, v3, v4, v5, v6, v7, v8


def forward_local_kernel(x, seg, kept, fa, rows, qkv, att, inv, e_out, t1, segt, ebuf, esem):
    turn_ids(seg, segt)
    for c in range(3):
        project(c, x, fa, rows, qkv)
    keep = kept[0]

    def one(i, _):
        c, r, pair = place_of(i)
        attend(i, qkv, seg, segt, keep, att, inv, ebuf)
        copy = pltpu.make_async_copy(ebuf, e_out.at[c, r, pair], esem.at[0])
        copy.start()
        copy.wait()
        return 0

    lax.fori_loop(0, 6 * (x.shape[0] // SEQ), one, 0)
    t1[...] = x[...].astype(F32) + (mm(att[...], fa[3].reshape(D, D)) + rows[2:3])


def forward_local(x, seg, kept, fa, rows):
    t = x.shape[0]
    n = t // SEQ
    return pl.pallas_call(
        forward_local_kernel,
        out_shape=(shape(3, t, D), shape(t, D), shape(t, D, dtype=F32), shape(3, n, 2, 2, SEQ, SEQ), shape(t, D, dtype=F32)),
        in_specs=[VM, VM, SM, VM, VM],
        out_specs=(VM, VM, VM, ANY, VM),
        scratch_shapes=[
            pltpu.VMEM((n, SEQ, 128), F32), pltpu.VMEM((2, SEQ, SEQ), BF), pltpu.SemaphoreType.DMA((1,)),
        ],
        compiler_params=params(),
        name="forward_local",
    )(x, seg, kept, fa, rows)


def ffn_local_kernel(
    t1, grad, rows, binner, kept, inv, fi, fo, fa, y, res, bg, dos, sums, bsum, g, hl, og, act, gp, t2, ob, tile, gsem, block=256
):
    sums[...] = jnp.zeros_like(sums)
    bsum[...] = jnp.zeros_like(bsum)
    t2[...] = t1[...]
    blocks = t1.shape[0] // block

    def first(i, _):
        ffn_inner(i, block, t2, rows, binner, kept[0], fi, hl, act, gp)
        return 0

    def second(i, _):
        wo = fa[3].reshape(D, D)
        ffn_outer(i, block, blocks, t2, grad, rows, kept[0], fi, fo, wo, inv, act, gp, ob, y, bg, dos, og, sums, bsum)
        return 0

    lax.fori_loop(0, blocks, first, 0)
    outer_product(0, block, fo, act, ob)
    lax.fori_loop(0, blocks, second, 0)
    res[...] = t2[...]

    def one(j, _):
        tile[...] = mm(act[j], og[...], TN).astype(BF).reshape(2, 4, TR, D)
        copy = pltpu.make_async_copy(tile, g.at[lax.div(j, 2), pl.ds(2 * lax.rem(j, 2), 2), 0:4], gsem.at[0])
        copy.start()
        copy.wait()
        tile[...] = mm(hl[...], gp[j], TN).astype(BF).reshape(2, 4, TR, D)
        copy = pltpu.make_async_copy(tile, g.at[:, :, 4 + j], gsem.at[0])
        copy.start()
        copy.wait()
        return 0

    lax.fori_loop(0, 4, one, 0)


def ffn_local(t1, grad, rows, binner, kept, inv, fi, fo, fa):
    t = t1.shape[0]
    return pl.pallas_call(
        ffn_local_kernel,
        out_shape=(
            shape(t, D), shape(t, D, dtype=F32), shape(t, D), shape(t, D),
            shape(8, D, dtype=F32), shape(1, FF, dtype=F32), shape(2, 4, 8, TR, D),
        ),
        in_specs=[VM] * 4 + [SM] + [VM] * 4,
        out_specs=(VM,) * 6 + (ANY,),
        scratch_shapes=[
            pltpu.VMEM((t, D), BF), pltpu.VMEM((t, D), BF), pltpu.VMEM((4, t, D), BF), pltpu.VMEM((4, t, D), BF),
            pltpu.VMEM((t, D), F32), pltpu.VMEM((256, D), F32), pltpu.VMEM((2, 4, TR, D), BF),
            pltpu.SemaphoreType.DMA((1,)),
        ],
        compiler_params=params(),
        name="ffn_local",
    )(t1, grad, rows, binner, kept, inv, fi, fo, fa)


def backward_local_kernel(x, qkv, e_in, att, dos, bg, res, fa, sums_in, out, gx, go, sums, dqkv, ebuf, esem):
    sums[...] = sums_in[...]
    go[...] = mm(att[...], bg[...], TN).astype(BF).reshape(4, 2, 1, TR, D)

    def one(i, _):
        c, r, pair = place_of(i)
        copy = pltpu.make_async_copy(e_in.at[c, r, pair], ebuf, esem.at[0])
        copy.start()
        copy.wait()
        attend_back(i, qkv, dos, att, ebuf, dqkv)

        @pl.when(lax.rem(i, 4) == 3)
        def _():
            chunk_grads(lax.div(i, 4), x, dqkv, gx, sums)

        return 0

    lax.fori_loop(0, 6 * (x.shape[0] // SEQ), one, 0)
    input_back(res, dqkv, fa, out)


def backward_local(x, qkv, e, att, dos, bg, res, fa, sums):
    t = x.shape[0]
    return pl.pallas_call(
        backward_local_kernel,
        out_shape=(shape(t, D), shape(3, 4, 2, 1, TR, D), shape(4, 2, 1, TR, D), shape(8, D, dtype=F32)),
        in_specs=[VM, VM, ANY] + [VM] * 6,
        out_specs=(VM,) * 4,
        scratch_shapes=[pltpu.VMEM((3, t, D), BF), pltpu.VMEM((2, SEQ, SEQ), BF), pltpu.SemaphoreType.DMA((1,))],
        compiler_params=params(),
        name="backward_local",
    )(x, qkv, e, att, dos, bg, res, fa, sums)


def gather_lax(wq, wk, wv, wo, wi, wr, eight, b_inner):
    def whole(a):
        return lax.all_gather(a.astype(BF), "shard", axis=0, tiled=True)

    wq, wk, wv, wo, wi, wr = (whole(a) for a in (wq, wk, wv, wo, wi, wr))
    chunks = [jnp.concatenate([a[:, c * CW : (c + 1) * CW] for a in (wq, wk, wv)], axis=1) for c in range(3)]
    fa = jnp.stack(chunks + [wo]).reshape(4, 8, TR, D)
    fi = jnp.stack([wi[:, q * D : (q + 1) * D] for q in range(4)]).reshape(4, 8, TR, D)
    rows = jnp.stack([whole(a) for a in eight]).astype(F32)
    return fa, fi, wr.reshape(8, 4, TR, D), rows, whole(b_inner).astype(F32).reshape(1, FF)


def reduce_lax(g, gx, go, sums, bsum):
    g = g.reshape(8, 8, TR, D)
    gr = g[:, 0:4].reshape(FF, D)
    gi = jnp.concatenate([g[:, 4 + j].reshape(D, D) for j in range(4)], axis=1)
    gx = gx.reshape(3, D, 3, CW)
    squares = [jnp.concatenate([gx[c, :, part] for c in range(3)], axis=1) for part in range(3)]

    def owned(a):
        a = lax.psum_scatter(a.astype(F32), "shard", scatter_dimension=0, tiled=True)
        return lax.psum(a.astype(BF), "width").astype(F32)

    matrices = [owned(a) for a in (*squares, go.reshape(D, D), gi, gr)]
    return matrices, [owned(sums[k]) for k in range(8)] + [owned(bsum[0])]


def body(
    layer_input, segment_ids, group_heads,
    w_query, b_query, w_key, w_value, b_value, w_out, b_out, gain_one, shift_one,
    w_inner, b_inner, w_outer, b_outer, gain_two, shift_two, out_grad,
):
    eight = (b_query, b_value, b_out, gain_one, shift_one, b_outer, gain_two, shift_two)
    weights = (w_query, w_key, w_value, w_out, w_inner, w_outer)
    own_kernels = lax.axis_size("width") == 4 and lax.axis_size("shard") == 8
    if own_kernels:
        sums, bsum, fa, qkv, att, e, y, res, bg, dos, hl, og, ai = forward(
            layer_input, segment_ids, group_heads, *weights, eight, b_inner, out_grad
        )
    else:
        fa, fi, fo, rows, binner = gather_lax(*weights, eight, b_inner)
        qkv, att, inv, e, t1 = forward_local(layer_input, segment_ids, group_heads, fa, rows)
        y, res, bg, dos, sums, bsum, g = ffn_local(t1, out_grad, rows, binner, group_heads, inv, fi, fo, fa)
    if own_kernels:
        input_grad, result, ovec = backward(layer_input, qkv, e, att, dos, bg, res, fa, hl, og, ai, sums, bsum)
        gq, gk, gv, go, gi, gr, input_grad, y, *vectors = finish(result, ovec, input_grad, y)
    else:
        input_grad, gx, go, sums = backward_local(layer_input, qkv, e, att, dos, bg, res, fa[0:3], sums)
        (gq, gk, gv, go, gi, gr), vectors = reduce_lax(g, gx, go, sums, bsum)
    return (
        y, input_grad, gq, vectors[0], gk, gv, vectors[1], go, vectors[2],
        vectors[3], vectors[4], gi, vectors[8], gr, vectors[5], vectors[6], vectors[7],
    )


def solution(mesh):
    placed = (
        P(("width", "shard"), None),
        P(("width", "shard"), None),
        P("width"),
        P("shard", None),
        P("shard"),
        P("shard", None),
        P("shard", None),
        P("shard"),
        P("shard", None),
        P("shard"),
        P("shard"),
        P("shard"),
        P("shard", None),
        P("shard"),
        P("shard", None),
        P("shard"),
        P("shard"),
        P("shard"),
        P(("width", "shard"), None),
    )
    return jax.shard_map(
        body,
        mesh=mesh,
        in_specs=placed,
        out_specs=(
            P(("width", "shard"), None),
            P(("width", "shard"), None),
            P("shard", None),
            P("shard"),
            P("shard", None),
            P("shard", None),
            P("shard"),
            P("shard", None),
            P("shard"),
            P("shard"),
            P("shard"),
            P("shard", None),
            P("shard"),
            P("shard", None),
            P("shard"),
            P("shard"),
            P("shard"),
        ),
        check_vma=False,
    )
```
